32 devices in a mesh: dp: 4 (over y, x), tensor: 8 (over z, core).
Axes of the slice: x: 2, y: 2, z: 4, core: 2. Of those that a mesh axis runs over, the one named last changes fastest.
Arguments:
- layer_input: bfloat16 [8192, 2048], P('dp', 'tensor'), may hold values from -6 to 6
- cotangent: bfloat16 [8192, 2048], P('dp', 'tensor'), may hold values from -6 to 6
- first_gain: bfloat16 [2048], P('dp'), may hold values from 0.099609375 to 1.8984375
- query_weight: bfloat16 [2048, 3072], P('dp', 'tensor'), may hold values from -0.125 to 0.125
- latent_down: bfloat16 [2048, 576], P('dp'), may hold values from -0.125 to 0.125
- latent_gain: bfloat16 [512], P('dp'), may hold values from 0.099609375 to 1.8984375
- latent_up: bfloat16 [512, 4096], P('dp', 'tensor'), may hold values from -0.25 to 0.25
- output_weight: bfloat16 [2048, 2048], P('tensor', 'dp'), may hold values from -1 to 1
- second_gain: bfloat16 [2048], P('dp'), may hold values from 0.099609375 to 1.8984375
- router_weight: bfloat16 [2048, 16], P('dp'), may hold values from -0.03125 to 0.03125
- expert_gate: bfloat16 [16, 2048, 1408], P(None, 'dp', 'tensor'), may hold values from -0.125 to 0.125
- expert_up: bfloat16 [16, 2048, 1408], P(None, 'dp', 'tensor'), may hold values from -0.125 to 0.125
- expert_down: bfloat16 [16, 1408, 2048], P(None, 'tensor', 'dp'), may hold values from -0.15625 to 0.15625
- shared_gate: bfloat16 [2048, 2816], P('dp', 'tensor'), may hold values from -0.125 to 0.125
- shared_up: bfloat16 [2048, 2816], P('dp', 'tensor'), may hold values from -0.125 to 0.125
- shared_down: bfloat16 [2816, 2048], P('tensor', 'dp'), may hold values from -0.109375 to 0.109375
- routes: int32 [8192, 6], P('dp'), may hold values from 0 to 15, all different within a row
Outputs:
- layer_output: bfloat16 [8192, 2048], P('dp', 'tensor')
- input_delta: float32 [8192, 2048], P('dp', 'tensor')
- first_gain_delta: float32 [2048], P('dp')
- query_weight_delta: float32 [2048, 3072], P('dp', 'tensor')
- latent_down_delta: float32 [2048, 576], P('dp')
- latent_gain_delta: float32 [512], P('dp')
- latent_up_delta: float32 [512, 4096], P('dp', 'tensor')
- output_weight_delta: float32 [2048, 2048], P('tensor', 'dp')
- second_gain_delta: float32 [2048], P('dp')
- router_weight_delta: float32 [2048, 16], P('dp')
- expert_gate_delta: float32 [16, 2048, 1408], P(None, 'dp', 'tensor')
- expert_up_delta: float32 [16, 2048, 1408], P(None, 'dp', 'tensor')
- expert_down_delta: float32 [16, 1408, 2048], P(None, 'tensor', 'dp')
- shared_gate_delta: float32 [2048, 2816], P('dp', 'tensor')
- shared_up_delta: float32 [2048, 2816], P('dp', 'tensor')
- shared_down_delta: float32 [2816, 2048], P('tensor', 'dp')
The draws below stay inside these ranges and needn't reach their ends.
Inputs may be any that keep to these rules, and one draw needn't show every extreme that they name: `routes`: each token names 6 different experts, in the order in which its pairs take slots; every expert is named by some token.
All inputs are finite; a program needn't handle non-finite values.
Results may differ from the reference program's by a relative error of at most 0.022.
Values may be sent and summed in bfloat16 or wider, within the bound.
No kernel may reach another device: no remote copies, remote signals or barrier semaphores. Data moves between devices by JAX's collectives and lax.ppermute only.
A program may use at most 1 GiB of HBM per device.

```python
import jax
import jax.numpy as jnp
from jax import lax

D = 2048
H = 16
DN = 128
DR = 64
DV = 128
R = 512
FE = 1408
FS = 2816
TOP = 6
E = 16
LEN = 1024
TOK = 2048
TOKENS = 8192
CAP = 864
N_DP = 4


def shard_levels(rng, dims, cuts, low, high):
    loudness, own = 1.0, jax.random.fold_in(rng, 6)
    for dim, parts in cuts:
        draws = jnp.exp(jax.random.uniform(jax.random.fold_in(own, dim), (parts,), jnp.float32, low / len(cuts), high / len(cuts)))
        loudness = loudness * jnp.repeat(draws, dims[dim] // parts).reshape([-1 if axis == dim else 1 for axis in range(len(dims))])
    return loudness


def distinct(key, rows, number_of, top, lift):
    order = jax.random.permutation(jax.random.fold_in(key, 1), number_of)
    boost = order
    for power in range(3):
        boost = boost * boost // number_of
    boost = boost * lift // number_of
    lots = jax.random.randint(jax.random.fold_in(key, 2), (rows, number_of), 0, 4096) + boost
    fixed_rows = jax.random.permutation(jax.random.fold_in(key, 3), rows)[jnp.arange(number_of) % rows]
    lots = jnp.where(jnp.arange(rows)[:, None] == fixed_rows[None, :], 1 << 14, lots)
    merit = lots * number_of + jnp.arange(number_of)
    return lax.top_k(merit.astype(jnp.int32), top)[1].astype(jnp.int32)


def normal_values(key, shape, deviation, reach, shards=(), kind=jnp.bfloat16):
    array = deviation * jax.random.normal(key, shape, jnp.float32)
    if shards:
        array = array * shard_levels(key, shape, shards, -0.22, 0.18)
    return jnp.clip(array, -reach, reach).astype(kind)


def setup_inputs(seed: int = 0) -> dict:
    seeds = jax.random.split(jax.random.key(seed), 18)
    return {
        "layer_input": normal_values(seeds[0], (TOKENS, D), 1.0, 6.0, ((0, 4), (1, 8))),
        "cotangent": normal_values(seeds[1], (TOKENS, D), 1.0, 6.0, ((0, 4), (1, 8))),
        "first_gain": jnp.clip(1.0 + 0.18 * jax.random.normal(seeds[2], (D,), jnp.float32), 0.099609375, 1.8984375).astype(jnp.bfloat16),
        "query_weight": normal_values(seeds[3], (D, H * (DN + DR)), D ** -0.5, 0.125, ((0, 4), (1, 8))),
        "latent_down": normal_values(seeds[4], (D, R + DR), D ** -0.5, 0.125, ((0, 4),)),
        "latent_gain": jnp.clip(1.0 + 0.18 * jax.random.normal(seeds[5], (R,), jnp.float32), 0.099609375, 1.8984375).astype(jnp.bfloat16),
        "latent_up": normal_values(seeds[6], (R, H * (DN + DV)), R ** -0.5, 0.25, ((0, 4), (1, 8))),
        "output_weight": normal_values(seeds[7], (H * DV, D), (H * DV // 64) ** -0.5, 1.0, ((0, 8), (1, 4))),
        "second_gain": jnp.clip(1.0 + 0.18 * jax.random.normal(seeds[8], (D,), jnp.float32), 0.099609375, 1.8984375).astype(jnp.bfloat16),
        "router_weight": normal_values(seeds[9], (D, E), (16 * D) ** -0.5, 0.03125, ((0, 4),)),
        "expert_gate": normal_values(seeds[10], (E, D, FE), D ** -0.5, 0.125, ((1, 4), (2, 8))),
        "expert_up": normal_values(seeds[11], (E, D, FE), D ** -0.5, 0.125, ((1, 4), (2, 8))),
        "expert_down": normal_values(seeds[12], (E, FE, D), FE ** -0.5, 0.15625, ((1, 8), (2, 4))),
        "shared_gate": normal_values(seeds[13], (D, FS), D ** -0.5, 0.125, ((0, 4), (1, 8))),
        "shared_up": normal_values(seeds[14], (D, FS), D ** -0.5, 0.125, ((0, 4), (1, 8))),
        "shared_down": normal_values(seeds[15], (FS, D), FS ** -0.5, 0.109375, ((0, 8), (1, 4))),
        "routes": distinct(seeds[16], TOKENS, E, TOP, 3072),
    }


EPSILON = 1e-06
HIGHEST = lax.Precision.HIGHEST

@jax.custom_vjp
def low(v):
    return lax.optimization_barrier(v.astype(jnp.bfloat16)).astype(jnp.float32)

@jax.custom_vjp
def low_back(v):
    return v

def low_keep(v):
    return (low(v), None)

def low_pass(kept, grad):
    return (grad,)

def back_keep(v):
    return (v, None)

def back_low(kept, grad):
    return (low(grad),)
low.defvjp(low_keep, low_pass)
low_back.defvjp(back_keep, back_low)

def normed(values, factor):
    return values * lax.rsqrt(lax.optimization_barrier(jnp.mean(values * values, axis=-1, keepdims=True)) + EPSILON) * factor

def angles(number, halfway):
    position = (jnp.arange(number, dtype=jnp.int32) % LEN).astype(jnp.float32)
    spread = 10000.0 ** (-jnp.arange(halfway, dtype=jnp.float32) / halfway)
    phases = position[:, None] * spread[None, :]
    return (jnp.cos(phases), jnp.sin(phases))

def rotate(values, cosine, sine_term):
    halfway = values.shape[-1] // 2
    leading = values[..., :halfway]
    trailing = values[..., halfway:]
    return jnp.concatenate([leading * cosine - trailing * sine_term, trailing * cosine + leading * sine_term], axis=-1)

def slot_plan(routes):
    number = routes.shape[0]
    flattened = routes.reshape(-1)
    matches = (flattened[:, None] == jnp.arange(E, dtype=jnp.int32)[None, :]).astype(jnp.int32)
    earlier = jnp.cumsum(matches, axis=0) - matches
    position = lax.optimization_barrier(jnp.sum(earlier * matches, axis=1))
    retained = position < CAP
    slot_index = jnp.where(retained, flattened * CAP + position, E * CAP).astype(jnp.int32)
    pair_owner = jnp.arange(number * TOP, dtype=jnp.int32) // TOP
    slot_owner = jnp.full((E * CAP + 1,), number, jnp.int32).at[slot_index].set(pair_owner)[:E * CAP]
    return (slot_index.reshape(number, TOP), retained.reshape(number, TOP), slot_owner)

def product(former, latter):
    return jnp.dot(former, latter, precision=HIGHEST)

def layer_forward(params, layer_input, routes):
    first_gain, query_weight, latent_down, latent_gain, latent_up, output_weight, second_gain, router_weight, expert_gate, expert_up, expert_down, shared_gate, shared_up, shared_down = params
    number = layer_input.shape[0]
    sequences = number // LEN
    cosine, sine_term = angles(number, DR // 2)
    first_round = low(normed(layer_input, first_gain))
    queries = low_back(product(first_round, query_weight)).reshape(number, H, DN + DR)
    queries = low(jnp.concatenate([queries[..., :DN], rotate(queries[..., DN:], cosine[:, None], sine_term[:, None])], axis=-1))
    compressed = low_back(product(first_round, latent_down))
    latent = low(normed(compressed[:, :R], latent_gain))
    rope_keys = low(rotate(compressed[:, R:], cosine, sine_term))
    keys_values = low(low_back(product(latent, latent_up))).reshape(number, H, DN + DV)
    keys_full = jnp.concatenate([keys_values[..., :DN], jnp.broadcast_to(rope_keys[:, None, :], (number, H, DR))], axis=-1)
    query_seq = queries.reshape(sequences, LEN, H, DN + DR)
    key_seq = keys_full.reshape(sequences, LEN, H, DN + DR)
    value_seq = keys_values[..., DN:].reshape(sequences, LEN, H, DV)
    scores = low_back(jnp.einsum('sihc,sjhc->shij', query_seq, key_seq, precision=HIGHEST) * (DN + DR) ** (-0.5))
    causal = jnp.arange(LEN)[:, None] >= jnp.arange(LEN)[None, :]
    scores = jnp.where(causal, scores, -1e+30)
    attend_weight = low(jax.nn.softmax(scores, axis=-1))
    mixed_rows = jnp.einsum('shij,sjhc->sihc', attend_weight, value_seq, precision=HIGHEST).reshape(number, H * DV)
    mixed_rows = low(low_back(mixed_rows))
    hidden_rows = layer_input + low_back(product(mixed_rows, output_weight))
    second_round = low(normed(hidden_rows, second_gain))
    gating = jax.nn.softmax(product(second_round, router_weight), axis=-1)
    slot_index, retained, slot_owner = slot_plan(routes)
    padded_rows = jnp.concatenate([second_round, jnp.zeros((1, D), jnp.float32)], axis=0)
    buffer = padded_rows[slot_owner].reshape(E, CAP, D)
    gate_hidden = low_back(jnp.einsum('ecd,edf->ecf', buffer, expert_gate, precision=HIGHEST))
    up_hidden = low_back(jnp.einsum('ecd,edf->ecf', buffer, expert_up, precision=HIGHEST))
    expert_act = low(jax.nn.silu(gate_hidden) * up_hidden)
    expert_result = low_back(jnp.einsum('ecf,efd->ecd', expert_act, expert_down, precision=HIGHEST)).reshape(E * CAP, D)
    expert_padded = jnp.concatenate([expert_result, jnp.zeros((1, D), jnp.float32)], axis=0)
    pair_weight = jnp.take_along_axis(gating, routes, axis=1) * retained.astype(jnp.float32)
    shared_pre = low_back(product(second_round, shared_gate))
    shared_lift = low_back(product(second_round, shared_up))
    shared_act = low(jax.nn.silu(shared_pre) * shared_lift)
    branch = low_back(product(shared_act, shared_down))
    for column in range(TOP):
        branch = branch + pair_weight[:, column:column + 1] * expert_padded[slot_index[:, column]]
    return hidden_rows + branch

def reference(layer_input, cotangent, first_gain, query_weight, latent_down, latent_gain, latent_up, output_weight, second_gain, router_weight, expert_gate, expert_up, expert_down, shared_gate, shared_up, shared_down, routes):
    params = jax.tree.map(lambda member: member.astype(jnp.float32), (first_gain, query_weight, latent_down, latent_gain, latent_up, output_weight, second_gain, router_weight, expert_gate, expert_up, expert_down, shared_gate, shared_up, shared_down))
    inputs_grouped = layer_input.astype(jnp.float32).reshape(N_DP, TOK, D)
    cotangent_grouped = cotangent.astype(jnp.float32).reshape(N_DP, TOK, D)
    routes_grouped = routes.reshape(N_DP, TOK, TOP)

    def one_group(running, pieces):
        group_input, group_cotangent, group_routes = pieces
        result, pullback = jax.vjp(lambda weights, row_block: layer_forward(weights, row_block, group_routes), params, group_input)
        weight_deltas, input_part = pullback(group_cotangent)
        running = jax.tree.map(lambda running_sum, member: running_sum + member, running, weight_deltas)
        return (running, (result.astype(jnp.bfloat16), input_part))
    starting = jax.tree.map(jnp.zeros_like, params)
    running, (outputs, input_parts) = lax.scan(one_group, starting, (inputs_grouped, cotangent_grouped, routes_grouped))
    return (outputs.reshape(TOKENS, D), input_parts.reshape(TOKENS, D), running[0], running[1], running[2], running[3], running[4], running[5], running[6], running[7], running[8], running[9], running[10], running[11], running[12], running[13])
```

```python
import jax
import jax.numpy as jnp
from jax import lax
from jax.sharding import PartitionSpec as P

D = 2048
DN = 128
DR = 64
DV = 128
R = 512
E = 16
LEN = 1024
CAP = 864
EPSILON = 1e-06
BF = jnp.bfloat16
F32 = jnp.float32


def dot(a, b, ca, cb, out=F32):
    return lax.dot_general(
        a, b, (((ca,), (cb,)), ((), ())), preferred_element_type=F32
    ).astype(out)


def angles(number, halfway):
    position = (jnp.arange(number, dtype=jnp.int32) % LEN).astype(F32)
    spread = 10000.0 ** (-jnp.arange(halfway, dtype=F32) / halfway)
    phases = position[:, None] * spread[None, :]
    return jnp.cos(phases), jnp.sin(phases)


def rotate(values, cosine, sine_term):
    halfway = values.shape[-1] // 2
    u, w = values[..., :halfway], values[..., halfway:]
    return jnp.concatenate([u * cosine - w * sine_term, w * cosine + u * sine_term], axis=-1)


class Line:
    def __init__(self):
        self.n = lax.axis_size("tensor")
        self.chips = self.n // 2
        index = lax.axis_index("tensor")
        self.index = index
        self.z = index // 2
        self.c = index % 2

    def swap(self, a):
        return lax.ppermute(a, "tensor", [(i, i ^ 1) for i in range(self.n)])

    def shift(self, a, step, sources):
        pairs = [
            (2 * s + c, 2 * (s + step) + c)
            for s in sources
            if 0 <= s + step < self.chips
            for c in (0, 1)
        ]
        return lax.ppermute(a, "tensor", pairs)

    def chip_gather(self, s):
        n = self.chips
        left, right = [s], [s]
        for k in range(1, n):
            left.append(self.shift(left[-1], 1, range(k - 1, n)))
            right.append(self.shift(right[-1], -1, range(0, n - k + 1)))
        return [s] + [jnp.where(self.z >= k, left[k], right[n - k]) for k in range(1, n)]

    def gather(self, s, order):
        n = self.chips
        own = self.chip_gather(s)
        out = jnp.zeros((self.n,) + s.shape, s.dtype)
        for k, piece in enumerate(own):
            other = self.swap(piece)
            chip = (self.z - k + n) % n
            start = (0,) * s.ndim
            out = lax.dynamic_update_slice(out, piece[None], (order(chip, self.c),) + start)
            out = lax.dynamic_update_slice(out, other[None], (order(chip, 1 - self.c),) + start)
        return out

    def chip_scatter(self, block):
        n = self.chips
        left = right = None
        for s in range(1, n):
            up = block(jnp.clip(n - s + self.z, 0, n - 1))
            down = block(jnp.clip(self.z - (n - s), 0, n - 1))
            if left is not None:
                up = (up.astype(F32) + left.astype(F32)).astype(BF)
                down = (down.astype(F32) + right.astype(F32)).astype(BF)
            left = self.shift(up, 1, range(0, s))
            right = self.shift(down, -1, range(n - s, n))
        return block(self.z).astype(F32) + left.astype(F32) + right.astype(F32)

    def row_scatter(self, p):
        half = p.shape[0] // 2
        ch = half // self.chips
        mine = lax.dynamic_slice_in_dim(p, self.c * half, half, 0)
        theirs = lax.dynamic_slice_in_dim(p, (1 - self.c) * half, half, 0)
        both = (mine.astype(F32) + self.swap(theirs).astype(F32)).astype(BF)
        return self.chip_scatter(lambda j: lax.dynamic_slice_in_dim(both, j * ch, ch, 0))

    def row_gather(self, s):
        out = self.gather(s, lambda chip, core: core * self.chips + chip)
        return out.reshape(self.n * s.shape[0], s.shape[1])

    def row_start(self, rows):
        ch = rows // self.n
        return (self.c * self.chips + self.z) * ch, ch

    def column_gather(self, s):
        out = self.gather(s, lambda chip, core: chip * 2 + core)
        return out.transpose(1, 0, 2).reshape(s.shape[0], self.n * s.shape[1])

    def column_scatter(self, p):
        rows, wide = p.shape
        ch = wide // self.n
        blocks = p.reshape(rows, self.chips, 2, ch).transpose(2, 1, 0, 3)
        mine = lax.dynamic_index_in_dim(blocks, self.c, 0, False)
        theirs = lax.dynamic_index_in_dim(blocks, 1 - self.c, 0, False)
        both = (mine.astype(F32) + self.swap(theirs).astype(F32)).astype(BF)
        return self.chip_scatter(lambda j: lax.dynamic_index_in_dim(both, j, 0, False))


def gather_rows(parts):
    packed = lax.all_gather(jnp.concatenate(parts, axis=0), "dp", axis=1, tiled=True)
    out, at = [], 0
    for part in parts:
        out.append(packed[at : at + part.shape[0]])
        at += part.shape[0]
    return out


def scatter_rows(parts):
    packed = jnp.concatenate([p.astype(BF) for p in parts], axis=0)
    summed = lax.psum_scatter(packed, "dp", scatter_dimension=1, tiled=True).astype(F32)
    out, at = [], 0
    for part in parts:
        out.append(summed[at : at + part.shape[0]])
        at += part.shape[0]
    return out


def ranks(mask):
    number = mask.shape[0]
    block = 128
    pieces = mask.reshape(number // block, block, E).astype(BF)
    lower = jnp.tril(jnp.ones((block, block), BF), -1)
    inside = jnp.einsum("ij,bje->bie", lower, pieces, preferred_element_type=F32)
    totals = jnp.sum(pieces.astype(F32), axis=1).astype(BF)
    ahead = jnp.tril(jnp.ones((number // block, number // block), BF), -1)
    before = dot(ahead, totals, 1, 0)
    return (inside + before[:, None, :]).reshape(number, E)


def per_device(
    layer_input, cotangent, first_gain, query_weight, latent_down, latent_gain, latent_up,
    output_weight, second_gain, router_weight, expert_gate, expert_up, expert_down,
    shared_gate, shared_up, shared_down, routes,
):
    line = Line()
    n_dp = lax.axis_size("dp")
    wide = D // n_dp
    number = layer_input.shape[0]
    sequences = number // LEN
    heads_here = output_weight.shape[0] // DV
    fe = expert_down.shape[1]
    my_columns = layer_input.shape[1]
    column_start = line.index * my_columns
    row_start, row_count = line.row_start(number)

    up_rows = latent_up.size // wide
    gains = jnp.zeros((16, wide), BF)
    gains = gains.at[0].set(first_gain).at[1].set(second_gain)
    gains = gains.at[2, : latent_gain.shape[0]].set(latent_gain)
    wq, wld, wup, gains, wr, wo = gather_rows(
        [query_weight.T, latent_down.T, latent_up.reshape(up_rows, wide), gains,
         router_weight.T, output_weight]
    )
    wup = wup.reshape(up_rows, n_dp, wide).transpose(1, 0, 2).reshape(R, -1)
    first_g = gains[0].astype(F32)
    second_g = gains[1].astype(F32)
    latent_g = gains[2].reshape(n_dp, wide)[:, : R // n_dp].reshape(R).astype(F32)

    eg = expert_gate.transpose(0, 2, 1)
    eu = expert_up.transpose(0, 2, 1)
    cut = E // 2
    packs = []
    for a, b in ((0, cut), (cut, E)):
        packs.append([m[a:b].reshape((b - a) * fe, wide) for m in (eg, eu, expert_down)])
    packs[-1] += [shared_gate.T, shared_up.T, shared_down]
    packs = [gather_rows(p) for p in packs]

    rows = line.column_gather(layer_input)
    v1 = rows.astype(F32)
    r1 = lax.rsqrt(jnp.mean(v1 * v1, axis=-1, keepdims=True) + EPSILON)
    first_round = (v1 * r1 * first_g).astype(BF)
    cosine, sine_term = angles(number, DR // 2)
    raw = dot(first_round, wq, 1, 1).reshape(number, heads_here, DN + DR)
    queries = jnp.concatenate(
        [raw[..., :DN], rotate(raw[..., DN:], cosine[:, None], sine_term[:, None])], axis=-1
    ).astype(BF)
    compressed = dot(first_round, wld, 1, 1)
    vl = compressed[:, :R]
    rl = lax.rsqrt(jnp.mean(vl * vl, axis=-1, keepdims=True) + EPSILON)
    latent = (vl * rl * latent_g).astype(BF)
    rope_keys = rotate(compressed[:, R:], cosine, sine_term).astype(BF)
    keys_values = dot(latent, wup, 1, 0, BF).reshape(number, heads_here, DN + DV)
    query_seq = queries.reshape(sequences, LEN, heads_here, DN + DR)
    nope_seq = keys_values[..., :DN].reshape(sequences, LEN, heads_here, DN)
    value_seq = keys_values[..., DN:].reshape(sequences, LEN, heads_here, DV)
    rope_seq = rope_keys.reshape(sequences, LEN, DR)
    scaling = (DN + DR) ** (-0.5)
    causal = jnp.arange(LEN)[:, None] >= jnp.arange(LEN)[None, :]

    def scores_of():
        content = jnp.einsum("sihc,sjhc->shij", query_seq[..., :DN], nope_seq, preferred_element_type=F32)
        content = content + jnp.einsum("sihc,sjc->shij", query_seq[..., DN:], rope_seq, preferred_element_type=F32)
        return jnp.where(causal, content * scaling, -1e30)

    scores = scores_of()
    highest = jnp.max(scores, axis=-1, keepdims=True)
    expanded = jnp.exp(scores - highest)
    totals = jnp.sum(expanded, axis=-1, keepdims=True)
    attend_weight = (expanded / totals).astype(BF)
    log_total = highest + jnp.log(totals)
    mixed = jnp.einsum("shij,sjhc->sihc", attend_weight, value_seq, preferred_element_type=F32)
    mixed = mixed.reshape(number, heads_here * DV).astype(BF)
    attend_rows = line.row_scatter(dot(mixed, wo, 1, 0, BF))
    hidden_chunk = lax.dynamic_slice_in_dim(rows, row_start, row_count, 0).astype(F32) + attend_rows
    hidden = line.row_gather(hidden_chunk.astype(BF))

    v2 = hidden.astype(F32)
    r2 = lax.rsqrt(jnp.mean(v2 * v2, axis=-1, keepdims=True) + EPSILON)
    second_round = (v2 * r2 * second_g).astype(BF)
    gating = jax.nn.softmax(dot(second_round, wr, 1, 1), axis=-1)
    named = jnp.any(routes[:, :, None] == jnp.arange(E, dtype=jnp.int32)[None, None, :], axis=1)
    kept = jnp.where(named & (ranks(named) < CAP), 1.0, 0.0)
    pair_weight = gating * kept
    grad = line.column_gather(cotangent)

    def hidden_units(second_round, grad, gate, up, down, weight):
        pre = dot(second_round, gate, 1, 1)
        lift = dot(second_round, up, 1, 1)
        back = dot(grad, down, 1, 1)
        s = jax.nn.sigmoid(pre)
        silu = pre * s
        act = silu * lift
        pair = None
        if weight is not None:
            count = weight.shape[1]
            pair = jnp.sum((act * back).reshape(number, count, fe), axis=-1)
            spread = jnp.broadcast_to(weight[:, :, None], (number, count, fe)).reshape(number, count * fe)
            act = act * spread
            back = back * spread
        act = act.astype(BF)
        pre_delta = (back * lift * (s * (1.0 + pre * (1.0 - s)))).astype(BF)
        lift_delta = (back * silu).astype(BF)
        out = dot(act, down, 1, 0)
        second = dot(pre_delta, gate, 1, 0) + dot(lift_delta, up, 1, 0)
        deltas = [dot(pre_delta, second_round, 0, 0, BF), dot(lift_delta, second_round, 0, 0, BF), dot(act, grad, 0, 0, BF)]
        return out, second, pair, deltas

    first_half = hidden_units(second_round, grad, *packs[0], pair_weight[:, :cut])
    first_deltas, (again_round, again_grad) = lax.optimization_barrier(
        (first_half[3], (second_round, grad))
    )
    half_deltas = [scatter_rows(first_deltas)]
    second_half = hidden_units(again_round, again_grad, *packs[1][:3], pair_weight[:, cut:])
    shared = hidden_units(again_round, again_grad, *packs[1][3:], None)
    branch = (first_half[0] + second_half[0] + shared[0]).astype(BF)
    second_terms = (first_half[1] + second_half[1] + shared[1]).astype(BF)
    pair_terms = jnp.concatenate([first_half[2], second_half[2]], axis=1)

    pad = jnp.zeros((number, 128 - E), BF)
    summed = line.row_scatter(jnp.concatenate([second_terms, pair_terms.astype(BF), pad], axis=1))

    def own_rows(a):
        return lax.dynamic_slice_in_dim(a, row_start, row_count, 0)

    gating_rows, kept_rows, x2 = own_rows(gating), own_rows(kept), own_rows(second_round)
    u = summed[:, D : D + E] * kept_rows
    logits_delta = gating_rows * (u - jnp.sum(gating_rows * u, axis=-1, keepdims=True))
    router_delta = dot(logits_delta.astype(BF), x2, 0, 0)
    d2 = summed[:, :D] + dot(logits_delta.astype(BF), wr, 1, 0)
    v2_rows, r2_rows = own_rows(hidden).astype(F32), own_rows(r2)
    vgd = jnp.mean(v2_rows * second_g * d2, axis=-1, keepdims=True)
    second_gain_delta = jnp.sum(d2 * v2_rows * r2_rows, axis=0)
    hidden_delta_rows = own_rows(grad).astype(F32) + r2_rows * second_g * d2 - v2_rows * (r2_rows**3) * vgd
    hidden_delta = line.row_gather(hidden_delta_rows.astype(BF))
    hidden_delta, late_deltas, half_deltas[0] = lax.optimization_barrier(
        (hidden_delta, second_half[3] + shared[3], half_deltas[0])
    )
    half_deltas.append(scatter_rows(late_deltas))

    branch_share = line.column_scatter(branch)
    layer_output = (
        lax.dynamic_slice_in_dim(hidden, column_start, my_columns, 1).astype(F32) + branch_share
    ).astype(BF)

    delta_wo = dot(mixed, hidden_delta, 0, 0)
    delta_mixed = dot(hidden_delta, wo, 1, 1, BF).reshape(sequences, LEN, heads_here, DV)
    again = jnp.exp(scores_of() - log_total)
    delta_values = jnp.einsum("shij,sihc->sjhc", again.astype(BF), delta_mixed, preferred_element_type=F32)
    delta_weight = jnp.einsum("sihc,sjhc->shij", delta_mixed, value_seq, preferred_element_type=F32)
    row_dot = jnp.sum(again * delta_weight, axis=-1, keepdims=True)
    delta_scores = (again * (delta_weight - row_dot)).astype(BF)
    dq_content = jnp.einsum("shij,sjhc->sihc", delta_scores, nope_seq, preferred_element_type=F32) * scaling
    dq_rope = jnp.einsum("shij,sjc->sihc", delta_scores, rope_seq, preferred_element_type=F32) * scaling
    dk_content = jnp.einsum("shij,sihc->sjhc", delta_scores, query_seq[..., :DN], preferred_element_type=F32) * scaling
    dk_rope = jnp.einsum("shij,sihc->sjc", delta_scores, query_seq[..., DN:], preferred_element_type=F32) * scaling
    dq_content = dq_content.reshape(number, heads_here, DN)
    dq_rope = rotate(dq_rope.reshape(number, heads_here, DR), cosine[:, None], -sine_term[:, None])
    delta_queries = jnp.concatenate([dq_content, dq_rope], axis=-1)
    query_dot = jnp.sum(delta_queries * raw, axis=(1, 2))[:, None]
    delta_queries = delta_queries.reshape(number, heads_here * (DN + DR)).astype(BF)
    delta_pairs = (
        jnp.concatenate([dk_content, delta_values], axis=-1).reshape(number, heads_here * (DN + DV)).astype(BF)
    )
    delta_wq = dot(delta_queries, first_round, 0, 0)
    first_terms = dot(delta_queries, wq, 1, 0, BF)
    delta_wup = dot(latent, delta_pairs, 0, 0)
    latent_terms = dot(delta_pairs, wup, 1, 1, BF)
    small = jnp.concatenate(
        [latent_terms, dk_rope.reshape(number, DR).astype(BF), query_dot.astype(BF), jnp.zeros((number, 63), BF)], axis=1
    )
    small, first_terms, layer_output = lax.optimization_barrier((small, first_terms, layer_output))
    small = line.row_scatter(small)
    dl = small[:, :R]
    vl_rows, rl_rows = own_rows(vl), own_rows(rl)
    latent_gain_delta = jnp.sum(dl * vl_rows * rl_rows, axis=0)
    head = rl_rows * latent_g * dl - vl_rows * (rl_rows**3) * jnp.mean(vl_rows * latent_g * dl, axis=-1, keepdims=True)
    tail = rotate(small[:, R : R + DR], own_rows(cosine), -own_rows(sine_term))
    dots = small[:, R + DR : R + DR + 1] + jnp.sum(jnp.concatenate([head, tail], axis=1) * own_rows(compressed), axis=-1, keepdims=True)
    small = jnp.concatenate([head, tail, dots, jnp.zeros((row_count, 63), F32)], axis=1).astype(BF)
    small = line.row_gather(small)
    delta_compressed = small[:, : R + DR]
    dots = small[:, R + DR : R + DR + 1].astype(F32)
    delta_wld = dot(delta_compressed, first_round, 0, 0)
    first_share = line.column_scatter(first_terms)
    first_share = first_share + dot(delta_compressed, lax.dynamic_slice_in_dim(wld, column_start, my_columns, 1), 1, 0)
    vc = layer_input.astype(F32)
    gc = lax.dynamic_slice_in_dim(first_g, column_start, my_columns, 0)
    input_delta = (
        lax.dynamic_slice_in_dim(hidden_delta, column_start, my_columns, 1).astype(F32)
        + r1 * gc * first_share
        - vc * (r1 * r1) * (dots / D)
    )
    first_gain_delta = lax.dynamic_update_slice(
        jnp.zeros((D,), F32), jnp.sum(first_share * vc * r1, axis=0), (column_start,)
    )
    vectors = jnp.concatenate(
        [router_delta, second_gain_delta[None], first_gain_delta[None],
         jnp.zeros((1, D), F32).at[0, :R].set(latent_gain_delta)], axis=0
    )
    vectors = lax.psum(vectors, ("dp", "tensor"))
    dp_index = lax.axis_index("dp")
    mine = lax.dynamic_slice_in_dim(vectors, dp_index * wide, wide, 1)
    my_latent = R // n_dp
    latent_gain_out = lax.dynamic_slice_in_dim(vectors[E + 2], dp_index * my_latent, my_latent, 0)

    wup_pack = delta_wup.reshape(n_dp, up_rows, wide).transpose(1, 0, 2).reshape(up_rows, D)
    attend_deltas, half_deltas[1] = lax.optimization_barrier(
        ([delta_wo.astype(BF), delta_wq.astype(BF), wup_pack.astype(BF), delta_wld.astype(BF)], half_deltas[1])
    )
    dwo, dwq, dwup, dwld = scatter_rows(attend_deltas)

    def expert_delta(i):
        return jnp.concatenate([half_deltas[0][i], half_deltas[1][i]], axis=0).reshape(E, fe, wide)

    return (
        layer_output, input_delta, mine[E + 1], dwq.T, dwld.T, latent_gain_out,
        dwup.reshape(latent_up.shape), dwo, mine[E], mine[:E].T,
        expert_delta(0).transpose(0, 2, 1), expert_delta(1).transpose(0, 2, 1), expert_delta(2),
        half_deltas[1][3].T, half_deltas[1][4].T, half_deltas[1][5],
    )


def solution(mesh):
    in_specs = (
        P("dp", "tensor"), P("dp", "tensor"), P("dp"), P("dp", "tensor"), P("dp", None), P("dp"),
        P("dp", "tensor"), P("tensor", "dp"), P("dp"), P("dp", None), P(None, "dp", "tensor"),
        P(None, "dp", "tensor"), P(None, "tensor", "dp"), P("dp", "tensor"), P("dp", "tensor"),
        P("tensor", "dp"), P("dp", None),
    )
    out_specs = (
        P("dp", "tensor"), P("dp", "tensor"), P("dp"), P("dp", "tensor"), P("dp", None), P("dp"),
        P("dp", "tensor"), P("tensor", "dp"), P("dp"), P("dp", None), P(None, "dp", "tensor"),
        P(None, "dp", "tensor"), P(None, "tensor", "dp"), P("dp", "tensor"), P("dp", "tensor"),
        P("tensor", "dp"),
    )
    return jax.shard_map(
        per_device, mesh=mesh, in_specs=in_specs, out_specs=out_specs, check_vma=False
    )
```

```python
import functools

import jax
import jax.numpy as jnp
import numpy as np
from jax import lax
from jax.experimental import pallas as pl
from jax.experimental.pallas import tpu as pltpu
from jax.sharding import PartitionSpec as P

D = 2048
DN = 128
DR = 64
DV = 128
R = 512
E = 16
LEN = 1024
CAP = 864
EPSILON = 1e-06
SCALE = (DN + DR) ** -0.5
BLOCK = 256
BF = jnp.bfloat16
F32 = jnp.float32


def dot(a, b, ca, cb, out=F32):
    return lax.dot_general(
        a, b, (((ca,), (cb,)), ((), ())), preferred_element_type=F32
    ).astype(out)


VMEM_LIMIT = 58 * 2**20
NT=(((1,),(1,)),((),()))
NN=(((1,),(0,)),((),()))
TN=(((0,),(0,)),((),()))

def mm(a,b,dims):
    return lax.dot_general(a,b,dims,preferred_element_type=F32)

def params(n):
    return pltpu.CompilerParams(dimension_semantics=("arbitrary",)*n, vmem_limit_bytes=VMEM_LIMIT)

def once(shape, index):
    return pl.BlockSpec(shape, index, pipeline_mode=pl.Buffered(1))

def place_matrix(fe, first, count, n):
    col=lax.broadcasted_iota(jnp.int32,(E,n),1); row=(lax.broadcasted_iota(jnp.int32,(E,n),0)-first)*fe
    return jnp.where((col>=row)&(col<row+fe)&(row<count*fe),1.0,0.0).astype(BF)

def units_kernel(fe, first, count, x_ref, wg_ref, wu_ref, b_ref, w_ref, out_ref, pair_ref):
    x=x_ref[...]; n=wg_ref.shape[0]
    pre=mm(x,wg_ref[...],NT); lift=mm(x,wu_ref[...],NT); back=b_ref[...].astype(F32)
    w=w_ref[...]; hi=w.astype(BF); lo=(w-hi.astype(F32)).astype(BF)
    place=place_matrix(fe,first,count,n)
    spread=mm(jnp.concatenate([hi,lo],axis=1),jnp.concatenate([place,place],axis=0),NN)
    if count*fe<n:
        spread=jnp.where(lax.broadcasted_iota(jnp.int32,spread.shape,1)>=count*fe,1.0,spread)
    s=0.5+0.5*jnp.tanh(0.5*pre)
    silu=pre*s
    act=silu*lift
    pair_ref[...]=mm((act*back).astype(BF),place,NT)
    back=back*spread
    out_ref[0]=(back*lift*(s+silu*(1.0-s))).astype(BF)
    out_ref[1]=(back*silu).astype(BF)
    out_ref[2]=(act*spread).astype(BF)

def units(x,packed,back,weight,fe,first,count,bt):
    T,D=x.shape; n=back.shape[1]; r=weight.shape[1]
    ins=[pl.BlockSpec((bt,D),lambda i:(i,0))]+[once((n,D),lambda i,k=k:(k,0)) for k in range(2)]
    ins+=[pl.BlockSpec((bt,n),lambda i:(i,0)),pl.BlockSpec((bt,r),lambda i:(i,0))]
    outs=[jax.ShapeDtypeStruct((3,T,n),BF),jax.ShapeDtypeStruct((T,r),F32)]
    return pl.pallas_call(functools.partial(units_kernel,fe,first,count),grid=(T//bt,),in_specs=ins,
        out_specs=[pl.BlockSpec((3,bt,n),lambda i:(0,i,0)),pl.BlockSpec((bt,r),lambda i:(i,0))],out_shape=outs,
        compiler_params=params(1),
        cost_estimate=pl.CostEstimate(flops=4*T*D*n,bytes_accessed=2*(T*D+2*n*D+4*T*n),transcendentals=T*n))(x,packed,packed,back,weight)

def lift_kernel(g_ref,w_ref,o_ref):
    o_ref[...]=mm(g_ref[...],w_ref[...],NT).astype(BF)

def lift_back(g,packed,at,n,bt):
    T,D=g.shape
    return pl.pallas_call(lift_kernel,grid=(T//bt,),
        in_specs=[pl.BlockSpec((bt,D),lambda i:(i,0)),once((n,D),lambda i:(at,0))],
        out_specs=pl.BlockSpec((bt,n),lambda i:(i,0)),out_shape=jax.ShapeDtypeStruct((T,n),BF),compiler_params=params(1),
        cost_estimate=pl.CostEstimate(flops=2*T*D*n,bytes_accessed=2*(T*D+n*D+T*n),transcendentals=0))(g,packed)

def back_kernel(pairs, added, beside, *refs):
    out=refs[-1]
    acc=None
    if added: acc=refs[0][...].astype(F32)
    rs=refs[added:]
    for k in range(pairs):
        a=rs[2*k]; b=rs[2*k+1]
        a=a[0] if len(a.shape)==3 else a[...]
        p=mm(a,b[...],NN)
        acc=p if acc is None else acc+p
    if beside:
        wide=acc.shape[1]
        out[:,:wide]=acc.astype(out.dtype)
        more=sum(r[...] for r in refs[-1-beside:-1])
        gap=jnp.zeros((acc.shape[0],out.shape[1]-wide-more.shape[1]),F32)
        out[:,wide:]=jnp.concatenate([more,gap],axis=1).astype(out.dtype)
    else:
        out[...]=acc.astype(out.dtype)

def core_kernel(pairs, core_ref, *refs):
    out=refs[-1]
    chips,_,w=out.shape
    for z in range(chips):
        at=pl.ds(pl.multiple_of((2*z+core_ref[0])*w,w),w)
        acc=None
        for k in range(pairs):
            a=refs[2*k]; b=refs[2*k+1]
            p=mm(a[0] if len(a.shape)==3 else a[...],b[:,at],NN)
            acc=p if acc is None else acc+p
        out[z]=acc.astype(BF)

def back(terms, added, out_dtype, bt, beside=(), core=None, chips=0):
    T=terms[0][0].shape[-2]; D=terms[0][2].shape[1]
    ins=[];args=[];fl=0;by=0
    if core is not None:
        ins.append(pl.BlockSpec(memory_space=pltpu.SMEM)); args.append(core)
    if added is not None:
        ins.append(pl.BlockSpec((bt,D),lambda i:(i,0))); args.append(added)
    for st,k,packed,n,at in terms:
        if st.ndim==3: ins.append(pl.BlockSpec((1,bt,n),lambda i,k=k:(k,i,0)))
        else: ins.append(pl.BlockSpec((bt,n),lambda i:(i,0)))
        ins.append(once((n,D),lambda i,at=at:(at,0)))
        args+= [st,packed]; fl+=2*T*D*n; by+=2*(T*n+n*D)
    for more in beside:
        ins.append(pl.BlockSpec((bt,more.shape[1]),lambda i:(i,0))); args.append(more)
    body=functools.partial(back_kernel,len(terms),0 if added is None else 1,len(beside))
    if beside:
        shape=(T,D+128); ospec=pl.BlockSpec((bt,D+128),lambda i:(i,0))
    elif core is not None:
        w=D//(2*chips); fl//=2
        shape=(chips,T,w); ospec=pl.BlockSpec((chips,bt,w),lambda i:(0,i,0))
        body=functools.partial(core_kernel,len(terms))
    else:
        shape=(T,D); ospec=pl.BlockSpec((bt,D),lambda i:(i,0))
    return pl.pallas_call(body,grid=(T//bt,),in_specs=ins,out_specs=ospec,out_shape=jax.ShapeDtypeStruct(shape,out_dtype),
        compiler_params=params(1),cost_estimate=pl.CostEstimate(flops=fl,bytes_accessed=by+4*T*D,transcendentals=0))(*args)

def outer_kernel(s_ref,x_ref,*refs):
    refs[-1][...]=mm(s_ref[0],x_ref[...],TN).astype(BF)

def outer(stack,first,count,x,total,at,into=None,bc=512):
    T,D=x.shape; n=stack.shape[2]
    ins=[pl.BlockSpec((1,T,n),lambda k,j:(first+k,0,0)),pl.BlockSpec((T,bc),lambda k,j:(0,j))]
    args=[stack,x]; al={}
    if into is not None:
        ins.append(pl.BlockSpec(memory_space=pl.ANY)); args.append(into); al={2:0}
    return pl.pallas_call(outer_kernel,grid=(count,D//bc),in_specs=ins,
        out_specs=pl.BlockSpec((n,bc),lambda k,j:(at+k,j)),out_shape=jax.ShapeDtypeStruct((total,D),BF),
        input_output_aliases=al,compiler_params=params(2),
        cost_estimate=pl.CostEstimate(flops=2*count*T*D*n,bytes_accessed=2*count*(T*n+n*D+T*D),transcendentals=0))(*args)


def place_columns_kernel(chips, norm, at_ref, *refs):
    pieces=refs[:2*chips]
    refs=refs[2*chips:]
    if norm:
        gain_ref, out_ref, round_ref, r_ref = refs
    else:
        (out_ref,) = refs
    w=pieces[0].shape[1]
    for k in range(2*chips):
        out_ref[:,pl.ds(pl.multiple_of(at_ref[k]*w,w),w)]=pieces[k][...]
    if norm:
        v=out_ref[...].astype(F32)
        r=lax.rsqrt(jnp.mean(v*v,axis=-1,keepdims=True)+EPSILON)
        round_ref[...]=(v*r*gain_ref[...]).astype(BF)
        r_ref[...]=r

def place_columns(pieces, at, gain=None, bt=256):
    T,w=pieces[0].shape; n=len(pieces)
    ins=[pl.BlockSpec(memory_space=pltpu.SMEM)]+[pl.BlockSpec((bt,w),lambda i:(i,0))]*n
    args=[at]+list(pieces)
    outs=[jax.ShapeDtypeStruct((T,n*w),BF)]; specs=[pl.BlockSpec((bt,n*w),lambda i:(i,0))]
    if gain is not None:
        ins.append(pl.BlockSpec((1,n*w),lambda i:(0,0))); args.append(gain[None])
        outs+=[jax.ShapeDtypeStruct((T,n*w),BF),jax.ShapeDtypeStruct((T,1),F32)]
        specs+=[pl.BlockSpec((bt,n*w),lambda i:(i,0)),pl.BlockSpec((bt,1),lambda i:(i,0))]
    return pl.pallas_call(functools.partial(place_columns_kernel,n//2,gain is not None),grid=(T//bt,),
        in_specs=ins,out_specs=specs,out_shape=outs,compiler_params=params(1),
        cost_estimate=pl.CostEstimate(flops=6*T*n*w,bytes_accessed=6*T*n*w,transcendentals=T))(*args)

def place_rows_kernel(n, at_ref, *refs):
    pieces=refs[:n]; out_ref=refs[n]; sem=refs[n+1]
    rows=pieces[0].shape[0]
    copies=[pltpu.make_async_copy(pieces[k],out_ref.at[pl.ds(pl.multiple_of(at_ref[k]*rows,rows),rows)],sem.at[k]) for k in range(n)]
    for c in copies: c.start()
    for c in copies: c.wait()

def place_rows(pieces, at):
    rows,w=pieces[0].shape; n=len(pieces)
    return pl.pallas_call(functools.partial(place_rows_kernel,n),
        in_specs=[pl.BlockSpec(memory_space=pltpu.SMEM)]+[pl.BlockSpec(memory_space=pltpu.VMEM)]*n,
        out_specs=pl.BlockSpec(memory_space=pl.ANY),out_shape=jax.ShapeDtypeStruct((n*rows,w),BF),
        scratch_shapes=[pltpu.SemaphoreType.DMA((n,))],compiler_params=pltpu.CompilerParams(vmem_limit_bytes=VMEM_LIMIT),
        cost_estimate=pl.CostEstimate(flops=0,bytes_accessed=4*n*rows*w,transcendentals=0))(at,*pieces)

def norm_rows_kernel(n, at_ref, col_ref, gain_ref, wr_ref, kept_ref, *refs):
    pieces=refs[:n]; round_ref,cols_ref,gating_ref,weight_ref,made,cut,sem,sem2=refs[n:]
    rows=pieces[0].shape[0]; w=cut.shape[2]
    copies=[]
    for k in range(n):
        v=pieces[k][...].astype(F32)
        r=lax.rsqrt(jnp.mean(v*v,axis=-1,keepdims=True)+EPSILON)
        made[k]=(v*r*gain_ref[...]).astype(BF)
        cut[k]=pieces[k][:,pl.ds(pl.multiple_of(col_ref[0]*w,w),w)]
        to=pl.ds(pl.multiple_of(at_ref[k]*rows,rows),rows)
        copies.append(pltpu.make_async_copy(made.at[k],round_ref.at[to],sem.at[k]))
        copies.append(pltpu.make_async_copy(cut.at[k],cols_ref.at[to],sem2.at[k]))
        copies[-2].start(); copies[-1].start()
        logits=mm(made[k],wr_ref[...],NT)
        e=jnp.exp(logits-jnp.max(logits,axis=-1,keepdims=True))
        gating=e/jnp.sum(e,axis=-1,keepdims=True)
        gating_ref[to]=gating
        weight_ref[to]=gating*kept_ref[to]
    for c in copies: c.wait()

def norm_rows(pieces, at, column, w, gain, router, kept):
    rows,wide=pieces[0].shape; n=len(pieces)
    vmem=pl.BlockSpec(memory_space=pltpu.VMEM)
    return pl.pallas_call(functools.partial(norm_rows_kernel,n),
        in_specs=[pl.BlockSpec(memory_space=pltpu.SMEM)]*2+[vmem]*(n+3),
        out_specs=[pl.BlockSpec(memory_space=pl.ANY)]*2+[vmem]*2,
        out_shape=[jax.ShapeDtypeStruct((n*rows,wide),BF),jax.ShapeDtypeStruct((n*rows,w),BF)]+[jax.ShapeDtypeStruct((n*rows,E),F32)]*2,
        scratch_shapes=[pltpu.VMEM((n,rows,wide),BF),pltpu.VMEM((n,rows,w),BF),pltpu.SemaphoreType.DMA((n,)),pltpu.SemaphoreType.DMA((n,))],
        compiler_params=pltpu.CompilerParams(vmem_limit_bytes=VMEM_LIMIT),
        cost_estimate=pl.CostEstimate(flops=6*n*rows*wide,bytes_accessed=4*n*rows*wide,transcendentals=n*rows))(at,column,gain[None],router,kept,*pieces)

def latent_back_kernel(small_ref, proj_ref, gain_ref, cos_ref, sin_ref, delta_ref, dots_ref, gain_delta_ref):
    i=pl.program_id(0)
    at=proj_ref.shape[1]-R-DN
    dl=small_ref[:,:R].astype(F32)
    vl=proj_ref[:,at:at+R]
    rl=lax.rsqrt(jnp.mean(vl*vl,axis=-1,keepdims=True)+EPSILON)
    gain=gain_ref[...]
    part=jnp.sum(dl*vl*rl,axis=0,keepdims=True)
    @pl.when(i==0)
    def _(): gain_delta_ref[...]=part
    @pl.when(i>0)
    def _(): gain_delta_ref[...]+=part
    gd=gain*dl
    head=rl*gd-vl*(rl*rl*rl)*jnp.mean(vl*gd,axis=-1,keepdims=True)
    beyond=small_ref[:,R:]
    row=lax.broadcasted_iota(jnp.int32,(DN,DN),0); col=lax.broadcasted_iota(jnp.int32,(DN,DN),1)
    h=DR//2
    put=jnp.where(((row<h)&(col==row))|((row>=h)&(row<DR)&(col==row+h)),1.0,0.0).astype(BF)
    spread=mm(beyond,put,NN)
    tail=spread*cos_ref[...]-pltpu.roll(spread,DR,1)*sin_ref[...]
    delta_ref[:,:R]=head.astype(BF)
    delta_ref[:,R:]=tail.astype(BF)
    own=jnp.sum(head*vl,axis=-1,keepdims=True)+jnp.sum(tail*proj_ref[:,at+R:],axis=-1,keepdims=True)
    lane=lax.broadcasted_iota(jnp.int32,beyond.shape,1)
    dots_ref[...]=own+jnp.sum(jnp.where(lane==DR,beyond.astype(F32),0.0),axis=-1,keepdims=True)

def latent_back(small, proj, gain, cosine, sine, bt=512):
    T,wide=small.shape; turns=LEN//bt
    return pl.pallas_call(latent_back_kernel,grid=(T//bt,),
        in_specs=[pl.BlockSpec((bt,wide),lambda i:(i,0)),pl.BlockSpec((bt,proj.shape[1]),lambda i:(i,0)),
                  pl.BlockSpec((1,R),lambda i:(0,0)),pl.BlockSpec((bt,DN),lambda i:(i%turns,0)),pl.BlockSpec((bt,DN),lambda i:(i%turns,0))],
        out_specs=[pl.BlockSpec((bt,R+DN),lambda i:(i,0)),pl.BlockSpec((bt,1),lambda i:(i,0)),pl.BlockSpec((1,R),lambda i:(0,0))],
        out_shape=[jax.ShapeDtypeStruct((T,R+DN),BF),jax.ShapeDtypeStruct((T,1),F32),jax.ShapeDtypeStruct((1,R),F32)],
        compiler_params=params(1),
        cost_estimate=pl.CostEstimate(flops=30*T*wide,bytes_accessed=8*T*wide,transcendentals=T))(small,proj,gain,cosine,sine)

def last_pack_kernel(delta_ref, x_ref, w_ref, small_ref, g_ref, latent_ref, out_ref):
    n=delta_ref.shape[1]
    d=mm(delta_ref[...],x_ref[...],TN)
    out_ref[:n]=d.astype(BF)
    sums=jnp.sum(w_ref[...].astype(F32)*d,axis=0,keepdims=True)
    row=lax.broadcasted_iota(jnp.int32,(32,DN),0); col=lax.broadcasted_iota(jnp.int32,(32,DN),1)
    at=DR+1
    pick=((row<E)&(col==row+at+2))|((row==E)&(col==at))|((row==E+1)&(col==at+1))
    v=mm(jnp.where(pick,1.0,0.0).astype(BF),small_ref[...],NT)
    line=lax.broadcasted_iota(jnp.int32,v.shape,0)
    v=jnp.where(line==E+1,(v+sums)/g_ref[...],v)
    out_ref[n:]=jnp.where(line==E+2,latent_ref[...],v).astype(BF)

def last_pack(delta, x, w, small, gain, latent_row, bc=512):
    T,D=x.shape; n=delta.shape[1]
    def cols(a): return pl.BlockSpec((a.shape[0],bc),lambda j:(0,j))
    return pl.pallas_call(last_pack_kernel,grid=(D//bc,),
        in_specs=[pl.BlockSpec((T,n),lambda j:(0,0)),cols(x),cols(w),pl.BlockSpec((bc,DN),lambda j:(j,R//DN)),cols(gain),cols(latent_row)],
        out_specs=pl.BlockSpec((n+32,bc),lambda j:(0,j)),out_shape=jax.ShapeDtypeStruct((n+32,D),BF),
        compiler_params=params(1),
        cost_estimate=pl.CostEstimate(flops=2*T*D*n,bytes_accessed=2*(T*D+2*n*D+T*n),transcendentals=0))(delta,x,w,small,gain,latent_row)


def turn(x, cosine, sine):
    return x*cosine+pltpu.roll(x,64,1)*sine

def slot_mask(shape, head):
    lane=lax.broadcasted_iota(jnp.int32,shape,1)
    low=head*(DR//2)
    inside=((lane>=low)&(lane<low+DR//2))|((lane>=low+DR)&(lane<low+DR+DR//2))
    return inside

def causal_scores(q, k, first):
    s=mm(q,k,NT)*SCALE
    row=lax.broadcasted_iota(jnp.int32,s.shape,0)+first
    col=lax.broadcasted_iota(jnp.int32,s.shape,1)
    return jnp.where(col<=row,s,-1e30)

def attend_kernel(heads, proj_ref, up_ref, gain_ref, cos_ref, sin_ref, q_ref, kr_ref, kv_ref, latent_ref, mixed_ref, lse_ref):
    content=heads*DN
    at=content+DN
    q_ref[:,:content]=proj_ref[:,:content].astype(BF)
    cosine,sine=cos_ref[...],sin_ref[...]
    q_ref[:,content:]=turn(proj_ref[:,content:at],cosine,sine).astype(BF)
    vl=proj_ref[:,at:at+R]
    latent_ref[...]=(vl*lax.rsqrt(jnp.mean(vl*vl,axis=-1,keepdims=True)+EPSILON)*gain_ref[...]).astype(BF)
    kr_ref[...]=turn(proj_ref[:,at+R:],cosine,sine).astype(BF)
    kv_ref[...]=mm(latent_ref[...],up_ref[...],NN).astype(BF)
    kr=kr_ref[...]
    for h in range(heads):
        kc=kv_ref[:,h*(DN+DV):h*(DN+DV)+DN]
        v=kv_ref[:,h*(DN+DV)+DN:(h+1)*(DN+DV)]
        k=jnp.concatenate([kc,jnp.where(slot_mask(kr.shape,h),kr,jnp.zeros_like(kr))],axis=1)
        for i in range(LEN//BLOCK):
            a,b=i*BLOCK,(i+1)*BLOCK
            q=jnp.concatenate([q_ref[a:b,h*DN:(h+1)*DN],q_ref[a:b,content:]],axis=1)
            s=causal_scores(q,k[:b],a)
            m=jnp.max(s,axis=-1,keepdims=True)
            e=jnp.exp(s-m)
            t=jnp.sum(e,axis=-1,keepdims=True)
            p=(e*(1.0/t)).astype(BF)
            mixed_ref[a:b,h*DV:(h+1)*DV]=mm(p,v[:b],NN).astype(BF)
            lse_ref[a:b,h:h+1]=m+jnp.log(t)

def attend(proj, up, gain, cosine, sine, heads):
    T=proj.shape[0]; wide=proj.shape[1]
    def rows(n): return pl.BlockSpec((LEN,n),lambda i:(i,0))
    def whole(a): return pl.BlockSpec(a.shape,lambda i:(0,0))
    qn=heads*DN+DN
    outs=[(qn,BF),(DN,BF),(heads*(DN+DV),BF),(R,BF),(heads*DV,BF),(heads,F32)]
    return pl.pallas_call(functools.partial(attend_kernel,heads),grid=(T//LEN,),
        in_specs=[rows(wide),whole(up),whole(gain),whole(cosine),whole(sine)],
        out_specs=[rows(n) for n,_ in outs],out_shape=[jax.ShapeDtypeStruct((T,n),d) for n,d in outs],
        compiler_params=params(1),
        cost_estimate=pl.CostEstimate(flops=T*LEN*heads*512,bytes_accessed=T*8000,transcendentals=T*LEN*heads//2))(proj,up,gain,cosine,sine)

def attend_back_kernel(heads, q_ref, kr_ref, kv_ref, mixed_ref, lse_ref, do_ref, cos_ref, sin_ref, dq_ref, dkv_ref, dkr_ref, dot_ref, dk_acc, dv_acc):
    content=heads*DN
    kr=kr_ref[...]
    for h in range(heads):
        kc=kv_ref[:,h*(DN+DV):h*(DN+DV)+DN]
        v=kv_ref[:,h*(DN+DV)+DN:(h+1)*(DN+DV)]
        mask=slot_mask(kr.shape,h)
        k=jnp.concatenate([kc,jnp.where(mask,kr,jnp.zeros_like(kr))],axis=1)
        for i in reversed(range(LEN//BLOCK)):
            a,b=i*BLOCK,(i+1)*BLOCK
            q=jnp.concatenate([q_ref[a:b,h*DN:(h+1)*DN],q_ref[a:b,content:]],axis=1)
            do=do_ref[a:b,h*DV:(h+1)*DV]
            p=jnp.exp(causal_scores(q,k[:b],a)-lse_ref[a:b,h:h+1])
            dp=mm(do,v[:b],NT)
            along=jnp.sum(do.astype(F32)*mixed_ref[a:b,h*DV:(h+1)*DV].astype(F32),axis=-1,keepdims=True)
            ds=(p*(dp-along)).astype(BF)
            pv=mm(p.astype(BF),do,TN)
            pk=mm(ds,q,TN)
            if i==LEN//BLOCK-1:
                dv_acc[...]=pv; dk_acc[...]=pk
            else:
                dv_acc[:b]+=pv; dk_acc[:b]+=pk
            dq=mm(ds,k[:b],NN)*SCALE
            d=jnp.sum(dq*q.astype(F32),axis=-1,keepdims=True)
            if h==0: dot_ref[a:b]=d
            else: dot_ref[a:b]+=d
            dq_ref[a:b,h*DN:(h+1)*DN]=dq[:,:DN].astype(BF)
            turned=turn(dq[:,DN:],cos_ref[a:b],-sin_ref[a:b])
            turned=jnp.where(mask[:b-a],turned,0.0).astype(BF)
            if h==0: dq_ref[a:b,content:]=turned
            else: dq_ref[a:b,content:]+=turned
        dkv_ref[:,h*(DN+DV):h*(DN+DV)+DN]=(dk_acc[:,:DN]*SCALE).astype(BF)
        dkv_ref[:,h*(DN+DV)+DN:(h+1)*(DN+DV)]=dv_acc[...].astype(BF)
        part=jnp.where(mask,dk_acc[:,DN:]*SCALE,0.0)
        if h==0: dkr_ref[...]=part
        else: dkr_ref[...]+=part

def attend_back(q,kr,kv,mixed,lse,do,cosine,sine,heads):
    T=q.shape[0]
    def rows(n): return pl.BlockSpec((LEN,n),lambda i:(i,0))
    def whole(a): return pl.BlockSpec(a.shape,lambda i:(0,0))
    args=(q,kr,kv,mixed,lse,do)
    outs=[(q.shape[1],BF),(kv.shape[1],BF),(DN,F32),(1,F32)]
    return pl.pallas_call(functools.partial(attend_back_kernel,heads),grid=(T//LEN,),
        in_specs=[rows(a.shape[1]) for a in args]+[whole(cosine),whole(sine)],
        out_specs=[rows(n) for n,_ in outs],out_shape=[jax.ShapeDtypeStruct((T,n),d) for n,d in outs],
        scratch_shapes=[pltpu.VMEM((LEN,2*DN),F32),pltpu.VMEM((LEN,DV),F32)],
        compiler_params=params(1),
        cost_estimate=pl.CostEstimate(flops=T*LEN*heads*1400,bytes_accessed=T*6000,transcendentals=T*LEN*heads//2))(*args,cosine,sine)

def tables():
    position=np.arange(LEN,dtype=np.float32)
    spread=(10000.0**(-np.arange(DR//2,dtype=np.float32)/(DR//2))).astype(np.float32)
    phase=(position[:,None]*spread[None,:]).astype(np.float32)
    c,s=np.cos(phase),np.sin(phase)
    return np.concatenate([c]*4,1).astype(np.float32),np.concatenate([-s,-s,s,s],1).astype(np.float32)


class Line:
    def __init__(self):
        self.n = lax.axis_size("tensor")
        self.chips = self.n // 2
        index = lax.axis_index("tensor")
        self.index = index
        self.z = index // 2
        self.c = index % 2

    def swap(self, a):
        return lax.ppermute(a, "tensor", [(i, i ^ 1) for i in range(self.n)])

    def shift(self, a, step, sources):
        pairs = [
            (2 * s + c, 2 * (s + step) + c)
            for s in sources
            if 0 <= s + step < self.chips
            for c in (0, 1)
        ]
        return lax.ppermute(a, "tensor", pairs)

    def chip_gather(self, s, jobs=None):
        n = self.chips
        left, right = [s], [s]
        for k in range(1, n):
            pair = (
                self.shift(left[-1], 1, range(k - 1, n)),
                self.shift(right[-1], -1, range(0, n - k + 1)),
            )
            pair = beside(pair, jobs)
            left.append(pair[0])
            right.append(pair[1])
        return [s] + [jnp.where(self.z >= k, left[k], right[n - k]) for k in range(1, n)]

    def pieces(self, own, order):
        n = self.chips
        out, at = [], []
        for k, piece in enumerate(own):
            chip = (self.z - k + n) % n
            out += [piece, self.swap(piece)]
            at += [order(chip, self.c), order(chip, 1 - self.c)]
        return out, jnp.stack(at).astype(jnp.int32)

    def row_pieces(self, s, jobs=None):
        return self.pieces(self.chip_gather(s, jobs), lambda chip, core: core * self.chips + chip)

    def column_pieces(self, own):
        return self.pieces(own, lambda chip, core: chip * 2 + core)

    def chip_scatter(self, block, jobs=None):
        n = self.chips
        left = right = None
        for s in range(1, n):
            up = block(jnp.clip(n - s + self.z, 0, n - 1))
            down = block(jnp.clip(self.z - (n - s), 0, n - 1))
            if left is not None:
                up = (up.astype(F32) + left.astype(F32)).astype(BF)
                down = (down.astype(F32) + right.astype(F32)).astype(BF)
            left = self.shift(up, 1, range(0, s))
            right = self.shift(down, -1, range(n - s, n))
            left, right = beside((left, right), jobs)
        return block(self.z).astype(F32) + left.astype(F32) + right.astype(F32)

    def row_pair(self, p):
        half = p.shape[0] // 2
        mine = lax.dynamic_slice_in_dim(p, self.c * half, half, 0)
        theirs = lax.dynamic_slice_in_dim(p, (1 - self.c) * half, half, 0)
        return (mine.astype(F32) + self.swap(theirs).astype(F32)).astype(BF)

    def row_scatter(self, both, jobs=None):
        ch = both.shape[0] // self.chips
        return self.chip_scatter(lambda j: lax.dynamic_slice_in_dim(both, j * ch, ch, 0), jobs)

    def row_start(self, rows):
        ch = rows // self.n
        return (self.c * self.chips + self.z) * ch, ch

    def column_scatter(self, mine, arrived, jobs=None):
        both = (mine.astype(F32) + arrived.astype(F32)).astype(BF)
        return self.chip_scatter(lambda j: lax.dynamic_index_in_dim(both, j, 0, False), jobs)


class Jobs:
    def __init__(self, *steps):
        self.steps = list(steps)
        self.made = {}

    def rest(self):
        while self.steps:
            self.made.update(self.steps.pop(0)(self.made))
        return self.made


def beside(arrived, jobs):
    if jobs is None or not jobs.steps:
        return lax.optimization_barrier(arrived)
    step = jobs.steps.pop(0)(jobs.made)
    arrived, step = lax.optimization_barrier((arrived, step))
    jobs.made.update(step)
    return arrived


def gather_rows(packed):
    return lax.all_gather(packed, "dp", axis=1, tiled=True)


def scatter_rows(packed):
    return lax.psum_scatter(packed, "dp", scatter_dimension=1, tiled=True)


def split_rows(packed, counts):
    out, at = [], 0
    for count in counts:
        out.append(packed[at : at + count])
        at += count
    return out


def ranks(mask):
    number = mask.shape[0]
    block = 128
    pieces = mask.reshape(number // block, block, E).astype(BF)
    lower = jnp.tril(jnp.ones((block, block), BF), -1)
    inside = jnp.einsum("ij,bje->bie", lower, pieces, preferred_element_type=F32)
    totals = jnp.sum(pieces.astype(F32), axis=1).astype(BF)
    ahead = jnp.tril(jnp.ones((number // block, number // block), BF), -1)
    before = dot(ahead, totals, 1, 0)
    return (inside + before[:, None, :]).reshape(number, E)


def per_device(
    layer_input, cotangent, first_gain, query_weight, latent_down, latent_gain, latent_up,
    output_weight, second_gain, router_weight, expert_gate, expert_up, expert_down,
    shared_gate, shared_up, shared_down, routes,
):
    line = Line()
    n_dp = lax.axis_size("dp")
    wide = D // n_dp
    number = layer_input.shape[0]
    heads_here = output_weight.shape[0] // DV
    fe = expert_down.shape[1]
    my_columns = layer_input.shape[1]
    column_start = line.index * my_columns
    row_start, row_count = line.row_start(number)

    half = DR // 2
    spare_heads = 2 - heads_here
    up_rows = latent_up.size // wide
    by_head = query_weight.T.reshape(heads_here, DN + DR, wide)
    blank = jnp.zeros((spare_heads * half, wide), BF)
    gains = jnp.zeros((16, wide), BF)
    gains = gains.at[0].set(first_gain).at[1].set(second_gain)
    gains = gains.at[2, : latent_gain.shape[0]].set(latent_gain)
    down = latent_down.T
    queries_wide = heads_here * DN + DN
    latent_wide = R + DN
    attend_pack = [
        by_head[:, :DN].reshape(heads_here * DN, wide),
        by_head[:, DN : DN + half].reshape(heads_here * half, wide), blank,
        by_head[:, DN + half :].reshape(heads_here * half, wide), blank,
        down[: R + half], down[R : R + half], down[R + half :], down[R + half :],
        latent_up.reshape(up_rows, wide), gains, router_weight.T, output_weight,
    ]
    attend_packed = gather_rows(jnp.concatenate([m for m in attend_pack if m.shape[0]], axis=0))
    wproj, wup, gains, wr, wo = split_rows(
        attend_packed, [queries_wide + latent_wide, up_rows, 16, E, output_weight.shape[0]]
    )
    wup = wup.reshape(up_rows, n_dp, wide).transpose(1, 0, 2).reshape(R, -1)
    first_g = gains[0].astype(F32)
    second_g = gains[1].astype(F32)
    latent_g = gains[2].reshape(n_dp, wide)[:, : R // n_dp].reshape(R).astype(F32)
    cosine, sine = (jnp.asarray(table) for table in tables())

    shared = shared_down.shape[0]
    units_here = (E * fe + shared) // 2
    cut = units_here // fe
    assert cut * fe == units_here
    gate = expert_gate.transpose(0, 2, 1).reshape(E * fe, wide)
    up = expert_up.transpose(0, 2, 1).reshape(E * fe, wide)
    jobs = Jobs(
        lambda made: {"down": jnp.concatenate([expert_down.reshape(E * fe, wide), shared_down], axis=0)},
        lambda made: {"early": jnp.concatenate([gate[:units_here], up[:units_here]], axis=0)},
        lambda made: {"late": jnp.concatenate(
            [gate[units_here:], shared_gate.T, up[units_here:], shared_up.T], axis=0)},
    )
    input_own = line.chip_gather(layer_input, jobs)
    packs = jobs.rest()
    downs, early, late = gather_rows(packs["down"]), gather_rows(packs["early"]), gather_rows(packs["late"])

    tile = 256
    core = line.c.reshape(1).astype(jnp.int32)
    input_pieces, input_at = line.column_pieces(input_own)
    input_pieces, cotangent = lax.optimization_barrier((input_pieces, cotangent))

    def project(made):
        rows, first_round, r1 = place_columns(input_pieces, input_at, first_g)
        return {"rows": rows, "first": first_round, "r1": r1, "proj": dot(first_round, wproj, 1, 1)}

    def attention(made):
        kept = attend(made["proj"], wup, latent_g[None], cosine, sine, heads_here)
        return {"attend": kept, "terms": dot(kept[4], wo, 1, 0, BF)}

    jobs = Jobs(project, attention, lambda made: {"both": line.row_pair(made["terms"])})
    grad_own = line.chip_gather(cotangent, jobs)
    made = jobs.rest()
    rows, first_round, r1, proj = made["rows"], made["first"], made["r1"], made["proj"]
    q, kr, kv, latent, mixed, log_total = made["attend"]
    jobs = Jobs(
        lambda made: {"grad": place_columns(*line.column_pieces(grad_own))[0]},
        lambda made: {},
        lambda made: {"back0": lift_back(made["grad"], downs, 0, units_here, tile)},
        lambda made: {"back1": lift_back(made["grad"], downs, 1, units_here, tile)},
    )
    attend_rows = line.row_scatter(made["both"], jobs)
    hidden_rows = (
        lax.dynamic_slice_in_dim(rows, row_start, row_count, 0).astype(F32) + attend_rows
    ).astype(BF)
    hidden_pieces, hidden_at = line.row_pieces(hidden_rows, jobs)
    made = jobs.rest()
    grad, back0, back1 = made["grad"], made["back0"], made["back1"]
    named = jnp.any(routes[:, :, None] == jnp.arange(E, dtype=jnp.int32)[None, None, :], axis=1)
    kept = jnp.where(named & (ranks(named) < CAP), 1.0, 0.0)
    second_round, hidden_columns, gating, weight = norm_rows(
        hidden_pieces, hidden_at, line.index.reshape(1).astype(jnp.int32), my_columns, second_g, wr, kept
    )

    stack0, pair0 = units(second_round, early, back0, weight, fe, 0, cut, tile)
    deltas = outer(stack0, 0, 2, second_round, 3 * units_here, 0)
    deltas = outer(stack0, 2, 1, grad, 3 * units_here, 2, deltas)
    deltas, stack0 = lax.optimization_barrier((deltas, stack0))
    early_sums = scatter_rows(deltas)
    second_terms = back([(stack0, 0, early, units_here, 0), (stack0, 1, early, units_here, 1)], None, F32, tile)
    stack1, pair1 = units(second_round, late, back1, weight, fe, cut, E - cut, tile)
    second_terms = back(
        [(stack1, 0, late, units_here, 0), (stack1, 1, late, units_here, 1)],
        second_terms, BF, tile, (pair0, pair1),
    )

    branch_terms = [(stack0, 2, downs, units_here, 0), (stack1, 2, downs, units_here, 1)]
    jobs = Jobs(
        lambda made: {"deltas": outer(stack1, 0, 1, second_round, 3 * units_here, 0)},
        lambda made: {"deltas": outer(stack1, 1, 1, second_round, 3 * units_here, 1, made["deltas"])},
        lambda made: {"deltas": outer(stack1, 2, 1, grad, 3 * units_here, 2, made["deltas"])},
        lambda made: {"theirs": back(branch_terms, None, BF, tile, (), 1 - core, line.chips)},
        lambda made: {"mine": back(branch_terms, None, BF, tile, (), core, line.chips)},
    )
    summed = line.row_scatter(line.row_pair(second_terms), jobs)
    early_sums, summed, jobs.made = lax.optimization_barrier((early_sums, summed, jobs.made))
    late_sums = scatter_rows(jobs.made["deltas"])

    def own_rows(a):
        return lax.dynamic_slice_in_dim(a, row_start, row_count, 0)

    gating_rows, kept_rows, x2 = own_rows(gating), own_rows(kept), own_rows(second_round)
    u = summed[:, D : D + E] * kept_rows
    logits_delta = gating_rows * (u - jnp.sum(gating_rows * u, axis=-1, keepdims=True))
    router_delta = dot(x2, logits_delta.astype(BF), 0, 0)
    d2 = summed[:, :D] + dot(logits_delta.astype(BF), wr, 1, 0)
    v2 = hidden_rows.astype(F32)
    r2 = lax.rsqrt(jnp.mean(v2 * v2, axis=-1, keepdims=True) + EPSILON)
    vgd = jnp.mean(v2 * second_g * d2, axis=-1, keepdims=True)
    second_gain_delta = jnp.sum(d2 * v2 * r2, axis=0)
    hidden_delta = own_rows(grad).astype(F32) + r2 * second_g * d2 - v2 * (r2**3) * vgd
    delta_pieces, delta_at = line.row_pieces(hidden_delta.astype(BF), jobs)
    made = jobs.rest()
    delta_pieces, theirs, mine = lax.optimization_barrier((delta_pieces, made["theirs"], made["mine"]))

    def into_heads(made):
        placed = place_rows(delta_pieces, delta_at)
        return {"hidden": placed, "mixed": dot(placed, wo, 1, 1, BF)}

    def heads_back(made):
        return {"heads": attend_back(q, kr, kv, mixed, log_total, made["mixed"], cosine, sine, heads_here)}

    def small_terms(made):
        delta_queries, delta_pairs, delta_kr, query_dot = made["heads"]
        delta_wq = dot(delta_queries, first_round, 0, 0)
        query_gain = jnp.sum(wproj[:queries_wide].astype(F32) * delta_wq, axis=0)
        per_entry = jnp.concatenate([second_gain_delta[:, None], query_gain[:, None], router_delta], axis=1)
        if number > D:
            per_entry = jnp.concatenate([per_entry, jnp.zeros((number - D, E + 2), F32)], axis=0)
        small = jnp.concatenate(
            [dot(delta_pairs, wup, 1, 1),
             delta_kr[:, :half] + delta_kr[:, half:DR], delta_kr[:, DR : DR + half] + delta_kr[:, DR + half :],
             query_dot, per_entry, jnp.zeros((number, 63 - 2 - E), F32)], axis=1,
        ).astype(BF)
        return {"small": small, "wq": delta_wq.astype(BF)}

    jobs = Jobs(into_heads, heads_back, small_terms)
    branch = line.column_scatter(mine, line.swap(theirs), jobs)
    made = jobs.rest()
    layer_output = (hidden_columns.astype(F32) + branch).astype(BF)
    hidden_delta, (delta_queries, delta_pairs) = made["hidden"], made["heads"][:2]
    first_terms = [(delta_queries, 0, attend_packed, queries_wide, 0)]

    def attend_deltas(made):
        delta_wup = dot(latent, delta_pairs, 0, 0, BF)
        return {"deltas": jnp.concatenate(
            [made["wq"], delta_wup.reshape(n_dp, up_rows, wide).transpose(1, 0, 2).reshape(up_rows, D),
             dot(mixed, hidden_delta, 0, 0, BF)], axis=0)}

    jobs = Jobs(
        lambda made: {"theirs": back(first_terms, None, BF, tile, (), 1 - core, line.chips)},
        lambda made: {"mine": back(first_terms, None, BF, tile, (), core, line.chips)},
        attend_deltas,
    )
    jobs.made["wq"] = made["wq"]
    small = line.row_scatter(line.row_pair(made["small"]), jobs).astype(BF)
    made = jobs.rest()
    deltas, small = lax.optimization_barrier((made["deltas"], small))
    attend_sums = scatter_rows(deltas).astype(F32)
    small_pieces, small_at = line.row_pieces(small)
    small_pieces, arrived, late_sums = lax.optimization_barrier(
        (small_pieces, line.swap(made["theirs"]), late_sums)
    )
    wld = wproj[queries_wide:]

    def last(made):
        small = place_rows(small_pieces, small_at)
        delta_latent, dots, gain_delta = latent_back(small, proj, latent_g[None], cosine, sine)
        latent_row = jnp.pad(gain_delta.reshape(n_dp, R // n_dp), ((0, 0), (0, wide - R // n_dp))).reshape(1, D)
        return {"delta": delta_latent, "dots": dots,
                "pack": last_pack(delta_latent, first_round, wld, small, first_g[None], latent_row)}

    jobs = Jobs(last)
    first_share = line.column_scatter(made["mine"], arrived, jobs)
    made = jobs.rest()
    last_sums = scatter_rows(made["pack"]).astype(F32)
    dwld, vectors = last_sums[:latent_wide], last_sums[latent_wide:]
    dwq, dwup, dwo = split_rows(attend_sums, [queries_wide, up_rows, output_weight.shape[0]])
    content = heads_here * DN
    dwq = jnp.concatenate(
        [dwq[:content].reshape(heads_here, DN, wide),
         dwq[content : content + heads_here * half].reshape(heads_here, half, wide),
         dwq[content + DR : content + DR + heads_here * half].reshape(heads_here, half, wide)], axis=1
    ).reshape(heads_here * (DN + DR), wide)
    dwld = jnp.concatenate([dwld[: R + half], dwld[R + DR : R + DR + half]], axis=0)

    first_share = first_share + dot(
        made["delta"], lax.dynamic_slice_in_dim(wld, column_start, my_columns, 1), 1, 0
    )
    vc = layer_input.astype(F32)
    gc = lax.dynamic_slice_in_dim(first_g, column_start, my_columns, 0)
    input_delta = (
        lax.dynamic_slice_in_dim(hidden_delta, column_start, my_columns, 1).astype(F32)
        + r1 * gc * first_share
        - vc * (r1 * r1) * (made["dots"] / D)
    )

    def expert_delta(k):
        first = early_sums[k * units_here : (k + 1) * units_here]
        second = late_sums[k * units_here : k * units_here + E * fe - units_here]
        return jnp.concatenate([first, second], axis=0).astype(F32).reshape(E, fe, wide)

    def shared_delta(k):
        return late_sums[(k + 1) * units_here - shared : (k + 1) * units_here].astype(F32)

    return (
        layer_output, input_delta, vectors[E + 1], dwq.T, dwld.T, vectors[E + 2, : R // n_dp],
        dwup.reshape(latent_up.shape), dwo, vectors[E], vectors[:E].T,
        expert_delta(0).transpose(0, 2, 1), expert_delta(1).transpose(0, 2, 1), expert_delta(2),
        shared_delta(0).T, shared_delta(1).T, shared_delta(2),
    )


def solution(mesh):
    in_specs = (
        P("dp", "tensor"), P("dp", "tensor"), P("dp"), P("dp", "tensor"), P("dp", None), P("dp"),
        P("dp", "tensor"), P("tensor", "dp"), P("dp"), P("dp", None), P(None, "dp", "tensor"),
        P(None, "dp", "tensor"), P(None, "tensor", "dp"), P("dp", "tensor"), P("dp", "tensor"),
        P("tensor", "dp"), P("dp", None),
    )
    out_specs = (
        P("dp", "tensor"), P("dp", "tensor"), P("dp"), P("dp", "tensor"), P("dp", None), P("dp"),
        P("dp", "tensor"), P("tensor", "dp"), P("dp"), P("dp", None), P(None, "dp", "tensor"),
        P(None, "dp", "tensor"), P(None, "tensor", "dp"), P("dp", "tensor"), P("dp", "tensor"),
        P("tensor", "dp"),
    )
    return jax.shard_map(
        per_device, mesh=mesh, in_specs=in_specs, out_specs=out_specs, check_vma=False
    )
```

```python
import functools

import jax
import jax.numpy as jnp
import numpy as np
from jax import lax
from jax.experimental import pallas as pl
from jax.experimental.pallas import tpu as pltpu
from jax.sharding import PartitionSpec as P

D = 2048
DN = 128
DR = 64
DV = 128
R = 512
E = 16
LEN = 1024
CAP = 864
EPSILON = 1e-06
SCALE = (DN + DR) ** -0.5
BLOCK = 256
BF = jnp.bfloat16
F32 = jnp.float32


def dot(a, b, ca, cb, out=F32):
    return lax.dot_general(
        a, b, (((ca,), (cb,)), ((), ())), preferred_element_type=F32
    ).astype(out)


VMEM_LIMIT = 58 * 2**20
NT=(((1,),(1,)),((),()))
NN=(((1,),(0,)),((),()))
TN=(((0,),(0,)),((),()))

def mm(a,b,dims):
    return lax.dot_general(a,b,dims,preferred_element_type=F32)

def params(n):
    return pltpu.CompilerParams(dimension_semantics=("arbitrary",)*n, vmem_limit_bytes=VMEM_LIMIT)

def once(shape, index):
    return pl.BlockSpec(shape, index, pipeline_mode=pl.Buffered(1))

def place_matrix(fe, first, n):
    col=lax.broadcasted_iota(jnp.int32,(E,n),1)+first; row=lax.broadcasted_iota(jnp.int32,(E,n),0)*fe
    return jnp.where((col>=row)&(col<row+fe),1.0,0.0).astype(BF)

def units_kernel(fe, first, x_ref, wg_ref, wu_ref, b_ref, w_ref, out_ref, pair_ref):
    x=x_ref[...]; n=wg_ref.shape[0]
    pre=mm(x,wg_ref[...],NT); lift=mm(x,wu_ref[...],NT); back=b_ref[...].astype(F32)
    w=w_ref[...]; hi=w.astype(BF); lo=(w-hi.astype(F32)).astype(BF)
    place=place_matrix(fe,first,n)
    spread=mm(jnp.concatenate([hi,lo],axis=1),jnp.concatenate([place,place],axis=0),NN)
    if first+n>E*fe:
        spread=jnp.where(lax.broadcasted_iota(jnp.int32,spread.shape,1)>=E*fe-first,1.0,spread)
    s=0.5+0.5*jnp.tanh(0.5*pre)
    silu=pre*s
    act=silu*lift
    pair_ref[...]=mm((act*back).astype(BF),place,NT)
    back=back*spread
    out_ref[0]=(back*lift*(s+silu*(1.0-s))).astype(BF)
    out_ref[1]=(back*silu).astype(BF)
    out_ref[2]=(act*spread).astype(BF)

def units(x,packed,back,weight,fe,first,bt):
    T,D=x.shape; n=back.shape[1]; r=weight.shape[1]
    ins=[pl.BlockSpec((bt,D),lambda i:(i,0))]+[once((n,D),lambda i,k=k:(k,0)) for k in range(2)]
    ins+=[pl.BlockSpec((bt,n),lambda i:(i,0)),pl.BlockSpec((bt,r),lambda i:(i,0))]
    outs=[jax.ShapeDtypeStruct((3,T,n),BF),jax.ShapeDtypeStruct((T,r),F32)]
    return pl.pallas_call(functools.partial(units_kernel,fe,first),grid=(T//bt,),in_specs=ins,
        out_specs=[pl.BlockSpec((3,bt,n),lambda i:(0,i,0)),pl.BlockSpec((bt,r),lambda i:(i,0))],out_shape=outs,
        compiler_params=params(1),
        cost_estimate=pl.CostEstimate(flops=4*T*D*n,bytes_accessed=2*(T*D+2*n*D+4*T*n),transcendentals=T*n))(x,packed,packed,back,weight)

def lift_kernel(g_ref,w_ref,o_ref):
    o_ref[...]=mm(g_ref[...],w_ref[...],NT).astype(BF)

def lift_back(g,packed,at,n,bt):
    T,D=g.shape
    return pl.pallas_call(lift_kernel,grid=(T//bt,),
        in_specs=[pl.BlockSpec((bt,D),lambda i:(i,0)),once((n,D),lambda i:(at,0))],
        out_specs=pl.BlockSpec((bt,n),lambda i:(i,0)),out_shape=jax.ShapeDtypeStruct((T,n),BF),compiler_params=params(1),
        cost_estimate=pl.CostEstimate(flops=2*T*D*n,bytes_accessed=2*(T*D+n*D+T*n),transcendentals=0))(g,packed)

def back_kernel(pairs, added, beside, *refs):
    out=refs[-1]
    acc=None
    if added: acc=refs[0][...].astype(F32)
    rs=refs[added:]
    for k in range(pairs):
        a=rs[2*k]; b=rs[2*k+1]
        a=a[0] if len(a.shape)==3 else a[...]
        p=mm(a,b[...],NN)
        acc=p if acc is None else acc+p
    if beside:
        wide=acc.shape[1]
        out[:,:wide]=acc.astype(out.dtype)
        more=sum(r[...] for r in refs[-1-beside:-1])
        gap=jnp.zeros((acc.shape[0],out.shape[1]-wide-more.shape[1]),F32)
        out[:,wide:]=jnp.concatenate([more,gap],axis=1).astype(out.dtype)
    else:
        out[...]=acc.astype(out.dtype)

def core_kernel(pairs, core_ref, *refs):
    out=refs[-1]
    chips,_,w=out.shape
    for z in range(chips):
        at=pl.ds(pl.multiple_of((2*z+core_ref[0])*w,w),w)
        acc=None
        for k in range(pairs):
            a=refs[2*k]; b=refs[2*k+1]
            p=mm(a[0] if len(a.shape)==3 else a[...],b[:,at],NN)
            acc=p if acc is None else acc+p
        out[z]=acc.astype(BF)

def back(terms, added, out_dtype, bt, beside=(), core=None, chips=0):
    T=terms[0][0].shape[-2]; D=terms[0][2].shape[1]
    ins=[];args=[];fl=0;by=0
    if core is not None:
        ins.append(pl.BlockSpec(memory_space=pltpu.SMEM)); args.append(core)
    if added is not None:
        ins.append(pl.BlockSpec((bt,D),lambda i:(i,0))); args.append(added)
    for st,k,packed,n,at in terms:
        if st.ndim==3: ins.append(pl.BlockSpec((1,bt,n),lambda i,k=k:(k,i,0)))
        else: ins.append(pl.BlockSpec((bt,n),lambda i:(i,0)))
        ins.append(once((n,D),lambda i,at=at:(at,0)))
        args+= [st,packed]; fl+=2*T*D*n; by+=2*(T*n+n*D)
    for more in beside:
        ins.append(pl.BlockSpec((bt,more.shape[1]),lambda i:(i,0))); args.append(more)
    body=functools.partial(back_kernel,len(terms),0 if added is None else 1,len(beside))
    if beside:
        shape=(T,D+128); ospec=pl.BlockSpec((bt,D+128),lambda i:(i,0))
    elif core is not None:
        w=D//(2*chips); fl//=2
        shape=(chips,T,w); ospec=pl.BlockSpec((chips,bt,w),lambda i:(0,i,0))
        body=functools.partial(core_kernel,len(terms))
    else:
        shape=(T,D); ospec=pl.BlockSpec((bt,D),lambda i:(i,0))
    return pl.pallas_call(body,grid=(T//bt,),in_specs=ins,out_specs=ospec,out_shape=jax.ShapeDtypeStruct(shape,out_dtype),
        compiler_params=params(1),cost_estimate=pl.CostEstimate(flops=fl,bytes_accessed=by+4*T*D,transcendentals=0))(*args)

def outer_kernel(s_ref,x_ref,*refs):
    refs[-1][...]=mm(s_ref[0],x_ref[...],TN).astype(BF)

def outer(stack,first,count,x,total,at,into=None,bc=512):
    T,D=x.shape; n=stack.shape[2]
    ins=[pl.BlockSpec((1,T,n),lambda k,j:(first+k,0,0)),pl.BlockSpec((T,bc),lambda k,j:(0,j))]
    args=[stack,x]; al={}
    if into is not None:
        ins.append(pl.BlockSpec(memory_space=pl.ANY)); args.append(into); al={2:0}
    return pl.pallas_call(outer_kernel,grid=(count,D//bc),in_specs=ins,
        out_specs=pl.BlockSpec((n,bc),lambda k,j:(at+k,j)),out_shape=jax.ShapeDtypeStruct((total,D),BF),
        input_output_aliases=al,compiler_params=params(2),
        cost_estimate=pl.CostEstimate(flops=2*count*T*D*n,bytes_accessed=2*count*(T*n+n*D+T*D),transcendentals=0))(*args)


def place_columns_kernel(chips, norm, at_ref, *refs):
    pieces=refs[:2*chips]
    refs=refs[2*chips:]
    if norm:
        gain_ref, out_ref, round_ref, r_ref = refs
    else:
        (out_ref,) = refs
    w=pieces[0].shape[1]
    for k in range(2*chips):
        out_ref[:,pl.ds(pl.multiple_of(at_ref[k]*w,w),w)]=pieces[k][...]
    if norm:
        v=out_ref[...].astype(F32)
        r=lax.rsqrt(jnp.mean(v*v,axis=-1,keepdims=True)+EPSILON)
        round_ref[...]=(v*r*gain_ref[...]).astype(BF)
        r_ref[...]=r

def place_columns(pieces, at, gain=None, bt=256):
    T,w=pieces[0].shape; n=len(pieces)
    ins=[pl.BlockSpec(memory_space=pltpu.SMEM)]+[pl.BlockSpec((bt,w),lambda i:(i,0))]*n
    args=[at]+list(pieces)
    outs=[jax.ShapeDtypeStruct((T,n*w),BF)]; specs=[pl.BlockSpec((bt,n*w),lambda i:(i,0))]
    if gain is not None:
        ins.append(pl.BlockSpec((1,n*w),lambda i:(0,0))); args.append(gain[None])
        outs+=[jax.ShapeDtypeStruct((T,n*w),BF),jax.ShapeDtypeStruct((T,1),F32)]
        specs+=[pl.BlockSpec((bt,n*w),lambda i:(i,0)),pl.BlockSpec((bt,1),lambda i:(i,0))]
    return pl.pallas_call(functools.partial(place_columns_kernel,n//2,gain is not None),grid=(T//bt,),
        in_specs=ins,out_specs=specs,out_shape=outs,compiler_params=params(1),
        cost_estimate=pl.CostEstimate(flops=6*T*n*w,bytes_accessed=6*T*n*w,transcendentals=T))(*args)

def place_rows_kernel(n, at_ref, *refs):
    pieces=refs[:n]; out_ref=refs[n]; sem=refs[n+1]
    rows=pieces[0].shape[0]
    copies=[pltpu.make_async_copy(pieces[k],out_ref.at[pl.ds(pl.multiple_of(at_ref[k]*rows,rows),rows)],sem.at[k]) for k in range(n)]
    for c in copies: c.start()
    for c in copies: c.wait()

def place_rows(pieces, at):
    rows,w=pieces[0].shape; n=len(pieces)
    return pl.pallas_call(functools.partial(place_rows_kernel,n),
        in_specs=[pl.BlockSpec(memory_space=pltpu.SMEM)]+[pl.BlockSpec(memory_space=pltpu.VMEM)]*n,
        out_specs=pl.BlockSpec(memory_space=pl.ANY),out_shape=jax.ShapeDtypeStruct((n*rows,w),BF),
        scratch_shapes=[pltpu.SemaphoreType.DMA((n,))],compiler_params=pltpu.CompilerParams(vmem_limit_bytes=VMEM_LIMIT),
        cost_estimate=pl.CostEstimate(flops=0,bytes_accessed=4*n*rows*w,transcendentals=0))(at,*pieces)

def norm_rows_kernel(n, at_ref, col_ref, gain_ref, wr_ref, kept_ref, *refs):
    pieces=refs[:n]; round_ref,cols_ref,gating_ref,weight_ref,made,cut,sem,sem2=refs[n:]
    rows=pieces[0].shape[0]; w=cut.shape[2]
    copies=[]
    for k in range(n):
        v=pieces[k][...].astype(F32)
        r=lax.rsqrt(jnp.mean(v*v,axis=-1,keepdims=True)+EPSILON)
        made[k]=(v*r*gain_ref[...]).astype(BF)
        cut[k]=pieces[k][:,pl.ds(pl.multiple_of(col_ref[0]*w,w),w)]
        to=pl.ds(pl.multiple_of(at_ref[k]*rows,rows),rows)
        copies.append(pltpu.make_async_copy(made.at[k],round_ref.at[to],sem.at[k]))
        copies.append(pltpu.make_async_copy(cut.at[k],cols_ref.at[to],sem2.at[k]))
        copies[-2].start(); copies[-1].start()
        logits=mm(made[k],wr_ref[...],NT)
        e=jnp.exp(logits-jnp.max(logits,axis=-1,keepdims=True))
        gating=e/jnp.sum(e,axis=-1,keepdims=True)
        gating_ref[to]=gating
        weight_ref[to]=gating*kept_ref[to]
    for c in copies: c.wait()

def norm_rows(pieces, at, column, w, gain, router, kept):
    rows,wide=pieces[0].shape; n=len(pieces)
    vmem=pl.BlockSpec(memory_space=pltpu.VMEM)
    return pl.pallas_call(functools.partial(norm_rows_kernel,n),
        in_specs=[pl.BlockSpec(memory_space=pltpu.SMEM)]*2+[vmem]*(n+3),
        out_specs=[pl.BlockSpec(memory_space=pl.ANY)]*2+[vmem]*2,
        out_shape=[jax.ShapeDtypeStruct((n*rows,wide),BF),jax.ShapeDtypeStruct((n*rows,w),BF)]+[jax.ShapeDtypeStruct((n*rows,E),F32)]*2,
        scratch_shapes=[pltpu.VMEM((n,rows,wide),BF),pltpu.VMEM((n,rows,w),BF),pltpu.SemaphoreType.DMA((n,)),pltpu.SemaphoreType.DMA((n,))],
        compiler_params=pltpu.CompilerParams(vmem_limit_bytes=VMEM_LIMIT),
        cost_estimate=pl.CostEstimate(flops=6*n*rows*wide,bytes_accessed=4*n*rows*wide,transcendentals=n*rows))(at,column,gain[None],router,kept,*pieces)

def latent_back_kernel(small_ref, proj_ref, gain_ref, cos_ref, sin_ref, delta_ref, dots_ref, gain_delta_ref):
    i=pl.program_id(0)
    at=proj_ref.shape[1]-R-DN
    dl=small_ref[:,:R].astype(F32)
    vl=proj_ref[:,at:at+R]
    rl=lax.rsqrt(jnp.mean(vl*vl,axis=-1,keepdims=True)+EPSILON)
    gain=gain_ref[...]
    part=jnp.sum(dl*vl*rl,axis=0,keepdims=True)
    @pl.when(i==0)
    def _(): gain_delta_ref[...]=part
    @pl.when(i>0)
    def _(): gain_delta_ref[...]+=part
    gd=gain*dl
    head=rl*gd-vl*(rl*rl*rl)*jnp.mean(vl*gd,axis=-1,keepdims=True)
    beyond=small_ref[:,R:]
    row=lax.broadcasted_iota(jnp.int32,(DN,DN),0); col=lax.broadcasted_iota(jnp.int32,(DN,DN),1)
    h=DR//2
    put=jnp.where(((row<h)&(col==row))|((row>=h)&(row<DR)&(col==row+h)),1.0,0.0).astype(BF)
    spread=mm(beyond,put,NN)
    tail=spread*cos_ref[...]-pltpu.roll(spread,DR,1)*sin_ref[...]
    delta_ref[:,:R]=head.astype(BF)
    delta_ref[:,R:]=tail.astype(BF)
    own=jnp.sum(head*vl,axis=-1,keepdims=True)+jnp.sum(tail*proj_ref[:,at+R:],axis=-1,keepdims=True)
    lane=lax.broadcasted_iota(jnp.int32,beyond.shape,1)
    dots_ref[...]=own+jnp.sum(jnp.where(lane==DR,beyond.astype(F32),0.0),axis=-1,keepdims=True)

def latent_back(small, proj, gain, cosine, sine, bt=512):
    T,wide=small.shape; turns=LEN//bt
    return pl.pallas_call(latent_back_kernel,grid=(T//bt,),
        in_specs=[pl.BlockSpec((bt,wide),lambda i:(i,0)),pl.BlockSpec((bt,proj.shape[1]),lambda i:(i,0)),
                  pl.BlockSpec((1,R),lambda i:(0,0)),pl.BlockSpec((bt,DN),lambda i:(i%turns,0)),pl.BlockSpec((bt,DN),lambda i:(i%turns,0))],
        out_specs=[pl.BlockSpec((bt,R+DN),lambda i:(i,0)),pl.BlockSpec((bt,1),lambda i:(i,0)),pl.BlockSpec((1,R),lambda i:(0,0))],
        out_shape=[jax.ShapeDtypeStruct((T,R+DN),BF),jax.ShapeDtypeStruct((T,1),F32),jax.ShapeDtypeStruct((1,R),F32)],
        compiler_params=params(1),
        cost_estimate=pl.CostEstimate(flops=30*T*wide,bytes_accessed=8*T*wide,transcendentals=T))(small,proj,gain,cosine,sine)

def last_pack_kernel(delta_ref, x_ref, w_ref, small_ref, g_ref, latent_ref, out_ref):
    n=delta_ref.shape[1]
    d=mm(delta_ref[...],x_ref[...],TN)
    out_ref[:n]=d.astype(BF)
    sums=jnp.sum(w_ref[...].astype(F32)*d,axis=0,keepdims=True)
    row=lax.broadcasted_iota(jnp.int32,(32,DN),0); col=lax.broadcasted_iota(jnp.int32,(32,DN),1)
    at=DR+1
    pick=((row<E)&(col==row+at+2))|((row==E)&(col==at))|((row==E+1)&(col==at+1))
    v=mm(jnp.where(pick,1.0,0.0).astype(BF),small_ref[...],NT)
    line=lax.broadcasted_iota(jnp.int32,v.shape,0)
    v=jnp.where(line==E+1,(v+sums)/g_ref[...],v)
    out_ref[n:]=jnp.where(line==E+2,latent_ref[...],v).astype(BF)

def last_pack(delta, x, w, small, gain, latent_row, bc=512):
    T,D=x.shape; n=delta.shape[1]
    def cols(a): return pl.BlockSpec((a.shape[0],bc),lambda j:(0,j))
    return pl.pallas_call(last_pack_kernel,grid=(D//bc,),
        in_specs=[pl.BlockSpec((T,n),lambda j:(0,0)),cols(x),cols(w),pl.BlockSpec((bc,DN),lambda j:(j,R//DN)),cols(gain),cols(latent_row)],
        out_specs=pl.BlockSpec((n+32,bc),lambda j:(0,j)),out_shape=jax.ShapeDtypeStruct((n+32,D),BF),
        compiler_params=params(1),
        cost_estimate=pl.CostEstimate(flops=2*T*D*n,bytes_accessed=2*(T*D+2*n*D+T*n),transcendentals=0))(delta,x,w,small,gain,latent_row)


def turn(x, cosine, sine):
    return x*cosine+pltpu.roll(x,64,1)*sine

def slot_mask(shape, head):
    lane=lax.broadcasted_iota(jnp.int32,shape,1)
    low=head*(DR//2)
    inside=((lane>=low)&(lane<low+DR//2))|((lane>=low+DR)&(lane<low+DR+DR//2))
    return inside

def causal_scores(q, k, first):
    s=mm(q,k,NT)*SCALE
    row=lax.broadcasted_iota(jnp.int32,s.shape,0)+first
    col=lax.broadcasted_iota(jnp.int32,s.shape,1)
    return jnp.where(col<=row,s,-1e30)

def attend_kernel(heads, proj_ref, up_ref, gain_ref, cos_ref, sin_ref, q_ref, kr_ref, kv_ref, latent_ref, mixed_ref, lse_ref):
    content=heads*DN
    at=content+DN
    q_ref[:,:content]=proj_ref[:,:content].astype(BF)
    cosine,sine=cos_ref[...],sin_ref[...]
    q_ref[:,content:]=turn(proj_ref[:,content:at],cosine,sine).astype(BF)
    vl=proj_ref[:,at:at+R]
    latent_ref[...]=(vl*lax.rsqrt(jnp.mean(vl*vl,axis=-1,keepdims=True)+EPSILON)*gain_ref[...]).astype(BF)
    kr_ref[...]=turn(proj_ref[:,at+R:],cosine,sine).astype(BF)
    kv_ref[...]=mm(latent_ref[...],up_ref[...],NN).astype(BF)
    kr=kr_ref[...]
    for h in range(heads):
        kc=kv_ref[:,h*(DN+DV):h*(DN+DV)+DN]
        v=kv_ref[:,h*(DN+DV)+DN:(h+1)*(DN+DV)]
        k=jnp.concatenate([kc,jnp.where(slot_mask(kr.shape,h),kr,jnp.zeros_like(kr))],axis=1)
        for i in range(LEN//BLOCK):
            a,b=i*BLOCK,(i+1)*BLOCK
            q=jnp.concatenate([q_ref[a:b,h*DN:(h+1)*DN],q_ref[a:b,content:]],axis=1)
            s=causal_scores(q,k[:b],a)
            m=jnp.max(s,axis=-1,keepdims=True)
            e=jnp.exp(s-m)
            t=jnp.sum(e,axis=-1,keepdims=True)
            p=(e*(1.0/t)).astype(BF)
            mixed_ref[a:b,h*DV:(h+1)*DV]=mm(p,v[:b],NN).astype(BF)
            lse_ref[a:b,h:h+1]=m+jnp.log(t)

def attend(proj, up, gain, cosine, sine, heads):
    T=proj.shape[0]; wide=proj.shape[1]
    def rows(n): return pl.BlockSpec((LEN,n),lambda i:(i,0))
    def whole(a): return pl.BlockSpec(a.shape,lambda i:(0,0))
    qn=heads*DN+DN
    outs=[(qn,BF),(DN,BF),(heads*(DN+DV),BF),(R,BF),(heads*DV,BF),(heads,F32)]
    return pl.pallas_call(functools.partial(attend_kernel,heads),grid=(T//LEN,),
        in_specs=[rows(wide),whole(up),whole(gain),whole(cosine),whole(sine)],
        out_specs=[rows(n) for n,_ in outs],out_shape=[jax.ShapeDtypeStruct((T,n),d) for n,d in outs],
        compiler_params=params(1),
        cost_estimate=pl.CostEstimate(flops=T*LEN*heads*512,bytes_accessed=T*8000,transcendentals=T*LEN*heads//2))(proj,up,gain,cosine,sine)

def attend_back_kernel(heads, q_ref, kr_ref, kv_ref, mixed_ref, lse_ref, do_ref, cos_ref, sin_ref, dq_ref, dkv_ref, dkr_ref, dot_ref, dk_acc, dv_acc):
    content=heads*DN
    kr=kr_ref[...]
    for h in range(heads):
        kc=kv_ref[:,h*(DN+DV):h*(DN+DV)+DN]
        v=kv_ref[:,h*(DN+DV)+DN:(h+1)*(DN+DV)]
        mask=slot_mask(kr.shape,h)
        k=jnp.concatenate([kc,jnp.where(mask,kr,jnp.zeros_like(kr))],axis=1)
        for i in reversed(range(LEN//BLOCK)):
            a,b=i*BLOCK,(i+1)*BLOCK
            q=jnp.concatenate([q_ref[a:b,h*DN:(h+1)*DN],q_ref[a:b,content:]],axis=1)
            do=do_ref[a:b,h*DV:(h+1)*DV]
            p=jnp.exp(causal_scores(q,k[:b],a)-lse_ref[a:b,h:h+1])
            dp=mm(do,v[:b],NT)
            along=jnp.sum(do.astype(F32)*mixed_ref[a:b,h*DV:(h+1)*DV].astype(F32),axis=-1,keepdims=True)
            ds=(p*(dp-along)).astype(BF)
            pv=mm(p.astype(BF),do,TN)
            pk=mm(ds,q,TN)
            if i==LEN//BLOCK-1:
                dv_acc[...]=pv; dk_acc[...]=pk
            else:
                dv_acc[:b]+=pv; dk_acc[:b]+=pk
            dq=mm(ds,k[:b],NN)*SCALE
            d=jnp.sum(dq*q.astype(F32),axis=-1,keepdims=True)
            if h==0: dot_ref[a:b]=d
            else: dot_ref[a:b]+=d
            dq_ref[a:b,h*DN:(h+1)*DN]=dq[:,:DN].astype(BF)
            turned=turn(dq[:,DN:],cos_ref[a:b],-sin_ref[a:b])
            turned=jnp.where(mask[:b-a],turned,0.0).astype(BF)
            if h==0: dq_ref[a:b,content:]=turned
            else: dq_ref[a:b,content:]+=turned
        dkv_ref[:,h*(DN+DV):h*(DN+DV)+DN]=(dk_acc[:,:DN]*SCALE).astype(BF)
        dkv_ref[:,h*(DN+DV)+DN:(h+1)*(DN+DV)]=dv_acc[...].astype(BF)
        part=jnp.where(mask,dk_acc[:,DN:]*SCALE,0.0)
        if h==0: dkr_ref[...]=part
        else: dkr_ref[...]+=part

def attend_back(q,kr,kv,mixed,lse,do,cosine,sine,heads):
    T=q.shape[0]
    def rows(n): return pl.BlockSpec((LEN,n),lambda i:(i,0))
    def whole(a): return pl.BlockSpec(a.shape,lambda i:(0,0))
    args=(q,kr,kv,mixed,lse,do)
    outs=[(q.shape[1],BF),(kv.shape[1],BF),(DN,F32),(1,F32)]
    return pl.pallas_call(functools.partial(attend_back_kernel,heads),grid=(T//LEN,),
        in_specs=[rows(a.shape[1]) for a in args]+[whole(cosine),whole(sine)],
        out_specs=[rows(n) for n,_ in outs],out_shape=[jax.ShapeDtypeStruct((T,n),d) for n,d in outs],
        scratch_shapes=[pltpu.VMEM((LEN,2*DN),F32),pltpu.VMEM((LEN,DV),F32)],
        compiler_params=params(1),
        cost_estimate=pl.CostEstimate(flops=T*LEN*heads*1400,bytes_accessed=T*6000,transcendentals=T*LEN*heads//2))(*args,cosine,sine)

def tables():
    position=np.arange(LEN,dtype=np.float32)
    spread=(10000.0**(-np.arange(DR//2,dtype=np.float32)/(DR//2))).astype(np.float32)
    phase=(position[:,None]*spread[None,:]).astype(np.float32)
    c,s=np.cos(phase),np.sin(phase)
    return np.concatenate([c]*4,1).astype(np.float32),np.concatenate([-s,-s,s,s],1).astype(np.float32)


class Line:
    def __init__(self):
        self.n = lax.axis_size("tensor")
        self.chips = self.n // 2
        index = lax.axis_index("tensor")
        self.index = index
        self.z = index // 2
        self.c = index % 2

    def swap(self, a):
        return lax.ppermute(a, "tensor", [(i, i ^ 1) for i in range(self.n)])

    def shift(self, a, step, sources):
        pairs = [
            (2 * s + c, 2 * (s + step) + c)
            for s in sources
            if 0 <= s + step < self.chips
            for c in (0, 1)
        ]
        return lax.ppermute(a, "tensor", pairs)

    def pieces(self, own, order):
        n = self.chips
        out, at = [], []
        for k, piece in enumerate(own):
            chip = (self.z - k + n) % n
            out += [piece, self.swap(piece)]
            at += [order(chip, self.c), order(chip, 1 - self.c)]
        return out, jnp.stack(at).astype(jnp.int32)

    def row_pieces(self, own):
        return self.pieces(own, lambda chip, core: core * self.chips + chip)

    def column_pieces(self, own):
        return self.pieces(own, lambda chip, core: chip * 2 + core)

    def halves(self, p):
        half = p.shape[0] // 2
        return [lax.dynamic_slice_in_dim(p, c * half, half, 0) for c in (self.c, 1 - self.c)]

    def row_scatter(self, both):
        ch = both.shape[0] // self.chips
        return Scatter(self, lambda j: lax.dynamic_slice_in_dim(both, j * ch, ch, 0))

    def column_scatter(self, both):
        return Scatter(self, lambda j: lax.dynamic_index_in_dim(both, j, 0, False))

    def row_start(self, rows):
        ch = rows // self.n
        return (self.c * self.chips + self.z) * ch, ch


def total(mine, arrived):
    return (mine.astype(F32) + arrived.astype(F32)).astype(BF)


class Gather:
    def __init__(self, line, block):
        self.line, self.left, self.right = line, [block], [block]

    def start(self):
        n, k = self.line.chips, len(self.left)
        return (
            self.line.shift(self.left[-1], 1, range(k - 1, n)),
            self.line.shift(self.right[-1], -1, range(0, n - k + 1)),
        )

    def take(self, arrived):
        self.left.append(arrived[0])
        self.right.append(arrived[1])

    def result(self):
        n, z = self.line.chips, self.line.z
        return self.left[:1] + [jnp.where(z >= k, self.left[k], self.right[n - k]) for k in range(1, n)]


class Scatter:
    def __init__(self, line, block):
        self.line, self.block, self.step, self.left, self.right = line, block, 0, None, None

    def start(self):
        self.step += 1
        n, s, z = self.line.chips, self.step, self.line.z
        up = self.block(jnp.clip(n - s + z, 0, n - 1))
        down = self.block(jnp.clip(z - (n - s), 0, n - 1))
        if self.left is not None:
            up, down = total(up, self.left), total(down, self.right)
        return self.line.shift(up, 1, range(0, s)), self.line.shift(down, -1, range(n - s, n))

    def take(self, arrived):
        self.left, self.right = arrived

    def result(self):
        return self.block(self.line.z).astype(F32) + self.left.astype(F32) + self.right.astype(F32)


def beside(moves, job=None):
    arrived, done = lax.optimization_barrier(([m.start() for m in moves], job() if job else None))
    for move, a in zip(moves, arrived):
        move.take(a)
    return done


def steps(move, count, jobs=()):
    made = []
    for k in range(count):
        made.append(beside([move], jobs[k] if k < len(jobs) else None))
    return made


def gather_rows(packed):
    return lax.all_gather(packed, "dp", axis=1, tiled=True)


def scatter_rows(packed):
    return lax.psum_scatter(packed, "dp", scatter_dimension=1, tiled=True)


def split_rows(packed, counts):
    out, at = [], 0
    for count in counts:
        out.append(packed[at : at + count])
        at += count
    return out


def ranks(mask):
    number = mask.shape[0]
    block = 128
    pieces = mask.reshape(number // block, block, E).astype(BF)
    lower = jnp.tril(jnp.ones((block, block), BF), -1)
    inside = jnp.einsum("ij,bje->bie", lower, pieces, preferred_element_type=F32)
    totals = jnp.sum(pieces.astype(F32), axis=1).astype(BF)
    ahead = jnp.tril(jnp.ones((number // block, number // block), BF), -1)
    before = dot(ahead, totals, 1, 0)
    return (inside + before[:, None, :]).reshape(number, E)


def per_device(
    layer_input, cotangent, first_gain, query_weight, latent_down, latent_gain, latent_up,
    output_weight, second_gain, router_weight, expert_gate, expert_up, expert_down,
    shared_gate, shared_up, shared_down, routes,
):
    line = Line()
    n_dp = lax.axis_size("dp")
    wide = D // n_dp
    number = layer_input.shape[0]
    heads_here = output_weight.shape[0] // DV
    fe = expert_down.shape[1]
    my_columns = layer_input.shape[1]
    column_start = line.index * my_columns
    row_start, row_count = line.row_start(number)

    half = DR // 2
    spare_heads = 2 - heads_here
    up_rows = latent_up.size // wide
    by_head = query_weight.T.reshape(heads_here, DN + DR, wide)
    blank = jnp.zeros((spare_heads * half, wide), BF)
    gains = jnp.zeros((16, wide), BF)
    gains = gains.at[0].set(first_gain).at[1].set(second_gain)
    gains = gains.at[2, : latent_gain.shape[0]].set(latent_gain)
    down = latent_down.T
    queries_wide = heads_here * DN + DN
    latent_wide = R + DN
    attend_pack = [
        by_head[:, :DN].reshape(heads_here * DN, wide),
        by_head[:, DN : DN + half].reshape(heads_here * half, wide), blank,
        by_head[:, DN + half :].reshape(heads_here * half, wide), blank,
        down[: R + half], down[R : R + half], down[R + half :], down[R + half :],
        latent_up.reshape(up_rows, wide), gains, router_weight.T, output_weight,
    ]
    attend_packed = gather_rows(jnp.concatenate([m for m in attend_pack if m.shape[0]], axis=0))
    wproj, wup, gains, wr, wo = split_rows(
        attend_packed, [queries_wide + latent_wide, up_rows, 16, E, output_weight.shape[0]]
    )
    wup = wup.reshape(up_rows, n_dp, wide).transpose(1, 0, 2).reshape(R, -1)
    first_g = gains[0].astype(F32)
    second_g = gains[1].astype(F32)
    latent_g = gains[2].reshape(n_dp, wide)[:, : R // n_dp].reshape(R).astype(F32)
    cosine, sine = (jnp.asarray(table) for table in tables())

    n_units = E * fe + shared_down.shape[0]
    n0 = n_units // 2 // 256 * 256
    n1 = n_units - n0
    last_step = line.chips - 1
    gate = expert_gate.transpose(0, 2, 1).reshape(E * fe, wide)
    up = expert_up.transpose(0, 2, 1).reshape(E * fe, wide)
    move = Gather(line, layer_input)
    downs, early, late = steps(move, 3, (
        lambda: jnp.concatenate([expert_down.reshape(E * fe, wide), shared_down], axis=0),
        lambda: jnp.concatenate([gate[:n0], up[:n0]], axis=0),
        lambda: jnp.concatenate([gate[n0:], shared_gate.T, up[n0:], shared_up.T], axis=0),
    ))
    steps(move, last_step - 3)
    downs, early, late = gather_rows(downs), gather_rows(early), gather_rows(late)
    down0, down1 = downs[:n0], downs[n0:]

    tile = 256
    core = line.c.reshape(1).astype(jnp.int32)
    input_pieces, input_at = line.column_pieces(move.result())
    input_pieces, cotangent = lax.optimization_barrier((input_pieces, cotangent))
    grad_move = Gather(line, cotangent)

    def project():
        rows, first_round, r1 = place_columns(input_pieces, input_at, first_g)
        return rows, first_round, r1, dot(first_round, wproj, 1, 1)

    rows, first_round, r1, proj = beside([grad_move], project)
    q, kr, kv, latent, mixed, log_total = attend(proj, wup, latent_g[None], cosine, sine, heads_here)
    mine, theirs = line.halves(mixed)
    arrived = line.swap(dot(theirs, wo, 1, 0, BF))
    move = line.row_scatter(total(dot(mine, wo, 1, 0, BF), arrived))
    for _ in range(last_step - 1):
        beside([move, grad_move])
    (grad,) = beside([move], lambda: place_columns(*line.column_pieces(grad_move.result())))
    hidden_rows = (
        lax.dynamic_slice_in_dim(rows, row_start, row_count, 0).astype(F32) + move.result()
    ).astype(BF)
    move = Gather(line, hidden_rows)
    back0, back1 = steps(move, 2, (
        lambda: lift_back(grad, down0, 0, n0, tile),
        lambda: lift_back(grad, down1, 0, n1, tile),
    ))
    steps(move, last_step - 2)
    hidden_pieces, hidden_at = line.row_pieces(move.result())
    named = jnp.any(routes[:, :, None] == jnp.arange(E, dtype=jnp.int32)[None, None, :], axis=1)
    kept = jnp.where(named & (ranks(named) < CAP), 1.0, 0.0)
    second_round, hidden_columns, gating, weight = norm_rows(
        hidden_pieces, hidden_at, line.index.reshape(1).astype(jnp.int32), my_columns, second_g, wr, kept
    )

    stack0, pair0 = units(second_round, early, back0, weight, fe, 0, tile)
    deltas = outer(stack0, 0, 2, second_round, 3 * n0, 0)
    deltas = outer(stack0, 2, 1, grad, 3 * n0, 2, deltas)
    deltas, stack0 = lax.optimization_barrier((deltas, stack0))
    early_sums = scatter_rows(deltas)
    second_terms = back([(stack0, 0, early, n0, 0), (stack0, 1, early, n0, 1)], None, F32, tile)
    stack1, pair1 = units(second_round, late, back1, weight, fe, n0, tile)
    second_terms = back(
        [(stack1, 0, late, n1, 0), (stack1, 1, late, n1, 1)], second_terms, BF, tile, (pair0, pair1)
    )

    branch_terms = [(stack0, 2, down0, n0, 0), (stack1, 2, down1, n1, 0)]
    mine, theirs = line.halves(second_terms)
    arrived, branch_theirs = lax.optimization_barrier(
        (line.swap(theirs), back(branch_terms, None, BF, tile, (), 1 - core, line.chips))
    )
    move = line.row_scatter(total(mine, arrived))
    deltas = beside([move], lambda: outer(stack1, 0, 1, second_round, 3 * n1, 0))
    deltas = beside([move], lambda: outer(stack1, 1, 1, second_round, 3 * n1, 1, deltas))
    branch_arrived = line.swap(branch_theirs)
    deltas, branch_arrived = beside(
        [move], lambda: (outer(stack1, 2, 1, grad, 3 * n1, 2, deltas), branch_arrived)
    )
    steps(move, last_step - 3)
    summed = move.result()
    early_sums, summed, deltas = lax.optimization_barrier((early_sums, summed, deltas))
    late_sums = scatter_rows(deltas)

    def own_rows(a):
        return lax.dynamic_slice_in_dim(a, row_start, row_count, 0)

    gating_rows, kept_rows, x2 = own_rows(gating), own_rows(kept), own_rows(second_round)
    u = summed[:, D : D + E] * kept_rows
    logits_delta = gating_rows * (u - jnp.sum(gating_rows * u, axis=-1, keepdims=True))
    d2 = summed[:, :D] + dot(logits_delta.astype(BF), wr, 1, 0)
    v2 = hidden_rows.astype(F32)
    r2 = lax.rsqrt(jnp.mean(v2 * v2, axis=-1, keepdims=True) + EPSILON)
    vgd = jnp.mean(v2 * second_g * d2, axis=-1, keepdims=True)
    hidden_delta = own_rows(grad).astype(F32) + r2 * second_g * d2 - v2 * (r2**3) * vgd
    move = Gather(line, hidden_delta.astype(BF))
    branch_mine = beside([move], lambda: back(branch_terms, None, BF, tile, (), core, line.chips))
    branch_move = line.column_scatter(total(branch_mine, branch_arrived))
    router_delta, second_gain_delta = beside([move, branch_move], lambda: (
        dot(x2, logits_delta.astype(BF), 0, 0), jnp.sum(d2 * v2 * r2, axis=0)
    ))
    for _ in range(last_step - 2):
        beside([move, branch_move])
    delta_pieces, delta_at = line.row_pieces(move.result())

    def heads_back():
        placed = place_rows(delta_pieces, delta_at)
        delta_mixed = dot(placed, wo, 1, 1, BF)
        return placed, attend_back(q, kr, kv, mixed, log_total, delta_mixed, cosine, sine, heads_here)

    hidden_delta, heads = beside([branch_move], heads_back)
    layer_output = (hidden_columns.astype(F32) + branch_move.result()).astype(BF)
    delta_queries, delta_pairs, delta_kr, query_dot = heads
    delta_wq = dot(delta_queries, first_round, 0, 0)
    query_gain = jnp.sum(wproj[:queries_wide].astype(F32) * delta_wq, axis=0)
    per_entry = jnp.concatenate([second_gain_delta[:, None], query_gain[:, None], router_delta], axis=1)
    if number > D:
        per_entry = jnp.concatenate([per_entry, jnp.zeros((number - D, E + 2), F32)], axis=0)
    small = jnp.concatenate(
        [dot(delta_pairs, wup, 1, 1),
         delta_kr[:, :half] + delta_kr[:, half:DR], delta_kr[:, DR : DR + half] + delta_kr[:, DR + half :],
         query_dot, per_entry, jnp.zeros((number, 63 - 2 - E), F32)], axis=1,
    ).astype(BF)
    first_terms = [(delta_queries, 0, attend_packed, queries_wide, 0)]
    mine, theirs = line.halves(small)
    move = line.row_scatter(total(mine, line.swap(theirs)))

    def attend_deltas():
        delta_wup = dot(latent, delta_pairs, 0, 0, BF)
        return jnp.concatenate(
            [delta_wq.astype(BF),
             delta_wup.reshape(n_dp, up_rows, wide).transpose(1, 0, 2).reshape(up_rows, D),
             dot(mixed, hidden_delta, 0, 0, BF)], axis=0)

    theirs, mine, deltas = steps(move, 3, (
        lambda: back(first_terms, None, BF, tile, (), 1 - core, line.chips),
        lambda: back(first_terms, None, BF, tile, (), core, line.chips),
        attend_deltas,
    ))
    steps(move, last_step - 3)
    small = move.result().astype(BF)
    deltas, small, layer_output = lax.optimization_barrier((deltas, small, layer_output))
    attend_sums = scatter_rows(deltas).astype(F32)
    move = Gather(line, small)
    first_move = line.column_scatter(total(mine, line.swap(theirs)))
    steps(move, last_step - 1)
    beside([move, first_move])
    small_pieces, small_at = line.row_pieces(move.result())
    small_pieces, late_sums = lax.optimization_barrier((small_pieces, late_sums))
    wld = wproj[queries_wide:]

    def last():
        small = place_rows(small_pieces, small_at)
        delta_latent, dots, gain_delta = latent_back(small, proj, latent_g[None], cosine, sine)
        latent_row = jnp.pad(gain_delta.reshape(n_dp, R // n_dp), ((0, 0), (0, wide - R // n_dp))).reshape(1, D)
        return delta_latent, dots, last_pack(delta_latent, first_round, wld, small, first_g[None], latent_row)

    delta_latent, dots, pack = beside([first_move], last)
    steps(first_move, last_step - 2)
    first_share = first_move.result()
    last_sums = scatter_rows(pack).astype(F32)
    dwld, vectors = last_sums[:latent_wide], last_sums[latent_wide:]
    dwq, dwup, dwo = split_rows(attend_sums, [queries_wide, up_rows, output_weight.shape[0]])
    content = heads_here * DN
    dwq = jnp.concatenate(
        [dwq[:content].reshape(heads_here, DN, wide),
         dwq[content : content + heads_here * half].reshape(heads_here, half, wide),
         dwq[content + DR : content + DR + heads_here * half].reshape(heads_here, half, wide)], axis=1
    ).reshape(heads_here * (DN + DR), wide)
    dwld = jnp.concatenate([dwld[: R + half], dwld[R + DR : R + DR + half]], axis=0)

    first_share = first_share + dot(
        delta_latent, lax.dynamic_slice_in_dim(wld, column_start, my_columns, 1), 1, 0
    )
    vc = layer_input.astype(F32)
    gc = lax.dynamic_slice_in_dim(first_g, column_start, my_columns, 0)
    input_delta = (
        lax.dynamic_slice_in_dim(hidden_delta, column_start, my_columns, 1).astype(F32)
        + r1 * gc * first_share
        - vc * (r1 * r1) * (dots / D)
    )

    def units_delta(k):
        return early_sums[k * n0 : (k + 1) * n0], late_sums[k * n1 : (k + 1) * n1]

    def expert_delta(k):
        first, second = units_delta(k)
        return jnp.concatenate([first, second[: E * fe - n0]], axis=0).astype(F32).reshape(E, fe, wide)

    def shared_delta(k):
        return units_delta(k)[1][E * fe - n0 :].astype(F32)

    return (
        layer_output, input_delta, vectors[E + 1], dwq.T, dwld.T, vectors[E + 2, : R // n_dp],
        dwup.reshape(latent_up.shape), dwo, vectors[E], vectors[:E].T,
        expert_delta(0).transpose(0, 2, 1), expert_delta(1).transpose(0, 2, 1), expert_delta(2),
        shared_delta(0).T, shared_delta(1).T, shared_delta(2),
    )


def solution(mesh):
    in_specs = (
        P("dp", "tensor"), P("dp", "tensor"), P("dp"), P("dp", "tensor"), P("dp", None), P("dp"),
        P("dp", "tensor"), P("tensor", "dp"), P("dp"), P("dp", None), P(None, "dp", "tensor"),
        P(None, "dp", "tensor"), P(None, "tensor", "dp"), P("dp", "tensor"), P("dp", "tensor"),
        P("tensor", "dp"), P("dp", None),
    )
    out_specs = (
        P("dp", "tensor"), P("dp", "tensor"), P("dp"), P("dp", "tensor"), P("dp", None), P("dp"),
        P("dp", "tensor"), P("tensor", "dp"), P("dp"), P("dp", None), P(None, "dp", "tensor"),
        P(None, "dp", "tensor"), P(None, "tensor", "dp"), P("dp", "tensor"), P("dp", "tensor"),
        P("tensor", "dp"),
    )
    return jax.shard_map(
        per_device, mesh=mesh, in_specs=in_specs, out_specs=out_specs, check_vma=False
    )
```

```python
import functools

import jax
import jax.numpy as jnp
import numpy as np
from jax import lax
from jax.experimental import pallas as pl
from jax.experimental.pallas import tpu as pltpu
from jax.sharding import PartitionSpec as P

D = 2048
DN = 128
DR = 64
DV = 128
R = 512
E = 16
LEN = 1024
CAP = 864
EPSILON = 1e-06
SCALE = (DN + DR) ** -0.5
BLOCK = 256
BF = jnp.bfloat16
F32 = jnp.float32


def dot(a, b, ca, cb, out=F32):
    return lax.dot_general(
        a, b, (((ca,), (cb,)), ((), ())), preferred_element_type=F32
    ).astype(out)


VMEM_LIMIT = 58 * 2**20
NT=(((1,),(1,)),((),()))
NN=(((1,),(0,)),((),()))
TN=(((0,),(0,)),((),()))

def mm(a,b,dims):
    return lax.dot_general(a,b,dims,preferred_element_type=F32)

def params(n):
    return pltpu.CompilerParams(dimension_semantics=("arbitrary",)*n, vmem_limit_bytes=VMEM_LIMIT)

def once(shape, index):
    return pl.BlockSpec(shape, index, pipeline_mode=pl.Buffered(1))

def rows_once(n, wide, first):
    return pl.BlockSpec((pl.Element(n), pl.Element(wide)), lambda i: (first, 0), pipeline_mode=pl.Buffered(1))

def place_matrix(fe, first, n):
    col=lax.broadcasted_iota(jnp.int32,(E,n),1)+first; row=lax.broadcasted_iota(jnp.int32,(E,n),0)*fe
    return jnp.where((col>=row)&(col<row+fe),1.0,0.0).astype(BF)

def units_kernel(fe, first, x_ref, wg_ref, wu_ref, b_ref, w_ref, out_ref, pair_ref):
    x=x_ref[...]; n=wg_ref.shape[0]
    pre=mm(x,wg_ref[...],NT); lift=mm(x,wu_ref[...],NT); back=b_ref[...].astype(F32)
    w=w_ref[...]; hi=w.astype(BF); lo=(w-hi.astype(F32)).astype(BF)
    place=place_matrix(fe,first,n)
    spread=mm(jnp.concatenate([hi,lo],axis=1),jnp.concatenate([place,place],axis=0),NN)
    if first+n>E*fe:
        spread=jnp.where(lax.broadcasted_iota(jnp.int32,spread.shape,1)>=E*fe-first,1.0,spread)
    s=0.5+0.5*jnp.tanh(0.5*pre)
    silu=pre*s
    act=silu*lift
    pair_ref[...]=mm((act*back).astype(BF),place,NT)
    back=back*spread
    out_ref[0]=(back*lift*(s+silu*(1.0-s))).astype(BF)
    out_ref[1]=(back*silu).astype(BF)
    out_ref[2]=(act*spread).astype(BF)

def units(x,packed,back,weight,fe,first,bt):
    T,D=x.shape; n=back.shape[1]; r=weight.shape[1]
    ins=[pl.BlockSpec((bt,D),lambda i:(i,0))]+[once((n,D),lambda i,k=k:(k,0)) for k in range(2)]
    ins+=[pl.BlockSpec((bt,n),lambda i:(i,0)),pl.BlockSpec((bt,r),lambda i:(i,0))]
    outs=[jax.ShapeDtypeStruct((3,T,n),BF),jax.ShapeDtypeStruct((T,r),F32)]
    return pl.pallas_call(functools.partial(units_kernel,fe,first),grid=(T//bt,),in_specs=ins,
        out_specs=[pl.BlockSpec((3,bt,n),lambda i:(0,i,0)),pl.BlockSpec((bt,r),lambda i:(i,0))],out_shape=outs,
        compiler_params=params(1),
        cost_estimate=pl.CostEstimate(flops=4*T*D*n,bytes_accessed=2*(T*D+2*n*D+4*T*n),transcendentals=T*n))(x,packed,packed,back,weight)

def lift_kernel(g_ref,w_ref,o_ref):
    o_ref[...]=mm(g_ref[...],w_ref[...],NT).astype(BF)

def lift_back(g,packed,at,n,bt):
    T,D=g.shape
    return pl.pallas_call(lift_kernel,grid=(T//bt,),
        in_specs=[pl.BlockSpec((bt,D),lambda i:(i,0)),rows_once(n,D,at)],
        out_specs=pl.BlockSpec((bt,n),lambda i:(i,0)),out_shape=jax.ShapeDtypeStruct((T,n),BF),compiler_params=params(1),
        cost_estimate=pl.CostEstimate(flops=2*T*D*n,bytes_accessed=2*(T*D+n*D+T*n),transcendentals=0))(g,packed)

def back_kernel(pairs, added, beside, *refs):
    out=refs[-1]
    acc=None
    if added: acc=refs[0][...].astype(F32)
    rs=refs[added:]
    for k in range(pairs):
        a=rs[2*k]; b=rs[2*k+1]
        a=a[0] if len(a.shape)==3 else a[...]
        p=mm(a,b[...],NN)
        acc=p if acc is None else acc+p
    if beside:
        wide=acc.shape[1]
        out[:,:wide]=acc.astype(out.dtype)
        more=sum(r[...] for r in refs[-1-beside:-1])
        gap=jnp.zeros((acc.shape[0],out.shape[1]-wide-more.shape[1]),F32)
        out[:,wide:]=jnp.concatenate([more,gap],axis=1).astype(out.dtype)
    else:
        out[...]=acc.astype(out.dtype)

def core_kernel(pairs, core_ref, *refs):
    out=refs[-1]
    chips,_,w=out.shape
    for z in range(chips):
        at=pl.ds(pl.multiple_of((2*z+core_ref[0])*w,w),w)
        acc=None
        for k in range(pairs):
            a=refs[2*k]; b=refs[2*k+1]
            p=mm(a[0] if len(a.shape)==3 else a[...],b[:,at],NN)
            acc=p if acc is None else acc+p
        out[z]=acc.astype(BF)

def back(terms, added, out_dtype, bt, beside=(), core=None, chips=0):
    T=terms[0][0].shape[-2]; D=terms[0][2].shape[1]
    ins=[];args=[];fl=0;by=0
    if core is not None:
        ins.append(pl.BlockSpec(memory_space=pltpu.SMEM)); args.append(core)
    if added is not None:
        ins.append(pl.BlockSpec((bt,D),lambda i:(i,0))); args.append(added)
    for st,k,packed,n,at in terms:
        if st.ndim==3: ins.append(pl.BlockSpec((1,bt,n),lambda i,k=k:(k,i,0)))
        else: ins.append(pl.BlockSpec((bt,n),lambda i:(i,0)))
        ins.append(rows_once(n,D,at))
        args+= [st,packed]; fl+=2*T*D*n; by+=2*(T*n+n*D)
    for more in beside:
        ins.append(pl.BlockSpec((bt,more.shape[1]),lambda i:(i,0))); args.append(more)
    body=functools.partial(back_kernel,len(terms),0 if added is None else 1,len(beside))
    if beside:
        shape=(T,D+128); ospec=pl.BlockSpec((bt,D+128),lambda i:(i,0))
    elif core is not None:
        w=D//(2*chips); fl//=2
        shape=(chips,T,w); ospec=pl.BlockSpec((chips,bt,w),lambda i:(0,i,0))
        body=functools.partial(core_kernel,len(terms))
    else:
        shape=(T,D); ospec=pl.BlockSpec((bt,D),lambda i:(i,0))
    return pl.pallas_call(body,grid=(T//bt,),in_specs=ins,out_specs=ospec,out_shape=jax.ShapeDtypeStruct(shape,out_dtype),
        compiler_params=params(1),cost_estimate=pl.CostEstimate(flops=fl,bytes_accessed=by+4*T*D,transcendentals=0))(*args)

def outer_kernel(s_ref,x_ref,*refs):
    refs[-1][...]=mm(s_ref[0],x_ref[...],TN).astype(BF)

def outer(stack,first,count,x,total,at,into=None,bc=512):
    T,D=x.shape; n=stack.shape[2]
    ins=[pl.BlockSpec((1,T,n),lambda k,j:(first+k,0,0)),pl.BlockSpec((T,bc),lambda k,j:(0,j))]
    args=[stack,x]; al={}
    if into is not None:
        ins.append(pl.BlockSpec(memory_space=pl.ANY)); args.append(into); al={2:0}
    return pl.pallas_call(outer_kernel,grid=(count,D//bc),in_specs=ins,
        out_specs=pl.BlockSpec((n,bc),lambda k,j:(at+k,j)),out_shape=jax.ShapeDtypeStruct((total,D),BF),
        input_output_aliases=al,compiler_params=params(2),
        cost_estimate=pl.CostEstimate(flops=2*count*T*D*n,bytes_accessed=2*count*(T*n+n*D+T*D),transcendentals=0))(*args)


def place_columns_kernel(chips, norm, at_ref, *refs):
    pieces=refs[:2*chips]
    refs=refs[2*chips:]
    if norm:
        gain_ref, w_ref, out_ref, round_ref, r_ref, proj_ref = refs
    else:
        (out_ref,) = refs
    w=pieces[0].shape[1]
    for k in range(2*chips):
        out_ref[:,pl.ds(pl.multiple_of(at_ref[k]*w,w),w)]=pieces[k][...]
    if norm:
        v=out_ref[...].astype(F32)
        r=lax.rsqrt(jnp.mean(v*v,axis=-1,keepdims=True)+EPSILON)
        round_ref[...]=(v*r*gain_ref[...]).astype(BF)
        r_ref[...]=r
        proj_ref[...]=mm(round_ref[...],w_ref[...],NT)

def place_columns(pieces, at, gain=None, packed=None, count=0, bt=256):
    T,w=pieces[0].shape; n=len(pieces)
    ins=[pl.BlockSpec(memory_space=pltpu.SMEM)]+[pl.BlockSpec((bt,w),lambda i:(i,0))]*n
    args=[at]+list(pieces)
    outs=[jax.ShapeDtypeStruct((T,n*w),BF)]; specs=[pl.BlockSpec((bt,n*w),lambda i:(i,0))]
    if gain is not None:
        ins+=[pl.BlockSpec((1,n*w),lambda i:(0,0)),rows_once(count,n*w,0)]; args+=[gain[None],packed]
        outs+=[jax.ShapeDtypeStruct((T,n*w),BF),jax.ShapeDtypeStruct((T,1),F32),jax.ShapeDtypeStruct((T,count),F32)]
        specs+=[pl.BlockSpec((bt,n*w),lambda i:(i,0)),pl.BlockSpec((bt,1),lambda i:(i,0)),pl.BlockSpec((bt,count),lambda i:(i,0))]
    return pl.pallas_call(functools.partial(place_columns_kernel,n//2,gain is not None),grid=(T//bt,),
        in_specs=ins,out_specs=specs,out_shape=outs,compiler_params=params(1),
        cost_estimate=pl.CostEstimate(flops=(6+2*count)*T*n*w,bytes_accessed=6*T*n*w,transcendentals=T))(*args)

def place_rows_kernel(n, times, at_ref, *refs):
    pieces=refs[:n]; refs=refs[n:]
    if times: w_ref,out_ref,made_ref,sem=refs
    else: out_ref,sem=refs
    rows=pieces[0].shape[0]
    to=[pl.ds(pl.multiple_of(at_ref[k]*rows,rows),rows) for k in range(n)]
    copies=[pltpu.make_async_copy(pieces[k],out_ref.at[to[k]],sem.at[k]) for k in range(n)]
    for c in copies: c.start()
    if times:
        for k in range(n): made_ref[to[k]]=mm(pieces[k][...],w_ref[...],NT).astype(BF)
    for c in copies: c.wait()

def place_rows(pieces, at, weight=None):
    rows,w=pieces[0].shape; n=len(pieces)
    vmem=pl.BlockSpec(memory_space=pltpu.VMEM)
    outs=[jax.ShapeDtypeStruct((n*rows,w),BF)]; specs=[pl.BlockSpec(memory_space=pl.ANY)]; more=[]
    if weight is not None:
        outs.append(jax.ShapeDtypeStruct((n*rows,weight.shape[0]),BF)); specs.append(vmem); more=[weight]
    return pl.pallas_call(functools.partial(place_rows_kernel,n,bool(more)),
        in_specs=[pl.BlockSpec(memory_space=pltpu.SMEM)]+[vmem]*(n+len(more)),
        out_specs=specs,out_shape=outs,
        scratch_shapes=[pltpu.SemaphoreType.DMA((n,))],compiler_params=pltpu.CompilerParams(vmem_limit_bytes=VMEM_LIMIT),
        cost_estimate=pl.CostEstimate(flops=2*n*rows*w*(weight.shape[0] if more else 0),bytes_accessed=4*n*rows*w,transcendentals=0))(at,*pieces,*more)

def norm_rows_kernel(n, at_ref, col_ref, gain_ref, wr_ref, kept_ref, *refs):
    pieces=refs[:n]; round_ref,cols_ref,gating_ref,weight_ref,made,cut,sem,sem2=refs[n:]
    rows=pieces[0].shape[0]; w=cut.shape[2]
    copies=[]
    for k in range(n):
        v=pieces[k][...].astype(F32)
        r=lax.rsqrt(jnp.mean(v*v,axis=-1,keepdims=True)+EPSILON)
        made[k]=(v*r*gain_ref[...]).astype(BF)
        cut[k]=pieces[k][:,pl.ds(pl.multiple_of(col_ref[0]*w,w),w)]
        to=pl.ds(pl.multiple_of(at_ref[k]*rows,rows),rows)
        copies.append(pltpu.make_async_copy(made.at[k],round_ref.at[to],sem.at[k]))
        copies.append(pltpu.make_async_copy(cut.at[k],cols_ref.at[to],sem2.at[k]))
        copies[-2].start(); copies[-1].start()
        logits=mm(made[k],wr_ref[...],NT)
        e=jnp.exp(logits-jnp.max(logits,axis=-1,keepdims=True))
        gating=e/jnp.sum(e,axis=-1,keepdims=True)
        gating_ref[to]=gating
        weight_ref[to]=gating*kept_ref[to]
    for c in copies: c.wait()

def norm_rows(pieces, at, column, w, gain, router, kept):
    rows,wide=pieces[0].shape; n=len(pieces)
    vmem=pl.BlockSpec(memory_space=pltpu.VMEM)
    return pl.pallas_call(functools.partial(norm_rows_kernel,n),
        in_specs=[pl.BlockSpec(memory_space=pltpu.SMEM)]*2+[vmem]*(n+3),
        out_specs=[pl.BlockSpec(memory_space=pl.ANY)]*2+[vmem]*2,
        out_shape=[jax.ShapeDtypeStruct((n*rows,wide),BF),jax.ShapeDtypeStruct((n*rows,w),BF)]+[jax.ShapeDtypeStruct((n*rows,E),F32)]*2,
        scratch_shapes=[pltpu.VMEM((n,rows,wide),BF),pltpu.VMEM((n,rows,w),BF),pltpu.SemaphoreType.DMA((n,)),pltpu.SemaphoreType.DMA((n,))],
        compiler_params=pltpu.CompilerParams(vmem_limit_bytes=VMEM_LIMIT),
        cost_estimate=pl.CostEstimate(flops=6*n*rows*wide,bytes_accessed=4*n*rows*wide,transcendentals=n*rows))(at,column,gain[None],router,kept,*pieces)

def small_kernel(pairs_ref, up_ref, kr_ref, dot_ref, entry_ref, out_ref):
    bt=out_ref.shape[0]
    out_ref[:,:R]=mm(pairs_ref[...],up_ref[...],NT).astype(BF)
    h=DR//2
    kr=kr_ref[...]
    gap=jnp.zeros((bt,DR-1-entry_ref.shape[1]),F32)
    out_ref[:,R:]=jnp.concatenate(
        [kr[:,:h]+kr[:,h:DR],kr[:,DR:DR+h]+kr[:,DR+h:],dot_ref[...],entry_ref[...],gap],axis=1).astype(BF)

def small_terms(pairs, up, kr, dots, entries, bt=512):
    T=pairs.shape[0]
    def rows(a): return pl.BlockSpec((bt,a.shape[1]),lambda i:(i,0))
    return pl.pallas_call(small_kernel,grid=(T//bt,),
        in_specs=[rows(pairs),pl.BlockSpec(up.shape,lambda i:(0,0)),rows(kr),rows(dots),rows(entries)],
        out_specs=pl.BlockSpec((bt,R+DN),lambda i:(i,0)),out_shape=jax.ShapeDtypeStruct((T,R+DN),BF),
        compiler_params=params(1),
        cost_estimate=pl.CostEstimate(flops=2*T*R*pairs.shape[1],bytes_accessed=8*T*R,transcendentals=0))(pairs,up,kr,dots,entries)

def latent_back_kernel(small_ref, proj_ref, gain_ref, cos_ref, sin_ref, delta_ref, dots_ref, gain_delta_ref):
    i=pl.program_id(0)
    at=proj_ref.shape[1]-R-DN
    dl=small_ref[:,:R].astype(F32)
    vl=proj_ref[:,at:at+R]
    rl=lax.rsqrt(jnp.mean(vl*vl,axis=-1,keepdims=True)+EPSILON)
    gain=gain_ref[...]
    part=jnp.sum(dl*vl*rl,axis=0,keepdims=True)
    @pl.when(i==0)
    def _(): gain_delta_ref[...]=part
    @pl.when(i>0)
    def _(): gain_delta_ref[...]+=part
    gd=gain*dl
    head=rl*gd-vl*(rl*rl*rl)*jnp.mean(vl*gd,axis=-1,keepdims=True)
    beyond=small_ref[:,R:]
    row=lax.broadcasted_iota(jnp.int32,(DN,DN),0); col=lax.broadcasted_iota(jnp.int32,(DN,DN),1)
    h=DR//2
    put=jnp.where(((row<h)&(col==row))|((row>=h)&(row<DR)&(col==row+h)),1.0,0.0).astype(BF)
    spread=mm(beyond,put,NN)
    tail=spread*cos_ref[...]-pltpu.roll(spread,DR,1)*sin_ref[...]
    delta_ref[:,:R]=head.astype(BF)
    delta_ref[:,R:]=tail.astype(BF)
    own=jnp.sum(head*vl,axis=-1,keepdims=True)+jnp.sum(tail*proj_ref[:,at+R:],axis=-1,keepdims=True)
    lane=lax.broadcasted_iota(jnp.int32,beyond.shape,1)
    dots_ref[...]=own+jnp.sum(jnp.where(lane==DR,beyond.astype(F32),0.0),axis=-1,keepdims=True)

def latent_back(small, proj, gain, cosine, sine, bt=512):
    T,wide=small.shape; turns=LEN//bt
    return pl.pallas_call(latent_back_kernel,grid=(T//bt,),
        in_specs=[pl.BlockSpec((bt,wide),lambda i:(i,0)),pl.BlockSpec((bt,proj.shape[1]),lambda i:(i,0)),
                  pl.BlockSpec((1,R),lambda i:(0,0)),pl.BlockSpec((bt,DN),lambda i:(i%turns,0)),pl.BlockSpec((bt,DN),lambda i:(i%turns,0))],
        out_specs=[pl.BlockSpec((bt,R+DN),lambda i:(i,0)),pl.BlockSpec((bt,1),lambda i:(i,0)),pl.BlockSpec((1,R),lambda i:(0,0))],
        out_shape=[jax.ShapeDtypeStruct((T,R+DN),BF),jax.ShapeDtypeStruct((T,1),F32),jax.ShapeDtypeStruct((1,R),F32)],
        compiler_params=params(1),
        cost_estimate=pl.CostEstimate(flops=30*T*wide,bytes_accessed=8*T*wide,transcendentals=T))(small,proj,gain,cosine,sine)

def last_pack_kernel(delta_ref, x_ref, w_ref, small_ref, g_ref, latent_ref, out_ref):
    n=delta_ref.shape[1]
    d=mm(delta_ref[...],x_ref[...],TN)
    out_ref[:n]=d.astype(BF)
    sums=jnp.sum(w_ref[...].astype(F32)*d,axis=0,keepdims=True)
    row=lax.broadcasted_iota(jnp.int32,(32,DN),0); col=lax.broadcasted_iota(jnp.int32,(32,DN),1)
    at=DR+1
    pick=((row<E)&(col==row+at+2))|((row==E)&(col==at))|((row==E+1)&(col==at+1))
    v=mm(jnp.where(pick,1.0,0.0).astype(BF),small_ref[...],NT)
    line=lax.broadcasted_iota(jnp.int32,v.shape,0)
    v=jnp.where(line==E+1,(v+sums)/g_ref[...],v)
    out_ref[n:]=jnp.where(line==E+2,latent_ref[...],v).astype(BF)

def last_pack(delta, x, w, small, gain, latent_row, bc=512):
    T,D=x.shape; n=delta.shape[1]
    def cols(a): return pl.BlockSpec((a.shape[0],bc),lambda j:(0,j))
    return pl.pallas_call(last_pack_kernel,grid=(D//bc,),
        in_specs=[pl.BlockSpec((T,n),lambda j:(0,0)),cols(x),cols(w),pl.BlockSpec((bc,DN),lambda j:(j,R//DN)),cols(gain),cols(latent_row)],
        out_specs=pl.BlockSpec((n+32,bc),lambda j:(0,j)),out_shape=jax.ShapeDtypeStruct((n+32,D),BF),
        compiler_params=params(1),
        cost_estimate=pl.CostEstimate(flops=2*T*D*n,bytes_accessed=2*(T*D+2*n*D+T*n),transcendentals=0))(delta,x,w,small,gain,latent_row)


def turn(x, cosine, sine):
    return x*cosine+pltpu.roll(x,64,1)*sine

def slot_mask(shape, head):
    lane=lax.broadcasted_iota(jnp.int32,shape,1)
    low=head*(DR//2)
    inside=((lane>=low)&(lane<low+DR//2))|((lane>=low+DR)&(lane<low+DR+DR//2))
    return inside

def causal_scores(q, k, first):
    s=mm(q,k,NT)*SCALE
    row=lax.broadcasted_iota(jnp.int32,s.shape,0)+first
    col=lax.broadcasted_iota(jnp.int32,s.shape,1)
    return jnp.where(col<=row,s,-1e30)

def attend_kernel(heads, proj_ref, up_ref, gain_ref, cos_ref, sin_ref, q_ref, kr_ref, kv_ref, latent_ref, mixed_ref, lse_ref):
    content=heads*DN
    at=content+DN
    q_ref[:,:content]=proj_ref[:,:content].astype(BF)
    cosine,sine=cos_ref[...],sin_ref[...]
    q_ref[:,content:]=turn(proj_ref[:,content:at],cosine,sine).astype(BF)
    vl=proj_ref[:,at:at+R]
    latent_ref[...]=(vl*lax.rsqrt(jnp.mean(vl*vl,axis=-1,keepdims=True)+EPSILON)*gain_ref[...]).astype(BF)
    kr_ref[...]=turn(proj_ref[:,at+R:],cosine,sine).astype(BF)
    kv_ref[...]=mm(latent_ref[...],up_ref[...],NN).astype(BF)
    kr=kr_ref[...]
    for h in range(heads):
        kc=kv_ref[:,h*(DN+DV):h*(DN+DV)+DN]
        v=kv_ref[:,h*(DN+DV)+DN:(h+1)*(DN+DV)]
        k=jnp.concatenate([kc,jnp.where(slot_mask(kr.shape,h),kr,jnp.zeros_like(kr))],axis=1)
        for i in range(LEN//BLOCK):
            a,b=i*BLOCK,(i+1)*BLOCK
            q=jnp.concatenate([q_ref[a:b,h*DN:(h+1)*DN],q_ref[a:b,content:]],axis=1)
            s=causal_scores(q,k[:b],a)
            m=jnp.max(s,axis=-1,keepdims=True)
            e=jnp.exp(s-m)
            t=jnp.sum(e,axis=-1,keepdims=True)
            p=(e*(1.0/t)).astype(BF)
            mixed_ref[a:b,h*DV:(h+1)*DV]=mm(p,v[:b],NN).astype(BF)
            lse_ref[a:b,h:h+1]=m+jnp.log(t)

def attend(proj, up, gain, cosine, sine, heads):
    T=proj.shape[0]; wide=proj.shape[1]
    def rows(n): return pl.BlockSpec((LEN,n),lambda i:(i,0))
    def whole(a): return pl.BlockSpec(a.shape,lambda i:(0,0))
    qn=heads*DN+DN
    outs=[(qn,BF),(DN,BF),(heads*(DN+DV),BF),(R,BF),(heads*DV,BF),(heads,F32)]
    return pl.pallas_call(functools.partial(attend_kernel,heads),grid=(T//LEN,),
        in_specs=[rows(wide),whole(up),whole(gain),whole(cosine),whole(sine)],
        out_specs=[rows(n) for n,_ in outs],out_shape=[jax.ShapeDtypeStruct((T,n),d) for n,d in outs],
        compiler_params=params(1),
        cost_estimate=pl.CostEstimate(flops=T*LEN*heads*512,bytes_accessed=T*8000,transcendentals=T*LEN*heads//2))(proj,up,gain,cosine,sine)

def attend_back_kernel(heads, q_ref, kr_ref, kv_ref, mixed_ref, lse_ref, do_ref, cos_ref, sin_ref, dq_ref, dkv_ref, dkr_ref, dot_ref, dk_acc, dv_acc):
    content=heads*DN
    kr=kr_ref[...]
    for h in range(heads):
        kc=kv_ref[:,h*(DN+DV):h*(DN+DV)+DN]
        v=kv_ref[:,h*(DN+DV)+DN:(h+1)*(DN+DV)]
        mask=slot_mask(kr.shape,h)
        k=jnp.concatenate([kc,jnp.where(mask,kr,jnp.zeros_like(kr))],axis=1)
        for i in reversed(range(LEN//BLOCK)):
            a,b=i*BLOCK,(i+1)*BLOCK
            q=jnp.concatenate([q_ref[a:b,h*DN:(h+1)*DN],q_ref[a:b,content:]],axis=1)
            do=do_ref[a:b,h*DV:(h+1)*DV]
            p=jnp.exp(causal_scores(q,k[:b],a)-lse_ref[a:b,h:h+1])
            dp=mm(do,v[:b],NT)
            along=jnp.sum(do.astype(F32)*mixed_ref[a:b,h*DV:(h+1)*DV].astype(F32),axis=-1,keepdims=True)
            ds=(p*(dp-along)).astype(BF)
            pv=mm(p.astype(BF),do,TN)
            pk=mm(ds,q,TN)
            if i==LEN//BLOCK-1:
                dv_acc[...]=pv; dk_acc[...]=pk
            else:
                dv_acc[:b]+=pv; dk_acc[:b]+=pk
            dq=mm(ds,k[:b],NN)*SCALE
            d=jnp.sum(dq*q.astype(F32),axis=-1,keepdims=True)
            if h==0: dot_ref[a:b]=d
            else: dot_ref[a:b]+=d
            dq_ref[a:b,h*DN:(h+1)*DN]=dq[:,:DN].astype(BF)
            turned=turn(dq[:,DN:],cos_ref[a:b],-sin_ref[a:b])
            turned=jnp.where(mask[:b-a],turned,0.0).astype(BF)
            if h==0: dq_ref[a:b,content:]=turned
            else: dq_ref[a:b,content:]+=turned
        dkv_ref[:,h*(DN+DV):h*(DN+DV)+DN]=(dk_acc[:,:DN]*SCALE).astype(BF)
        dkv_ref[:,h*(DN+DV)+DN:(h+1)*(DN+DV)]=dv_acc[...].astype(BF)
        part=jnp.where(mask,dk_acc[:,DN:]*SCALE,0.0)
        if h==0: dkr_ref[...]=part
        else: dkr_ref[...]+=part

def attend_back(q,kr,kv,mixed,lse,do,cosine,sine,heads):
    T=q.shape[0]
    def rows(n): return pl.BlockSpec((LEN,n),lambda i:(i,0))
    def whole(a): return pl.BlockSpec(a.shape,lambda i:(0,0))
    args=(q,kr,kv,mixed,lse,do)
    outs=[(q.shape[1],BF),(kv.shape[1],BF),(DN,F32),(1,F32)]
    return pl.pallas_call(functools.partial(attend_back_kernel,heads),grid=(T//LEN,),
        in_specs=[rows(a.shape[1]) for a in args]+[whole(cosine),whole(sine)],
        out_specs=[rows(n) for n,_ in outs],out_shape=[jax.ShapeDtypeStruct((T,n),d) for n,d in outs],
        scratch_shapes=[pltpu.VMEM((LEN,2*DN),F32),pltpu.VMEM((LEN,DV),F32)],
        compiler_params=params(1),
        cost_estimate=pl.CostEstimate(flops=T*LEN*heads*1400,bytes_accessed=T*6000,transcendentals=T*LEN*heads//2))(*args,cosine,sine)

def tables():
    position=np.arange(LEN,dtype=np.float32)
    spread=(10000.0**(-np.arange(DR//2,dtype=np.float32)/(DR//2))).astype(np.float32)
    phase=(position[:,None]*spread[None,:]).astype(np.float32)
    c,s=np.cos(phase),np.sin(phase)
    return np.concatenate([c]*4,1).astype(np.float32),np.concatenate([-s,-s,s,s],1).astype(np.float32)


class Line:
    def __init__(self):
        self.n = lax.axis_size("tensor")
        self.chips = self.n // 2
        index = lax.axis_index("tensor")
        self.index = index
        self.z = index // 2
        self.c = index % 2

    def swap(self, a):
        return lax.ppermute(a, "tensor", [(i, i ^ 1) for i in range(self.n)])

    def shift(self, a, step, sources):
        pairs = [
            (2 * s + c, 2 * (s + step) + c)
            for s in sources
            if 0 <= s + step < self.chips
            for c in (0, 1)
        ]
        return lax.ppermute(a, "tensor", pairs)

    def pieces(self, own, order):
        n = self.chips
        out, at = [], []
        for k, piece in enumerate(own):
            chip = (self.z - k + n) % n
            out += [piece, self.swap(piece)]
            at += [order(chip, self.c), order(chip, 1 - self.c)]
        return out, jnp.stack(at).astype(jnp.int32)

    def row_pieces(self, own):
        return self.pieces(own, lambda chip, core: core * self.chips + chip)

    def column_pieces(self, own):
        return self.pieces(own, lambda chip, core: chip * 2 + core)

    def halves(self, p):
        half = p.shape[0] // 2
        return [lax.dynamic_slice_in_dim(p, c * half, half, 0) for c in (self.c, 1 - self.c)]

    def row_scatter(self, both):
        ch = both.shape[0] // self.chips
        return Scatter(self, lambda j: lax.dynamic_slice_in_dim(both, j * ch, ch, 0))

    def column_scatter(self, both):
        return Scatter(self, lambda j: lax.dynamic_index_in_dim(both, j, 0, False))

    def row_start(self, rows):
        ch = rows // self.n
        return (self.c * self.chips + self.z) * ch, ch


def total(mine, arrived):
    return (mine.astype(F32) + arrived.astype(F32)).astype(BF)


class Gather:
    def __init__(self, line, block):
        self.line, self.left, self.right = line, [block], [block]

    def start(self):
        n, k = self.line.chips, len(self.left)
        return (
            self.line.shift(self.left[-1], 1, range(k - 1, n)),
            self.line.shift(self.right[-1], -1, range(0, n - k + 1)),
        )

    def take(self, arrived):
        self.left.append(arrived[0])
        self.right.append(arrived[1])

    def result(self):
        n, z = self.line.chips, self.line.z
        return self.left[:1] + [jnp.where(z >= k, self.left[k], self.right[n - k]) for k in range(1, n)]


class Scatter:
    def __init__(self, line, block):
        self.line, self.block, self.step, self.left, self.right = line, block, 0, None, None

    def start(self):
        self.step += 1
        n, s, z = self.line.chips, self.step, self.line.z
        up = self.block(jnp.clip(n - s + z, 0, n - 1))
        down = self.block(jnp.clip(z - (n - s), 0, n - 1))
        if self.left is not None:
            up, down = total(up, self.left), total(down, self.right)
        return self.line.shift(up, 1, range(0, s)), self.line.shift(down, -1, range(n - s, n))

    def take(self, arrived):
        self.left, self.right = arrived

    def result(self):
        return self.block(self.line.z).astype(F32) + self.left.astype(F32) + self.right.astype(F32)


def beside(moves, job=None):
    arrived, done = lax.optimization_barrier(([m.start() for m in moves], job() if job else None))
    for move, a in zip(moves, arrived):
        move.take(a)
    return done


def steps(move, count, jobs=()):
    made = []
    for k in range(count):
        made.append(beside([move], jobs[k] if k < len(jobs) else None))
    return made


def gather_rows(packed):
    return lax.all_gather(packed, "dp", axis=1, tiled=True)


def scatter_rows(packed):
    return lax.psum_scatter(packed, "dp", scatter_dimension=1, tiled=True)


def split_rows(packed, counts):
    out, at = [], 0
    for count in counts:
        out.append(packed[at : at + count])
        at += count
    return out


def ranks(mask):
    number = mask.shape[0]
    block = 128
    pieces = mask.reshape(number // block, block, E).astype(BF)
    lower = jnp.tril(jnp.ones((block, block), BF), -1)
    inside = jnp.einsum("ij,bje->bie", lower, pieces, preferred_element_type=F32)
    totals = jnp.sum(pieces.astype(F32), axis=1).astype(BF)
    ahead = jnp.tril(jnp.ones((number // block, number // block), BF), -1)
    before = dot(ahead, totals, 1, 0)
    return (inside + before[:, None, :]).reshape(number, E)


def per_device(
    layer_input, cotangent, first_gain, query_weight, latent_down, latent_gain, latent_up,
    output_weight, second_gain, router_weight, expert_gate, expert_up, expert_down,
    shared_gate, shared_up, shared_down, routes,
):
    line = Line()
    n_dp = lax.axis_size("dp")
    wide = D // n_dp
    number = layer_input.shape[0]
    heads_here = output_weight.shape[0] // DV
    fe = expert_down.shape[1]
    my_columns = layer_input.shape[1]
    column_start = line.index * my_columns
    row_start, row_count = line.row_start(number)

    half = DR // 2
    spare_heads = 2 - heads_here
    up_rows = latent_up.size // wide
    by_head = query_weight.T.reshape(heads_here, DN + DR, wide)
    blank = jnp.zeros((spare_heads * half, wide), BF)
    gains = jnp.zeros((16, wide), BF)
    gains = gains.at[0].set(first_gain).at[1].set(second_gain)
    gains = gains.at[2, : latent_gain.shape[0]].set(latent_gain)
    down = latent_down.T
    queries_wide = heads_here * DN + DN
    latent_wide = R + DN
    attend_pack = [
        by_head[:, :DN].reshape(heads_here * DN, wide),
        by_head[:, DN : DN + half].reshape(heads_here * half, wide), blank,
        by_head[:, DN + half :].reshape(heads_here * half, wide), blank,
        down[: R + half], down[R : R + half], down[R + half :], down[R + half :],
        latent_up.reshape(up_rows, wide), gains, router_weight.T, output_weight,
    ]
    attend_packed = gather_rows(jnp.concatenate([m for m in attend_pack if m.shape[0]], axis=0))
    wproj, wup, gains, wr, wo = split_rows(
        attend_packed, [queries_wide + latent_wide, up_rows, 16, E, output_weight.shape[0]]
    )
    wup = wup.reshape(up_rows, n_dp, wide).transpose(1, 0, 2).reshape(R, -1)
    first_g = gains[0].astype(F32)
    second_g = gains[1].astype(F32)
    latent_g = gains[2].reshape(n_dp, wide)[:, : R // n_dp].reshape(R).astype(F32)
    cosine, sine = (jnp.asarray(table) for table in tables())

    n_units = E * fe + shared_down.shape[0]
    n0 = n_units // 2 // 256 * 256
    n1 = n_units - n0
    last_step = line.chips - 1
    gate = expert_gate.transpose(0, 2, 1).reshape(E * fe, wide)
    up = expert_up.transpose(0, 2, 1).reshape(E * fe, wide)
    move = Gather(line, layer_input)
    downs, early, late = steps(move, 3, (
        lambda: jnp.concatenate([expert_down.reshape(E * fe, wide), shared_down], axis=0),
        lambda: jnp.concatenate([gate[:n0], up[:n0]], axis=0),
        lambda: jnp.concatenate([gate[n0:], shared_gate.T, up[n0:], shared_up.T], axis=0),
    ))
    steps(move, last_step - 3)
    downs, early, late = gather_rows(downs), gather_rows(early), gather_rows(late)

    tile = 256
    core = line.c.reshape(1).astype(jnp.int32)
    input_pieces, input_at = line.column_pieces(move.result())
    input_pieces, cotangent = lax.optimization_barrier((input_pieces, cotangent))
    grad_move = Gather(line, cotangent)

    def project():
        return place_columns(input_pieces, input_at, first_g, attend_packed, queries_wide + latent_wide)

    rows, first_round, r1, proj = beside([grad_move], project)
    q, kr, kv, latent, mixed, log_total = attend(proj, wup, latent_g[None], cosine, sine, heads_here)
    mine, theirs = line.halves(mixed)
    arrived = line.swap(dot(theirs, wo, 1, 0, BF))
    move = line.row_scatter(total(dot(mine, wo, 1, 0, BF), arrived))
    for _ in range(last_step - 1):
        beside([move, grad_move])
    (grad,) = beside([move], lambda: place_columns(*line.column_pieces(grad_move.result())))
    hidden_rows = (
        lax.dynamic_slice_in_dim(rows, row_start, row_count, 0).astype(F32) + move.result()
    ).astype(BF)
    move = Gather(line, hidden_rows)
    back0, back1 = steps(move, 2, (
        lambda: lift_back(grad, downs, 0, n0, tile),
        lambda: lift_back(grad, downs, n0, n1, tile),
    ))
    steps(move, last_step - 2)
    hidden_pieces, hidden_at = line.row_pieces(move.result())
    named = jnp.any(routes[:, :, None] == jnp.arange(E, dtype=jnp.int32)[None, None, :], axis=1)
    kept = jnp.where(named & (ranks(named) < CAP), 1.0, 0.0)
    second_round, hidden_columns, gating, weight = norm_rows(
        hidden_pieces, hidden_at, line.index.reshape(1).astype(jnp.int32), my_columns, second_g, wr, kept
    )

    stack0, pair0 = units(second_round, early, back0, weight, fe, 0, tile)
    deltas = outer(stack0, 0, 2, second_round, 3 * n0, 0)
    deltas = outer(stack0, 2, 1, grad, 3 * n0, 2, deltas)
    deltas, stack0 = lax.optimization_barrier((deltas, stack0))
    early_sums = scatter_rows(deltas)
    second_terms = back([(stack0, 0, early, n0, 0), (stack0, 1, early, n0, n0)], None, F32, tile)
    stack1, pair1 = units(second_round, late, back1, weight, fe, n0, tile)
    second_terms = back(
        [(stack1, 0, late, n1, 0), (stack1, 1, late, n1, n1)], second_terms, BF, tile, (pair0, pair1)
    )

    branch_terms = [(stack0, 2, downs, n0, 0), (stack1, 2, downs, n1, n0)]
    mine, theirs = line.halves(second_terms)
    arrived, branch_theirs = lax.optimization_barrier(
        (line.swap(theirs), back(branch_terms, None, BF, tile, (), 1 - core, line.chips))
    )
    move = line.row_scatter(total(mine, arrived))
    deltas = beside([move], lambda: outer(stack1, 0, 1, second_round, 3 * n1, 0))
    deltas = beside([move], lambda: outer(stack1, 1, 1, second_round, 3 * n1, 1, deltas))
    branch_arrived = line.swap(branch_theirs)
    deltas, branch_arrived = beside(
        [move], lambda: (outer(stack1, 2, 1, grad, 3 * n1, 2, deltas), branch_arrived)
    )
    steps(move, last_step - 3)
    summed = move.result()
    early_sums, summed, deltas = lax.optimization_barrier((early_sums, summed, deltas))
    late_sums = scatter_rows(deltas)

    def own_rows(a):
        return lax.dynamic_slice_in_dim(a, row_start, row_count, 0)

    gating_rows, kept_rows, x2 = own_rows(gating), own_rows(kept), own_rows(second_round)
    u = summed[:, D : D + E] * kept_rows
    logits_delta = gating_rows * (u - jnp.sum(gating_rows * u, axis=-1, keepdims=True))
    d2 = summed[:, :D] + dot(logits_delta.astype(BF), wr, 1, 0)
    v2 = hidden_rows.astype(F32)
    r2 = lax.rsqrt(jnp.mean(v2 * v2, axis=-1, keepdims=True) + EPSILON)
    vgd = jnp.mean(v2 * second_g * d2, axis=-1, keepdims=True)
    hidden_delta = own_rows(grad).astype(F32) + r2 * second_g * d2 - v2 * (r2**3) * vgd
    move = Gather(line, hidden_delta.astype(BF))
    branch_mine = beside([move], lambda: back(branch_terms, None, BF, tile, (), core, line.chips))
    branch_move = line.column_scatter(total(branch_mine, branch_arrived))
    router_delta, second_gain_delta = beside([move, branch_move], lambda: (
        dot(x2, logits_delta.astype(BF), 0, 0), jnp.sum(d2 * v2 * r2, axis=0)
    ))
    for _ in range(last_step - 2):
        beside([move, branch_move])
    delta_pieces, delta_at = line.row_pieces(move.result())

    def heads_back():
        placed, delta_mixed = place_rows(delta_pieces, delta_at, wo)
        return placed, attend_back(q, kr, kv, mixed, log_total, delta_mixed, cosine, sine, heads_here)

    hidden_delta, heads = beside([branch_move], heads_back)
    layer_output = (hidden_columns.astype(F32) + branch_move.result()).astype(BF)
    delta_queries, delta_pairs, delta_kr, query_dot = heads
    delta_wq = dot(delta_queries, first_round, 0, 0)
    query_gain = jnp.sum(wproj[:queries_wide].astype(F32) * delta_wq, axis=0)
    per_entry = jnp.concatenate([second_gain_delta[:, None], query_gain[:, None], router_delta], axis=1)
    if number > D:
        per_entry = jnp.concatenate([per_entry, jnp.zeros((number - D, E + 2), F32)], axis=0)
    small = small_terms(delta_pairs, wup, delta_kr, query_dot, per_entry)
    first_terms = [(delta_queries, 0, attend_packed, queries_wide, 0)]
    mine, theirs = line.halves(small)
    move = line.row_scatter(total(mine, line.swap(theirs)))

    def attend_deltas():
        delta_wup = dot(latent, delta_pairs, 0, 0, BF)
        return jnp.concatenate(
            [delta_wq.astype(BF),
             delta_wup.reshape(n_dp, up_rows, wide).transpose(1, 0, 2).reshape(up_rows, D),
             dot(mixed, hidden_delta, 0, 0, BF)], axis=0)

    theirs, mine = steps(move, 2, (
        lambda: back(first_terms, None, BF, tile, (), 1 - core, line.chips),
        lambda: back(first_terms, None, BF, tile, (), core, line.chips),
    ))
    steps(move, last_step - 2)
    small, theirs, mine, layer_output = lax.optimization_barrier(
        (move.result().astype(BF), theirs, mine, layer_output)
    )
    move = Gather(line, small)
    deltas, arrived = beside([move], lambda: (attend_deltas(), line.swap(theirs)))
    attend_sums = scatter_rows(deltas).astype(F32)
    steps(move, last_step - 2)
    both, ahead = lax.optimization_barrier((total(mine, arrived), (move.left[-1], move.right[-1])))
    move.left[-1], move.right[-1] = ahead
    first_move = line.column_scatter(both)
    beside([move, first_move])
    small_pieces, small_at = line.row_pieces(move.result())
    small_pieces, late_sums = lax.optimization_barrier((small_pieces, late_sums))
    wld = wproj[queries_wide:]

    def last():
        (small,) = place_rows(small_pieces, small_at)
        delta_latent, dots, gain_delta = latent_back(small, proj, latent_g[None], cosine, sine)
        latent_row = jnp.pad(gain_delta.reshape(n_dp, R // n_dp), ((0, 0), (0, wide - R // n_dp))).reshape(1, D)
        return delta_latent, dots, last_pack(delta_latent, first_round, wld, small, first_g[None], latent_row)

    delta_latent, dots, pack = beside([first_move], last)
    steps(first_move, last_step - 2)
    first_share = first_move.result()
    last_sums = scatter_rows(pack).astype(F32)
    dwld, vectors = last_sums[:latent_wide], last_sums[latent_wide:]
    dwq, dwup, dwo = split_rows(attend_sums, [queries_wide, up_rows, output_weight.shape[0]])
    content = heads_here * DN
    dwq = jnp.concatenate(
        [dwq[:content].reshape(heads_here, DN, wide),
         dwq[content : content + heads_here * half].reshape(heads_here, half, wide),
         dwq[content + DR : content + DR + heads_here * half].reshape(heads_here, half, wide)], axis=1
    ).reshape(heads_here * (DN + DR), wide)
    dwld = jnp.concatenate([dwld[: R + half], dwld[R + DR : R + DR + half]], axis=0)

    first_share = first_share + dot(
        delta_latent, lax.dynamic_slice_in_dim(wld, column_start, my_columns, 1), 1, 0
    )
    vc = layer_input.astype(F32)
    gc = lax.dynamic_slice_in_dim(first_g, column_start, my_columns, 0)
    input_delta = (
        lax.dynamic_slice_in_dim(hidden_delta, column_start, my_columns, 1).astype(F32)
        + r1 * gc * first_share
        - vc * (r1 * r1) * (dots / D)
    )

    def units_delta(k):
        return early_sums[k * n0 : (k + 1) * n0], late_sums[k * n1 : (k + 1) * n1]

    def expert_delta(k):
        first, second = units_delta(k)
        return jnp.concatenate([first, second[: E * fe - n0]], axis=0).astype(F32).reshape(E, fe, wide)

    def shared_delta(k):
        return units_delta(k)[1][E * fe - n0 :].astype(F32)

    return (
        layer_output, input_delta, vectors[E + 1], dwq.T, dwld.T, vectors[E + 2, : R // n_dp],
        dwup.reshape(latent_up.shape), dwo, vectors[E], vectors[:E].T,
        expert_delta(0).transpose(0, 2, 1), expert_delta(1).transpose(0, 2, 1), expert_delta(2),
        shared_delta(0).T, shared_delta(1).T, shared_delta(2),
    )


def solution(mesh):
    in_specs = (
        P("dp", "tensor"), P("dp", "tensor"), P("dp"), P("dp", "tensor"), P("dp", None), P("dp"),
        P("dp", "tensor"), P("tensor", "dp"), P("dp"), P("dp", None), P(None, "dp", "tensor"),
        P(None, "dp", "tensor"), P(None, "tensor", "dp"), P("dp", "tensor"), P("dp", "tensor"),
        P("tensor", "dp"), P("dp", None),
    )
    out_specs = (
        P("dp", "tensor"), P("dp", "tensor"), P("dp"), P("dp", "tensor"), P("dp", None), P("dp"),
        P("dp", "tensor"), P("tensor", "dp"), P("dp"), P("dp", None), P(None, "dp", "tensor"),
        P(None, "dp", "tensor"), P(None, "tensor", "dp"), P("dp", "tensor"), P("dp", "tensor"),
        P("tensor", "dp"),
    )
    return jax.shard_map(
        per_device, mesh=mesh, in_specs=in_specs, out_specs=out_specs, check_vma=False
    )
```

```python
import functools

import jax
import jax.numpy as jnp
import numpy as np
from jax import lax
from jax.experimental import pallas as pl
from jax.experimental.pallas import tpu as pltpu
from jax.sharding import PartitionSpec as P

D = 2048
DN = 128
DR = 64
DV = 128
R = 512
E = 16
LEN = 1024
CAP = 864
EPSILON = 1e-06
SCALE = (DN + DR) ** -0.5
BLOCK = 256
BF = jnp.bfloat16
F32 = jnp.float32


def dot(a, b, ca, cb, out=F32):
    return lax.dot_general(
        a, b, (((ca,), (cb,)), ((), ())), preferred_element_type=F32
    ).astype(out)


VMEM_LIMIT = 58 * 2**20
NT=(((1,),(1,)),((),()))
NN=(((1,),(0,)),((),()))
TN=(((0,),(0,)),((),()))

def mm(a,b,dims):
    return lax.dot_general(a,b,dims,preferred_element_type=F32)

def params(n):
    return pltpu.CompilerParams(dimension_semantics=("arbitrary",)*n, vmem_limit_bytes=VMEM_LIMIT)

def once(shape, index):
    return pl.BlockSpec(shape, index, pipeline_mode=pl.Buffered(1))

def rows_once(n, wide, first):
    return pl.BlockSpec((pl.Element(n), pl.Element(wide)), lambda i: (first, 0), pipeline_mode=pl.Buffered(1))

def place_matrix(fe, first, n):
    col=lax.broadcasted_iota(jnp.int32,(E,n),1)+first; row=lax.broadcasted_iota(jnp.int32,(E,n),0)*fe
    return jnp.where((col>=row)&(col<row+fe),1.0,0.0).astype(BF)

def units_kernel(fe, first, x_ref, wg_ref, wu_ref, b_ref, w_ref, out_ref, pair_ref):
    x=x_ref[...]; n=wg_ref.shape[0]
    pre=mm(x,wg_ref[...],NT); lift=mm(x,wu_ref[...],NT); back=b_ref[...].astype(F32)
    w=w_ref[...]; hi=w.astype(BF); lo=(w-hi.astype(F32)).astype(BF)
    place=place_matrix(fe,first,n)
    spread=mm(jnp.concatenate([hi,lo],axis=1),jnp.concatenate([place,place],axis=0),NN)
    if first+n>E*fe:
        spread=jnp.where(lax.broadcasted_iota(jnp.int32,spread.shape,1)>=E*fe-first,1.0,spread)
    s=0.5+0.5*jnp.tanh(0.5*pre)
    silu=pre*s
    act=silu*lift
    pair_ref[...]=mm((act*back).astype(BF),place,NT)
    back=back*spread
    out_ref[0]=(back*lift*(s+silu*(1.0-s))).astype(BF)
    out_ref[1]=(back*silu).astype(BF)
    out_ref[2]=(act*spread).astype(BF)

def units(x,packed,back,weight,fe,first,bt):
    T,D=x.shape; n=back.shape[1]; r=weight.shape[1]
    ins=[pl.BlockSpec((bt,D),lambda i:(i,0))]+[once((n,D),lambda i,k=k:(k,0)) for k in range(2)]
    ins+=[pl.BlockSpec((bt,n),lambda i:(i,0)),pl.BlockSpec((bt,r),lambda i:(i,0))]
    outs=[jax.ShapeDtypeStruct((3,T,n),BF),jax.ShapeDtypeStruct((T,r),F32)]
    return pl.pallas_call(functools.partial(units_kernel,fe,first),grid=(T//bt,),in_specs=ins,
        out_specs=[pl.BlockSpec((3,bt,n),lambda i:(0,i,0)),pl.BlockSpec((bt,r),lambda i:(i,0))],out_shape=outs,
        compiler_params=params(1),
        cost_estimate=pl.CostEstimate(flops=4*T*D*n,bytes_accessed=2*(T*D+2*n*D+4*T*n),transcendentals=T*n))(x,packed,packed,back,weight)

def lift_kernel(g_ref,w_ref,o_ref):
    o_ref[...]=mm(g_ref[...],w_ref[...],NT).astype(BF)

def lift_back(g,packed,at,n,bt):
    T,D=g.shape
    return pl.pallas_call(lift_kernel,grid=(T//bt,),
        in_specs=[pl.BlockSpec((bt,D),lambda i:(i,0)),rows_once(n,D,at)],
        out_specs=pl.BlockSpec((bt,n),lambda i:(i,0)),out_shape=jax.ShapeDtypeStruct((T,n),BF),compiler_params=params(1),
        cost_estimate=pl.CostEstimate(flops=2*T*D*n,bytes_accessed=2*(T*D+n*D+T*n),transcendentals=0))(g,packed)

def back_kernel(pairs, added, beside, *refs):
    out=refs[-1]
    acc=None
    if added: acc=refs[0][...].astype(F32)
    rs=refs[added:]
    for k in range(pairs):
        a=rs[2*k]; b=rs[2*k+1]
        a=a[0] if len(a.shape)==3 else a[...]
        p=mm(a,b[...],NN)
        acc=p if acc is None else acc+p
    if beside:
        wide=acc.shape[1]
        out[:,:wide]=acc.astype(out.dtype)
        more=sum(r[...] for r in refs[-1-beside:-1])
        gap=jnp.zeros((acc.shape[0],out.shape[1]-wide-more.shape[1]),F32)
        out[:,wide:]=jnp.concatenate([more,gap],axis=1).astype(out.dtype)
    else:
        out[...]=acc.astype(out.dtype)

def core_kernel(pairs, core_ref, *refs):
    out=refs[-1]
    chips,_,w=out.shape
    for z in range(chips):
        at=pl.ds(pl.multiple_of((2*z+core_ref[0])*w,w),w)
        acc=None
        for k in range(pairs):
            a=refs[2*k]; b=refs[2*k+1]
            p=mm(a[0] if len(a.shape)==3 else a[...],b[:,at],NN)
            acc=p if acc is None else acc+p
        out[z]=acc.astype(BF)

def back(terms, added, out_dtype, bt, beside=(), core=None, chips=0):
    T=terms[0][0].shape[-2]; D=terms[0][2].shape[1]
    ins=[];args=[];fl=0;by=0
    if core is not None:
        ins.append(pl.BlockSpec(memory_space=pltpu.SMEM)); args.append(core)
    if added is not None:
        ins.append(pl.BlockSpec((bt,D),lambda i:(i,0))); args.append(added)
    for st,k,packed,n,at in terms:
        if st.ndim==3: ins.append(pl.BlockSpec((1,bt,n),lambda i,k=k:(k,i,0)))
        else: ins.append(pl.BlockSpec((bt,n),lambda i:(i,0)))
        ins.append(rows_once(n,D,at))
        args+= [st,packed]; fl+=2*T*D*n; by+=2*(T*n+n*D)
    for more in beside:
        ins.append(pl.BlockSpec((bt,more.shape[1]),lambda i:(i,0))); args.append(more)
    body=functools.partial(back_kernel,len(terms),0 if added is None else 1,len(beside))
    if beside:
        shape=(T,D+128); ospec=pl.BlockSpec((bt,D+128),lambda i:(i,0))
    elif core is not None:
        w=D//(2*chips); fl//=2
        shape=(chips,T,w); ospec=pl.BlockSpec((chips,bt,w),lambda i:(0,i,0))
        body=functools.partial(core_kernel,len(terms))
    else:
        shape=(T,D); ospec=pl.BlockSpec((bt,D),lambda i:(i,0))
    return pl.pallas_call(body,grid=(T//bt,),in_specs=ins,out_specs=ospec,out_shape=jax.ShapeDtypeStruct(shape,out_dtype),
        compiler_params=params(1),cost_estimate=pl.CostEstimate(flops=fl,bytes_accessed=by+4*T*D,transcendentals=0))(*args)

def outer_kernel(s_ref,x_ref,*refs):
    refs[-1][...]=mm(s_ref[0],x_ref[...],TN).astype(BF)

def outer(stack,first,count,x,total,at,into=None,bc=512):
    T,D=x.shape; n=stack.shape[2]
    ins=[pl.BlockSpec((1,T,n),lambda k,j:(first+k,0,0)),pl.BlockSpec((T,bc),lambda k,j:(0,j))]
    args=[stack,x]; al={}
    if into is not None:
        ins.append(pl.BlockSpec(memory_space=pl.ANY)); args.append(into); al={2:0}
    return pl.pallas_call(outer_kernel,grid=(count,D//bc),in_specs=ins,
        out_specs=pl.BlockSpec((n,bc),lambda k,j:(at+k,j)),out_shape=jax.ShapeDtypeStruct((total,D),BF),
        input_output_aliases=al,compiler_params=params(2),
        cost_estimate=pl.CostEstimate(flops=2*count*T*D*n,bytes_accessed=2*count*(T*n+n*D+T*D),transcendentals=0))(*args)


def place_columns_kernel(chips, norm, at_ref, *refs):
    pieces=refs[:2*chips]
    refs=refs[2*chips:]
    if norm:
        gain_ref, w_ref = refs[:2]
        out_ref, round_ref, r_ref, proj_ref = refs[-4:]
    else:
        (out_ref,) = refs
    w=pieces[0].shape[1]
    for k in range(2*chips):
        out_ref[:,pl.ds(pl.multiple_of(at_ref[k]*w,w),w)]=pieces[k][...]
    if norm:
        v=out_ref[...].astype(F32)
        r=lax.rsqrt(jnp.mean(v*v,axis=-1,keepdims=True)+EPSILON)
        round_ref[...]=(v*r*gain_ref[...]).astype(BF)
        r_ref[...]=r
        proj_ref[...]=mm(round_ref[...],w_ref[...],NT)

def place_columns(pieces, at, gain=None, packed=None, count=0, rows=None, first=0, into=(), bt=256):
    T,w=pieces[0].shape; n=len(pieces)
    total_rows=rows or T
    start=first//bt
    ins=[pl.BlockSpec(memory_space=pltpu.SMEM)]+[pl.BlockSpec((bt,w),lambda i:(i,0))]*n
    args=[at]+list(pieces)
    wides=[(n*w,BF)]
    if gain is not None:
        ins+=[pl.BlockSpec((1,n*w),lambda i:(0,0)),rows_once(count,n*w,0)]; args+=[gain[None],packed]
        wides+=[(n*w,BF),(1,F32),(count,F32)]
    aliases={len(args)+k:k for k in range(len(into))}
    ins+=[pl.BlockSpec(memory_space=pl.ANY)]*len(into); args+=list(into)
    return pl.pallas_call(functools.partial(place_columns_kernel,n//2,gain is not None),grid=(T//bt,),
        in_specs=ins,out_specs=[pl.BlockSpec((bt,m),lambda i:(i+start,0)) for m,_ in wides],
        out_shape=[jax.ShapeDtypeStruct((total_rows,m),d) for m,d in wides],
        input_output_aliases=aliases,compiler_params=params(1),
        cost_estimate=pl.CostEstimate(flops=(6+2*count)*T*n*w,bytes_accessed=6*T*n*w,transcendentals=T))(*args)

def place_rows_kernel(n, times, at_ref, *refs):
    pieces=refs[:n]; refs=refs[n:]
    if times: w_ref,out_ref,made_ref,sem=refs
    else: out_ref,sem=refs
    rows=pieces[0].shape[0]
    to=[pl.ds(pl.multiple_of(at_ref[k]*rows,rows),rows) for k in range(n)]
    copies=[pltpu.make_async_copy(pieces[k],out_ref.at[to[k]],sem.at[k]) for k in range(n)]
    for c in copies: c.start()
    if times:
        for k in range(n): made_ref[to[k]]=mm(pieces[k][...],w_ref[...],NT).astype(BF)
    for c in copies: c.wait()

def place_rows(pieces, at, weight=None):
    rows,w=pieces[0].shape; n=len(pieces)
    vmem=pl.BlockSpec(memory_space=pltpu.VMEM)
    outs=[jax.ShapeDtypeStruct((n*rows,w),BF)]; specs=[pl.BlockSpec(memory_space=pl.ANY)]; more=[]
    if weight is not None:
        outs.append(jax.ShapeDtypeStruct((n*rows,weight.shape[0]),BF)); specs.append(vmem); more=[weight]
    return pl.pallas_call(functools.partial(place_rows_kernel,n,bool(more)),
        in_specs=[pl.BlockSpec(memory_space=pltpu.SMEM)]+[vmem]*(n+len(more)),
        out_specs=specs,out_shape=outs,
        scratch_shapes=[pltpu.SemaphoreType.DMA((n,))],compiler_params=pltpu.CompilerParams(vmem_limit_bytes=VMEM_LIMIT),
        cost_estimate=pl.CostEstimate(flops=2*n*rows*w*(weight.shape[0] if more else 0),bytes_accessed=4*n*rows*w,transcendentals=0))(at,*pieces,*more)

def norm_rows_kernel(n, at_ref, col_ref, gain_ref, wr_ref, kept_ref, *refs):
    pieces=refs[:n]; round_ref,cols_ref,gating_ref,weight_ref,made,cut,sem,sem2=refs[n:]
    rows=pieces[0].shape[0]; w=cut.shape[2]
    copies=[]
    for k in range(n):
        v=pieces[k][...].astype(F32)
        r=lax.rsqrt(jnp.mean(v*v,axis=-1,keepdims=True)+EPSILON)
        made[k]=(v*r*gain_ref[...]).astype(BF)
        cut[k]=pieces[k][:,pl.ds(pl.multiple_of(col_ref[0]*w,w),w)]
        to=pl.ds(pl.multiple_of(at_ref[k]*rows,rows),rows)
        copies.append(pltpu.make_async_copy(made.at[k],round_ref.at[to],sem.at[k]))
        copies.append(pltpu.make_async_copy(cut.at[k],cols_ref.at[to],sem2.at[k]))
        copies[-2].start(); copies[-1].start()
        logits=mm(made[k],wr_ref[...],NT)
        e=jnp.exp(logits-jnp.max(logits,axis=-1,keepdims=True))
        gating=e/jnp.sum(e,axis=-1,keepdims=True)
        gating_ref[to]=gating
        weight_ref[to]=gating*kept_ref[to]
    for c in copies: c.wait()

def norm_rows(pieces, at, column, w, gain, router, kept):
    rows,wide=pieces[0].shape; n=len(pieces)
    vmem=pl.BlockSpec(memory_space=pltpu.VMEM)
    return pl.pallas_call(functools.partial(norm_rows_kernel,n),
        in_specs=[pl.BlockSpec(memory_space=pltpu.SMEM)]*2+[vmem]*(n+3),
        out_specs=[pl.BlockSpec(memory_space=pl.ANY)]*2+[vmem]*2,
        out_shape=[jax.ShapeDtypeStruct((n*rows,wide),BF),jax.ShapeDtypeStruct((n*rows,w),BF)]+[jax.ShapeDtypeStruct((n*rows,E),F32)]*2,
        scratch_shapes=[pltpu.VMEM((n,rows,wide),BF),pltpu.VMEM((n,rows,w),BF),pltpu.SemaphoreType.DMA((n,)),pltpu.SemaphoreType.DMA((n,))],
        compiler_params=pltpu.CompilerParams(vmem_limit_bytes=VMEM_LIMIT),
        cost_estimate=pl.CostEstimate(flops=6*n*rows*wide,bytes_accessed=4*n*rows*wide,transcendentals=n*rows))(at,column,gain[None],router,kept,*pieces)

def small_kernel(pairs_ref, up_ref, kr_ref, dot_ref, entry_ref, out_ref):
    bt=out_ref.shape[0]
    out_ref[:,:R]=mm(pairs_ref[...],up_ref[...],NT).astype(BF)
    h=DR//2
    kr=kr_ref[...]
    gap=jnp.zeros((bt,DR-1-entry_ref.shape[1]),F32)
    out_ref[:,R:]=jnp.concatenate(
        [kr[:,:h]+kr[:,h:DR],kr[:,DR:DR+h]+kr[:,DR+h:],dot_ref[...],entry_ref[...],gap],axis=1).astype(BF)

def small_terms(pairs, up, kr, dots, entries, bt=512):
    T=pairs.shape[0]
    def rows(a): return pl.BlockSpec((bt,a.shape[1]),lambda i:(i,0))
    return pl.pallas_call(small_kernel,grid=(T//bt,),
        in_specs=[rows(pairs),pl.BlockSpec(up.shape,lambda i:(0,0)),rows(kr),rows(dots),rows(entries)],
        out_specs=pl.BlockSpec((bt,R+DN),lambda i:(i,0)),out_shape=jax.ShapeDtypeStruct((T,R+DN),BF),
        compiler_params=params(1),
        cost_estimate=pl.CostEstimate(flops=2*T*R*pairs.shape[1],bytes_accessed=8*T*R,transcendentals=0))(pairs,up,kr,dots,entries)

def latent_back_kernel(small_ref, proj_ref, gain_ref, cos_ref, sin_ref, delta_ref, dots_ref, gain_delta_ref):
    i=pl.program_id(0)
    at=proj_ref.shape[1]-R-DN
    dl=small_ref[:,:R].astype(F32)
    vl=proj_ref[:,at:at+R]
    rl=lax.rsqrt(jnp.mean(vl*vl,axis=-1,keepdims=True)+EPSILON)
    gain=gain_ref[...]
    part=jnp.sum(dl*vl*rl,axis=0,keepdims=True)
    @pl.when(i==0)
    def _(): gain_delta_ref[...]=part
    @pl.when(i>0)
    def _(): gain_delta_ref[...]+=part
    gd=gain*dl
    head=rl*gd-vl*(rl*rl*rl)*jnp.mean(vl*gd,axis=-1,keepdims=True)
    beyond=small_ref[:,R:]
    row=lax.broadcasted_iota(jnp.int32,(DN,DN),0); col=lax.broadcasted_iota(jnp.int32,(DN,DN),1)
    h=DR//2
    put=jnp.where(((row<h)&(col==row))|((row>=h)&(row<DR)&(col==row+h)),1.0,0.0).astype(BF)
    spread=mm(beyond,put,NN)
    tail=spread*cos_ref[...]-pltpu.roll(spread,DR,1)*sin_ref[...]
    delta_ref[:,:R]=head.astype(BF)
    delta_ref[:,R:]=tail.astype(BF)
    own=jnp.sum(head*vl,axis=-1,keepdims=True)+jnp.sum(tail*proj_ref[:,at+R:],axis=-1,keepdims=True)
    lane=lax.broadcasted_iota(jnp.int32,beyond.shape,1)
    dots_ref[...]=own+jnp.sum(jnp.where(lane==DR,beyond.astype(F32),0.0),axis=-1,keepdims=True)

def latent_back(small, proj, gain, cosine, sine, bt=512):
    T,wide=small.shape; turns=LEN//bt
    return pl.pallas_call(latent_back_kernel,grid=(T//bt,),
        in_specs=[pl.BlockSpec((bt,wide),lambda i:(i,0)),pl.BlockSpec((bt,proj.shape[1]),lambda i:(i,0)),
                  pl.BlockSpec((1,R),lambda i:(0,0)),pl.BlockSpec((bt,DN),lambda i:(i%turns,0)),pl.BlockSpec((bt,DN),lambda i:(i%turns,0))],
        out_specs=[pl.BlockSpec((bt,R+DN),lambda i:(i,0)),pl.BlockSpec((bt,1),lambda i:(i,0)),pl.BlockSpec((1,R),lambda i:(0,0))],
        out_shape=[jax.ShapeDtypeStruct((T,R+DN),BF),jax.ShapeDtypeStruct((T,1),F32),jax.ShapeDtypeStruct((1,R),F32)],
        compiler_params=params(1),
        cost_estimate=pl.CostEstimate(flops=30*T*wide,bytes_accessed=8*T*wide,transcendentals=T))(small,proj,gain,cosine,sine)

def last_pack_kernel(delta_ref, x_ref, w_ref, small_ref, g_ref, latent_ref, out_ref):
    n=delta_ref.shape[1]
    d=mm(delta_ref[...],x_ref[...],TN)
    out_ref[:n]=d.astype(BF)
    sums=jnp.sum(w_ref[...].astype(F32)*d,axis=0,keepdims=True)
    row=lax.broadcasted_iota(jnp.int32,(32,DN),0); col=lax.broadcasted_iota(jnp.int32,(32,DN),1)
    at=DR+1
    pick=((row<E)&(col==row+at+2))|((row==E)&(col==at))|((row==E+1)&(col==at+1))
    v=mm(jnp.where(pick,1.0,0.0).astype(BF),small_ref[...],NT)
    line=lax.broadcasted_iota(jnp.int32,v.shape,0)
    v=jnp.where(line==E+1,(v+sums)/g_ref[...],v)
    out_ref[n:]=jnp.where(line==E+2,latent_ref[...],v).astype(BF)

def last_pack(delta, x, w, small, gain, latent_row, bc=512):
    T,D=x.shape; n=delta.shape[1]
    def cols(a): return pl.BlockSpec((a.shape[0],bc),lambda j:(0,j))
    return pl.pallas_call(last_pack_kernel,grid=(D//bc,),
        in_specs=[pl.BlockSpec((T,n),lambda j:(0,0)),cols(x),cols(w),pl.BlockSpec((bc,DN),lambda j:(j,R//DN)),cols(gain),cols(latent_row)],
        out_specs=pl.BlockSpec((n+32,bc),lambda j:(0,j)),out_shape=jax.ShapeDtypeStruct((n+32,D),BF),
        compiler_params=params(1),
        cost_estimate=pl.CostEstimate(flops=2*T*D*n,bytes_accessed=2*(T*D+2*n*D+T*n),transcendentals=0))(delta,x,w,small,gain,latent_row)


def turn(x, cosine, sine):
    return x*cosine+pltpu.roll(x,64,1)*sine

def slot_mask(shape, head):
    lane=lax.broadcasted_iota(jnp.int32,shape,1)
    low=head*(DR//2)
    inside=((lane>=low)&(lane<low+DR//2))|((lane>=low+DR)&(lane<low+DR+DR//2))
    return inside

def causal_scores(q, k, first):
    s=mm(q,k,NT)*SCALE
    row=lax.broadcasted_iota(jnp.int32,s.shape,0)+first
    col=lax.broadcasted_iota(jnp.int32,s.shape,1)
    return jnp.where(col<=row,s,-1e30)

def attend_kernel(heads, proj_ref, up_ref, gain_ref, cos_ref, sin_ref, *refs):
    q_ref, kr_ref, kv_ref, latent_ref, mixed_ref, lse_ref = refs[-6:]
    content=heads*DN
    at=content+DN
    q_ref[:,:content]=proj_ref[:,:content].astype(BF)
    cosine,sine=cos_ref[...],sin_ref[...]
    q_ref[:,content:]=turn(proj_ref[:,content:at],cosine,sine).astype(BF)
    vl=proj_ref[:,at:at+R]
    latent_ref[...]=(vl*lax.rsqrt(jnp.mean(vl*vl,axis=-1,keepdims=True)+EPSILON)*gain_ref[...]).astype(BF)
    kr_ref[...]=turn(proj_ref[:,at+R:],cosine,sine).astype(BF)
    kv_ref[...]=mm(latent_ref[...],up_ref[...],NN).astype(BF)
    kr=kr_ref[...]
    for h in range(heads):
        kc=kv_ref[:,h*(DN+DV):h*(DN+DV)+DN]
        v=kv_ref[:,h*(DN+DV)+DN:(h+1)*(DN+DV)]
        k=jnp.concatenate([kc,jnp.where(slot_mask(kr.shape,h),kr,jnp.zeros_like(kr))],axis=1)
        for i in range(LEN//BLOCK):
            a,b=i*BLOCK,(i+1)*BLOCK
            q=jnp.concatenate([q_ref[a:b,h*DN:(h+1)*DN],q_ref[a:b,content:]],axis=1)
            s=causal_scores(q,k[:b],a)
            m=jnp.max(s,axis=-1,keepdims=True)
            e=jnp.exp(s-m)
            t=jnp.sum(e,axis=-1,keepdims=True)
            p=(e*(1.0/t)).astype(BF)
            mixed_ref[a:b,h*DV:(h+1)*DV]=mm(p,v[:b],NN).astype(BF)
            lse_ref[a:b,h:h+1]=m+jnp.log(t)

def attend(proj, up, gain, cosine, sine, heads, sequence, into=()):
    T=proj.shape[0]; wide=proj.shape[1]
    def rows(n): return pl.BlockSpec((LEN,n),lambda i:(sequence,0))
    def whole(a): return pl.BlockSpec(a.shape,lambda i:(0,0))
    qn=heads*DN+DN
    outs=[(qn,BF),(DN,BF),(heads*(DN+DV),BF),(R,BF),(heads*DV,BF),(heads,F32)]
    args=[proj,up,gain,cosine,sine]
    return pl.pallas_call(functools.partial(attend_kernel,heads),grid=(1,),
        in_specs=[rows(wide)]+[whole(a) for a in args[1:]]+[pl.BlockSpec(memory_space=pl.ANY)]*len(into),
        out_specs=[rows(n) for n,_ in outs],out_shape=[jax.ShapeDtypeStruct((T,n),d) for n,d in outs],
        input_output_aliases={len(args)+k:k for k in range(len(into))},compiler_params=params(1),
        cost_estimate=pl.CostEstimate(flops=LEN*LEN*heads*512,bytes_accessed=LEN*8000,transcendentals=LEN*LEN*heads//2))(*args,*into)

def attend_back_kernel(heads, q_ref, kr_ref, kv_ref, mixed_ref, lse_ref, do_ref, cos_ref, sin_ref, dq_ref, dkv_ref, dkr_ref, dot_ref, dk_acc, dv_acc):
    content=heads*DN
    kr=kr_ref[...]
    for h in range(heads):
        kc=kv_ref[:,h*(DN+DV):h*(DN+DV)+DN]
        v=kv_ref[:,h*(DN+DV)+DN:(h+1)*(DN+DV)]
        mask=slot_mask(kr.shape,h)
        k=jnp.concatenate([kc,jnp.where(mask,kr,jnp.zeros_like(kr))],axis=1)
        for i in reversed(range(LEN//BLOCK)):
            a,b=i*BLOCK,(i+1)*BLOCK
            q=jnp.concatenate([q_ref[a:b,h*DN:(h+1)*DN],q_ref[a:b,content:]],axis=1)
            do=do_ref[a:b,h*DV:(h+1)*DV]
            p=jnp.exp(causal_scores(q,k[:b],a)-lse_ref[a:b,h:h+1])
            dp=mm(do,v[:b],NT)
            along=jnp.sum(do.astype(F32)*mixed_ref[a:b,h*DV:(h+1)*DV].astype(F32),axis=-1,keepdims=True)
            ds=(p*(dp-along)).astype(BF)
            pv=mm(p.astype(BF),do,TN)
            pk=mm(ds,q,TN)
            if i==LEN//BLOCK-1:
                dv_acc[...]=pv; dk_acc[...]=pk
            else:
                dv_acc[:b]+=pv; dk_acc[:b]+=pk
            dq=mm(ds,k[:b],NN)*SCALE
            d=jnp.sum(dq*q.astype(F32),axis=-1,keepdims=True)
            if h==0: dot_ref[a:b]=d
            else: dot_ref[a:b]+=d
            dq_ref[a:b,h*DN:(h+1)*DN]=dq[:,:DN].astype(BF)
            turned=turn(dq[:,DN:],cos_ref[a:b],-sin_ref[a:b])
            turned=jnp.where(mask[:b-a],turned,0.0).astype(BF)
            if h==0: dq_ref[a:b,content:]=turned
            else: dq_ref[a:b,content:]+=turned
        dkv_ref[:,h*(DN+DV):h*(DN+DV)+DN]=(dk_acc[:,:DN]*SCALE).astype(BF)
        dkv_ref[:,h*(DN+DV)+DN:(h+1)*(DN+DV)]=dv_acc[...].astype(BF)
        part=jnp.where(mask,dk_acc[:,DN:]*SCALE,0.0)
        if h==0: dkr_ref[...]=part
        else: dkr_ref[...]+=part

def attend_back(q,kr,kv,mixed,lse,do,cosine,sine,heads):
    T=q.shape[0]
    def rows(n): return pl.BlockSpec((LEN,n),lambda i:(i,0))
    def whole(a): return pl.BlockSpec(a.shape,lambda i:(0,0))
    args=(q,kr,kv,mixed,lse,do)
    outs=[(q.shape[1],BF),(kv.shape[1],BF),(DN,F32),(1,F32)]
    return pl.pallas_call(functools.partial(attend_back_kernel,heads),grid=(T//LEN,),
        in_specs=[rows(a.shape[1]) for a in args]+[whole(cosine),whole(sine)],
        out_specs=[rows(n) for n,_ in outs],out_shape=[jax.ShapeDtypeStruct((T,n),d) for n,d in outs],
        scratch_shapes=[pltpu.VMEM((LEN,2*DN),F32),pltpu.VMEM((LEN,DV),F32)],
        compiler_params=params(1),
        cost_estimate=pl.CostEstimate(flops=T*LEN*heads*1400,bytes_accessed=T*6000,transcendentals=T*LEN*heads//2))(*args,cosine,sine)

def tables():
    position=np.arange(LEN,dtype=np.float32)
    spread=(10000.0**(-np.arange(DR//2,dtype=np.float32)/(DR//2))).astype(np.float32)
    phase=(position[:,None]*spread[None,:]).astype(np.float32)
    c,s=np.cos(phase),np.sin(phase)
    return np.concatenate([c]*4,1).astype(np.float32),np.concatenate([-s,-s,s,s],1).astype(np.float32)


class Line:
    def __init__(self):
        self.n = lax.axis_size("tensor")
        self.chips = self.n // 2
        index = lax.axis_index("tensor")
        self.index = index
        self.z = index // 2
        self.c = index % 2

    def swap(self, a):
        return lax.ppermute(a, "tensor", [(i, i ^ 1) for i in range(self.n)])

    def shift(self, a, step, sources):
        pairs = [
            (2 * s + c, 2 * (s + step) + c)
            for s in sources
            if 0 <= s + step < self.chips
            for c in (0, 1)
        ]
        return lax.ppermute(a, "tensor", pairs)

    def pieces(self, own, order):
        n = self.chips
        out, at = [], []
        for k, piece in enumerate(own):
            chip = (self.z - k + n) % n
            out += [piece, self.swap(piece)]
            at += [order(chip, self.c), order(chip, 1 - self.c)]
        return out, jnp.stack(at).astype(jnp.int32)

    def row_pieces(self, own):
        return self.pieces(own, lambda chip, core: core * self.chips + chip)

    def column_pieces(self, own):
        return self.pieces(own, lambda chip, core: chip * 2 + core)

    def halves(self, p):
        half = p.shape[0] // 2
        return [lax.dynamic_slice_in_dim(p, c * half, half, 0) for c in (self.c, 1 - self.c)]

    def row_scatter(self, both):
        ch = both.shape[0] // self.chips
        return Scatter(self, lambda j: lax.dynamic_slice_in_dim(both, j * ch, ch, 0))

    def column_scatter(self, both):
        return Scatter(self, lambda j: lax.dynamic_index_in_dim(both, j, 0, False))

    def row_start(self, rows):
        ch = rows // self.n
        return (self.c * self.chips + self.z) * ch, ch


def total(mine, arrived):
    return (mine.astype(F32) + arrived.astype(F32)).astype(BF)


class Gather:
    def __init__(self, line, block):
        self.line, self.left, self.right = line, [block], [block]

    def start(self):
        n, k = self.line.chips, len(self.left)
        return (
            self.line.shift(self.left[-1], 1, range(k - 1, n)),
            self.line.shift(self.right[-1], -1, range(0, n - k + 1)),
        )

    def take(self, arrived):
        self.left.append(arrived[0])
        self.right.append(arrived[1])

    def result(self):
        n, z = self.line.chips, self.line.z
        return self.left[:1] + [jnp.where(z >= k, self.left[k], self.right[n - k]) for k in range(1, n)]


class Scatter:
    def __init__(self, line, block):
        self.line, self.block, self.step, self.left, self.right = line, block, 0, None, None

    def start(self):
        self.step += 1
        n, s, z = self.line.chips, self.step, self.line.z
        up = self.block(jnp.clip(n - s + z, 0, n - 1))
        down = self.block(jnp.clip(z - (n - s), 0, n - 1))
        if self.left is not None:
            up, down = total(up, self.left), total(down, self.right)
        return self.line.shift(up, 1, range(0, s)), self.line.shift(down, -1, range(n - s, n))

    def take(self, arrived):
        self.left, self.right = arrived

    def result(self):
        return self.block(self.line.z).astype(F32) + self.left.astype(F32) + self.right.astype(F32)


def beside(moves, job=None):
    arrived, done = lax.optimization_barrier(([m.start() for m in moves], job() if job else None))
    for move, a in zip(moves, arrived):
        move.take(a)
    return done


def steps(move, count, jobs=()):
    made = []
    for k in range(count):
        made.append(beside([move], jobs[k] if k < len(jobs) else None))
    return made


def gather_rows(packed):
    return lax.all_gather(packed, "dp", axis=1, tiled=True)


def scatter_rows(packed):
    return lax.psum_scatter(packed, "dp", scatter_dimension=1, tiled=True)


def split_rows(packed, counts):
    out, at = [], 0
    for count in counts:
        out.append(packed[at : at + count])
        at += count
    return out


def ranks(mask):
    number = mask.shape[0]
    block = 128
    pieces = mask.reshape(number // block, block, E).astype(BF)
    lower = jnp.tril(jnp.ones((block, block), BF), -1)
    inside = jnp.einsum("ij,bje->bie", lower, pieces, preferred_element_type=F32)
    totals = jnp.sum(pieces.astype(F32), axis=1).astype(BF)
    ahead = jnp.tril(jnp.ones((number // block, number // block), BF), -1)
    before = dot(ahead, totals, 1, 0)
    return (inside + before[:, None, :]).reshape(number, E)


def per_device(
    layer_input, cotangent, first_gain, query_weight, latent_down, latent_gain, latent_up,
    output_weight, second_gain, router_weight, expert_gate, expert_up, expert_down,
    shared_gate, shared_up, shared_down, routes,
):
    line = Line()
    n_dp = lax.axis_size("dp")
    wide = D // n_dp
    number = layer_input.shape[0]
    heads_here = output_weight.shape[0] // DV
    fe = expert_down.shape[1]
    my_columns = layer_input.shape[1]
    column_start = line.index * my_columns
    row_start, row_count = line.row_start(number)

    half = DR // 2
    spare_heads = 2 - heads_here
    up_rows = latent_up.size // wide
    by_head = query_weight.T.reshape(heads_here, DN + DR, wide)
    blank = jnp.zeros((spare_heads * half, wide), BF)
    gains = jnp.zeros((16, wide), BF)
    gains = gains.at[0].set(first_gain).at[1].set(second_gain)
    gains = gains.at[2, : latent_gain.shape[0]].set(latent_gain)
    down = latent_down.T
    queries_wide = heads_here * DN + DN
    latent_wide = R + DN
    attend_pack = [
        by_head[:, :DN].reshape(heads_here * DN, wide),
        by_head[:, DN : DN + half].reshape(heads_here * half, wide), blank,
        by_head[:, DN + half :].reshape(heads_here * half, wide), blank,
        down[: R + half], down[R : R + half], down[R + half :], down[R + half :],
        latent_up.reshape(up_rows, wide), gains, router_weight.T, output_weight,
    ]
    attend_packed = gather_rows(jnp.concatenate([m for m in attend_pack if m.shape[0]], axis=0))
    wproj, wup, gains, wr, wo = split_rows(
        attend_packed, [queries_wide + latent_wide, up_rows, 16, E, output_weight.shape[0]]
    )
    wup = wup.reshape(up_rows, n_dp, wide).transpose(1, 0, 2).reshape(R, -1)
    first_g = gains[0].astype(F32)
    second_g = gains[1].astype(F32)
    latent_g = gains[2].reshape(n_dp, wide)[:, : R // n_dp].reshape(R).astype(F32)
    cosine, sine = (jnp.asarray(table) for table in tables())

    n_units = E * fe + shared_down.shape[0]
    n0 = n_units // 2 // 256 * 256
    n1 = n_units - n0
    last_step = line.chips - 1
    gate = expert_gate.transpose(0, 2, 1).reshape(E * fe, wide)
    up = expert_up.transpose(0, 2, 1).reshape(E * fe, wide)
    move = Gather(line, layer_input[:LEN])
    downs, early, late = steps(move, 3, (
        lambda: jnp.concatenate([expert_down.reshape(E * fe, wide), shared_down], axis=0),
        lambda: jnp.concatenate([gate[:n0], up[:n0]], axis=0),
        lambda: jnp.concatenate([gate[n0:], shared_gate.T, up[n0:], shared_up.T], axis=0),
    ))
    steps(move, last_step - 3)
    downs, early, late = gather_rows(downs), gather_rows(early), gather_rows(late)

    tile = 256
    core = line.c.reshape(1).astype(jnp.int32)
    placed, attended = (), ()

    def place(move, sequence):
        pieces, at = line.column_pieces(move.result())
        return place_columns(
            pieces, at, first_g, attend_packed, queries_wide + latent_wide, number, sequence * LEN, placed
        )

    def attention(sequence):
        return attend(placed[3], wup, latent_g[None], cosine, sine, heads_here, sequence, attended)

    for sequence in range(1, number // LEN):
        ahead, after = move, layer_input[sequence * LEN : (sequence + 1) * LEN]
        ahead.left[-1], ahead.right[-1], after = lax.optimization_barrier((ahead.left[-1], ahead.right[-1], after))
        move = Gather(line, after)
        beside([move])
        placed = beside([move], lambda: place(ahead, sequence - 1))
        steps(move, last_step - 3)
        attended = beside([move], lambda: attention(sequence - 1))
    move.left[-1], move.right[-1], cotangent = lax.optimization_barrier((move.left[-1], move.right[-1], cotangent))
    grad_move = Gather(line, cotangent)
    placed = place(move, number // LEN - 1)
    attended = beside([grad_move], lambda: attention(number // LEN - 1))
    rows, first_round, r1, proj = placed
    q, kr, kv, latent, mixed, log_total = attended
    mine, theirs = line.halves(mixed)
    arrived = line.swap(dot(theirs, wo, 1, 0, BF))
    move = line.row_scatter(total(dot(mine, wo, 1, 0, BF), arrived))
    for _ in range(last_step - 1):
        beside([move, grad_move])
    (grad,) = beside([move], lambda: place_columns(*line.column_pieces(grad_move.result())))
    hidden_rows = (
        lax.dynamic_slice_in_dim(rows, row_start, row_count, 0).astype(F32) + move.result()
    ).astype(BF)
    move = Gather(line, hidden_rows)
    back0, back1 = steps(move, 2, (
        lambda: lift_back(grad, downs, 0, n0, tile),
        lambda: lift_back(grad, downs, n0, n1, tile),
    ))
    steps(move, last_step - 2)
    hidden_pieces, hidden_at = line.row_pieces(move.result())
    named = jnp.any(routes[:, :, None] == jnp.arange(E, dtype=jnp.int32)[None, None, :], axis=1)
    kept = jnp.where(named & (ranks(named) < CAP), 1.0, 0.0)
    second_round, hidden_columns, gating, weight = norm_rows(
        hidden_pieces, hidden_at, line.index.reshape(1).astype(jnp.int32), my_columns, second_g, wr, kept
    )

    stack0, pair0 = units(second_round, early, back0, weight, fe, 0, tile)
    deltas = outer(stack0, 0, 2, second_round, 3 * n0, 0)
    deltas = outer(stack0, 2, 1, grad, 3 * n0, 2, deltas)
    deltas, stack0 = lax.optimization_barrier((deltas, stack0))
    early_sums = scatter_rows(deltas)
    stack1, pair1 = units(second_round, late, back1, weight, fe, n0, tile)
    second_terms = back(
        [(stack0, 0, early, n0, 0), (stack0, 1, early, n0, n0), (stack1, 0, late, n1, 0), (stack1, 1, late, n1, n1)],
        None, BF, tile, (pair0, pair1),
    )

    branch_terms = [(stack0, 2, downs, n0, 0), (stack1, 2, downs, n1, n0)]
    mine, theirs = line.halves(second_terms)
    move = line.row_scatter(total(mine, line.swap(theirs)))
    deltas = beside([move], lambda: outer(stack1, 0, 1, second_round, 3 * n1, 0))
    deltas = beside([move], lambda: outer(stack1, 1, 1, second_round, 3 * n1, 1, deltas))
    branch_theirs = beside([move], lambda: back(branch_terms, None, BF, tile, (), 1 - core, line.chips))
    steps(move, last_step - 3)
    summed = move.result()

    def own_rows(a):
        return lax.dynamic_slice_in_dim(a, row_start, row_count, 0)

    gating_rows, kept_rows, x2 = own_rows(gating), own_rows(kept), own_rows(second_round)
    u = summed[:, D : D + E] * kept_rows
    logits_delta = gating_rows * (u - jnp.sum(gating_rows * u, axis=-1, keepdims=True))
    d2 = summed[:, :D] + dot(logits_delta.astype(BF), wr, 1, 0)
    v2 = hidden_rows.astype(F32)
    r2 = lax.rsqrt(jnp.mean(v2 * v2, axis=-1, keepdims=True) + EPSILON)
    vgd = jnp.mean(v2 * second_g * d2, axis=-1, keepdims=True)
    hidden_delta = own_rows(grad).astype(F32) + r2 * second_g * d2 - v2 * (r2**3) * vgd
    move = Gather(line, hidden_delta.astype(BF))
    branch_mine, branch_arrived = beside([move], lambda: (
        back(branch_terms, None, BF, tile, (), core, line.chips), line.swap(branch_theirs)
    ))
    branch_move = line.column_scatter(total(branch_mine, branch_arrived))
    deltas = beside([move, branch_move], lambda: outer(stack1, 2, 1, grad, 3 * n1, 2, deltas))
    router_delta = dot(x2, logits_delta.astype(BF), 0, 0)
    second_gain_delta = jnp.sum(d2 * v2 * r2, axis=0)
    early_sums, deltas, move.left[-1] = lax.optimization_barrier((early_sums, deltas, move.left[-1]))
    late_sums = scatter_rows(deltas)
    for _ in range(last_step - 2):
        beside([move, branch_move])
    delta_pieces, delta_at = line.row_pieces(move.result())

    def heads_back():
        placed, delta_mixed = place_rows(delta_pieces, delta_at, wo)
        return placed, attend_back(q, kr, kv, mixed, log_total, delta_mixed, cosine, sine, heads_here)

    hidden_delta, heads = beside([branch_move], heads_back)
    layer_output = (hidden_columns.astype(F32) + branch_move.result()).astype(BF)
    delta_queries, delta_pairs, delta_kr, query_dot = heads
    delta_wq = dot(delta_queries, first_round, 0, 0)
    query_gain = jnp.sum(wproj[:queries_wide].astype(F32) * delta_wq, axis=0)
    per_entry = jnp.concatenate([second_gain_delta[:, None], query_gain[:, None], router_delta], axis=1)
    if number > D:
        per_entry = jnp.concatenate([per_entry, jnp.zeros((number - D, E + 2), F32)], axis=0)
    small = small_terms(delta_pairs, wup, delta_kr, query_dot, per_entry)
    first_terms = [(delta_queries, 0, attend_packed, queries_wide, 0)]
    mine, theirs = line.halves(small)
    move = line.row_scatter(total(mine, line.swap(theirs)))

    def attend_deltas():
        delta_wup = dot(latent, delta_pairs, 0, 0, BF)
        return jnp.concatenate(
            [delta_wq.astype(BF),
             delta_wup.reshape(n_dp, up_rows, wide).transpose(1, 0, 2).reshape(up_rows, D),
             dot(mixed, hidden_delta, 0, 0, BF)], axis=0)

    theirs, mine = steps(move, 2, (
        lambda: back(first_terms, None, BF, tile, (), 1 - core, line.chips),
        lambda: back(first_terms, None, BF, tile, (), core, line.chips),
    ))
    arrived = beside([move], lambda: line.swap(theirs))
    steps(move, last_step - 3)
    small, both, layer_output = lax.optimization_barrier(
        (move.result().astype(BF), total(mine, arrived), layer_output)
    )
    move = Gather(line, small)
    first_move = line.column_scatter(both)
    deltas = beside([move, first_move], attend_deltas)
    attend_sums = scatter_rows(deltas).astype(F32)
    steps(move, last_step - 1)
    small_pieces, small_at = line.row_pieces(move.result())
    small_pieces, late_sums = lax.optimization_barrier((small_pieces, late_sums))
    wld = wproj[queries_wide:]

    def last():
        (small,) = place_rows(small_pieces, small_at)
        delta_latent, dots, gain_delta = latent_back(small, proj, latent_g[None], cosine, sine)
        latent_row = jnp.pad(gain_delta.reshape(n_dp, R // n_dp), ((0, 0), (0, wide - R // n_dp))).reshape(1, D)
        return delta_latent, dots, last_pack(delta_latent, first_round, wld, small, first_g[None], latent_row)

    delta_latent, dots, pack = beside([first_move], last)
    steps(first_move, last_step - 2)
    first_share = first_move.result()
    last_sums = scatter_rows(pack).astype(F32)
    dwld, vectors = last_sums[:latent_wide], last_sums[latent_wide:]
    dwq, dwup, dwo = split_rows(attend_sums, [queries_wide, up_rows, output_weight.shape[0]])
    content = heads_here * DN
    dwq = jnp.concatenate(
        [dwq[:content].reshape(heads_here, DN, wide),
         dwq[content : content + heads_here * half].reshape(heads_here, half, wide),
         dwq[content + DR : content + DR + heads_here * half].reshape(heads_here, half, wide)], axis=1
    ).reshape(heads_here * (DN + DR), wide)
    dwld = jnp.concatenate([dwld[: R + half], dwld[R + DR : R + DR + half]], axis=0)

    first_share = first_share + dot(
        delta_latent, lax.dynamic_slice_in_dim(wld, column_start, my_columns, 1), 1, 0
    )
    vc = layer_input.astype(F32)
    gc = lax.dynamic_slice_in_dim(first_g, column_start, my_columns, 0)
    input_delta = (
        lax.dynamic_slice_in_dim(hidden_delta, column_start, my_columns, 1).astype(F32)
        + r1 * gc * first_share
        - vc * (r1 * r1) * (dots / D)
    )

    def units_delta(k):
        return early_sums[k * n0 : (k + 1) * n0], late_sums[k * n1 : (k + 1) * n1]

    def expert_delta(k):
        first, second = units_delta(k)
        return jnp.concatenate([first, second[: E * fe - n0]], axis=0).astype(F32).reshape(E, fe, wide)

    def shared_delta(k):
        return units_delta(k)[1][E * fe - n0 :].astype(F32)

    return (
        layer_output, input_delta, vectors[E + 1], dwq.T, dwld.T, vectors[E + 2, : R // n_dp],
        dwup.reshape(latent_up.shape), dwo, vectors[E], vectors[:E].T,
        expert_delta(0).transpose(0, 2, 1), expert_delta(1).transpose(0, 2, 1), expert_delta(2),
        shared_delta(0).T, shared_delta(1).T, shared_delta(2),
    )


def solution(mesh):
    in_specs = (
        P("dp", "tensor"), P("dp", "tensor"), P("dp"), P("dp", "tensor"), P("dp", None), P("dp"),
        P("dp", "tensor"), P("tensor", "dp"), P("dp"), P("dp", None), P(None, "dp", "tensor"),
        P(None, "dp", "tensor"), P(None, "tensor", "dp"), P("dp", "tensor"), P("dp", "tensor"),
        P("tensor", "dp"), P("dp", None),
    )
    out_specs = (
        P("dp", "tensor"), P("dp", "tensor"), P("dp"), P("dp", "tensor"), P("dp", None), P("dp"),
        P("dp", "tensor"), P("tensor", "dp"), P("dp"), P("dp", None), P(None, "dp", "tensor"),
        P(None, "dp", "tensor"), P(None, "tensor", "dp"), P("dp", "tensor"), P("dp", "tensor"),
        P("tensor", "dp"),
    )
    return jax.shard_map(
        per_device, mesh=mesh, in_specs=in_specs, out_specs=out_specs, check_vma=False
    )
```

```python
import functools

import jax
import jax.numpy as jnp
import numpy as np
from jax import lax
from jax.experimental import pallas as pl
from jax.experimental.pallas import tpu as pltpu
from jax.sharding import PartitionSpec as P

D = 2048
DN = 128
DR = 64
DV = 128
R = 512
E = 16
LEN = 1024
CAP = 864
EPSILON = 1e-06
SCALE = (DN + DR) ** -0.5
BLOCK = 256
BF = jnp.bfloat16
F32 = jnp.float32


def dot(a, b, ca, cb, out=F32):
    return lax.dot_general(
        a, b, (((ca,), (cb,)), ((), ())), preferred_element_type=F32
    ).astype(out)


VMEM_LIMIT = 58 * 2**20
NT=(((1,),(1,)),((),()))
NN=(((1,),(0,)),((),()))
TN=(((0,),(0,)),((),()))

def mm(a,b,dims):
    return lax.dot_general(a,b,dims,preferred_element_type=F32)

def params(n):
    return pltpu.CompilerParams(dimension_semantics=("arbitrary",)*n, vmem_limit_bytes=VMEM_LIMIT)

def once(shape, index):
    return pl.BlockSpec(shape, index, pipeline_mode=pl.Buffered(1))

def rows_once(n, wide, first):
    return pl.BlockSpec((pl.Element(n), pl.Element(wide)), lambda i: (first, 0), pipeline_mode=pl.Buffered(1))

def place_matrix(fe, first, n):
    col=lax.broadcasted_iota(jnp.int32,(E,n),1)+first; row=lax.broadcasted_iota(jnp.int32,(E,n),0)*fe
    return jnp.where((col>=row)&(col<row+fe),1.0,0.0).astype(BF)

def units_kernel(fe, first, x_ref, wg_ref, wu_ref, b_ref, w_ref, out_ref, pair_ref):
    x=x_ref[...]; n=wg_ref.shape[0]
    pre=mm(x,wg_ref[...],NT); lift=mm(x,wu_ref[...],NT); back=b_ref[...].astype(F32)
    w=w_ref[...]; hi=w.astype(BF); lo=(w-hi.astype(F32)).astype(BF)
    place=place_matrix(fe,first,n)
    spread=mm(jnp.concatenate([hi,lo],axis=1),jnp.concatenate([place,place],axis=0),NN)
    if first+n>E*fe:
        spread=jnp.where(lax.broadcasted_iota(jnp.int32,spread.shape,1)>=E*fe-first,1.0,spread)
    s=0.5+0.5*jnp.tanh(0.5*pre)
    silu=pre*s
    act=silu*lift
    pair_ref[...]=mm((act*back).astype(BF),place,NT)
    back=back*spread
    out_ref[0]=(back*lift*(s+silu*(1.0-s))).astype(BF)
    out_ref[1]=(back*silu).astype(BF)
    out_ref[2]=(act*spread).astype(BF)

def units(x,packed,back,weight,fe,first,bt):
    T,D=x.shape; n=back.shape[1]; r=weight.shape[1]
    ins=[pl.BlockSpec((bt,D),lambda i:(i,0))]+[once((n,D),lambda i,k=k:(k,0)) for k in range(2)]
    ins+=[pl.BlockSpec((bt,n),lambda i:(i,0)),pl.BlockSpec((bt,r),lambda i:(i,0))]
    outs=[jax.ShapeDtypeStruct((3,T,n),BF),jax.ShapeDtypeStruct((T,r),F32)]
    return pl.pallas_call(functools.partial(units_kernel,fe,first),grid=(T//bt,),in_specs=ins,
        out_specs=[pl.BlockSpec((3,bt,n),lambda i:(0,i,0)),pl.BlockSpec((bt,r),lambda i:(i,0))],out_shape=outs,
        compiler_params=params(1),
        cost_estimate=pl.CostEstimate(flops=4*T*D*n,bytes_accessed=2*(T*D+2*n*D+4*T*n),transcendentals=T*n))(x,packed,packed,back,weight)

def lift_kernel(g_ref,w_ref,o_ref):
    o_ref[...]=mm(g_ref[...],w_ref[...],NT).astype(BF)

def lift_back(g,packed,at,n,bt):
    T,D=g.shape
    return pl.pallas_call(lift_kernel,grid=(T//bt,),
        in_specs=[pl.BlockSpec((bt,D),lambda i:(i,0)),rows_once(n,D,at)],
        out_specs=pl.BlockSpec((bt,n),lambda i:(i,0)),out_shape=jax.ShapeDtypeStruct((T,n),BF),compiler_params=params(1),
        cost_estimate=pl.CostEstimate(flops=2*T*D*n,bytes_accessed=2*(T*D+n*D+T*n),transcendentals=0))(g,packed)

def back_kernel(pairs, added, beside, *refs):
    out=refs[-1]
    acc=None
    if added: acc=refs[0][...].astype(F32)
    rs=refs[added:]
    for k in range(pairs):
        a=rs[2*k]; b=rs[2*k+1]
        a=a[0] if len(a.shape)==3 else a[...]
        p=mm(a,b[...],NN)
        acc=p if acc is None else acc+p
    if beside:
        wide=acc.shape[1]
        out[:,:wide]=acc.astype(out.dtype)
        more=sum(r[...] for r in refs[-1-beside:-1])
        gap=jnp.zeros((acc.shape[0],out.shape[1]-wide-more.shape[1]),F32)
        out[:,wide:]=jnp.concatenate([more,gap],axis=1).astype(out.dtype)
    else:
        out[...]=acc.astype(out.dtype)

def core_kernel(pairs, core_ref, *refs):
    out=refs[-1]
    chips,_,w=out.shape
    for z in range(chips):
        at=pl.ds(pl.multiple_of((2*z+core_ref[0])*w,w),w)
        acc=None
        for k in range(pairs):
            a=refs[2*k]; b=refs[2*k+1]
            p=mm(a[0] if len(a.shape)==3 else a[...],b[:,at],NN)
            acc=p if acc is None else acc+p
        out[z]=acc.astype(BF)

def back(terms, added, out_dtype, bt, beside=(), core=None, chips=0):
    T=terms[0][0].shape[-2]; D=terms[0][2].shape[1]
    ins=[];args=[];fl=0;by=0
    if core is not None:
        ins.append(pl.BlockSpec(memory_space=pltpu.SMEM)); args.append(core)
    if added is not None:
        ins.append(pl.BlockSpec((bt,D),lambda i:(i,0))); args.append(added)
    for st,k,packed,n,at in terms:
        if st.ndim==3: ins.append(pl.BlockSpec((1,bt,n),lambda i,k=k:(k,i,0)))
        else: ins.append(pl.BlockSpec((bt,n),lambda i:(i,0)))
        ins.append(rows_once(n,D,at))
        args+= [st,packed]; fl+=2*T*D*n; by+=2*(T*n+n*D)
    for more in beside:
        ins.append(pl.BlockSpec((bt,more.shape[1]),lambda i:(i,0))); args.append(more)
    body=functools.partial(back_kernel,len(terms),0 if added is None else 1,len(beside))
    if beside:
        shape=(T,D+128); ospec=pl.BlockSpec((bt,D+128),lambda i:(i,0))
    elif core is not None:
        w=D//(2*chips); fl//=2
        shape=(chips,T,w); ospec=pl.BlockSpec((chips,bt,w),lambda i:(0,i,0))
        body=functools.partial(core_kernel,len(terms))
    else:
        shape=(T,D); ospec=pl.BlockSpec((bt,D),lambda i:(i,0))
    return pl.pallas_call(body,grid=(T//bt,),in_specs=ins,out_specs=ospec,out_shape=jax.ShapeDtypeStruct(shape,out_dtype),
        compiler_params=params(1),cost_estimate=pl.CostEstimate(flops=fl,bytes_accessed=by+4*T*D,transcendentals=0))(*args)

def outer_kernel(s_ref,x_ref,*refs):
    refs[-1][...]=mm(s_ref[0],x_ref[...],TN).astype(BF)

def outer(stack,first,count,x,total,at,into=None,bc=512):
    T,D=x.shape; n=stack.shape[2]
    ins=[pl.BlockSpec((1,T,n),lambda k,j:(first+k,0,0)),pl.BlockSpec((T,bc),lambda k,j:(0,j))]
    args=[stack,x]; al={}
    if into is not None:
        ins.append(pl.BlockSpec(memory_space=pl.ANY)); args.append(into); al={2:0}
    return pl.pallas_call(outer_kernel,grid=(count,D//bc),in_specs=ins,
        out_specs=pl.BlockSpec((n,bc),lambda k,j:(at+k,j)),out_shape=jax.ShapeDtypeStruct((total,D),BF),
        input_output_aliases=al,compiler_params=params(2),
        cost_estimate=pl.CostEstimate(flops=2*count*T*D*n,bytes_accessed=2*count*(T*n+n*D+T*D),transcendentals=0))(*args)


def place_columns_kernel(chips, norm, at_ref, *refs):
    pieces=refs[:2*chips]
    refs=refs[2*chips:]
    if norm:
        gain_ref, w_ref = refs[:2]
        out_ref, round_ref, r_ref, proj_ref = refs[-4:]
    else:
        (out_ref,) = refs
    w=pieces[0].shape[1]
    for k in range(2*chips):
        out_ref[:,pl.ds(pl.multiple_of(at_ref[k]*w,w),w)]=pieces[k][...]
    if norm:
        v=out_ref[...].astype(F32)
        r=lax.rsqrt(jnp.mean(v*v,axis=-1,keepdims=True)+EPSILON)
        round_ref[...]=(v*r*gain_ref[...]).astype(BF)
        r_ref[...]=r
        proj_ref[...]=mm(round_ref[...],w_ref[...],NT)

def place_columns(pieces, at, gain=None, packed=None, count=0, rows=None, first=0, into=(), bt=256):
    T,w=pieces[0].shape; n=len(pieces)
    total_rows=rows or T
    start=first//bt
    ins=[pl.BlockSpec(memory_space=pltpu.SMEM)]+[pl.BlockSpec((bt,w),lambda i:(i,0))]*n
    args=[at]+list(pieces)
    wides=[(n*w,BF)]
    if gain is not None:
        ins+=[pl.BlockSpec((1,n*w),lambda i:(0,0)),rows_once(count,n*w,0)]; args+=[gain[None],packed]
        wides+=[(n*w,BF),(1,F32),(count,F32)]
    aliases={len(args)+k:k for k in range(len(into))}
    ins+=[pl.BlockSpec(memory_space=pl.ANY)]*len(into); args+=list(into)
    return pl.pallas_call(functools.partial(place_columns_kernel,n//2,gain is not None),grid=(T//bt,),
        in_specs=ins,out_specs=[pl.BlockSpec((bt,m),lambda i:(i+start,0)) for m,_ in wides],
        out_shape=[jax.ShapeDtypeStruct((total_rows,m),d) for m,d in wides],
        input_output_aliases=aliases,compiler_params=params(1),
        cost_estimate=pl.CostEstimate(flops=(6+2*count)*T*n*w,bytes_accessed=6*T*n*w,transcendentals=T))(*args)

def place_rows_kernel(n, times, at_ref, *refs):
    pieces=refs[:n]; refs=refs[n:]
    if times: w_ref,out_ref,made_ref,sem=refs
    else: out_ref,sem=refs
    rows=pieces[0].shape[0]
    to=[pl.ds(pl.multiple_of(at_ref[k]*rows,rows),rows) for k in range(n)]
    copies=[pltpu.make_async_copy(pieces[k],out_ref.at[to[k]],sem.at[k]) for k in range(n)]
    for c in copies: c.start()
    if times:
        for k in range(n): made_ref[to[k]]=mm(pieces[k][...],w_ref[...],NT).astype(BF)
    for c in copies: c.wait()

def place_rows(pieces, at, weight=None):
    rows,w=pieces[0].shape; n=len(pieces)
    vmem=pl.BlockSpec(memory_space=pltpu.VMEM)
    outs=[jax.ShapeDtypeStruct((n*rows,w),BF)]; specs=[pl.BlockSpec(memory_space=pl.ANY)]; more=[]
    if weight is not None:
        outs.append(jax.ShapeDtypeStruct((n*rows,weight.shape[0]),BF)); specs.append(vmem); more=[weight]
    return pl.pallas_call(functools.partial(place_rows_kernel,n,bool(more)),
        in_specs=[pl.BlockSpec(memory_space=pltpu.SMEM)]+[vmem]*(n+len(more)),
        out_specs=specs,out_shape=outs,
        scratch_shapes=[pltpu.SemaphoreType.DMA((n,))],compiler_params=pltpu.CompilerParams(vmem_limit_bytes=VMEM_LIMIT),
        cost_estimate=pl.CostEstimate(flops=2*n*rows*w*(weight.shape[0] if more else 0),bytes_accessed=4*n*rows*w,transcendentals=0))(at,*pieces,*more)

def norm_rows_kernel(n, at_ref, col_ref, gain_ref, wr_ref, kept_ref, *refs):
    pieces=refs[:n]; round_ref,cols_ref,gating_ref,weight_ref,made,cut,sem,sem2=refs[n:]
    rows=pieces[0].shape[0]; w=cut.shape[2]
    copies=[]
    for k in range(n):
        v=pieces[k][...].astype(F32)
        r=lax.rsqrt(jnp.mean(v*v,axis=-1,keepdims=True)+EPSILON)
        made[k]=(v*r*gain_ref[...]).astype(BF)
        cut[k]=pieces[k][:,pl.ds(pl.multiple_of(col_ref[0]*w,w),w)]
        to=pl.ds(pl.multiple_of(at_ref[k]*rows,rows),rows)
        copies.append(pltpu.make_async_copy(made.at[k],round_ref.at[to],sem.at[k]))
        copies.append(pltpu.make_async_copy(cut.at[k],cols_ref.at[to],sem2.at[k]))
        copies[-2].start(); copies[-1].start()
        logits=mm(made[k],wr_ref[...],NT)
        e=jnp.exp(logits-jnp.max(logits,axis=-1,keepdims=True))
        gating=e/jnp.sum(e,axis=-1,keepdims=True)
        gating_ref[to]=gating
        weight_ref[to]=gating*kept_ref[to]
    for c in copies: c.wait()

def norm_rows(pieces, at, column, w, gain, router, kept):
    rows,wide=pieces[0].shape; n=len(pieces)
    vmem=pl.BlockSpec(memory_space=pltpu.VMEM)
    return pl.pallas_call(functools.partial(norm_rows_kernel,n),
        in_specs=[pl.BlockSpec(memory_space=pltpu.SMEM)]*2+[vmem]*(n+3),
        out_specs=[pl.BlockSpec(memory_space=pl.ANY)]*2+[vmem]*2,
        out_shape=[jax.ShapeDtypeStruct((n*rows,wide),BF),jax.ShapeDtypeStruct((n*rows,w),BF)]+[jax.ShapeDtypeStruct((n*rows,E),F32)]*2,
        scratch_shapes=[pltpu.VMEM((n,rows,wide),BF),pltpu.VMEM((n,rows,w),BF),pltpu.SemaphoreType.DMA((n,)),pltpu.SemaphoreType.DMA((n,))],
        compiler_params=pltpu.CompilerParams(vmem_limit_bytes=VMEM_LIMIT),
        cost_estimate=pl.CostEstimate(flops=6*n*rows*wide,bytes_accessed=4*n*rows*wide,transcendentals=n*rows))(at,column,gain[None],router,kept,*pieces)

def small_kernel(pairs_ref, up_ref, kr_ref, dot_ref, entry_ref, out_ref):
    bt=out_ref.shape[0]
    out_ref[:,:R]=mm(pairs_ref[...],up_ref[...],NT).astype(BF)
    h=DR//2
    kr=kr_ref[...]
    gap=jnp.zeros((bt,DR-1-entry_ref.shape[1]),F32)
    out_ref[:,R:]=jnp.concatenate(
        [kr[:,:h]+kr[:,h:DR],kr[:,DR:DR+h]+kr[:,DR+h:],dot_ref[...],entry_ref[...],gap],axis=1).astype(BF)

def small_terms(pairs, up, kr, dots, entries, bt=512):
    T=pairs.shape[0]
    def rows(a): return pl.BlockSpec((bt,a.shape[1]),lambda i:(i,0))
    return pl.pallas_call(small_kernel,grid=(T//bt,),
        in_specs=[rows(pairs),pl.BlockSpec(up.shape,lambda i:(0,0)),rows(kr),rows(dots),rows(entries)],
        out_specs=pl.BlockSpec((bt,R+DN),lambda i:(i,0)),out_shape=jax.ShapeDtypeStruct((T,R+DN),BF),
        compiler_params=params(1),
        cost_estimate=pl.CostEstimate(flops=2*T*R*pairs.shape[1],bytes_accessed=8*T*R,transcendentals=0))(pairs,up,kr,dots,entries)

def latent_back_kernel(small_ref, proj_ref, gain_ref, cos_ref, sin_ref, delta_ref, dots_ref, gain_delta_ref):
    i=pl.program_id(0)
    at=proj_ref.shape[1]-R-DN
    dl=small_ref[:,:R].astype(F32)
    vl=proj_ref[:,at:at+R]
    rl=lax.rsqrt(jnp.mean(vl*vl,axis=-1,keepdims=True)+EPSILON)
    gain=gain_ref[...]
    part=jnp.sum(dl*vl*rl,axis=0,keepdims=True)
    @pl.when(i==0)
    def _(): gain_delta_ref[...]=part
    @pl.when(i>0)
    def _(): gain_delta_ref[...]+=part
    gd=gain*dl
    head=rl*gd-vl*(rl*rl*rl)*jnp.mean(vl*gd,axis=-1,keepdims=True)
    beyond=small_ref[:,R:]
    row=lax.broadcasted_iota(jnp.int32,(DN,DN),0); col=lax.broadcasted_iota(jnp.int32,(DN,DN),1)
    h=DR//2
    put=jnp.where(((row<h)&(col==row))|((row>=h)&(row<DR)&(col==row+h)),1.0,0.0).astype(BF)
    spread=mm(beyond,put,NN)
    tail=spread*cos_ref[...]-pltpu.roll(spread,DR,1)*sin_ref[...]
    delta_ref[:,:R]=head.astype(BF)
    delta_ref[:,R:]=tail.astype(BF)
    own=jnp.sum(head*vl,axis=-1,keepdims=True)+jnp.sum(tail*proj_ref[:,at+R:],axis=-1,keepdims=True)
    lane=lax.broadcasted_iota(jnp.int32,beyond.shape,1)
    dots_ref[...]=own+jnp.sum(jnp.where(lane==DR,beyond.astype(F32),0.0),axis=-1,keepdims=True)

def latent_back(small, proj, gain, cosine, sine, bt=512):
    T,wide=small.shape; turns=LEN//bt
    return pl.pallas_call(latent_back_kernel,grid=(T//bt,),
        in_specs=[pl.BlockSpec((bt,wide),lambda i:(i,0)),pl.BlockSpec((bt,proj.shape[1]),lambda i:(i,0)),
                  pl.BlockSpec((1,R),lambda i:(0,0)),pl.BlockSpec((bt,DN),lambda i:(i%turns,0)),pl.BlockSpec((bt,DN),lambda i:(i%turns,0))],
        out_specs=[pl.BlockSpec((bt,R+DN),lambda i:(i,0)),pl.BlockSpec((bt,1),lambda i:(i,0)),pl.BlockSpec((1,R),lambda i:(0,0))],
        out_shape=[jax.ShapeDtypeStruct((T,R+DN),BF),jax.ShapeDtypeStruct((T,1),F32),jax.ShapeDtypeStruct((1,R),F32)],
        compiler_params=params(1),
        cost_estimate=pl.CostEstimate(flops=30*T*wide,bytes_accessed=8*T*wide,transcendentals=T))(small,proj,gain,cosine,sine)

def last_pack_kernel(delta_ref, x_ref, w_ref, small_ref, g_ref, latent_ref, out_ref):
    n=delta_ref.shape[1]
    d=mm(delta_ref[...],x_ref[...],TN)
    out_ref[:n]=d.astype(BF)
    sums=jnp.sum(w_ref[...].astype(F32)*d,axis=0,keepdims=True)
    row=lax.broadcasted_iota(jnp.int32,(32,DN),0); col=lax.broadcasted_iota(jnp.int32,(32,DN),1)
    at=DR+1
    pick=((row<E)&(col==row+at+2))|((row==E)&(col==at))|((row==E+1)&(col==at+1))
    v=mm(jnp.where(pick,1.0,0.0).astype(BF),small_ref[...],NT)
    line=lax.broadcasted_iota(jnp.int32,v.shape,0)
    v=jnp.where(line==E+1,(v+sums)/g_ref[...],v)
    out_ref[n:]=jnp.where(line==E+2,latent_ref[...],v).astype(BF)

def last_pack(delta, x, packed, first, small, gain, latent_row, bc=512):
    T,D=x.shape; n=delta.shape[1]
    def cols(a): return pl.BlockSpec((a.shape[0],bc),lambda j:(0,j))
    return pl.pallas_call(last_pack_kernel,grid=(D//bc,),
        in_specs=[pl.BlockSpec((T,n),lambda j:(0,0)),cols(x),
                  pl.BlockSpec((pl.Element(n),pl.Element(bc)),lambda j:(first,j*bc)),pl.BlockSpec((bc,DN),lambda j:(j,R//DN)),cols(gain),cols(latent_row)],
        out_specs=pl.BlockSpec((n+32,bc),lambda j:(0,j)),out_shape=jax.ShapeDtypeStruct((n+32,D),BF),
        compiler_params=params(1),
        cost_estimate=pl.CostEstimate(flops=2*T*D*n,bytes_accessed=2*(T*D+2*n*D+T*n),transcendentals=0))(delta,x,packed,small,gain,latent_row)


def turn(x, cosine, sine):
    return x*cosine+pltpu.roll(x,64,1)*sine

def slot_mask(shape, head):
    lane=lax.broadcasted_iota(jnp.int32,shape,1)
    low=head*(DR//2)
    inside=((lane>=low)&(lane<low+DR//2))|((lane>=low+DR)&(lane<low+DR+DR//2))
    return inside

def causal_scores(q, k, first):
    s=mm(q,k,NT)*SCALE
    row=lax.broadcasted_iota(jnp.int32,s.shape,0)+first
    col=lax.broadcasted_iota(jnp.int32,s.shape,1)
    return jnp.where(col<=row,s,-1e30)

def attend_kernel(heads, proj_ref, up_ref, gain_ref, cos_ref, sin_ref, *refs):
    q_ref, kr_ref, kv_ref, latent_ref, mixed_ref, lse_ref = refs[-6:]
    content=heads*DN
    at=content+DN
    q_ref[:,:content]=proj_ref[:,:content].astype(BF)
    cosine,sine=cos_ref[...],sin_ref[...]
    q_ref[:,content:]=turn(proj_ref[:,content:at],cosine,sine).astype(BF)
    vl=proj_ref[:,at:at+R]
    latent_ref[...]=(vl*lax.rsqrt(jnp.mean(vl*vl,axis=-1,keepdims=True)+EPSILON)*gain_ref[...]).astype(BF)
    kr_ref[...]=turn(proj_ref[:,at+R:],cosine,sine).astype(BF)
    kv_ref[...]=mm(latent_ref[...],up_ref[...],NN).astype(BF)
    kr=kr_ref[...]
    for h in range(heads):
        kc=kv_ref[:,h*(DN+DV):h*(DN+DV)+DN]
        v=kv_ref[:,h*(DN+DV)+DN:(h+1)*(DN+DV)]
        k=jnp.concatenate([kc,jnp.where(slot_mask(kr.shape,h),kr,jnp.zeros_like(kr))],axis=1)
        for i in range(LEN//BLOCK):
            a,b=i*BLOCK,(i+1)*BLOCK
            q=jnp.concatenate([q_ref[a:b,h*DN:(h+1)*DN],q_ref[a:b,content:]],axis=1)
            s=causal_scores(q,k[:b],a)
            m=jnp.max(s,axis=-1,keepdims=True)
            e=jnp.exp(s-m)
            t=jnp.sum(e,axis=-1,keepdims=True)
            p=(e*(1.0/t)).astype(BF)
            mixed_ref[a:b,h*DV:(h+1)*DV]=mm(p,v[:b],NN).astype(BF)
            lse_ref[a:b,h:h+1]=m+jnp.log(t)

def attend(proj, up, gain, cosine, sine, heads, sequence, into=()):
    T=proj.shape[0]; wide=proj.shape[1]
    def rows(n): return pl.BlockSpec((LEN,n),lambda i:(sequence,0))
    def whole(a): return pl.BlockSpec(a.shape,lambda i:(0,0))
    qn=heads*DN+DN
    outs=[(qn,BF),(DN,BF),(heads*(DN+DV),BF),(R,BF),(heads*DV,BF),(heads,F32)]
    args=[proj,up,gain,cosine,sine]
    return pl.pallas_call(functools.partial(attend_kernel,heads),grid=(1,),
        in_specs=[rows(wide)]+[whole(a) for a in args[1:]]+[pl.BlockSpec(memory_space=pl.ANY)]*len(into),
        out_specs=[rows(n) for n,_ in outs],out_shape=[jax.ShapeDtypeStruct((T,n),d) for n,d in outs],
        input_output_aliases={len(args)+k:k for k in range(len(into))},compiler_params=params(1),
        cost_estimate=pl.CostEstimate(flops=LEN*LEN*heads*512,bytes_accessed=LEN*8000,transcendentals=LEN*LEN*heads//2))(*args,*into)

def attend_back_kernel(heads, q_ref, kr_ref, kv_ref, mixed_ref, lse_ref, do_ref, cos_ref, sin_ref, dq_ref, dkv_ref, dkr_ref, dot_ref, dk_acc, dv_acc):
    content=heads*DN
    kr=kr_ref[...]
    for h in range(heads):
        kc=kv_ref[:,h*(DN+DV):h*(DN+DV)+DN]
        v=kv_ref[:,h*(DN+DV)+DN:(h+1)*(DN+DV)]
        mask=slot_mask(kr.shape,h)
        k=jnp.concatenate([kc,jnp.where(mask,kr,jnp.zeros_like(kr))],axis=1)
        for i in reversed(range(LEN//BLOCK)):
            a,b=i*BLOCK,(i+1)*BLOCK
            q=jnp.concatenate([q_ref[a:b,h*DN:(h+1)*DN],q_ref[a:b,content:]],axis=1)
            do=do_ref[a:b,h*DV:(h+1)*DV]
            p=jnp.exp(causal_scores(q,k[:b],a)-lse_ref[a:b,h:h+1])
            dp=mm(do,v[:b],NT)
            along=jnp.sum(do.astype(F32)*mixed_ref[a:b,h*DV:(h+1)*DV].astype(F32),axis=-1,keepdims=True)
            ds=(p*(dp-along)).astype(BF)
            pv=mm(p.astype(BF),do,TN)
            pk=mm(ds,q,TN)
            if i==LEN//BLOCK-1:
                dv_acc[...]=pv; dk_acc[...]=pk
            else:
                dv_acc[:b]+=pv; dk_acc[:b]+=pk
            dq=mm(ds,k[:b],NN)*SCALE
            d=jnp.sum(dq*q.astype(F32),axis=-1,keepdims=True)
            if h==0: dot_ref[a:b]=d
            else: dot_ref[a:b]+=d
            dq_ref[a:b,h*DN:(h+1)*DN]=dq[:,:DN].astype(BF)
            turned=turn(dq[:,DN:],cos_ref[a:b],-sin_ref[a:b])
            turned=jnp.where(mask[:b-a],turned,0.0).astype(BF)
            if h==0: dq_ref[a:b,content:]=turned
            else: dq_ref[a:b,content:]+=turned
        dkv_ref[:,h*(DN+DV):h*(DN+DV)+DN]=(dk_acc[:,:DN]*SCALE).astype(BF)
        dkv_ref[:,h*(DN+DV)+DN:(h+1)*(DN+DV)]=dv_acc[...].astype(BF)
        part=jnp.where(mask,dk_acc[:,DN:]*SCALE,0.0)
        if h==0: dkr_ref[...]=part
        else: dkr_ref[...]+=part

def attend_back(q,kr,kv,mixed,lse,do,cosine,sine,heads):
    T=q.shape[0]
    def rows(n): return pl.BlockSpec((LEN,n),lambda i:(i,0))
    def whole(a): return pl.BlockSpec(a.shape,lambda i:(0,0))
    args=(q,kr,kv,mixed,lse,do)
    outs=[(q.shape[1],BF),(kv.shape[1],BF),(DN,F32),(1,F32)]
    return pl.pallas_call(functools.partial(attend_back_kernel,heads),grid=(T//LEN,),
        in_specs=[rows(a.shape[1]) for a in args]+[whole(cosine),whole(sine)],
        out_specs=[rows(n) for n,_ in outs],out_shape=[jax.ShapeDtypeStruct((T,n),d) for n,d in outs],
        scratch_shapes=[pltpu.VMEM((LEN,2*DN),F32),pltpu.VMEM((LEN,DV),F32)],
        compiler_params=params(1),
        cost_estimate=pl.CostEstimate(flops=T*LEN*heads*1400,bytes_accessed=T*6000,transcendentals=T*LEN*heads//2))(*args,cosine,sine)

def tables():
    position=np.arange(LEN,dtype=np.float32)
    spread=(10000.0**(-np.arange(DR//2,dtype=np.float32)/(DR//2))).astype(np.float32)
    phase=(position[:,None]*spread[None,:]).astype(np.float32)
    c,s=np.cos(phase),np.sin(phase)
    return np.concatenate([c]*4,1).astype(np.float32),np.concatenate([-s,-s,s,s],1).astype(np.float32)


class Line:
    def __init__(self):
        self.n = lax.axis_size("tensor")
        self.chips = self.n // 2
        index = lax.axis_index("tensor")
        self.index = index
        self.z = index // 2
        self.c = index % 2

    def swap(self, a):
        return lax.ppermute(a, "tensor", [(i, i ^ 1) for i in range(self.n)])

    def shift(self, a, step, sources):
        pairs = [
            (2 * s + c, 2 * (s + step) + c)
            for s in sources
            if 0 <= s + step < self.chips
            for c in (0, 1)
        ]
        return lax.ppermute(a, "tensor", pairs)

    def pieces(self, own, order):
        n = self.chips
        out, at = [], []
        for k, piece in enumerate(own):
            chip = (self.z - k + n) % n
            out += [piece, self.swap(piece)]
            at += [order(chip, self.c), order(chip, 1 - self.c)]
        return out, jnp.stack(at).astype(jnp.int32)

    def row_pieces(self, own):
        return self.pieces(own, lambda chip, core: core * self.chips + chip)

    def column_pieces(self, own):
        return self.pieces(own, lambda chip, core: chip * 2 + core)

    def halves(self, p):
        half = p.shape[0] // 2
        return [lax.dynamic_slice_in_dim(p, c * half, half, 0) for c in (self.c, 1 - self.c)]

    def row_scatter(self, both):
        ch = both.shape[0] // self.chips
        return Scatter(self, lambda j: lax.dynamic_slice_in_dim(both, j * ch, ch, 0))

    def column_scatter(self, both):
        return Scatter(self, lambda j: lax.dynamic_index_in_dim(both, j, 0, False))

    def row_start(self, rows):
        ch = rows // self.n
        return (self.c * self.chips + self.z) * ch, ch


def total(mine, arrived):
    return (mine.astype(F32) + arrived.astype(F32)).astype(BF)


class Gather:
    def __init__(self, line, block):
        self.line, self.left, self.right = line, [block], [block]

    def start(self):
        n, k = self.line.chips, len(self.left)
        return (
            self.line.shift(self.left[-1], 1, range(k - 1, n)),
            self.line.shift(self.right[-1], -1, range(0, n - k + 1)),
        )

    def take(self, arrived):
        self.left.append(arrived[0])
        self.right.append(arrived[1])

    def result(self):
        n, z = self.line.chips, self.line.z
        return self.left[:1] + [jnp.where(z >= k, self.left[k], self.right[n - k]) for k in range(1, n)]


class Scatter:
    def __init__(self, line, block):
        self.line, self.block, self.step, self.left, self.right = line, block, 0, None, None

    def start(self):
        self.step += 1
        n, s, z = self.line.chips, self.step, self.line.z
        up = self.block(jnp.clip(n - s + z, 0, n - 1))
        down = self.block(jnp.clip(z - (n - s), 0, n - 1))
        if self.left is not None:
            up, down = total(up, self.left), total(down, self.right)
        return self.line.shift(up, 1, range(0, s)), self.line.shift(down, -1, range(n - s, n))

    def take(self, arrived):
        self.left, self.right = arrived

    def result(self):
        return self.block(self.line.z).astype(F32) + self.left.astype(F32) + self.right.astype(F32)


def beside(moves, job=None):
    arrived, done = lax.optimization_barrier(([m.start() for m in moves], job() if job else None))
    for move, a in zip(moves, arrived):
        move.take(a)
    return done


def steps(move, count, jobs=()):
    made = []
    for k in range(count):
        made.append(beside([move], jobs[k] if k < len(jobs) else None))
    return made


def gather_rows(packed):
    return lax.all_gather(packed, "dp", axis=1, tiled=True)


def scatter_rows(packed):
    return lax.psum_scatter(packed, "dp", scatter_dimension=1, tiled=True)


def split_rows(packed, counts):
    out, at = [], 0
    for count in counts:
        out.append(packed[at : at + count])
        at += count
    return out


def ranks(mask):
    number = mask.shape[0]
    block = 128
    pieces = mask.reshape(number // block, block, E).astype(BF)
    lower = jnp.tril(jnp.ones((block, block), BF), -1)
    inside = jnp.einsum("ij,bje->bie", lower, pieces, preferred_element_type=F32)
    totals = jnp.sum(pieces.astype(F32), axis=1).astype(BF)
    ahead = jnp.tril(jnp.ones((number // block, number // block), BF), -1)
    before = dot(ahead, totals, 1, 0)
    return (inside + before[:, None, :]).reshape(number, E)


def per_device(
    layer_input, cotangent, first_gain, query_weight, latent_down, latent_gain, latent_up,
    output_weight, second_gain, router_weight, expert_gate, expert_up, expert_down,
    shared_gate, shared_up, shared_down, routes,
):
    line = Line()
    n_dp = lax.axis_size("dp")
    wide = D // n_dp
    number = layer_input.shape[0]
    heads_here = output_weight.shape[0] // DV
    fe = expert_down.shape[1]
    my_columns = layer_input.shape[1]
    column_start = line.index * my_columns
    row_start, row_count = line.row_start(number)

    half = DR // 2
    spare_heads = 2 - heads_here
    up_rows = latent_up.size // wide
    by_head = query_weight.T.reshape(heads_here, DN + DR, wide)
    blank = jnp.zeros((spare_heads * half, wide), BF)
    gains = jnp.zeros((16, wide), BF)
    gains = gains.at[0].set(first_gain).at[1].set(second_gain)
    gains = gains.at[2, : latent_gain.shape[0]].set(latent_gain)
    down = latent_down.T
    queries_wide = heads_here * DN + DN
    latent_wide = R + DN
    attend_pack = [
        by_head[:, :DN].reshape(heads_here * DN, wide),
        by_head[:, DN : DN + half].reshape(heads_here * half, wide), blank,
        by_head[:, DN + half :].reshape(heads_here * half, wide), blank,
        down[: R + half], down[R : R + half], down[R + half :], down[R + half :],
        latent_up.reshape(up_rows, wide), gains, router_weight.T, output_weight,
    ]
    attend_packed = gather_rows(jnp.concatenate([m for m in attend_pack if m.shape[0]], axis=0))
    wproj, wup, gains, wr, wo = split_rows(
        attend_packed, [queries_wide + latent_wide, up_rows, 16, E, output_weight.shape[0]]
    )
    wup = wup.reshape(up_rows, n_dp, wide).transpose(1, 0, 2).reshape(R, -1)
    first_g = gains[0].astype(F32)
    second_g = gains[1].astype(F32)
    latent_g = gains[2].reshape(n_dp, wide)[:, : R // n_dp].reshape(R).astype(F32)
    cosine, sine = (jnp.asarray(table) for table in tables())

    n_units = E * fe + shared_down.shape[0]
    n0 = (n_units // 512 + 1) * 256
    n1 = n_units - n0
    last_step = line.chips - 1
    gate = expert_gate.transpose(0, 2, 1).reshape(E * fe, wide)
    up = expert_up.transpose(0, 2, 1).reshape(E * fe, wide)
    move = Gather(line, layer_input[:LEN])
    downs, early, late = steps(move, 3, (
        lambda: jnp.concatenate([expert_down.reshape(E * fe, wide), shared_down], axis=0),
        lambda: jnp.concatenate([gate[:n0], up[:n0]], axis=0),
        lambda: jnp.concatenate([gate[n0:], shared_gate.T, up[n0:], shared_up.T], axis=0),
    ))
    steps(move, last_step - 3)
    downs, early, late = gather_rows(downs), gather_rows(early), gather_rows(late)

    tile = 256
    core = line.c.reshape(1).astype(jnp.int32)
    placed, attended = (), ()

    def place(move, sequence):
        pieces, at = line.column_pieces(move.result())
        return place_columns(
            pieces, at, first_g, attend_packed, queries_wide + latent_wide, number, sequence * LEN, placed
        )

    def attention(sequence):
        return attend(placed[3], wup, latent_g[None], cosine, sine, heads_here, sequence, attended)

    for sequence in range(1, number // LEN):
        ahead, after = move, layer_input[sequence * LEN : (sequence + 1) * LEN]
        ahead.left[-1], ahead.right[-1], after = lax.optimization_barrier((ahead.left[-1], ahead.right[-1], after))
        move = Gather(line, after)
        beside([move])
        placed = beside([move], lambda: place(ahead, sequence - 1))
        steps(move, last_step - 3)
        attended = beside([move], lambda: attention(sequence - 1))
    move.left[-1], move.right[-1], cotangent = lax.optimization_barrier((move.left[-1], move.right[-1], cotangent))
    grad_move = Gather(line, cotangent)
    placed = place(move, number // LEN - 1)
    attended = beside([grad_move], lambda: attention(number // LEN - 1))
    rows, first_round, r1, proj = placed
    q, kr, kv, latent, mixed, log_total = attended
    mine, theirs = line.halves(mixed)
    arrived = line.swap(dot(theirs, wo, 1, 0, BF))
    move = line.row_scatter(total(dot(mine, wo, 1, 0, BF), arrived))
    for _ in range(last_step - 1):
        beside([move, grad_move])
    (grad,) = beside([move], lambda: place_columns(*line.column_pieces(grad_move.result())))
    hidden_rows = (
        lax.dynamic_slice_in_dim(rows, row_start, row_count, 0).astype(F32) + move.result()
    ).astype(BF)
    move = Gather(line, hidden_rows)
    back0, back1 = steps(move, 2, (
        lambda: lift_back(grad, downs, 0, n0, tile),
        lambda: lift_back(grad, downs, n0, n1, tile),
    ))
    steps(move, last_step - 2)
    hidden_pieces, hidden_at = line.row_pieces(move.result())
    named = jnp.any(routes[:, :, None] == jnp.arange(E, dtype=jnp.int32)[None, None, :], axis=1)
    kept = jnp.where(named & (ranks(named) < CAP), 1.0, 0.0)
    second_round, hidden_columns, gating, weight = norm_rows(
        hidden_pieces, hidden_at, line.index.reshape(1).astype(jnp.int32), my_columns, second_g, wr, kept
    )

    stack0, pair0 = units(second_round, early, back0, weight, fe, 0, tile)
    deltas = outer(stack0, 0, 2, second_round, 3 * n0, 0)
    deltas = outer(stack0, 2, 1, grad, 3 * n0, 2, deltas)
    deltas, stack0 = lax.optimization_barrier((deltas, stack0))
    early_sums = scatter_rows(deltas)
    stack1, pair1 = units(second_round, late, back1, weight, fe, n0, tile)
    second_terms = back(
        [(stack0, 0, early, n0, 0), (stack0, 1, early, n0, n0), (stack1, 0, late, n1, 0), (stack1, 1, late, n1, n1)],
        None, BF, tile, (pair0, pair1),
    )

    branch_terms = [(stack0, 2, downs, n0, 0), (stack1, 2, downs, n1, n0)]
    mine, theirs = line.halves(second_terms)
    move = line.row_scatter(total(mine, line.swap(theirs)))
    deltas = beside([move], lambda: outer(stack1, 0, 1, second_round, 3 * n1, 0))
    deltas = beside([move], lambda: outer(stack1, 1, 1, second_round, 3 * n1, 1, deltas))
    branch_theirs = beside([move], lambda: back(branch_terms, None, BF, tile, (), 1 - core, line.chips))
    steps(move, last_step - 3)
    summed = move.result()

    def own_rows(a):
        return lax.dynamic_slice_in_dim(a, row_start, row_count, 0)

    gating_rows, kept_rows, x2 = own_rows(gating), own_rows(kept), own_rows(second_round)
    u = summed[:, D : D + E] * kept_rows
    logits_delta = gating_rows * (u - jnp.sum(gating_rows * u, axis=-1, keepdims=True))
    d2 = summed[:, :D] + dot(logits_delta.astype(BF), wr, 1, 0)
    v2 = hidden_rows.astype(F32)
    r2 = lax.rsqrt(jnp.mean(v2 * v2, axis=-1, keepdims=True) + EPSILON)
    vgd = jnp.mean(v2 * second_g * d2, axis=-1, keepdims=True)
    hidden_delta = own_rows(grad).astype(F32) + r2 * second_g * d2 - v2 * (r2**3) * vgd
    move = Gather(line, hidden_delta.astype(BF))
    branch_mine, branch_arrived = beside([move], lambda: (
        back(branch_terms, None, BF, tile, (), core, line.chips), line.swap(branch_theirs)
    ))
    branch_move = line.column_scatter(total(branch_mine, branch_arrived))
    deltas = beside([move, branch_move], lambda: outer(stack1, 2, 1, grad, 3 * n1, 2, deltas))
    router_delta = dot(x2, logits_delta.astype(BF), 0, 0)
    second_gain_delta = jnp.sum(d2 * v2 * r2, axis=0)
    early_sums, deltas, move.left[-1] = lax.optimization_barrier((early_sums, deltas, move.left[-1]))
    late_sums = scatter_rows(deltas)
    for _ in range(last_step - 2):
        beside([move, branch_move])
    delta_pieces, delta_at = line.row_pieces(move.result())

    def heads_back():
        placed, delta_mixed = place_rows(delta_pieces, delta_at, wo)
        return placed, attend_back(q, kr, kv, mixed, log_total, delta_mixed, cosine, sine, heads_here)

    hidden_delta, heads = beside([branch_move], heads_back)
    layer_output = (hidden_columns.astype(F32) + branch_move.result()).astype(BF)
    delta_queries, delta_pairs, delta_kr, query_dot = heads
    delta_wq = dot(delta_queries, first_round, 0, 0)
    query_gain = jnp.sum(wproj[:queries_wide].astype(F32) * delta_wq, axis=0)
    per_entry = jnp.concatenate([second_gain_delta[:, None], query_gain[:, None], router_delta], axis=1)
    if number > D:
        per_entry = jnp.concatenate([per_entry, jnp.zeros((number - D, E + 2), F32)], axis=0)
    small = small_terms(delta_pairs, wup, delta_kr, query_dot, per_entry)
    first_terms = [(delta_queries, 0, attend_packed, queries_wide, 0)]
    mine, theirs = line.halves(small)
    move = line.row_scatter(total(mine, line.swap(theirs)))

    def attend_deltas():
        delta_wup = dot(latent, delta_pairs, 0, 0, BF)
        return jnp.concatenate(
            [delta_wq.astype(BF),
             delta_wup.reshape(n_dp, up_rows, wide).transpose(1, 0, 2).reshape(up_rows, D),
             dot(mixed, hidden_delta, 0, 0, BF)], axis=0)

    theirs, mine = steps(move, 2, (
        lambda: back(first_terms, None, BF, tile, (), 1 - core, line.chips),
        lambda: back(first_terms, None, BF, tile, (), core, line.chips),
    ))
    deltas, arrived = beside([move], lambda: (attend_deltas(), line.swap(theirs)))
    attend_sums = scatter_rows(deltas).astype(F32)
    steps(move, last_step - 3)
    small, both, layer_output = lax.optimization_barrier(
        (move.result().astype(BF), total(mine, arrived), layer_output)
    )
    move = Gather(line, small)
    steps(move, last_step - 1)
    move.left[-1], move.right[-1], both = lax.optimization_barrier((move.left[-1], move.right[-1], both))
    first_move = line.column_scatter(both)
    beside([move, first_move])
    small_pieces, small_at = line.row_pieces(move.result())
    small_pieces, late_sums = lax.optimization_barrier((small_pieces, late_sums))
    wld = wproj[queries_wide:]

    def last():
        (small,) = place_rows(small_pieces, small_at)
        delta_latent, dots, gain_delta = latent_back(small, proj, latent_g[None], cosine, sine)
        latent_row = jnp.pad(gain_delta.reshape(n_dp, R // n_dp), ((0, 0), (0, wide - R // n_dp))).reshape(1, D)
        return delta_latent, dots, last_pack(
            delta_latent, first_round, attend_packed, queries_wide, small, first_g[None], latent_row)

    delta_latent, dots, pack = beside([first_move], last)
    steps(first_move, last_step - 2)
    first_share = first_move.result()
    last_sums = scatter_rows(pack).astype(F32)
    dwld, vectors = last_sums[:latent_wide], last_sums[latent_wide:]
    dwq, dwup, dwo = split_rows(attend_sums, [queries_wide, up_rows, output_weight.shape[0]])
    content = heads_here * DN
    dwq = jnp.concatenate(
        [dwq[:content].reshape(heads_here, DN, wide),
         dwq[content : content + heads_here * half].reshape(heads_here, half, wide),
         dwq[content + DR : content + DR + heads_here * half].reshape(heads_here, half, wide)], axis=1
    ).reshape(heads_here * (DN + DR), wide)
    dwld = jnp.concatenate([dwld[: R + half], dwld[R + DR : R + DR + half]], axis=0)

    first_share = first_share + dot(
        delta_latent, lax.dynamic_slice_in_dim(wld, column_start, my_columns, 1), 1, 0
    )
    vc = layer_input.astype(F32)
    gc = lax.dynamic_slice_in_dim(first_g, column_start, my_columns, 0)
    input_delta = (
        lax.dynamic_slice_in_dim(hidden_delta, column_start, my_columns, 1).astype(F32)
        + r1 * gc * first_share
        - vc * (r1 * r1) * (dots / D)
    )

    def units_delta(k):
        return early_sums[k * n0 : (k + 1) * n0], late_sums[k * n1 : (k + 1) * n1]

    def expert_delta(k):
        first, second = units_delta(k)
        return jnp.concatenate([first, second[: E * fe - n0]], axis=0).astype(F32).reshape(E, fe, wide)

    def shared_delta(k):
        return units_delta(k)[1][E * fe - n0 :].astype(F32)

    return (
        layer_output, input_delta, vectors[E + 1], dwq.T, dwld.T, vectors[E + 2, : R // n_dp],
        dwup.reshape(latent_up.shape), dwo, vectors[E], vectors[:E].T,
        expert_delta(0).transpose(0, 2, 1), expert_delta(1).transpose(0, 2, 1), expert_delta(2),
        shared_delta(0).T, shared_delta(1).T, shared_delta(2),
    )


def solution(mesh):
    in_specs = (
        P("dp", "tensor"), P("dp", "tensor"), P("dp"), P("dp", "tensor"), P("dp", None), P("dp"),
        P("dp", "tensor"), P("tensor", "dp"), P("dp"), P("dp", None), P(None, "dp", "tensor"),
        P(None, "dp", "tensor"), P(None, "tensor", "dp"), P("dp", "tensor"), P("dp", "tensor"),
        P("tensor", "dp"), P("dp", None),
    )
    out_specs = (
        P("dp", "tensor"), P("dp", "tensor"), P("dp"), P("dp", "tensor"), P("dp", None), P("dp"),
        P("dp", "tensor"), P("tensor", "dp"), P("dp"), P("dp", None), P(None, "dp", "tensor"),
        P(None, "dp", "tensor"), P(None, "tensor", "dp"), P("dp", "tensor"), P("dp", "tensor"),
        P("tensor", "dp"),
    )
    return jax.shard_map(
        per_device, mesh=mesh, in_specs=in_specs, out_specs=out_specs, check_vma=False
    )
```

```python
import functools

import jax
import jax.numpy as jnp
import numpy as np
from jax import lax
from jax.experimental import pallas as pl
from jax.experimental.pallas import tpu as pltpu
from jax.sharding import PartitionSpec as P

D = 2048
DN = 128
DR = 64
DV = 128
R = 512
E = 16
LEN = 1024
CAP = 864
EPSILON = 1e-06
SCALE = (DN + DR) ** -0.5
BLOCK = 256
BF = jnp.bfloat16
F32 = jnp.float32


def dot(a, b, ca, cb, out=F32):
    return lax.dot_general(
        a, b, (((ca,), (cb,)), ((), ())), preferred_element_type=F32
    ).astype(out)


VMEM_LIMIT = 58 * 2**20
NT=(((1,),(1,)),((),()))
NN=(((1,),(0,)),((),()))
TN=(((0,),(0,)),((),()))

def mm(a,b,dims):
    return lax.dot_general(a,b,dims,preferred_element_type=F32)

def params(n):
    return pltpu.CompilerParams(dimension_semantics=("arbitrary",)*n, vmem_limit_bytes=VMEM_LIMIT)

def once(shape, index):
    return pl.BlockSpec(shape, index, pipeline_mode=pl.Buffered(1))

def rows_once(n, wide, first):
    return pl.BlockSpec((pl.Element(n), pl.Element(wide)), lambda i: (first, 0), pipeline_mode=pl.Buffered(1))

def place_matrix(fe, first, n):
    col=lax.broadcasted_iota(jnp.int32,(E,n),1)+first; row=lax.broadcasted_iota(jnp.int32,(E,n),0)*fe
    return jnp.where((col>=row)&(col<row+fe),1.0,0.0).astype(BF)

def units_kernel(fe, first, x_ref, wg_ref, wu_ref, b_ref, w_ref, out_ref, pair_ref):
    x=x_ref[...]; n=wg_ref.shape[0]
    pre=mm(x,wg_ref[...],NT); lift=mm(x,wu_ref[...],NT); back=b_ref[...].astype(F32)
    w=w_ref[...]; hi=w.astype(BF); lo=(w-hi.astype(F32)).astype(BF)
    place=place_matrix(fe,first,n)
    spread=mm(jnp.concatenate([hi,lo],axis=1),jnp.concatenate([place,place],axis=0),NN)
    if first+n>E*fe:
        spread=jnp.where(lax.broadcasted_iota(jnp.int32,spread.shape,1)>=E*fe-first,1.0,spread)
    s=0.5+0.5*jnp.tanh(0.5*pre)
    silu=pre*s
    act=silu*lift
    pair_ref[...]=mm((act*back).astype(BF),place,NT)
    back=back*spread
    out_ref[0]=(back*lift*(s+silu*(1.0-s))).astype(BF)
    out_ref[1]=(back*silu).astype(BF)
    out_ref[2]=(act*spread).astype(BF)

def units(x,packed,back,weight,fe,first,bt):
    T,D=x.shape; n=back.shape[1]; r=weight.shape[1]
    ins=[pl.BlockSpec((bt,D),lambda i:(i,0))]+[once((n,D),lambda i,k=k:(k,0)) for k in range(2)]
    ins+=[pl.BlockSpec((bt,n),lambda i:(i,0)),pl.BlockSpec((bt,r),lambda i:(i,0))]
    outs=[jax.ShapeDtypeStruct((3,T,n),BF),jax.ShapeDtypeStruct((T,r),F32)]
    return pl.pallas_call(functools.partial(units_kernel,fe,first),grid=(T//bt,),in_specs=ins,
        out_specs=[pl.BlockSpec((3,bt,n),lambda i:(0,i,0)),pl.BlockSpec((bt,r),lambda i:(i,0))],out_shape=outs,
        compiler_params=params(1),
        cost_estimate=pl.CostEstimate(flops=4*T*D*n,bytes_accessed=2*(T*D+2*n*D+4*T*n),transcendentals=T*n))(x,packed,packed,back,weight)

def lift_kernel(g_ref,w_ref,o_ref):
    o_ref[...]=mm(g_ref[...],w_ref[...],NT).astype(BF)

def lift_back(g,packed,at,n,bt):
    T,D=g.shape
    return pl.pallas_call(lift_kernel,grid=(T//bt,),
        in_specs=[pl.BlockSpec((bt,D),lambda i:(i,0)),rows_once(n,D,at)],
        out_specs=pl.BlockSpec((bt,n),lambda i:(i,0)),out_shape=jax.ShapeDtypeStruct((T,n),BF),compiler_params=params(1),
        cost_estimate=pl.CostEstimate(flops=2*T*D*n,bytes_accessed=2*(T*D+n*D+T*n),transcendentals=0))(g,packed)

def back_kernel(pairs, added, beside, *refs):
    out=refs[-1]
    acc=None
    if added: acc=refs[0][...].astype(F32)
    rs=refs[added:]
    for k in range(pairs):
        a=rs[2*k]; b=rs[2*k+1]
        a=a[0] if len(a.shape)==3 else a[...]
        p=mm(a,b[...],NN)
        acc=p if acc is None else acc+p
    if beside:
        wide=acc.shape[1]
        out[:,:wide]=acc.astype(out.dtype)
        more=sum(r[...] for r in refs[-1-beside:-1])
        gap=jnp.zeros((acc.shape[0],out.shape[1]-wide-more.shape[1]),F32)
        out[:,wide:]=jnp.concatenate([more,gap],axis=1).astype(out.dtype)
    else:
        out[...]=acc.astype(out.dtype)

def core_kernel(pairs, core_ref, *refs):
    out=refs[-1]
    chips,_,w=out.shape
    for z in range(chips):
        at=pl.ds(pl.multiple_of((2*z+core_ref[0])*w,w),w)
        acc=None
        for k in range(pairs):
            a=refs[2*k]; b=refs[2*k+1]
            p=mm(a[0] if len(a.shape)==3 else a[...],b[:,at],NN)
            acc=p if acc is None else acc+p
        out[z]=acc.astype(BF)

def back(terms, added, out_dtype, bt, beside=(), core=None, chips=0):
    T=terms[0][0].shape[-2]; D=terms[0][2].shape[1]
    ins=[];args=[];fl=0;by=0
    if core is not None:
        ins.append(pl.BlockSpec(memory_space=pltpu.SMEM)); args.append(core)
    if added is not None:
        ins.append(pl.BlockSpec((bt,D),lambda i:(i,0))); args.append(added)
    for st,k,packed,n,at in terms:
        if st.ndim==3: ins.append(pl.BlockSpec((1,bt,n),lambda i,k=k:(k,i,0)))
        else: ins.append(pl.BlockSpec((bt,n),lambda i:(i,0)))
        ins.append(rows_once(n,D,at))
        args+= [st,packed]; fl+=2*T*D*n; by+=2*(T*n+n*D)
    for more in beside:
        ins.append(pl.BlockSpec((bt,more.shape[1]),lambda i:(i,0))); args.append(more)
    body=functools.partial(back_kernel,len(terms),0 if added is None else 1,len(beside))
    if beside:
        shape=(T,D+128); ospec=pl.BlockSpec((bt,D+128),lambda i:(i,0))
    elif core is not None:
        w=D//(2*chips); fl//=2
        shape=(chips,T,w); ospec=pl.BlockSpec((chips,bt,w),lambda i:(0,i,0))
        body=functools.partial(core_kernel,len(terms))
    else:
        shape=(T,D); ospec=pl.BlockSpec((bt,D),lambda i:(i,0))
    return pl.pallas_call(body,grid=(T//bt,),in_specs=ins,out_specs=ospec,out_shape=jax.ShapeDtypeStruct(shape,out_dtype),
        compiler_params=params(1),cost_estimate=pl.CostEstimate(flops=fl,bytes_accessed=by+4*T*D,transcendentals=0))(*args)

def outer_kernel(s_ref,x_ref,*refs):
    refs[-1][...]=mm(s_ref[0],x_ref[...],TN).astype(BF)

def outer(stack,first,count,x,total,at,into=None,bc=512):
    T,D=x.shape; n=stack.shape[2]
    ins=[pl.BlockSpec((1,T,n),lambda k,j:(first+k,0,0)),pl.BlockSpec((T,bc),lambda k,j:(0,j))]
    args=[stack,x]; al={}
    if into is not None:
        ins.append(pl.BlockSpec(memory_space=pl.ANY)); args.append(into); al={2:0}
    return pl.pallas_call(outer_kernel,grid=(count,D//bc),in_specs=ins,
        out_specs=pl.BlockSpec((n,bc),lambda k,j:(at+k,j)),out_shape=jax.ShapeDtypeStruct((total,D),BF),
        input_output_aliases=al,compiler_params=params(2),
        cost_estimate=pl.CostEstimate(flops=2*count*T*D*n,bytes_accessed=2*count*(T*n+n*D+T*D),transcendentals=0))(*args)


def place_columns_kernel(chips, norm, at_ref, *refs):
    pieces=refs[:2*chips]
    refs=refs[2*chips:]
    if norm:
        gain_ref, w_ref = refs[:2]
        out_ref, round_ref, r_ref, proj_ref = refs[-4:]
    else:
        (out_ref,) = refs
    w=pieces[0].shape[1]
    for k in range(2*chips):
        out_ref[:,pl.ds(pl.multiple_of(at_ref[k]*w,w),w)]=pieces[k][...]
    if norm:
        v=out_ref[...].astype(F32)
        r=lax.rsqrt(jnp.mean(v*v,axis=-1,keepdims=True)+EPSILON)
        round_ref[...]=(v*r*gain_ref[...]).astype(BF)
        r_ref[...]=r
        proj_ref[...]=mm(round_ref[...],w_ref[...],NT)

def place_columns(pieces, at, gain=None, packed=None, count=0, rows=None, first=0, into=(), bt=256):
    T,w=pieces[0].shape; n=len(pieces)
    total_rows=rows or T
    start=first//bt
    ins=[pl.BlockSpec(memory_space=pltpu.SMEM)]+[pl.BlockSpec((bt,w),lambda i:(i,0))]*n
    args=[at]+list(pieces)
    wides=[(n*w,BF)]
    if gain is not None:
        ins+=[pl.BlockSpec((1,n*w),lambda i:(0,0)),rows_once(count,n*w,0)]; args+=[gain[None],packed]
        wides+=[(n*w,BF),(1,F32),(count,F32)]
    aliases={len(args)+k:k for k in range(len(into))}
    ins+=[pl.BlockSpec(memory_space=pl.ANY)]*len(into); args+=list(into)
    return pl.pallas_call(functools.partial(place_columns_kernel,n//2,gain is not None),grid=(T//bt,),
        in_specs=ins,out_specs=[pl.BlockSpec((bt,m),lambda i:(i+start,0)) for m,_ in wides],
        out_shape=[jax.ShapeDtypeStruct((total_rows,m),d) for m,d in wides],
        input_output_aliases=aliases,compiler_params=params(1),
        cost_estimate=pl.CostEstimate(flops=(6+2*count)*T*n*w,bytes_accessed=6*T*n*w,transcendentals=T))(*args)

def place_rows_kernel(n, times, at_ref, *refs):
    pieces=refs[:n]; refs=refs[n:]
    if times: w_ref,out_ref,made_ref,sem=refs
    else: out_ref,sem=refs
    rows=pieces[0].shape[0]
    to=[pl.ds(pl.multiple_of(at_ref[k]*rows,rows),rows) for k in range(n)]
    copies=[pltpu.make_async_copy(pieces[k],out_ref.at[to[k]],sem.at[k]) for k in range(n)]
    for c in copies: c.start()
    if times:
        for k in range(n): made_ref[to[k]]=mm(pieces[k][...],w_ref[...],NT).astype(BF)
    for c in copies: c.wait()

def place_rows(pieces, at, weight=None):
    rows,w=pieces[0].shape; n=len(pieces)
    vmem=pl.BlockSpec(memory_space=pltpu.VMEM)
    outs=[jax.ShapeDtypeStruct((n*rows,w),BF)]; specs=[pl.BlockSpec(memory_space=pl.ANY)]; more=[]
    if weight is not None:
        outs.append(jax.ShapeDtypeStruct((n*rows,weight.shape[0]),BF)); specs.append(vmem); more=[weight]
    return pl.pallas_call(functools.partial(place_rows_kernel,n,bool(more)),
        in_specs=[pl.BlockSpec(memory_space=pltpu.SMEM)]+[vmem]*(n+len(more)),
        out_specs=specs,out_shape=outs,
        scratch_shapes=[pltpu.SemaphoreType.DMA((n,))],compiler_params=pltpu.CompilerParams(vmem_limit_bytes=VMEM_LIMIT),
        cost_estimate=pl.CostEstimate(flops=2*n*rows*w*(weight.shape[0] if more else 0),bytes_accessed=4*n*rows*w,transcendentals=0))(at,*pieces,*more)

def norm_rows_kernel(n, at_ref, col_ref, gain_ref, wr_ref, kept_ref, *refs):
    pieces=refs[:n]; round_ref,cols_ref,gating_ref,weight_ref,made,cut,sem,sem2=refs[n:]
    rows=pieces[0].shape[0]; w=cut.shape[2]
    copies=[]
    for k in range(n):
        v=pieces[k][...].astype(F32)
        r=lax.rsqrt(jnp.mean(v*v,axis=-1,keepdims=True)+EPSILON)
        made[k]=(v*r*gain_ref[...]).astype(BF)
        cut[k]=pieces[k][:,pl.ds(pl.multiple_of(col_ref[0]*w,w),w)]
        to=pl.ds(pl.multiple_of(at_ref[k]*rows,rows),rows)
        copies.append(pltpu.make_async_copy(made.at[k],round_ref.at[to],sem.at[k]))
        copies.append(pltpu.make_async_copy(cut.at[k],cols_ref.at[to],sem2.at[k]))
        copies[-2].start(); copies[-1].start()
        logits=mm(made[k],wr_ref[...],NT)
        e=jnp.exp(logits-jnp.max(logits,axis=-1,keepdims=True))
        gating=e/jnp.sum(e,axis=-1,keepdims=True)
        gating_ref[to]=gating
        weight_ref[to]=gating*kept_ref[to]
    for c in copies: c.wait()

def norm_rows(pieces, at, column, w, gain, router, kept):
    rows,wide=pieces[0].shape; n=len(pieces)
    vmem=pl.BlockSpec(memory_space=pltpu.VMEM)
    return pl.pallas_call(functools.partial(norm_rows_kernel,n),
        in_specs=[pl.BlockSpec(memory_space=pltpu.SMEM)]*2+[vmem]*(n+3),
        out_specs=[pl.BlockSpec(memory_space=pl.ANY)]*2+[vmem]*2,
        out_shape=[jax.ShapeDtypeStruct((n*rows,wide),BF),jax.ShapeDtypeStruct((n*rows,w),BF)]+[jax.ShapeDtypeStruct((n*rows,E),F32)]*2,
        scratch_shapes=[pltpu.VMEM((n,rows,wide),BF),pltpu.VMEM((n,rows,w),BF),pltpu.SemaphoreType.DMA((n,)),pltpu.SemaphoreType.DMA((n,))],
        compiler_params=pltpu.CompilerParams(vmem_limit_bytes=VMEM_LIMIT),
        cost_estimate=pl.CostEstimate(flops=6*n*rows*wide,bytes_accessed=4*n*rows*wide,transcendentals=n*rows))(at,column,gain[None],router,kept,*pieces)

def small_kernel(pairs_ref, up_ref, kr_ref, dot_ref, entry_ref, out_ref):
    bt=out_ref.shape[0]
    out_ref[:,:R]=mm(pairs_ref[...],up_ref[...],NT).astype(BF)
    h=DR//2
    kr=kr_ref[...]
    gap=jnp.zeros((bt,DR-1-entry_ref.shape[1]),F32)
    out_ref[:,R:]=jnp.concatenate(
        [kr[:,:h]+kr[:,h:DR],kr[:,DR:DR+h]+kr[:,DR+h:],dot_ref[...],entry_ref[...],gap],axis=1).astype(BF)

def small_terms(pairs, up, kr, dots, entries, bt=512):
    T=pairs.shape[0]
    def rows(a): return pl.BlockSpec((bt,a.shape[1]),lambda i:(i,0))
    return pl.pallas_call(small_kernel,grid=(T//bt,),
        in_specs=[rows(pairs),pl.BlockSpec(up.shape,lambda i:(0,0)),rows(kr),rows(dots),rows(entries)],
        out_specs=pl.BlockSpec((bt,R+DN),lambda i:(i,0)),out_shape=jax.ShapeDtypeStruct((T,R+DN),BF),
        compiler_params=params(1),
        cost_estimate=pl.CostEstimate(flops=2*T*R*pairs.shape[1],bytes_accessed=8*T*R,transcendentals=0))(pairs,up,kr,dots,entries)

def latent_back_kernel(small_ref, proj_ref, gain_ref, cos_ref, sin_ref, delta_ref, dots_ref, gain_delta_ref):
    i=pl.program_id(0)
    at=proj_ref.shape[1]-R-DN
    dl=small_ref[:,:R].astype(F32)
    vl=proj_ref[:,at:at+R]
    rl=lax.rsqrt(jnp.mean(vl*vl,axis=-1,keepdims=True)+EPSILON)
    gain=gain_ref[...]
    part=jnp.sum(dl*vl*rl,axis=0,keepdims=True)
    @pl.when(i==0)
    def _(): gain_delta_ref[...]=part
    @pl.when(i>0)
    def _(): gain_delta_ref[...]+=part
    gd=gain*dl
    head=rl*gd-vl*(rl*rl*rl)*jnp.mean(vl*gd,axis=-1,keepdims=True)
    beyond=small_ref[:,R:]
    row=lax.broadcasted_iota(jnp.int32,(DN,DN),0); col=lax.broadcasted_iota(jnp.int32,(DN,DN),1)
    h=DR//2
    put=jnp.where(((row<h)&(col==row))|((row>=h)&(row<DR)&(col==row+h)),1.0,0.0).astype(BF)
    spread=mm(beyond,put,NN)
    tail=spread*cos_ref[...]-pltpu.roll(spread,DR,1)*sin_ref[...]
    delta_ref[:,:R]=head.astype(BF)
    delta_ref[:,R:]=tail.astype(BF)
    own=jnp.sum(head*vl,axis=-1,keepdims=True)+jnp.sum(tail*proj_ref[:,at+R:],axis=-1,keepdims=True)
    lane=lax.broadcasted_iota(jnp.int32,beyond.shape,1)
    dots_ref[...]=own+jnp.sum(jnp.where(lane==DR,beyond.astype(F32),0.0),axis=-1,keepdims=True)

def latent_back(small, proj, gain, cosine, sine, bt=512):
    T,wide=small.shape; turns=LEN//bt
    return pl.pallas_call(latent_back_kernel,grid=(T//bt,),
        in_specs=[pl.BlockSpec((bt,wide),lambda i:(i,0)),pl.BlockSpec((bt,proj.shape[1]),lambda i:(i,0)),
                  pl.BlockSpec((1,R),lambda i:(0,0)),pl.BlockSpec((bt,DN),lambda i:(i%turns,0)),pl.BlockSpec((bt,DN),lambda i:(i%turns,0))],
        out_specs=[pl.BlockSpec((bt,R+DN),lambda i:(i,0)),pl.BlockSpec((bt,1),lambda i:(i,0)),pl.BlockSpec((1,R),lambda i:(0,0))],
        out_shape=[jax.ShapeDtypeStruct((T,R+DN),BF),jax.ShapeDtypeStruct((T,1),F32),jax.ShapeDtypeStruct((1,R),F32)],
        compiler_params=params(1),
        cost_estimate=pl.CostEstimate(flops=30*T*wide,bytes_accessed=8*T*wide,transcendentals=T))(small,proj,gain,cosine,sine)

def last_pack_kernel(delta_ref, x_ref, w_ref, small_ref, g_ref, latent_ref, out_ref):
    n=delta_ref.shape[1]
    d=mm(delta_ref[...],x_ref[...],TN)
    out_ref[:n]=d.astype(BF)
    sums=jnp.sum(w_ref[...].astype(F32)*d,axis=0,keepdims=True)
    row=lax.broadcasted_iota(jnp.int32,(32,DN),0); col=lax.broadcasted_iota(jnp.int32,(32,DN),1)
    at=DR+1
    pick=((row<E)&(col==row+at+2))|((row==E)&(col==at))|((row==E+1)&(col==at+1))
    v=mm(jnp.where(pick,1.0,0.0).astype(BF),small_ref[...],NT)
    line=lax.broadcasted_iota(jnp.int32,v.shape,0)
    v=jnp.where(line==E+1,(v+sums)/g_ref[...],v)
    out_ref[n:]=jnp.where(line==E+2,latent_ref[...],v).astype(BF)

def last_pack(delta, x, packed, first, small, gain, latent_row, bc=512):
    T,D=x.shape; n=delta.shape[1]
    def cols(a): return pl.BlockSpec((a.shape[0],bc),lambda j:(0,j))
    return pl.pallas_call(last_pack_kernel,grid=(D//bc,),
        in_specs=[pl.BlockSpec((T,n),lambda j:(0,0)),cols(x),
                  pl.BlockSpec((pl.Element(n),pl.Element(bc)),lambda j:(first,j*bc)),pl.BlockSpec((bc,DN),lambda j:(j,R//DN)),cols(gain),cols(latent_row)],
        out_specs=pl.BlockSpec((n+32,bc),lambda j:(0,j)),out_shape=jax.ShapeDtypeStruct((n+32,D),BF),
        compiler_params=params(1),
        cost_estimate=pl.CostEstimate(flops=2*T*D*n,bytes_accessed=2*(T*D+2*n*D+T*n),transcendentals=0))(delta,x,packed,small,gain,latent_row)


def turn(x, cosine, sine):
    return x*cosine+pltpu.roll(x,64,1)*sine

def slot_mask(shape, head):
    lane=lax.broadcasted_iota(jnp.int32,shape,1)
    low=head*(DR//2)
    inside=((lane>=low)&(lane<low+DR//2))|((lane>=low+DR)&(lane<low+DR+DR//2))
    return inside

def causal_scores(q, k, first):
    s=mm(q,k,NT)*SCALE
    row=lax.broadcasted_iota(jnp.int32,s.shape,0)+first
    col=lax.broadcasted_iota(jnp.int32,s.shape,1)
    return jnp.where(col<=row,s,-1e30)

def attend_kernel(heads, proj_ref, up_ref, gain_ref, cos_ref, sin_ref, *refs):
    q_ref, kr_ref, kv_ref, latent_ref, mixed_ref, lse_ref = refs[-6:]
    content=heads*DN
    at=content+DN
    q_ref[:,:content]=proj_ref[:,:content].astype(BF)
    cosine,sine=cos_ref[...],sin_ref[...]
    q_ref[:,content:]=turn(proj_ref[:,content:at],cosine,sine).astype(BF)
    vl=proj_ref[:,at:at+R]
    latent_ref[...]=(vl*lax.rsqrt(jnp.mean(vl*vl,axis=-1,keepdims=True)+EPSILON)*gain_ref[...]).astype(BF)
    kr_ref[...]=turn(proj_ref[:,at+R:],cosine,sine).astype(BF)
    kv_ref[...]=mm(latent_ref[...],up_ref[...],NN).astype(BF)
    kr=kr_ref[...]
    for h in range(heads):
        kc=kv_ref[:,h*(DN+DV):h*(DN+DV)+DN]
        v=kv_ref[:,h*(DN+DV)+DN:(h+1)*(DN+DV)]
        k=jnp.concatenate([kc,jnp.where(slot_mask(kr.shape,h),kr,jnp.zeros_like(kr))],axis=1)
        for i in range(LEN//BLOCK):
            a,b=i*BLOCK,(i+1)*BLOCK
            q=jnp.concatenate([q_ref[a:b,h*DN:(h+1)*DN],q_ref[a:b,content:]],axis=1)
            s=causal_scores(q,k[:b],a)
            m=jnp.max(s,axis=-1,keepdims=True)
            e=jnp.exp(s-m)
            t=jnp.sum(e,axis=-1,keepdims=True)
            p=(e*(1.0/t)).astype(BF)
            mixed_ref[a:b,h*DV:(h+1)*DV]=mm(p,v[:b],NN).astype(BF)
            lse_ref[a:b,h:h+1]=m+jnp.log(t)

def attend(proj, up, gain, cosine, sine, heads, sequence, into=()):
    T=proj.shape[0]; wide=proj.shape[1]
    def rows(n): return pl.BlockSpec((LEN,n),lambda i:(sequence,0))
    def whole(a): return pl.BlockSpec(a.shape,lambda i:(0,0))
    qn=heads*DN+DN
    outs=[(qn,BF),(DN,BF),(heads*(DN+DV),BF),(R,BF),(heads*DV,BF),(heads,F32)]
    args=[proj,up,gain,cosine,sine]
    return pl.pallas_call(functools.partial(attend_kernel,heads),grid=(1,),
        in_specs=[rows(wide)]+[whole(a) for a in args[1:]]+[pl.BlockSpec(memory_space=pl.ANY)]*len(into),
        out_specs=[rows(n) for n,_ in outs],out_shape=[jax.ShapeDtypeStruct((T,n),d) for n,d in outs],
        input_output_aliases={len(args)+k:k for k in range(len(into))},compiler_params=params(1),
        cost_estimate=pl.CostEstimate(flops=LEN*LEN*heads*512,bytes_accessed=LEN*8000,transcendentals=LEN*LEN*heads//2))(*args,*into)

def attend_back_kernel(heads, q_ref, kr_ref, kv_ref, mixed_ref, lse_ref, do_ref, cos_ref, sin_ref, dq_ref, dkv_ref, dkr_ref, dot_ref, dk_acc, dv_acc):
    content=heads*DN
    kr=kr_ref[...]
    for h in range(heads):
        kc=kv_ref[:,h*(DN+DV):h*(DN+DV)+DN]
        v=kv_ref[:,h*(DN+DV)+DN:(h+1)*(DN+DV)]
        mask=slot_mask(kr.shape,h)
        k=jnp.concatenate([kc,jnp.where(mask,kr,jnp.zeros_like(kr))],axis=1)
        for i in reversed(range(LEN//BLOCK)):
            a,b=i*BLOCK,(i+1)*BLOCK
            q=jnp.concatenate([q_ref[a:b,h*DN:(h+1)*DN],q_ref[a:b,content:]],axis=1)
            do=do_ref[a:b,h*DV:(h+1)*DV]
            p=jnp.exp(causal_scores(q,k[:b],a)-lse_ref[a:b,h:h+1])
            dp=mm(do,v[:b],NT)
            along=jnp.sum(do.astype(F32)*mixed_ref[a:b,h*DV:(h+1)*DV].astype(F32),axis=-1,keepdims=True)
            ds=(p*(dp-along)).astype(BF)
            pv=mm(p.astype(BF),do,TN)
            pk=mm(ds,q,TN)
            if i==LEN//BLOCK-1:
                dv_acc[...]=pv; dk_acc[...]=pk
            else:
                dv_acc[:b]+=pv; dk_acc[:b]+=pk
            dq=mm(ds,k[:b],NN)*SCALE
            d=jnp.sum(dq*q.astype(F32),axis=-1,keepdims=True)
            if h==0: dot_ref[a:b]=d
            else: dot_ref[a:b]+=d
            dq_ref[a:b,h*DN:(h+1)*DN]=dq[:,:DN].astype(BF)
            turned=turn(dq[:,DN:],cos_ref[a:b],-sin_ref[a:b])
            turned=jnp.where(mask[:b-a],turned,0.0).astype(BF)
            if h==0: dq_ref[a:b,content:]=turned
            else: dq_ref[a:b,content:]+=turned
        dkv_ref[:,h*(DN+DV):h*(DN+DV)+DN]=(dk_acc[:,:DN]*SCALE).astype(BF)
        dkv_ref[:,h*(DN+DV)+DN:(h+1)*(DN+DV)]=dv_acc[...].astype(BF)
        part=jnp.where(mask,dk_acc[:,DN:]*SCALE,0.0)
        if h==0: dkr_ref[...]=part
        else: dkr_ref[...]+=part

def attend_back(q,kr,kv,mixed,lse,do,cosine,sine,heads):
    T=q.shape[0]
    def rows(n): return pl.BlockSpec((LEN,n),lambda i:(i,0))
    def whole(a): return pl.BlockSpec(a.shape,lambda i:(0,0))
    args=(q,kr,kv,mixed,lse,do)
    outs=[(q.shape[1],BF),(kv.shape[1],BF),(DN,F32),(1,F32)]
    return pl.pallas_call(functools.partial(attend_back_kernel,heads),grid=(T//LEN,),
        in_specs=[rows(a.shape[1]) for a in args]+[whole(cosine),whole(sine)],
        out_specs=[rows(n) for n,_ in outs],out_shape=[jax.ShapeDtypeStruct((T,n),d) for n,d in outs],
        scratch_shapes=[pltpu.VMEM((LEN,2*DN),F32),pltpu.VMEM((LEN,DV),F32)],
        compiler_params=params(1),
        cost_estimate=pl.CostEstimate(flops=T*LEN*heads*1400,bytes_accessed=T*6000,transcendentals=T*LEN*heads//2))(*args,cosine,sine)

def tables():
    position=np.arange(LEN,dtype=np.float32)
    spread=(10000.0**(-np.arange(DR//2,dtype=np.float32)/(DR//2))).astype(np.float32)
    phase=(position[:,None]*spread[None,:]).astype(np.float32)
    c,s=np.cos(phase),np.sin(phase)
    return np.concatenate([c]*4,1).astype(np.float32),np.concatenate([-s,-s,s,s],1).astype(np.float32)


class Line:
    def __init__(self):
        self.n = lax.axis_size("tensor")
        self.chips = self.n // 2
        index = lax.axis_index("tensor")
        self.index = index
        self.z = index // 2
        self.c = index % 2

    def swap(self, a):
        return lax.ppermute(a, "tensor", [(i, i ^ 1) for i in range(self.n)])

    def shift(self, a, step, sources):
        pairs = [
            (2 * s + c, 2 * (s + step) + c)
            for s in sources
            if 0 <= s + step < self.chips
            for c in (0, 1)
        ]
        return lax.ppermute(a, "tensor", pairs)

    def pieces(self, own, order):
        n = self.chips
        out, at = [], []
        for k, piece in enumerate(own):
            chip = (self.z - k + n) % n
            out += [piece, self.swap(piece)]
            at += [order(chip, self.c), order(chip, 1 - self.c)]
        return out, jnp.stack(at).astype(jnp.int32)

    def row_pieces(self, own):
        return self.pieces(own, lambda chip, core: core * self.chips + chip)

    def column_pieces(self, own):
        return self.pieces(own, lambda chip, core: chip * 2 + core)

    def half(self, p, core):
        count = p.shape[0] // 2
        return lax.dynamic_slice_in_dim(p, core * count, count, 0)

    def row_scatter(self, p, first, arrived):
        ch = arrived.shape[0] // self.chips
        return Scatter(self, lambda j: total(
            lax.dynamic_slice_in_dim(p, first + j * ch, ch, 0), lax.dynamic_slice_in_dim(arrived, j * ch, ch, 0)
        ))

    def column_scatter(self, mine, arrived):
        return Scatter(self, lambda j: total(
            lax.dynamic_index_in_dim(mine, j, 0, False), lax.dynamic_index_in_dim(arrived, j, 0, False)
        ))

    def row_start(self, rows):
        ch = rows // self.n
        return (self.c * self.chips + self.z) * ch, ch


def total(mine, arrived):
    return (mine.astype(F32) + arrived.astype(F32)).astype(BF)


class Gather:
    def __init__(self, line, block):
        self.line, self.left, self.right = line, [block], [block]

    def start(self):
        n, k = self.line.chips, len(self.left)
        return (
            self.line.shift(self.left[-1], 1, range(k - 1, n)),
            self.line.shift(self.right[-1], -1, range(0, n - k + 1)),
        )

    def take(self, arrived):
        self.left.append(arrived[0])
        self.right.append(arrived[1])

    def result(self):
        n, z = self.line.chips, self.line.z
        return self.left[:1] + [jnp.where(z >= k, self.left[k], self.right[n - k]) for k in range(1, n)]


class Scatter:
    def __init__(self, line, block):
        self.line, self.block, self.step, self.left, self.right = line, block, 0, None, None

    def start(self):
        self.step += 1
        n, s, z = self.line.chips, self.step, self.line.z
        up = self.block(jnp.clip(n - s + z, 0, n - 1))
        down = self.block(jnp.clip(z - (n - s), 0, n - 1))
        if self.left is not None:
            up, down = total(up, self.left), total(down, self.right)
        return self.line.shift(up, 1, range(0, s)), self.line.shift(down, -1, range(n - s, n))

    def take(self, arrived):
        self.left, self.right = arrived

    def result(self):
        return self.block(self.line.z).astype(F32) + self.left.astype(F32) + self.right.astype(F32)


def beside(moves, job=None):
    arrived, done = lax.optimization_barrier(([m.start() for m in moves], job() if job else None))
    for move, a in zip(moves, arrived):
        move.take(a)
    return done


def steps(move, count, jobs=()):
    made = []
    for k in range(count):
        made.append(beside([move], jobs[k] if k < len(jobs) else None))
    return made


def gather_rows(packed):
    return lax.all_gather(packed, "dp", axis=1, tiled=True)


def scatter_rows(packed):
    return lax.psum_scatter(packed, "dp", scatter_dimension=1, tiled=True)


def split_rows(packed, counts):
    out, at = [], 0
    for count in counts:
        out.append(packed[at : at + count])
        at += count
    return out


def ranks(mask):
    number = mask.shape[0]
    block = 128
    pieces = mask.reshape(number // block, block, E).astype(BF)
    lower = jnp.tril(jnp.ones((block, block), BF), -1)
    inside = jnp.einsum("ij,bje->bie", lower, pieces, preferred_element_type=F32)
    totals = jnp.sum(pieces.astype(F32), axis=1).astype(BF)
    ahead = jnp.tril(jnp.ones((number // block, number // block), BF), -1)
    before = dot(ahead, totals, 1, 0)
    return (inside + before[:, None, :]).reshape(number, E)


def per_device(
    layer_input, cotangent, first_gain, query_weight, latent_down, latent_gain, latent_up,
    output_weight, second_gain, router_weight, expert_gate, expert_up, expert_down,
    shared_gate, shared_up, shared_down, routes,
):
    line = Line()
    n_dp = lax.axis_size("dp")
    wide = D // n_dp
    number = layer_input.shape[0]
    heads_here = output_weight.shape[0] // DV
    fe = expert_down.shape[1]
    my_columns = layer_input.shape[1]
    column_start = line.index * my_columns
    row_start, row_count = line.row_start(number)

    half = DR // 2
    spare_heads = 2 - heads_here
    up_rows = latent_up.size // wide
    by_head = query_weight.T.reshape(heads_here, DN + DR, wide)
    blank = jnp.zeros((spare_heads * half, wide), BF)
    gains = jnp.zeros((16, wide), BF)
    gains = gains.at[0].set(first_gain).at[1].set(second_gain)
    gains = gains.at[2, : latent_gain.shape[0]].set(latent_gain)
    down = latent_down.T
    queries_wide = heads_here * DN + DN
    latent_wide = R + DN
    attend_pack = [
        by_head[:, :DN].reshape(heads_here * DN, wide),
        by_head[:, DN : DN + half].reshape(heads_here * half, wide), blank,
        by_head[:, DN + half :].reshape(heads_here * half, wide), blank,
        down[: R + half], down[R : R + half], down[R + half :], down[R + half :],
        latent_up.reshape(up_rows, wide), gains, router_weight.T, output_weight,
    ]
    attend_packed = gather_rows(jnp.concatenate([m for m in attend_pack if m.shape[0]], axis=0))
    wproj, wup, gains, wr, wo = split_rows(
        attend_packed, [queries_wide + latent_wide, up_rows, 16, E, output_weight.shape[0]]
    )
    wup = wup.reshape(up_rows, n_dp, wide).transpose(1, 0, 2).reshape(R, -1)
    first_g = gains[0].astype(F32)
    second_g = gains[1].astype(F32)
    latent_g = gains[2].reshape(n_dp, wide)[:, : R // n_dp].reshape(R).astype(F32)
    cosine, sine = (jnp.asarray(table) for table in tables())

    n_units = E * fe + shared_down.shape[0]
    n0 = n_units // 2 // 256 * 256
    n1 = n_units - n0
    last_step = line.chips - 1
    gate = expert_gate.transpose(0, 2, 1).reshape(E * fe, wide)
    up = expert_up.transpose(0, 2, 1).reshape(E * fe, wide)
    move = Gather(line, layer_input[:LEN])
    downs, early, late = steps(move, 3, (
        lambda: jnp.concatenate([expert_down.reshape(E * fe, wide), shared_down], axis=0),
        lambda: jnp.concatenate([gate[:n0], up[:n0]], axis=0),
        lambda: jnp.concatenate([gate[n0:], shared_gate.T, up[n0:], shared_up.T], axis=0),
    ))
    steps(move, last_step - 3)
    downs, early, late = gather_rows(downs), gather_rows(early), gather_rows(late)

    tile = 256
    core = line.c.reshape(1).astype(jnp.int32)
    placed, attended = (), ()

    def place(move, sequence):
        pieces, at = line.column_pieces(move.result())
        return place_columns(
            pieces, at, first_g, attend_packed, queries_wide + latent_wide, number, sequence * LEN, placed
        )

    def attention(sequence):
        return attend(placed[3], wup, latent_g[None], cosine, sine, heads_here, sequence, attended)

    for sequence in range(1, number // LEN):
        ahead, after = move, layer_input[sequence * LEN : (sequence + 1) * LEN]
        ahead.left[-1], ahead.right[-1], after = lax.optimization_barrier((ahead.left[-1], ahead.right[-1], after))
        move = Gather(line, after)
        beside([move])
        placed = beside([move], lambda: place(ahead, sequence - 1))
        steps(move, last_step - 3)
        attended = beside([move], lambda: attention(sequence - 1))
    move.left[-1], move.right[-1], cotangent = lax.optimization_barrier((move.left[-1], move.right[-1], cotangent))
    grad_move = Gather(line, cotangent)
    placed = place(move, number // LEN - 1)
    attended = beside([grad_move], lambda: attention(number // LEN - 1))
    rows, first_round, r1, proj = placed
    q, kr, kv, latent, mixed, log_total = attended
    arrived = line.swap(dot(line.half(mixed, 1 - line.c), wo, 1, 0, BF))
    move = line.row_scatter(dot(line.half(mixed, line.c), wo, 1, 0, BF), 0, arrived)
    for _ in range(last_step - 1):
        beside([move, grad_move])
    (grad,) = beside([move], lambda: place_columns(*line.column_pieces(grad_move.result())))
    hidden_rows = (
        lax.dynamic_slice_in_dim(rows, row_start, row_count, 0).astype(F32) + move.result()
    ).astype(BF)
    move = Gather(line, hidden_rows)
    back0, back1 = steps(move, 2, (
        lambda: lift_back(grad, downs, 0, n0, tile),
        lambda: lift_back(grad, downs, n0, n1, tile),
    ))
    steps(move, last_step - 2)
    hidden_pieces, hidden_at = line.row_pieces(move.result())
    named = jnp.any(routes[:, :, None] == jnp.arange(E, dtype=jnp.int32)[None, None, :], axis=1)
    kept = jnp.where(named & (ranks(named) < CAP), 1.0, 0.0)
    second_round, hidden_columns, gating, weight = norm_rows(
        hidden_pieces, hidden_at, line.index.reshape(1).astype(jnp.int32), my_columns, second_g, wr, kept
    )

    stack0, pair0 = units(second_round, early, back0, weight, fe, 0, tile)
    deltas = outer(stack0, 0, 2, second_round, 3 * n0, 0)
    deltas = outer(stack0, 2, 1, grad, 3 * n0, 2, deltas)
    deltas, stack0 = lax.optimization_barrier((deltas, stack0))
    early_sums = scatter_rows(deltas)
    stack1, pair1 = units(second_round, late, back1, weight, fe, n0, tile)
    second_terms = back(
        [(stack0, 0, early, n0, 0), (stack0, 1, early, n0, n0), (stack1, 0, late, n1, 0), (stack1, 1, late, n1, n1)],
        None, BF, tile, (pair0, pair1),
    )

    branch_terms = [(stack0, 2, downs, n0, 0), (stack1, 2, downs, n1, n0)]
    move = line.row_scatter(
        second_terms, line.c * (number // 2), line.swap(line.half(second_terms, 1 - line.c))
    )
    deltas = beside([move], lambda: outer(stack1, 0, 1, second_round, 3 * n1, 0))
    deltas = beside([move], lambda: outer(stack1, 1, 1, second_round, 3 * n1, 1, deltas))
    branch_theirs = beside([move], lambda: back(branch_terms, None, BF, tile, (), 1 - core, line.chips))
    steps(move, last_step - 3)
    summed = move.result()

    def own_rows(a):
        return lax.dynamic_slice_in_dim(a, row_start, row_count, 0)

    gating_rows, kept_rows, x2 = own_rows(gating), own_rows(kept), own_rows(second_round)
    u = summed[:, D : D + E] * kept_rows
    logits_delta = gating_rows * (u - jnp.sum(gating_rows * u, axis=-1, keepdims=True))
    d2 = summed[:, :D] + dot(logits_delta.astype(BF), wr, 1, 0)
    v2 = hidden_rows.astype(F32)
    r2 = lax.rsqrt(jnp.mean(v2 * v2, axis=-1, keepdims=True) + EPSILON)
    vgd = jnp.mean(v2 * second_g * d2, axis=-1, keepdims=True)
    hidden_delta = own_rows(grad).astype(F32) + r2 * second_g * d2 - v2 * (r2**3) * vgd
    move = Gather(line, hidden_delta.astype(BF))
    branch_mine, branch_arrived = beside([move], lambda: (
        back(branch_terms, None, BF, tile, (), core, line.chips), line.swap(branch_theirs)
    ))
    branch_move = line.column_scatter(branch_mine, branch_arrived)
    deltas = beside([move, branch_move], lambda: outer(stack1, 2, 1, grad, 3 * n1, 2, deltas))
    router_delta = dot(x2, logits_delta.astype(BF), 0, 0)
    second_gain_delta = jnp.sum(d2 * v2 * r2, axis=0)
    early_sums, deltas, move.left[-1] = lax.optimization_barrier((early_sums, deltas, move.left[-1]))
    late_sums = scatter_rows(deltas)
    for _ in range(last_step - 2):
        beside([move, branch_move])
    delta_pieces, delta_at = line.row_pieces(move.result())

    def heads_back():
        placed, delta_mixed = place_rows(delta_pieces, delta_at, wo)
        return placed, attend_back(q, kr, kv, mixed, log_total, delta_mixed, cosine, sine, heads_here)

    hidden_delta, heads = beside([branch_move], heads_back)
    layer_output = (hidden_columns.astype(F32) + branch_move.result()).astype(BF)
    delta_queries, delta_pairs, delta_kr, query_dot = heads
    delta_wq = dot(delta_queries, first_round, 0, 0)
    query_gain = jnp.sum(wproj[:queries_wide].astype(F32) * delta_wq, axis=0)
    per_entry = jnp.concatenate([second_gain_delta[:, None], query_gain[:, None], router_delta], axis=1)
    if number > D:
        per_entry = jnp.concatenate([per_entry, jnp.zeros((number - D, E + 2), F32)], axis=0)
    small = small_terms(delta_pairs, wup, delta_kr, query_dot, per_entry)
    first_terms = [(delta_queries, 0, attend_packed, queries_wide, 0)]
    move = line.row_scatter(small, line.c * (number // 2), line.swap(line.half(small, 1 - line.c)))

    beside([move])
    delta_wo = beside([move], lambda: dot(mixed, hidden_delta, 0, 0, BF))

    def attend_deltas():
        delta_wup = dot(latent, delta_pairs, 0, 0, BF)
        return jnp.concatenate(
            [delta_wq.astype(BF),
             delta_wup.reshape(n_dp, up_rows, wide).transpose(1, 0, 2).reshape(up_rows, D), delta_wo], axis=0)

    deltas = beside([move], attend_deltas)
    attend_sums = scatter_rows(deltas).astype(F32)
    steps(move, last_step - 3)
    small, layer_output = lax.optimization_barrier((move.result().astype(BF), layer_output))
    move = Gather(line, small)
    theirs = beside([move], lambda: back(first_terms, None, BF, tile, (), 1 - core, line.chips))
    mine, arrived = beside([move], lambda: (
        back(first_terms, None, BF, tile, (), core, line.chips), line.swap(theirs)
    ))
    steps(move, last_step - 3)
    first_move = line.column_scatter(mine, arrived)
    beside([move, first_move])
    small_pieces, small_at = line.row_pieces(move.result())
    small_pieces, late_sums = lax.optimization_barrier((small_pieces, late_sums))
    wld = wproj[queries_wide:]

    def last():
        (small,) = place_rows(small_pieces, small_at)
        delta_latent, dots, gain_delta = latent_back(small, proj, latent_g[None], cosine, sine)
        latent_row = jnp.pad(gain_delta.reshape(n_dp, R // n_dp), ((0, 0), (0, wide - R // n_dp))).reshape(1, D)
        return delta_latent, dots, last_pack(
            delta_latent, first_round, attend_packed, queries_wide, small, first_g[None], latent_row)

    delta_latent, dots, pack = beside([first_move], last)
    steps(first_move, last_step - 2)
    first_share = first_move.result()
    last_sums = scatter_rows(pack).astype(F32)
    dwld, vectors = last_sums[:latent_wide], last_sums[latent_wide:]
    dwq, dwup, dwo = split_rows(attend_sums, [queries_wide, up_rows, output_weight.shape[0]])
    content = heads_here * DN
    dwq = jnp.concatenate(
        [dwq[:content].reshape(heads_here, DN, wide),
         dwq[content : content + heads_here * half].reshape(heads_here, half, wide),
         dwq[content + DR : content + DR + heads_here * half].reshape(heads_here, half, wide)], axis=1
    ).reshape(heads_here * (DN + DR), wide)
    dwld = jnp.concatenate([dwld[: R + half], dwld[R + DR : R + DR + half]], axis=0)

    first_share = first_share + dot(
        delta_latent, lax.dynamic_slice_in_dim(wld, column_start, my_columns, 1), 1, 0
    )
    vc = layer_input.astype(F32)
    gc = lax.dynamic_slice_in_dim(first_g, column_start, my_columns, 0)
    input_delta = (
        lax.dynamic_slice_in_dim(hidden_delta, column_start, my_columns, 1).astype(F32)
        + r1 * gc * first_share
        - vc * (r1 * r1) * (dots / D)
    )

    def units_delta(k):
        return early_sums[k * n0 : (k + 1) * n0], late_sums[k * n1 : (k + 1) * n1]

    def expert_delta(k):
        first, second = units_delta(k)
        return jnp.concatenate([first, second[: E * fe - n0]], axis=0).astype(F32).reshape(E, fe, wide)

    def shared_delta(k):
        return units_delta(k)[1][E * fe - n0 :].astype(F32)

    return (
        layer_output, input_delta, vectors[E + 1], dwq.T, dwld.T, vectors[E + 2, : R // n_dp],
        dwup.reshape(latent_up.shape), dwo, vectors[E], vectors[:E].T,
        expert_delta(0).transpose(0, 2, 1), expert_delta(1).transpose(0, 2, 1), expert_delta(2),
        shared_delta(0).T, shared_delta(1).T, shared_delta(2),
    )


def solution(mesh):
    in_specs = (
        P("dp", "tensor"), P("dp", "tensor"), P("dp"), P("dp", "tensor"), P("dp", None), P("dp"),
        P("dp", "tensor"), P("tensor", "dp"), P("dp"), P("dp", None), P(None, "dp", "tensor"),
        P(None, "dp", "tensor"), P(None, "tensor", "dp"), P("dp", "tensor"), P("dp", "tensor"),
        P("tensor", "dp"), P("dp", None),
    )
    out_specs = (
        P("dp", "tensor"), P("dp", "tensor"), P("dp"), P("dp", "tensor"), P("dp", None), P("dp"),
        P("dp", "tensor"), P("tensor", "dp"), P("dp"), P("dp", None), P(None, "dp", "tensor"),
        P(None, "dp", "tensor"), P(None, "tensor", "dp"), P("dp", "tensor"), P("dp", "tensor"),
        P("tensor", "dp"),
    )
    return jax.shard_map(
        per_device, mesh=mesh, in_specs=in_specs, out_specs=out_specs, check_vma=False
    )
```

```python
import functools

import jax
import jax.numpy as jnp
import numpy as np
from jax import lax
from jax.experimental import pallas as pl
from jax.experimental.pallas import tpu as pltpu
from jax.sharding import PartitionSpec as P

D = 2048
DN = 128
DR = 64
DV = 128
R = 512
E = 16
LEN = 1024
CAP = 864
EPSILON = 1e-06
SCALE = (DN + DR) ** -0.5
BLOCK = 256
BF = jnp.bfloat16
F32 = jnp.float32


def dot(a, b, ca, cb, out=F32):
    return lax.dot_general(
        a, b, (((ca,), (cb,)), ((), ())), preferred_element_type=F32
    ).astype(out)


VMEM_LIMIT = 58 * 2**20
NT=(((1,),(1,)),((),()))
NN=(((1,),(0,)),((),()))
TN=(((0,),(0,)),((),()))

def mm(a,b,dims):
    return lax.dot_general(a,b,dims,preferred_element_type=F32)

def params(n):
    return pltpu.CompilerParams(dimension_semantics=("arbitrary",)*n, vmem_limit_bytes=VMEM_LIMIT)

def once(shape, index):
    return pl.BlockSpec(shape, index, pipeline_mode=pl.Buffered(1))

def rows_once(n, wide, first):
    return pl.BlockSpec((pl.Element(n), pl.Element(wide)), lambda i: (first, 0), pipeline_mode=pl.Buffered(1))

def place_matrix(fe, first, n):
    col=lax.broadcasted_iota(jnp.int32,(E,n),1)+first; row=lax.broadcasted_iota(jnp.int32,(E,n),0)*fe
    return jnp.where((col>=row)&(col<row+fe),1.0,0.0).astype(BF)

def units_kernel(fe, first, x_ref, wg_ref, wu_ref, b_ref, w_ref, out_ref, pair_ref):
    x=x_ref[...]; n=wg_ref.shape[0]
    pre=mm(x,wg_ref[...],NT); lift=mm(x,wu_ref[...],NT); back=b_ref[...].astype(F32)
    w=w_ref[...]; hi=w.astype(BF); lo=(w-hi.astype(F32)).astype(BF)
    place=place_matrix(fe,first,n)
    spread=mm(jnp.concatenate([hi,lo],axis=1),jnp.concatenate([place,place],axis=0),NN)
    if first+n>E*fe:
        spread=jnp.where(lax.broadcasted_iota(jnp.int32,spread.shape,1)>=E*fe-first,1.0,spread)
    s=0.5+0.5*jnp.tanh(0.5*pre)
    silu=pre*s
    act=silu*lift
    pair_ref[...]=mm((act*back).astype(BF),place,NT)
    back=back*spread
    out_ref[0]=(back*lift*(s+silu*(1.0-s))).astype(BF)
    out_ref[1]=(back*silu).astype(BF)
    out_ref[2]=(act*spread).astype(BF)

def units(x,packed,back,weight,fe,first,bt):
    T,D=x.shape; n=back.shape[1]; r=weight.shape[1]
    ins=[pl.BlockSpec((bt,D),lambda i:(i,0))]+[once((n,D),lambda i,k=k:(k,0)) for k in range(2)]
    ins+=[pl.BlockSpec((bt,n),lambda i:(i,0)),pl.BlockSpec((bt,r),lambda i:(i,0))]
    outs=[jax.ShapeDtypeStruct((3,T,n),BF),jax.ShapeDtypeStruct((T,r),F32)]
    return pl.pallas_call(functools.partial(units_kernel,fe,first),grid=(T//bt,),in_specs=ins,
        out_specs=[pl.BlockSpec((3,bt,n),lambda i:(0,i,0)),pl.BlockSpec((bt,r),lambda i:(i,0))],out_shape=outs,
        compiler_params=params(1),
        cost_estimate=pl.CostEstimate(flops=4*T*D*n,bytes_accessed=2*(T*D+2*n*D+4*T*n),transcendentals=T*n))(x,packed,packed,back,weight)

def lift_kernel(g_ref,w_ref,o_ref):
    o_ref[...]=mm(g_ref[...],w_ref[...],NT).astype(BF)

def lift_back(g,packed,at,n,bt):
    T,D=g.shape
    return pl.pallas_call(lift_kernel,grid=(T//bt,),
        in_specs=[pl.BlockSpec((bt,D),lambda i:(i,0)),rows_once(n,D,at)],
        out_specs=pl.BlockSpec((bt,n),lambda i:(i,0)),out_shape=jax.ShapeDtypeStruct((T,n),BF),compiler_params=params(1),
        cost_estimate=pl.CostEstimate(flops=2*T*D*n,bytes_accessed=2*(T*D+n*D+T*n),transcendentals=0))(g,packed)

def back_kernel(pairs, added, beside, *refs):
    out=refs[-1]
    acc=None
    if added: acc=refs[0][...].astype(F32)
    rs=refs[added:]
    for k in range(pairs):
        a=rs[2*k]; b=rs[2*k+1]
        a=a[0] if len(a.shape)==3 else a[...]
        p=mm(a,b[...],NN)
        acc=p if acc is None else acc+p
    if beside:
        wide=acc.shape[1]
        out[:,:wide]=acc.astype(out.dtype)
        more=sum(r[...] for r in refs[-1-beside:-1])
        gap=jnp.zeros((acc.shape[0],out.shape[1]-wide-more.shape[1]),F32)
        out[:,wide:]=jnp.concatenate([more,gap],axis=1).astype(out.dtype)
    else:
        out[...]=acc.astype(out.dtype)

def core_kernel(pairs, core_ref, *refs):
    out=refs[-1]
    chips,_,w=out.shape
    for z in range(chips):
        at=pl.ds(pl.multiple_of((2*z+core_ref[0])*w,w),w)
        acc=None
        for k in range(pairs):
            a=refs[2*k]; b=refs[2*k+1]
            p=mm(a[0] if len(a.shape)==3 else a[...],b[:,at],NN)
            acc=p if acc is None else acc+p
        out[z]=acc.astype(BF)

def back(terms, added, out_dtype, bt, beside=(), core=None, chips=0):
    T=terms[0][0].shape[-2]; D=terms[0][2].shape[1]
    ins=[];args=[];fl=0;by=0
    if core is not None:
        ins.append(pl.BlockSpec(memory_space=pltpu.SMEM)); args.append(core)
    if added is not None:
        ins.append(pl.BlockSpec((bt,D),lambda i:(i,0))); args.append(added)
    for st,k,packed,n,at in terms:
        if st.ndim==3: ins.append(pl.BlockSpec((1,bt,n),lambda i,k=k:(k,i,0)))
        else: ins.append(pl.BlockSpec((bt,n),lambda i:(i,0)))
        ins.append(rows_once(n,D,at))
        args+= [st,packed]; fl+=2*T*D*n; by+=2*(T*n+n*D)
    for more in beside:
        ins.append(pl.BlockSpec((bt,more.shape[1]),lambda i:(i,0))); args.append(more)
    body=functools.partial(back_kernel,len(terms),0 if added is None else 1,len(beside))
    if beside:
        shape=(T,D+128); ospec=pl.BlockSpec((bt,D+128),lambda i:(i,0))
    elif core is not None:
        w=D//(2*chips); fl//=2
        shape=(chips,T,w); ospec=pl.BlockSpec((chips,bt,w),lambda i:(0,i,0))
        body=functools.partial(core_kernel,len(terms))
    else:
        shape=(T,D); ospec=pl.BlockSpec((bt,D),lambda i:(i,0))
    return pl.pallas_call(body,grid=(T//bt,),in_specs=ins,out_specs=ospec,out_shape=jax.ShapeDtypeStruct(shape,out_dtype),
        compiler_params=params(1),cost_estimate=pl.CostEstimate(flops=fl,bytes_accessed=by+4*T*D,transcendentals=0))(*args)

def outer_kernel(s_ref,x_ref,*refs):
    refs[-1][...]=mm(s_ref[0],x_ref[...],TN).astype(BF)

def outer(stack,first,count,x,total,at,into=None,bc=512):
    T,D=x.shape; n=stack.shape[2]
    ins=[pl.BlockSpec((1,T,n),lambda k,j:(first+k,0,0)),pl.BlockSpec((T,bc),lambda k,j:(0,j))]
    args=[stack,x]; al={}
    if into is not None:
        ins.append(pl.BlockSpec(memory_space=pl.ANY)); args.append(into); al={2:0}
    return pl.pallas_call(outer_kernel,grid=(count,D//bc),in_specs=ins,
        out_specs=pl.BlockSpec((n,bc),lambda k,j:(at+k,j)),out_shape=jax.ShapeDtypeStruct((total,D),BF),
        input_output_aliases=al,compiler_params=params(2),
        cost_estimate=pl.CostEstimate(flops=2*count*T*D*n,bytes_accessed=2*count*(T*n+n*D+T*D),transcendentals=0))(*args)


def place_columns_kernel(chips, norm, at_ref, *refs):
    pieces=refs[:2*chips]
    refs=refs[2*chips:]
    if norm:
        gain_ref, w_ref = refs[:2]
        out_ref, round_ref, r_ref, proj_ref = refs[-4:]
    else:
        (out_ref,) = refs
    w=pieces[0].shape[1]
    for k in range(2*chips):
        out_ref[:,pl.ds(pl.multiple_of(at_ref[k]*w,w),w)]=pieces[k][...]
    if norm:
        v=out_ref[...].astype(F32)
        r=lax.rsqrt(jnp.mean(v*v,axis=-1,keepdims=True)+EPSILON)
        round_ref[...]=(v*r*gain_ref[...]).astype(BF)
        r_ref[...]=r
        proj_ref[...]=mm(round_ref[...],w_ref[...],NT)

def place_columns(pieces, at, gain=None, packed=None, count=0, rows=None, first=0, into=(), bt=256):
    T,w=pieces[0].shape; n=len(pieces)
    total_rows=rows or T
    start=first//bt
    ins=[pl.BlockSpec(memory_space=pltpu.SMEM)]+[pl.BlockSpec((bt,w),lambda i:(i,0))]*n
    args=[at]+list(pieces)
    wides=[(n*w,BF)]
    if gain is not None:
        ins+=[pl.BlockSpec((1,n*w),lambda i:(0,0)),rows_once(count,n*w,0)]; args+=[gain[None],packed]
        wides+=[(n*w,BF),(1,F32),(count,F32)]
    aliases={len(args)+k:k for k in range(len(into))}
    ins+=[pl.BlockSpec(memory_space=pl.ANY)]*len(into); args+=list(into)
    return pl.pallas_call(functools.partial(place_columns_kernel,n//2,gain is not None),grid=(T//bt,),
        in_specs=ins,out_specs=[pl.BlockSpec((bt,m),lambda i:(i+start,0)) for m,_ in wides],
        out_shape=[jax.ShapeDtypeStruct((total_rows,m),d) for m,d in wides],
        input_output_aliases=aliases,compiler_params=params(1),
        cost_estimate=pl.CostEstimate(flops=(6+2*count)*T*n*w,bytes_accessed=6*T*n*w,transcendentals=T))(*args)

def place_rows_kernel(n, times, at_ref, *refs):
    pieces=refs[:n]; refs=refs[n:]
    if times: w_ref,out_ref,made_ref,sem=refs
    else: out_ref,sem=refs
    rows=pieces[0].shape[0]
    to=[pl.ds(pl.multiple_of(at_ref[k]*rows,rows),rows) for k in range(n)]
    copies=[pltpu.make_async_copy(pieces[k],out_ref.at[to[k]],sem.at[k]) for k in range(n)]
    for c in copies: c.start()
    if times:
        for k in range(n): made_ref[to[k]]=mm(pieces[k][...],w_ref[...],NT).astype(BF)
    for c in copies: c.wait()

def place_rows(pieces, at, weight=None):
    rows,w=pieces[0].shape; n=len(pieces)
    vmem=pl.BlockSpec(memory_space=pltpu.VMEM)
    outs=[jax.ShapeDtypeStruct((n*rows,w),BF)]; specs=[pl.BlockSpec(memory_space=pl.ANY)]; more=[]
    if weight is not None:
        outs.append(jax.ShapeDtypeStruct((n*rows,weight.shape[0]),BF)); specs.append(vmem); more=[weight]
    return pl.pallas_call(functools.partial(place_rows_kernel,n,bool(more)),
        in_specs=[pl.BlockSpec(memory_space=pltpu.SMEM)]+[vmem]*(n+len(more)),
        out_specs=specs,out_shape=outs,
        scratch_shapes=[pltpu.SemaphoreType.DMA((n,))],compiler_params=pltpu.CompilerParams(vmem_limit_bytes=VMEM_LIMIT),
        cost_estimate=pl.CostEstimate(flops=2*n*rows*w*(weight.shape[0] if more else 0),bytes_accessed=4*n*rows*w,transcendentals=0))(at,*pieces,*more)

def norm_rows_kernel(n, at_ref, col_ref, gain_ref, wr_ref, kept_ref, *refs):
    pieces=refs[:n]; round_ref,cols_ref,gating_ref,weight_ref,made,cut,sem,sem2=refs[n:]
    rows=pieces[0].shape[0]; w=cut.shape[2]
    copies=[]
    for k in range(n):
        v=pieces[k][...].astype(F32)
        r=lax.rsqrt(jnp.mean(v*v,axis=-1,keepdims=True)+EPSILON)
        made[k]=(v*r*gain_ref[...]).astype(BF)
        cut[k]=pieces[k][:,pl.ds(pl.multiple_of(col_ref[0]*w,w),w)]
        to=pl.ds(pl.multiple_of(at_ref[k]*rows,rows),rows)
        copies.append(pltpu.make_async_copy(made.at[k],round_ref.at[to],sem.at[k]))
        copies.append(pltpu.make_async_copy(cut.at[k],cols_ref.at[to],sem2.at[k]))
        copies[-2].start(); copies[-1].start()
        logits=mm(made[k],wr_ref[...],NT)
        e=jnp.exp(logits-jnp.max(logits,axis=-1,keepdims=True))
        gating=e/jnp.sum(e,axis=-1,keepdims=True)
        gating_ref[to]=gating
        weight_ref[to]=gating*kept_ref[to]
    for c in copies: c.wait()

def norm_rows(pieces, at, column, w, gain, router, kept):
    rows,wide=pieces[0].shape; n=len(pieces)
    vmem=pl.BlockSpec(memory_space=pltpu.VMEM)
    return pl.pallas_call(functools.partial(norm_rows_kernel,n),
        in_specs=[pl.BlockSpec(memory_space=pltpu.SMEM)]*2+[vmem]*(n+3),
        out_specs=[pl.BlockSpec(memory_space=pl.ANY)]*2+[vmem]*2,
        out_shape=[jax.ShapeDtypeStruct((n*rows,wide),BF),jax.ShapeDtypeStruct((n*rows,w),BF)]+[jax.ShapeDtypeStruct((n*rows,E),F32)]*2,
        scratch_shapes=[pltpu.VMEM((n,rows,wide),BF),pltpu.VMEM((n,rows,w),BF),pltpu.SemaphoreType.DMA((n,)),pltpu.SemaphoreType.DMA((n,))],
        compiler_params=pltpu.CompilerParams(vmem_limit_bytes=VMEM_LIMIT),
        cost_estimate=pl.CostEstimate(flops=6*n*rows*wide,bytes_accessed=4*n*rows*wide,transcendentals=n*rows))(at,column,gain[None],router,kept,*pieces)

def small_kernel(pairs_ref, up_ref, kr_ref, dot_ref, entry_ref, out_ref):
    bt=out_ref.shape[0]
    out_ref[:,:R]=mm(pairs_ref[...],up_ref[...],NT).astype(BF)
    h=DR//2
    kr=kr_ref[...]
    gap=jnp.zeros((bt,DR-1-entry_ref.shape[1]),F32)
    out_ref[:,R:]=jnp.concatenate(
        [kr[:,:h]+kr[:,h:DR],kr[:,DR:DR+h]+kr[:,DR+h:],dot_ref[...],entry_ref[...],gap],axis=1).astype(BF)

def small_terms(pairs, up, kr, dots, entries, bt=512):
    T=pairs.shape[0]
    def rows(a): return pl.BlockSpec((bt,a.shape[1]),lambda i:(i,0))
    return pl.pallas_call(small_kernel,grid=(T//bt,),
        in_specs=[rows(pairs),pl.BlockSpec(up.shape,lambda i:(0,0)),rows(kr),rows(dots),rows(entries)],
        out_specs=pl.BlockSpec((bt,R+DN),lambda i:(i,0)),out_shape=jax.ShapeDtypeStruct((T,R+DN),BF),
        compiler_params=params(1),
        cost_estimate=pl.CostEstimate(flops=2*T*R*pairs.shape[1],bytes_accessed=8*T*R,transcendentals=0))(pairs,up,kr,dots,entries)

def latent_back_kernel(small_ref, proj_ref, gain_ref, cos_ref, sin_ref, delta_ref, dots_ref, gain_delta_ref):
    i=pl.program_id(0)
    at=proj_ref.shape[1]-R-DN
    dl=small_ref[:,:R].astype(F32)
    vl=proj_ref[:,at:at+R]
    rl=lax.rsqrt(jnp.mean(vl*vl,axis=-1,keepdims=True)+EPSILON)
    gain=gain_ref[...]
    part=jnp.sum(dl*vl*rl,axis=0,keepdims=True)
    @pl.when(i==0)
    def _(): gain_delta_ref[...]=part
    @pl.when(i>0)
    def _(): gain_delta_ref[...]+=part
    gd=gain*dl
    head=rl*gd-vl*(rl*rl*rl)*jnp.mean(vl*gd,axis=-1,keepdims=True)
    beyond=small_ref[:,R:]
    row=lax.broadcasted_iota(jnp.int32,(DN,DN),0); col=lax.broadcasted_iota(jnp.int32,(DN,DN),1)
    h=DR//2
    put=jnp.where(((row<h)&(col==row))|((row>=h)&(row<DR)&(col==row+h)),1.0,0.0).astype(BF)
    spread=mm(beyond,put,NN)
    tail=spread*cos_ref[...]-pltpu.roll(spread,DR,1)*sin_ref[...]
    delta_ref[:,:R]=head.astype(BF)
    delta_ref[:,R:]=tail.astype(BF)
    own=jnp.sum(head*vl,axis=-1,keepdims=True)+jnp.sum(tail*proj_ref[:,at+R:],axis=-1,keepdims=True)
    lane=lax.broadcasted_iota(jnp.int32,beyond.shape,1)
    dots_ref[...]=own+jnp.sum(jnp.where(lane==DR,beyond.astype(F32),0.0),axis=-1,keepdims=True)

def latent_back(small, proj, gain, cosine, sine, bt=512):
    T,wide=small.shape; turns=LEN//bt
    return pl.pallas_call(latent_back_kernel,grid=(T//bt,),
        in_specs=[pl.BlockSpec((bt,wide),lambda i:(i,0)),pl.BlockSpec((bt,proj.shape[1]),lambda i:(i,0)),
                  pl.BlockSpec((1,R),lambda i:(0,0)),pl.BlockSpec((bt,DN),lambda i:(i%turns,0)),pl.BlockSpec((bt,DN),lambda i:(i%turns,0))],
        out_specs=[pl.BlockSpec((bt,R+DN),lambda i:(i,0)),pl.BlockSpec((bt,1),lambda i:(i,0)),pl.BlockSpec((1,R),lambda i:(0,0))],
        out_shape=[jax.ShapeDtypeStruct((T,R+DN),BF),jax.ShapeDtypeStruct((T,1),F32),jax.ShapeDtypeStruct((1,R),F32)],
        compiler_params=params(1),
        cost_estimate=pl.CostEstimate(flops=30*T*wide,bytes_accessed=8*T*wide,transcendentals=T))(small,proj,gain,cosine,sine)

def last_pack_kernel(delta_ref, x_ref, w_ref, small_ref, g_ref, latent_ref, more_ref, out_ref):
    n=delta_ref.shape[1]
    d=mm(delta_ref[...],x_ref[...],TN)
    out_ref[:n]=d.astype(BF)
    sums=jnp.sum(w_ref[...].astype(F32)*d,axis=0,keepdims=True)
    row=lax.broadcasted_iota(jnp.int32,(32,DN),0); col=lax.broadcasted_iota(jnp.int32,(32,DN),1)
    at=DR+1
    pick=((row<E)&(col==row+at+2))|((row==E)&(col==at))|((row==E+1)&(col==at+1))
    v=mm(jnp.where(pick,1.0,0.0).astype(BF),small_ref[...],NT)
    line=lax.broadcasted_iota(jnp.int32,v.shape,0)
    v=jnp.where(line==E+1,(v+sums)/g_ref[...],v)
    out_ref[n:n+32]=jnp.where(line==E+2,latent_ref[...],v).astype(BF)
    out_ref[n+32:]=more_ref[...]

def last_pack(delta, x, packed, first, small, gain, latent_row, more, bc=512):
    T,D=x.shape; n=delta.shape[1]
    def cols(a): return pl.BlockSpec((a.shape[0],bc),lambda j:(0,j))
    return pl.pallas_call(last_pack_kernel,grid=(D//bc,),
        in_specs=[pl.BlockSpec((T,n),lambda j:(0,0)),cols(x),
                  pl.BlockSpec((pl.Element(n),pl.Element(bc)),lambda j:(first,j*bc)),pl.BlockSpec((bc,DN),lambda j:(j,R//DN)),cols(gain),cols(latent_row),cols(more)],
        out_specs=pl.BlockSpec((n+32+more.shape[0],bc),lambda j:(0,j)),out_shape=jax.ShapeDtypeStruct((n+32+more.shape[0],D),BF),
        compiler_params=params(1),
        cost_estimate=pl.CostEstimate(flops=2*T*D*n,bytes_accessed=2*(T*D+2*n*D+T*n),transcendentals=0))(delta,x,packed,small,gain,latent_row,more)


def turn(x, cosine, sine):
    return x*cosine+pltpu.roll(x,64,1)*sine

def slot_mask(shape, head):
    lane=lax.broadcasted_iota(jnp.int32,shape,1)
    low=head*(DR//2)
    inside=((lane>=low)&(lane<low+DR//2))|((lane>=low+DR)&(lane<low+DR+DR//2))
    return inside

def causal_scores(q, k, first):
    s=mm(q,k,NT)*SCALE
    row=lax.broadcasted_iota(jnp.int32,s.shape,0)+first
    col=lax.broadcasted_iota(jnp.int32,s.shape,1)
    return jnp.where(col<=row,s,-1e30)

def attend_kernel(heads, proj_ref, up_ref, gain_ref, cos_ref, sin_ref, *refs):
    q_ref, kr_ref, kv_ref, latent_ref, mixed_ref, lse_ref = refs[-6:]
    content=heads*DN
    at=content+DN
    q_ref[:,:content]=proj_ref[:,:content].astype(BF)
    cosine,sine=cos_ref[...],sin_ref[...]
    q_ref[:,content:]=turn(proj_ref[:,content:at],cosine,sine).astype(BF)
    vl=proj_ref[:,at:at+R]
    latent_ref[...]=(vl*lax.rsqrt(jnp.mean(vl*vl,axis=-1,keepdims=True)+EPSILON)*gain_ref[...]).astype(BF)
    kr_ref[...]=turn(proj_ref[:,at+R:],cosine,sine).astype(BF)
    kv_ref[...]=mm(latent_ref[...],up_ref[...],NN).astype(BF)
    kr=kr_ref[...]
    for h in range(heads):
        kc=kv_ref[:,h*(DN+DV):h*(DN+DV)+DN]
        v=kv_ref[:,h*(DN+DV)+DN:(h+1)*(DN+DV)]
        k=jnp.concatenate([kc,jnp.where(slot_mask(kr.shape,h),kr,jnp.zeros_like(kr))],axis=1)
        for i in range(LEN//BLOCK):
            a,b=i*BLOCK,(i+1)*BLOCK
            q=jnp.concatenate([q_ref[a:b,h*DN:(h+1)*DN],q_ref[a:b,content:]],axis=1)
            s=causal_scores(q,k[:b],a)
            m=jnp.max(s,axis=-1,keepdims=True)
            e=jnp.exp(s-m)
            t=jnp.sum(e,axis=-1,keepdims=True)
            p=(e*(1.0/t)).astype(BF)
            mixed_ref[a:b,h*DV:(h+1)*DV]=mm(p,v[:b],NN).astype(BF)
            lse_ref[a:b,h:h+1]=m+jnp.log(t)

def attend(proj, up, gain, cosine, sine, heads, sequence, into=()):
    T=proj.shape[0]; wide=proj.shape[1]
    def rows(n): return pl.BlockSpec((LEN,n),lambda i:(sequence,0))
    def whole(a): return pl.BlockSpec(a.shape,lambda i:(0,0))
    qn=heads*DN+DN
    outs=[(qn,BF),(DN,BF),(heads*(DN+DV),BF),(R,BF),(heads*DV,BF),(heads,F32)]
    args=[proj,up,gain,cosine,sine]
    return pl.pallas_call(functools.partial(attend_kernel,heads),grid=(1,),
        in_specs=[rows(wide)]+[whole(a) for a in args[1:]]+[pl.BlockSpec(memory_space=pl.ANY)]*len(into),
        out_specs=[rows(n) for n,_ in outs],out_shape=[jax.ShapeDtypeStruct((T,n),d) for n,d in outs],
        input_output_aliases={len(args)+k:k for k in range(len(into))},compiler_params=params(1),
        cost_estimate=pl.CostEstimate(flops=LEN*LEN*heads*512,bytes_accessed=LEN*8000,transcendentals=LEN*LEN*heads//2))(*args,*into)

def attend_back_kernel(heads, q_ref, kr_ref, kv_ref, mixed_ref, lse_ref, do_ref, cos_ref, sin_ref, dq_ref, dkv_ref, dkr_ref, dot_ref, dk_acc, dv_acc):
    content=heads*DN
    kr=kr_ref[...]
    for h in range(heads):
        kc=kv_ref[:,h*(DN+DV):h*(DN+DV)+DN]
        v=kv_ref[:,h*(DN+DV)+DN:(h+1)*(DN+DV)]
        mask=slot_mask(kr.shape,h)
        k=jnp.concatenate([kc,jnp.where(mask,kr,jnp.zeros_like(kr))],axis=1)
        for i in reversed(range(LEN//BLOCK)):
            a,b=i*BLOCK,(i+1)*BLOCK
            q=jnp.concatenate([q_ref[a:b,h*DN:(h+1)*DN],q_ref[a:b,content:]],axis=1)
            do=do_ref[a:b,h*DV:(h+1)*DV]
            p=jnp.exp(causal_scores(q,k[:b],a)-lse_ref[a:b,h:h+1])
            dp=mm(do,v[:b],NT)
            along=jnp.sum(do.astype(F32)*mixed_ref[a:b,h*DV:(h+1)*DV].astype(F32),axis=-1,keepdims=True)
            ds=(p*(dp-along)).astype(BF)
            pv=mm(p.astype(BF),do,TN)
            pk=mm(ds,q,TN)
            if i==LEN//BLOCK-1:
                dv_acc[...]=pv; dk_acc[...]=pk
            else:
                dv_acc[:b]+=pv; dk_acc[:b]+=pk
            dq=mm(ds,k[:b],NN)*SCALE
            d=jnp.sum(dq*q.astype(F32),axis=-1,keepdims=True)
            if h==0: dot_ref[a:b]=d
            else: dot_ref[a:b]+=d
            dq_ref[a:b,h*DN:(h+1)*DN]=dq[:,:DN].astype(BF)
            turned=turn(dq[:,DN:],cos_ref[a:b],-sin_ref[a:b])
            turned=jnp.where(mask[:b-a],turned,0.0).astype(BF)
            if h==0: dq_ref[a:b,content:]=turned
            else: dq_ref[a:b,content:]+=turned
        dkv_ref[:,h*(DN+DV):h*(DN+DV)+DN]=(dk_acc[:,:DN]*SCALE).astype(BF)
        dkv_ref[:,h*(DN+DV)+DN:(h+1)*(DN+DV)]=dv_acc[...].astype(BF)
        part=jnp.where(mask,dk_acc[:,DN:]*SCALE,0.0)
        if h==0: dkr_ref[...]=part
        else: dkr_ref[...]+=part

def attend_back(q,kr,kv,mixed,lse,do,cosine,sine,heads):
    T=q.shape[0]
    def rows(n): return pl.BlockSpec((LEN,n),lambda i:(i,0))
    def whole(a): return pl.BlockSpec(a.shape,lambda i:(0,0))
    args=(q,kr,kv,mixed,lse,do)
    outs=[(q.shape[1],BF),(kv.shape[1],BF),(DN,F32),(1,F32)]
    return pl.pallas_call(functools.partial(attend_back_kernel,heads),grid=(T//LEN,),
        in_specs=[rows(a.shape[1]) for a in args]+[whole(cosine),whole(sine)],
        out_specs=[rows(n) for n,_ in outs],out_shape=[jax.ShapeDtypeStruct((T,n),d) for n,d in outs],
        scratch_shapes=[pltpu.VMEM((LEN,2*DN),F32),pltpu.VMEM((LEN,DV),F32)],
        compiler_params=params(1),
        cost_estimate=pl.CostEstimate(flops=T*LEN*heads*1400,bytes_accessed=T*6000,transcendentals=T*LEN*heads//2))(*args,cosine,sine)

def tables():
    position=np.arange(LEN,dtype=np.float32)
    spread=(10000.0**(-np.arange(DR//2,dtype=np.float32)/(DR//2))).astype(np.float32)
    phase=(position[:,None]*spread[None,:]).astype(np.float32)
    c,s=np.cos(phase),np.sin(phase)
    return np.concatenate([c]*4,1).astype(np.float32),np.concatenate([-s,-s,s,s],1).astype(np.float32)


class Line:
    def __init__(self):
        self.n = lax.axis_size("tensor")
        self.chips = self.n // 2
        index = lax.axis_index("tensor")
        self.index = index
        self.z = index // 2
        self.c = index % 2

    def swap(self, a):
        return lax.ppermute(a, "tensor", [(i, i ^ 1) for i in range(self.n)])

    def shift(self, a, step, sources):
        pairs = [
            (2 * s + c, 2 * (s + step) + c)
            for s in sources
            if 0 <= s + step < self.chips
            for c in (0, 1)
        ]
        return lax.ppermute(a, "tensor", pairs)

    def across(self, a, step):
        n = self.chips
        pairs = [(2 * k + c, 2 * ((k + step) % n) + c) for k in range(n) for c in (0, 1)]
        return lax.ppermute(a, "tensor", pairs)

    def pieces(self, own, order):
        n = self.chips
        out, at = [], []
        for k, piece in enumerate(own):
            chip = (self.z - k + n) % n
            out += [piece, self.swap(piece)]
            at += [order(chip, self.c), order(chip, 1 - self.c)]
        return out, jnp.stack(at).astype(jnp.int32)

    def row_pieces(self, own):
        return self.pieces(own, lambda chip, core: core * self.chips + chip)

    def column_pieces(self, own):
        return self.pieces(own, lambda chip, core: chip * 2 + core)

    def half(self, p, core):
        count = p.shape[0] // 2
        return lax.dynamic_slice_in_dim(p, core * count, count, 0)

    def row_scatter(self, p, first, arrived):
        ch = arrived.shape[0] // self.chips
        return Scatter(self, lambda j: total(
            lax.dynamic_slice_in_dim(p, first + j * ch, ch, 0), lax.dynamic_slice_in_dim(arrived, j * ch, ch, 0)
        ))

    def column_scatter(self, mine, arrived):
        return Scatter(self, lambda j: total(
            lax.dynamic_index_in_dim(mine, j, 0, False), lax.dynamic_index_in_dim(arrived, j, 0, False)
        ))

    def row_start(self, rows):
        ch = rows // self.n
        return (self.c * self.chips + self.z) * ch, ch


def total(mine, arrived):
    return (mine.astype(F32) + arrived.astype(F32)).astype(BF)


class Gather:
    def __init__(self, line, block):
        self.line, self.left, self.right = line, [block], [block]

    def start(self):
        n, k = self.line.chips, len(self.left)
        return (
            self.line.shift(self.left[-1], 1, range(k - 1, n)),
            self.line.shift(self.right[-1], -1, range(0, n - k + 1)),
        )

    def take(self, arrived):
        self.left.append(arrived[0])
        self.right.append(arrived[1])

    def result(self):
        n, z = self.line.chips, self.line.z
        return self.left[:1] + [jnp.where(z >= k, self.left[k], self.right[n - k]) for k in range(1, n)]


class Scatter:
    def __init__(self, line, block):
        self.line, self.block, self.step, self.left, self.right = line, block, 0, None, None

    def start(self):
        self.step += 1
        n, s, z = self.line.chips, self.step, self.line.z
        up = self.block(jnp.clip(n - s + z, 0, n - 1))
        down = self.block(jnp.clip(z - (n - s), 0, n - 1))
        if self.left is not None:
            up, down = total(up, self.left), total(down, self.right)
        return self.line.shift(up, 1, range(0, s)), self.line.shift(down, -1, range(n - s, n))

    def take(self, arrived):
        self.left, self.right = arrived

    def result(self):
        return self.block(self.line.z).astype(F32) + self.left.astype(F32) + self.right.astype(F32)


class GatherAtOnce:
    def __init__(self, line, block):
        self.line, self.block = line, block

    def start(self):
        return [self.line.across(self.block, k) for k in range(1, self.line.chips)]

    def take(self, arrived):
        self.arrived = list(arrived)

    def result(self):
        return [self.block] + self.arrived


class ScatterAtOnce:
    def __init__(self, line, block):
        self.line, self.block = line, block

    def start(self):
        n, z = self.line.chips, self.line.z
        return [self.line.across(self.block((z + k) % n), k) for k in range(1, n)]

    def take(self, arrived):
        self.arrived = list(arrived)

    def result(self):
        return sum((a.astype(F32) for a in self.arrived), self.block(self.line.z).astype(F32))


def beside(moves, job=None):
    arrived, done = lax.optimization_barrier(([m.start() for m in moves], job() if job else None))
    for move, a in zip(moves, arrived):
        move.take(a)
    return done


def steps(move, count, jobs=()):
    made = []
    for k in range(count):
        made.append(beside([move], jobs[k] if k < len(jobs) else None))
    return made


def gather_rows(packed):
    return lax.all_gather(packed, "dp", axis=1, tiled=True)


def scatter_rows(packed):
    return lax.psum_scatter(packed, "dp", scatter_dimension=1, tiled=True)


def split_rows(packed, counts):
    out, at = [], 0
    for count in counts:
        out.append(packed[at : at + count])
        at += count
    return out


def ranks(mask):
    number = mask.shape[0]
    block = 128
    pieces = mask.reshape(number // block, block, E).astype(BF)
    lower = jnp.tril(jnp.ones((block, block), BF), -1)
    inside = jnp.einsum("ij,bje->bie", lower, pieces, preferred_element_type=F32)
    totals = jnp.sum(pieces.astype(F32), axis=1).astype(BF)
    ahead = jnp.tril(jnp.ones((number // block, number // block), BF), -1)
    before = dot(ahead, totals, 1, 0)
    return (inside + before[:, None, :]).reshape(number, E)


def per_device(
    layer_input, cotangent, first_gain, query_weight, latent_down, latent_gain, latent_up,
    output_weight, second_gain, router_weight, expert_gate, expert_up, expert_down,
    shared_gate, shared_up, shared_down, routes,
):
    line = Line()
    n_dp = lax.axis_size("dp")
    wide = D // n_dp
    number = layer_input.shape[0]
    heads_here = output_weight.shape[0] // DV
    fe = expert_down.shape[1]
    my_columns = layer_input.shape[1]
    column_start = line.index * my_columns
    row_start, row_count = line.row_start(number)

    half = DR // 2
    spare_heads = 2 - heads_here
    up_rows = latent_up.size // wide
    by_head = query_weight.T.reshape(heads_here, DN + DR, wide)
    blank = jnp.zeros((spare_heads * half, wide), BF)
    gains = jnp.zeros((16, wide), BF)
    gains = gains.at[0].set(first_gain).at[1].set(second_gain)
    gains = gains.at[2, : latent_gain.shape[0]].set(latent_gain)
    down = latent_down.T
    queries_wide = heads_here * DN + DN
    latent_wide = R + DN
    attend_pack = [
        by_head[:, :DN].reshape(heads_here * DN, wide),
        by_head[:, DN : DN + half].reshape(heads_here * half, wide), blank,
        by_head[:, DN + half :].reshape(heads_here * half, wide), blank,
        down[: R + half], down[R : R + half], down[R + half :], down[R + half :],
        latent_up.reshape(up_rows, wide), gains, router_weight.T, output_weight,
    ]
    attend_packed = gather_rows(jnp.concatenate([m for m in attend_pack if m.shape[0]], axis=0))
    wproj, wup, gains, wr, wo = split_rows(
        attend_packed, [queries_wide + latent_wide, up_rows, 16, E, output_weight.shape[0]]
    )
    wup = wup.reshape(up_rows, n_dp, wide).transpose(1, 0, 2).reshape(R, -1)
    first_g = gains[0].astype(F32)
    second_g = gains[1].astype(F32)
    latent_g = gains[2].reshape(n_dp, wide)[:, : R // n_dp].reshape(R).astype(F32)
    cosine, sine = (jnp.asarray(table) for table in tables())

    n_units = E * fe + shared_down.shape[0]
    n0 = n_units // 2 // 256 * 256
    n1 = n_units - n0
    last_step = line.chips - 1
    gate = expert_gate.transpose(0, 2, 1).reshape(E * fe, wide)
    up = expert_up.transpose(0, 2, 1).reshape(E * fe, wide)
    move = Gather(line, layer_input[:LEN])
    downs, early, late = steps(move, 3, (
        lambda: jnp.concatenate([expert_down.reshape(E * fe, wide), shared_down], axis=0),
        lambda: jnp.concatenate([gate[:n0], up[:n0]], axis=0),
        lambda: jnp.concatenate([gate[n0:], shared_gate.T, up[n0:], shared_up.T], axis=0),
    ))
    steps(move, last_step - 3)
    downs, early, late = gather_rows(downs), gather_rows(early), gather_rows(late)

    tile = 256
    core = line.c.reshape(1).astype(jnp.int32)
    placed, attended = (), ()

    def place(move, sequence):
        pieces, at = line.column_pieces(move.result())
        return place_columns(
            pieces, at, first_g, attend_packed, queries_wide + latent_wide, number, sequence * LEN, placed
        )

    def attention(sequence):
        return attend(placed[3], wup, latent_g[None], cosine, sine, heads_here, sequence, attended)

    for sequence in range(1, number // LEN):
        ahead, after = move, layer_input[sequence * LEN : (sequence + 1) * LEN]
        ahead.left[-1], ahead.right[-1], after = lax.optimization_barrier((ahead.left[-1], ahead.right[-1], after))
        move = Gather(line, after)
        beside([move])
        placed = beside([move], lambda: place(ahead, sequence - 1))
        steps(move, last_step - 3)
        attended = beside([move], lambda: attention(sequence - 1))
    move.left[-1], move.right[-1], cotangent = lax.optimization_barrier((move.left[-1], move.right[-1], cotangent))
    grad_move = Gather(line, cotangent)
    placed = place(move, number // LEN - 1)
    attended = beside([grad_move], lambda: attention(number // LEN - 1))
    rows, first_round, r1, proj = placed
    q, kr, kv, latent, mixed, log_total = attended
    arrived = line.swap(dot(line.half(mixed, 1 - line.c), wo, 1, 0, BF))
    move = line.row_scatter(dot(line.half(mixed, line.c), wo, 1, 0, BF), 0, arrived)
    for _ in range(last_step - 1):
        beside([move, grad_move])
    (grad,) = beside([move], lambda: place_columns(*line.column_pieces(grad_move.result())))
    hidden_rows = (
        lax.dynamic_slice_in_dim(rows, row_start, row_count, 0).astype(F32) + move.result()
    ).astype(BF)
    move = Gather(line, hidden_rows)
    back0, back1 = steps(move, 2, (
        lambda: lift_back(grad, downs, 0, n0, tile),
        lambda: lift_back(grad, downs, n0, n1, tile),
    ))
    steps(move, last_step - 2)
    hidden_pieces, hidden_at = line.row_pieces(move.result())
    named = jnp.any(routes[:, :, None] == jnp.arange(E, dtype=jnp.int32)[None, None, :], axis=1)
    kept = jnp.where(named & (ranks(named) < CAP), 1.0, 0.0)
    second_round, hidden_columns, gating, weight = norm_rows(
        hidden_pieces, hidden_at, line.index.reshape(1).astype(jnp.int32), my_columns, second_g, wr, kept
    )

    stack0, pair0 = units(second_round, early, back0, weight, fe, 0, tile)
    deltas = outer(stack0, 0, 2, second_round, 3 * n0, 0)
    deltas = outer(stack0, 2, 1, grad, 3 * n0, 2, deltas)
    deltas, stack0 = lax.optimization_barrier((deltas, stack0))
    early_sums = scatter_rows(deltas)
    stack1, pair1 = units(second_round, late, back1, weight, fe, n0, tile)
    second_terms = back(
        [(stack0, 0, early, n0, 0), (stack0, 1, early, n0, n0), (stack1, 0, late, n1, 0), (stack1, 1, late, n1, n1)],
        None, BF, tile, (pair0, pair1),
    )

    branch_terms = [(stack0, 2, downs, n0, 0), (stack1, 2, downs, n1, n0)]
    move = line.row_scatter(
        second_terms, line.c * (number // 2), line.swap(line.half(second_terms, 1 - line.c))
    )
    deltas = beside([move], lambda: outer(stack1, 0, 1, second_round, 3 * n1, 0))
    deltas = beside([move], lambda: outer(stack1, 1, 1, second_round, 3 * n1, 1, deltas))
    branch_theirs = beside([move], lambda: back(branch_terms, None, BF, tile, (), 1 - core, line.chips))
    steps(move, last_step - 3)
    summed = move.result()

    def own_rows(a):
        return lax.dynamic_slice_in_dim(a, row_start, row_count, 0)

    gating_rows, kept_rows, x2 = own_rows(gating), own_rows(kept), own_rows(second_round)
    u = summed[:, D : D + E] * kept_rows
    logits_delta = gating_rows * (u - jnp.sum(gating_rows * u, axis=-1, keepdims=True))
    d2 = summed[:, :D] + dot(logits_delta.astype(BF), wr, 1, 0)
    v2 = hidden_rows.astype(F32)
    r2 = lax.rsqrt(jnp.mean(v2 * v2, axis=-1, keepdims=True) + EPSILON)
    vgd = jnp.mean(v2 * second_g * d2, axis=-1, keepdims=True)
    hidden_delta = own_rows(grad).astype(F32) + r2 * second_g * d2 - v2 * (r2**3) * vgd
    move = Gather(line, hidden_delta.astype(BF))
    branch_mine, branch_arrived = beside([move], lambda: (
        back(branch_terms, None, BF, tile, (), core, line.chips), line.swap(branch_theirs)
    ))
    branch_move = line.column_scatter(branch_mine, branch_arrived)
    deltas = beside([move, branch_move], lambda: outer(stack1, 2, 1, grad, 3 * n1, 2, deltas))
    router_delta = dot(x2, logits_delta.astype(BF), 0, 0)
    second_gain_delta = jnp.sum(d2 * v2 * r2, axis=0)
    early_sums, deltas, move.left[-1] = lax.optimization_barrier((early_sums, deltas, move.left[-1]))
    late_sums = scatter_rows(deltas)
    for _ in range(last_step - 2):
        beside([move, branch_move])
    delta_pieces, delta_at = line.row_pieces(move.result())

    def heads_back():
        placed, delta_mixed = place_rows(delta_pieces, delta_at, wo)
        return placed, attend_back(q, kr, kv, mixed, log_total, delta_mixed, cosine, sine, heads_here)

    hidden_delta, heads = beside([branch_move], heads_back)
    layer_output = (hidden_columns.astype(F32) + branch_move.result()).astype(BF)
    delta_queries, delta_pairs, delta_kr, query_dot = heads
    delta_wq = dot(delta_queries, first_round, 0, 0)
    query_gain = jnp.sum(wproj[:queries_wide].astype(F32) * delta_wq, axis=0)
    per_entry = jnp.concatenate([second_gain_delta[:, None], query_gain[:, None], router_delta], axis=1)
    if number > D:
        per_entry = jnp.concatenate([per_entry, jnp.zeros((number - D, E + 2), F32)], axis=0)
    small = small_terms(delta_pairs, wup, delta_kr, query_dot, per_entry)
    move = line.row_scatter(small, line.c * (number // 2), line.swap(line.half(small, 1 - line.c)))

    move = ScatterAtOnce(line, move.block)

    def attend_deltas():
        delta_wup = dot(latent, delta_pairs, 0, 0, BF)
        return jnp.concatenate(
            [delta_wq.astype(BF),
             delta_wup.reshape(n_dp, up_rows, wide).transpose(1, 0, 2).reshape(up_rows, D),
             dot(mixed, hidden_delta, 0, 0, BF)], axis=0)

    deltas = beside([move], attend_deltas)
    small, layer_output, late_queries = lax.optimization_barrier(
        (move.result().astype(BF), layer_output, delta_queries)
    )
    first_terms = [(late_queries, 0, attend_packed, queries_wide, 0)]
    move = GatherAtOnce(line, small)

    def first_products():
        theirs = back(first_terms, None, BF, tile, (), 1 - core, line.chips)
        return back(first_terms, None, BF, tile, (), core, line.chips), line.swap(theirs)

    mine, arrived = beside([move], first_products)
    small_pieces, small_at = line.row_pieces(move.result())
    small_pieces, late_sums, mine = lax.optimization_barrier((small_pieces, late_sums, mine))
    first_move = line.column_scatter(mine, arrived)
    wld = wproj[queries_wide:]

    def last():
        (small,) = place_rows(small_pieces, small_at)
        delta_latent, dots, gain_delta = latent_back(small, proj, latent_g[None], cosine, sine)
        latent_row = jnp.pad(gain_delta.reshape(n_dp, R // n_dp), ((0, 0), (0, wide - R // n_dp))).reshape(1, D)
        return delta_latent, dots, last_pack(
            delta_latent, first_round, attend_packed, queries_wide, small, first_g[None], latent_row, deltas)

    delta_latent, dots, pack = beside([first_move], last)
    steps(first_move, last_step - 1)
    first_share = first_move.result()
    dwld, vectors, dwq, dwup, dwo = split_rows(
        scatter_rows(pack).astype(F32), [latent_wide, 32, queries_wide, up_rows, output_weight.shape[0]]
    )
    content = heads_here * DN
    dwq = jnp.concatenate(
        [dwq[:content].reshape(heads_here, DN, wide),
         dwq[content : content + heads_here * half].reshape(heads_here, half, wide),
         dwq[content + DR : content + DR + heads_here * half].reshape(heads_here, half, wide)], axis=1
    ).reshape(heads_here * (DN + DR), wide)
    dwld = jnp.concatenate([dwld[: R + half], dwld[R + DR : R + DR + half]], axis=0)

    first_share = first_share + dot(
        delta_latent, lax.dynamic_slice_in_dim(wld, column_start, my_columns, 1), 1, 0
    )
    vc = layer_input.astype(F32)
    gc = lax.dynamic_slice_in_dim(first_g, column_start, my_columns, 0)
    input_delta = (
        lax.dynamic_slice_in_dim(hidden_delta, column_start, my_columns, 1).astype(F32)
        + r1 * gc * first_share
        - vc * (r1 * r1) * (dots / D)
    )

    def units_delta(k):
        return early_sums[k * n0 : (k + 1) * n0], late_sums[k * n1 : (k + 1) * n1]

    def expert_delta(k):
        first, second = units_delta(k)
        return jnp.concatenate([first, second[: E * fe - n0]], axis=0).astype(F32).reshape(E, fe, wide)

    def shared_delta(k):
        return units_delta(k)[1][E * fe - n0 :].astype(F32)

    return (
        layer_output, input_delta, vectors[E + 1], dwq.T, dwld.T, vectors[E + 2, : R // n_dp],
        dwup.reshape(latent_up.shape), dwo, vectors[E], vectors[:E].T,
        expert_delta(0).transpose(0, 2, 1), expert_delta(1).transpose(0, 2, 1), expert_delta(2),
        shared_delta(0).T, shared_delta(1).T, shared_delta(2),
    )


def solution(mesh):
    in_specs = (
        P("dp", "tensor"), P("dp", "tensor"), P("dp"), P("dp", "tensor"), P("dp", None), P("dp"),
        P("dp", "tensor"), P("tensor", "dp"), P("dp"), P("dp", None), P(None, "dp", "tensor"),
        P(None, "dp", "tensor"), P(None, "tensor", "dp"), P("dp", "tensor"), P("dp", "tensor"),
        P("tensor", "dp"), P("dp", None),
    )
    out_specs = (
        P("dp", "tensor"), P("dp", "tensor"), P("dp"), P("dp", "tensor"), P("dp", None), P("dp"),
        P("dp", "tensor"), P("tensor", "dp"), P("dp"), P("dp", None), P(None, "dp", "tensor"),
        P(None, "dp", "tensor"), P(None, "tensor", "dp"), P("dp", "tensor"), P("dp", "tensor"),
        P("tensor", "dp"),
    )
    return jax.shard_map(
        per_device, mesh=mesh, in_specs=in_specs, out_specs=out_specs, check_vma=False
    )
```

```python
import functools

import jax
import jax.numpy as jnp
import numpy as np
from jax import lax
from jax.experimental import pallas as pl
from jax.experimental.pallas import tpu as pltpu
from jax.sharding import PartitionSpec as P

D = 2048
DN = 128
DR = 64
DV = 128
R = 512
E = 16
LEN = 1024
CAP = 864
EPSILON = 1e-06
SCALE = (DN + DR) ** -0.5
BLOCK = 256
BF = jnp.bfloat16
F32 = jnp.float32


def dot(a, b, ca, cb, out=F32):
    return lax.dot_general(
        a, b, (((ca,), (cb,)), ((), ())), preferred_element_type=F32
    ).astype(out)


VMEM_LIMIT = 58 * 2**20
NT=(((1,),(1,)),((),()))
NN=(((1,),(0,)),((),()))
TN=(((0,),(0,)),((),()))

def mm(a,b,dims):
    return lax.dot_general(a,b,dims,preferred_element_type=F32)

def params(n):
    return pltpu.CompilerParams(dimension_semantics=("arbitrary",)*n, vmem_limit_bytes=VMEM_LIMIT)

def once(shape, index):
    return pl.BlockSpec(shape, index, pipeline_mode=pl.Buffered(1))

def rows_once(n, wide, first):
    return pl.BlockSpec((pl.Element(n), pl.Element(wide)), lambda i: (first, 0), pipeline_mode=pl.Buffered(1))

def place_matrix(fe, first, n):
    col=lax.broadcasted_iota(jnp.int32,(E,n),1)+first; row=lax.broadcasted_iota(jnp.int32,(E,n),0)*fe
    return jnp.where((col>=row)&(col<row+fe),1.0,0.0).astype(BF)

def units_kernel(fe, first, x_ref, wg_ref, wu_ref, b_ref, w_ref, out_ref, pair_ref):
    x=x_ref[...]; n=wg_ref.shape[0]
    pre=mm(x,wg_ref[...],NT); lift=mm(x,wu_ref[...],NT); back=b_ref[...].astype(F32)
    w=w_ref[...]; hi=w.astype(BF); lo=(w-hi.astype(F32)).astype(BF)
    place=place_matrix(fe,first,n)
    spread=mm(jnp.concatenate([hi,lo],axis=1),jnp.concatenate([place,place],axis=0),NN)
    if first+n>E*fe:
        spread=jnp.where(lax.broadcasted_iota(jnp.int32,spread.shape,1)>=E*fe-first,1.0,spread)
    s=0.5+0.5*jnp.tanh(0.5*pre)
    silu=pre*s
    act=silu*lift
    pair_ref[...]=mm((act*back).astype(BF),place,NT)
    back=back*spread
    out_ref[0]=(back*lift*(s+silu*(1.0-s))).astype(BF)
    out_ref[1]=(back*silu).astype(BF)
    out_ref[2]=(act*spread).astype(BF)

def units(x,packed,back,weight,fe,first,bt):
    T,D=x.shape; n=back.shape[1]; r=weight.shape[1]
    ins=[pl.BlockSpec((bt,D),lambda i:(i,0))]+[once((n,D),lambda i,k=k:(k,0)) for k in range(2)]
    ins+=[pl.BlockSpec((bt,n),lambda i:(i,0)),pl.BlockSpec((bt,r),lambda i:(i,0))]
    outs=[jax.ShapeDtypeStruct((3,T,n),BF),jax.ShapeDtypeStruct((T,r),F32)]
    return pl.pallas_call(functools.partial(units_kernel,fe,first),grid=(T//bt,),in_specs=ins,
        out_specs=[pl.BlockSpec((3,bt,n),lambda i:(0,i,0)),pl.BlockSpec((bt,r),lambda i:(i,0))],out_shape=outs,
        compiler_params=params(1),
        cost_estimate=pl.CostEstimate(flops=4*T*D*n,bytes_accessed=2*(T*D+2*n*D+4*T*n),transcendentals=T*n))(x,packed,packed,back,weight)

def lift_kernel(g_ref,w_ref,o_ref):
    o_ref[...]=mm(g_ref[...],w_ref[...],NT).astype(BF)

def lift_back(g,packed,at,n,bt):
    T,D=g.shape
    return pl.pallas_call(lift_kernel,grid=(T//bt,),
        in_specs=[pl.BlockSpec((bt,D),lambda i:(i,0)),rows_once(n,D,at)],
        out_specs=pl.BlockSpec((bt,n),lambda i:(i,0)),out_shape=jax.ShapeDtypeStruct((T,n),BF),compiler_params=params(1),
        cost_estimate=pl.CostEstimate(flops=2*T*D*n,bytes_accessed=2*(T*D+n*D+T*n),transcendentals=0))(g,packed)

def back_kernel(pairs, added, beside, *refs):
    out=refs[-1]
    acc=None
    if added: acc=refs[0][...].astype(F32)
    rs=refs[added:]
    for k in range(pairs):
        a=rs[2*k]; b=rs[2*k+1]
        a=a[0] if len(a.shape)==3 else a[...]
        p=mm(a,b[...],NN)
        acc=p if acc is None else acc+p
    if beside:
        wide=acc.shape[1]
        out[:,:wide]=acc.astype(out.dtype)
        more=sum(r[...] for r in refs[-1-beside:-1])
        gap=jnp.zeros((acc.shape[0],out.shape[1]-wide-more.shape[1]),F32)
        out[:,wide:]=jnp.concatenate([more,gap],axis=1).astype(out.dtype)
    else:
        out[...]=acc.astype(out.dtype)

def core_kernel(pairs, core_ref, *refs):
    out=refs[-1]
    chips,_,w=out.shape
    for z in range(chips):
        at=pl.ds(pl.multiple_of((2*z+core_ref[0])*w,w),w)
        acc=None
        for k in range(pairs):
            a=refs[2*k]; b=refs[2*k+1]
            p=mm(a[0] if len(a.shape)==3 else a[...],b[:,at],NN)
            acc=p if acc is None else acc+p
        out[z]=acc.astype(BF)

def back(terms, added, out_dtype, bt, beside=(), core=None, chips=0):
    T=terms[0][0].shape[-2]; D=terms[0][2].shape[1]
    ins=[];args=[];fl=0;by=0
    if core is not None:
        ins.append(pl.BlockSpec(memory_space=pltpu.SMEM)); args.append(core)
    if added is not None:
        ins.append(pl.BlockSpec((bt,D),lambda i:(i,0))); args.append(added)
    for st,k,packed,n,at in terms:
        if st.ndim==3: ins.append(pl.BlockSpec((1,bt,n),lambda i,k=k:(k,i,0)))
        else: ins.append(pl.BlockSpec((bt,n),lambda i:(i,0)))
        ins.append(rows_once(n,D,at))
        args+= [st,packed]; fl+=2*T*D*n; by+=2*(T*n+n*D)
    for more in beside:
        ins.append(pl.BlockSpec((bt,more.shape[1]),lambda i:(i,0))); args.append(more)
    body=functools.partial(back_kernel,len(terms),0 if added is None else 1,len(beside))
    if beside:
        shape=(T,D+128); ospec=pl.BlockSpec((bt,D+128),lambda i:(i,0))
    elif core is not None:
        w=D//(2*chips); fl//=2
        shape=(chips,T,w); ospec=pl.BlockSpec((chips,bt,w),lambda i:(0,i,0))
        body=functools.partial(core_kernel,len(terms))
    else:
        shape=(T,D); ospec=pl.BlockSpec((bt,D),lambda i:(i,0))
    return pl.pallas_call(body,grid=(T//bt,),in_specs=ins,out_specs=ospec,out_shape=jax.ShapeDtypeStruct(shape,out_dtype),
        compiler_params=params(1),cost_estimate=pl.CostEstimate(flops=fl,bytes_accessed=by+4*T*D,transcendentals=0))(*args)

def outer_kernel(s_ref,x_ref,*refs):
    refs[-1][...]=mm(s_ref[0],x_ref[...],TN).astype(BF)

def outer(stack,first,count,x,total,at,into=None,bc=512):
    T,D=x.shape; n=stack.shape[2]
    ins=[pl.BlockSpec((1,T,n),lambda k,j:(first+k,0,0)),pl.BlockSpec((T,bc),lambda k,j:(0,j))]
    args=[stack,x]; al={}
    if into is not None:
        ins.append(pl.BlockSpec(memory_space=pl.ANY)); args.append(into); al={2:0}
    return pl.pallas_call(outer_kernel,grid=(count,D//bc),in_specs=ins,
        out_specs=pl.BlockSpec((n,bc),lambda k,j:(at+k,j)),out_shape=jax.ShapeDtypeStruct((total,D),BF),
        input_output_aliases=al,compiler_params=params(2),
        cost_estimate=pl.CostEstimate(flops=2*count*T*D*n,bytes_accessed=2*count*(T*n+n*D+T*D),transcendentals=0))(*args)


def place_columns_kernel(chips, norm, at_ref, *refs):
    pieces=refs[:2*chips]
    refs=refs[2*chips:]
    if norm:
        gain_ref, w_ref = refs[:2]
        out_ref, round_ref, r_ref, proj_ref = refs[-4:]
    else:
        (out_ref,) = refs
    w=pieces[0].shape[1]
    for k in range(2*chips):
        out_ref[:,pl.ds(pl.multiple_of(at_ref[k]*w,w),w)]=pieces[k][...]
    if norm:
        v=out_ref[...].astype(F32)
        r=lax.rsqrt(jnp.mean(v*v,axis=-1,keepdims=True)+EPSILON)
        round_ref[...]=(v*r*gain_ref[...]).astype(BF)
        r_ref[...]=r
        proj_ref[...]=mm(round_ref[...],w_ref[...],NT)

def place_columns(pieces, at, gain=None, packed=None, count=0, rows=None, first=0, into=(), bt=256):
    T,w=pieces[0].shape; n=len(pieces)
    total_rows=rows or T
    start=first//bt
    ins=[pl.BlockSpec(memory_space=pltpu.SMEM)]+[pl.BlockSpec((bt,w),lambda i:(i,0))]*n
    args=[at]+list(pieces)
    wides=[(n*w,BF)]
    if gain is not None:
        ins+=[pl.BlockSpec((1,n*w),lambda i:(0,0)),rows_once(count,n*w,0)]; args+=[gain[None],packed]
        wides+=[(n*w,BF),(1,F32),(count,F32)]
    aliases={len(args)+k:k for k in range(len(into))}
    ins+=[pl.BlockSpec(memory_space=pl.ANY)]*len(into); args+=list(into)
    return pl.pallas_call(functools.partial(place_columns_kernel,n//2,gain is not None),grid=(T//bt,),
        in_specs=ins,out_specs=[pl.BlockSpec((bt,m),lambda i:(i+start,0)) for m,_ in wides],
        out_shape=[jax.ShapeDtypeStruct((total_rows,m),d) for m,d in wides],
        input_output_aliases=aliases,compiler_params=params(1),
        cost_estimate=pl.CostEstimate(flops=(6+2*count)*T*n*w,bytes_accessed=6*T*n*w,transcendentals=T))(*args)

def place_rows_kernel(n, times, at_ref, *refs):
    pieces=refs[:n]; refs=refs[n:]
    if times: w_ref,out_ref,made_ref,sem=refs
    else: out_ref,sem=refs
    rows=pieces[0].shape[0]
    to=[pl.ds(pl.multiple_of(at_ref[k]*rows,rows),rows) for k in range(n)]
    copies=[pltpu.make_async_copy(pieces[k],out_ref.at[to[k]],sem.at[k]) for k in range(n)]
    for c in copies: c.start()
    if times:
        for k in range(n): made_ref[to[k]]=mm(pieces[k][...],w_ref[...],NT).astype(BF)
    for c in copies: c.wait()

def place_rows(pieces, at, weight=None):
    rows,w=pieces[0].shape; n=len(pieces)
    vmem=pl.BlockSpec(memory_space=pltpu.VMEM)
    outs=[jax.ShapeDtypeStruct((n*rows,w),BF)]; specs=[pl.BlockSpec(memory_space=pl.ANY)]; more=[]
    if weight is not None:
        outs.append(jax.ShapeDtypeStruct((n*rows,weight.shape[0]),BF)); specs.append(vmem); more=[weight]
    return pl.pallas_call(functools.partial(place_rows_kernel,n,bool(more)),
        in_specs=[pl.BlockSpec(memory_space=pltpu.SMEM)]+[vmem]*(n+len(more)),
        out_specs=specs,out_shape=outs,
        scratch_shapes=[pltpu.SemaphoreType.DMA((n,))],compiler_params=pltpu.CompilerParams(vmem_limit_bytes=VMEM_LIMIT),
        cost_estimate=pl.CostEstimate(flops=2*n*rows*w*(weight.shape[0] if more else 0),bytes_accessed=4*n*rows*w,transcendentals=0))(at,*pieces,*more)

def norm_rows_kernel(n, at_ref, col_ref, gain_ref, wr_ref, kept_ref, *refs):
    pieces=refs[:n]; round_ref,cols_ref,gating_ref,weight_ref,made,cut,sem,sem2=refs[n:]
    rows=pieces[0].shape[0]; w=cut.shape[2]
    copies=[]
    for k in range(n):
        v=pieces[k][...].astype(F32)
        r=lax.rsqrt(jnp.mean(v*v,axis=-1,keepdims=True)+EPSILON)
        made[k]=(v*r*gain_ref[...]).astype(BF)
        cut[k]=pieces[k][:,pl.ds(pl.multiple_of(col_ref[0]*w,w),w)]
        to=pl.ds(pl.multiple_of(at_ref[k]*rows,rows),rows)
        copies.append(pltpu.make_async_copy(made.at[k],round_ref.at[to],sem.at[k]))
        copies.append(pltpu.make_async_copy(cut.at[k],cols_ref.at[to],sem2.at[k]))
        copies[-2].start(); copies[-1].start()
        logits=mm(made[k],wr_ref[...],NT)
        e=jnp.exp(logits-jnp.max(logits,axis=-1,keepdims=True))
        gating=e/jnp.sum(e,axis=-1,keepdims=True)
        gating_ref[to]=gating
        weight_ref[to]=gating*kept_ref[to]
    for c in copies: c.wait()

def norm_rows(pieces, at, column, w, gain, router, kept):
    rows,wide=pieces[0].shape; n=len(pieces)
    vmem=pl.BlockSpec(memory_space=pltpu.VMEM)
    return pl.pallas_call(functools.partial(norm_rows_kernel,n),
        in_specs=[pl.BlockSpec(memory_space=pltpu.SMEM)]*2+[vmem]*(n+3),
        out_specs=[pl.BlockSpec(memory_space=pl.ANY)]*2+[vmem]*2,
        out_shape=[jax.ShapeDtypeStruct((n*rows,wide),BF),jax.ShapeDtypeStruct((n*rows,w),BF)]+[jax.ShapeDtypeStruct((n*rows,E),F32)]*2,
        scratch_shapes=[pltpu.VMEM((n,rows,wide),BF),pltpu.VMEM((n,rows,w),BF),pltpu.SemaphoreType.DMA((n,)),pltpu.SemaphoreType.DMA((n,))],
        compiler_params=pltpu.CompilerParams(vmem_limit_bytes=VMEM_LIMIT),
        cost_estimate=pl.CostEstimate(flops=6*n*rows*wide,bytes_accessed=4*n*rows*wide,transcendentals=n*rows))(at,column,gain[None],router,kept,*pieces)

def small_kernel(pairs_ref, up_ref, kr_ref, dot_ref, entry_ref, out_ref):
    bt=out_ref.shape[0]
    out_ref[:,:R]=mm(pairs_ref[...],up_ref[...],NT).astype(BF)
    h=DR//2
    kr=kr_ref[...]
    gap=jnp.zeros((bt,DR-1-entry_ref.shape[1]),F32)
    out_ref[:,R:]=jnp.concatenate(
        [kr[:,:h]+kr[:,h:DR],kr[:,DR:DR+h]+kr[:,DR+h:],dot_ref[...],entry_ref[...],gap],axis=1).astype(BF)

def small_terms(pairs, up, kr, dots, entries, bt=512):
    T=pairs.shape[0]
    def rows(a): return pl.BlockSpec((bt,a.shape[1]),lambda i:(i,0))
    return pl.pallas_call(small_kernel,grid=(T//bt,),
        in_specs=[rows(pairs),pl.BlockSpec(up.shape,lambda i:(0,0)),rows(kr),rows(dots),rows(entries)],
        out_specs=pl.BlockSpec((bt,R+DN),lambda i:(i,0)),out_shape=jax.ShapeDtypeStruct((T,R+DN),BF),
        compiler_params=params(1),
        cost_estimate=pl.CostEstimate(flops=2*T*R*pairs.shape[1],bytes_accessed=8*T*R,transcendentals=0))(pairs,up,kr,dots,entries)

def latent_back_kernel(small_ref, proj_ref, gain_ref, cos_ref, sin_ref, delta_ref, dots_ref, gain_delta_ref):
    i=pl.program_id(0)
    at=proj_ref.shape[1]-R-DN
    dl=small_ref[:,:R].astype(F32)
    vl=proj_ref[:,at:at+R]
    rl=lax.rsqrt(jnp.mean(vl*vl,axis=-1,keepdims=True)+EPSILON)
    gain=gain_ref[...]
    part=jnp.sum(dl*vl*rl,axis=0,keepdims=True)
    @pl.when(i==0)
    def _(): gain_delta_ref[...]=part
    @pl.when(i>0)
    def _(): gain_delta_ref[...]+=part
    gd=gain*dl
    head=rl*gd-vl*(rl*rl*rl)*jnp.mean(vl*gd,axis=-1,keepdims=True)
    beyond=small_ref[:,R:]
    row=lax.broadcasted_iota(jnp.int32,(DN,DN),0); col=lax.broadcasted_iota(jnp.int32,(DN,DN),1)
    h=DR//2
    put=jnp.where(((row<h)&(col==row))|((row>=h)&(row<DR)&(col==row+h)),1.0,0.0).astype(BF)
    spread=mm(beyond,put,NN)
    tail=spread*cos_ref[...]-pltpu.roll(spread,DR,1)*sin_ref[...]
    delta_ref[:,:R]=head.astype(BF)
    delta_ref[:,R:]=tail.astype(BF)
    own=jnp.sum(head*vl,axis=-1,keepdims=True)+jnp.sum(tail*proj_ref[:,at+R:],axis=-1,keepdims=True)
    lane=lax.broadcasted_iota(jnp.int32,beyond.shape,1)
    dots_ref[...]=own+jnp.sum(jnp.where(lane==DR,beyond.astype(F32),0.0),axis=-1,keepdims=True)

def latent_back(small, proj, gain, cosine, sine, bt=512):
    T,wide=small.shape; turns=LEN//bt
    return pl.pallas_call(latent_back_kernel,grid=(T//bt,),
        in_specs=[pl.BlockSpec((bt,wide),lambda i:(i,0)),pl.BlockSpec((bt,proj.shape[1]),lambda i:(i,0)),
                  pl.BlockSpec((1,R),lambda i:(0,0)),pl.BlockSpec((bt,DN),lambda i:(i%turns,0)),pl.BlockSpec((bt,DN),lambda i:(i%turns,0))],
        out_specs=[pl.BlockSpec((bt,R+DN),lambda i:(i,0)),pl.BlockSpec((bt,1),lambda i:(i,0)),pl.BlockSpec((1,R),lambda i:(0,0))],
        out_shape=[jax.ShapeDtypeStruct((T,R+DN),BF),jax.ShapeDtypeStruct((T,1),F32),jax.ShapeDtypeStruct((1,R),F32)],
        compiler_params=params(1),
        cost_estimate=pl.CostEstimate(flops=30*T*wide,bytes_accessed=8*T*wide,transcendentals=T))(small,proj,gain,cosine,sine)

def last_pack_kernel(delta_ref, x_ref, w_ref, small_ref, g_ref, latent_ref, more_ref, out_ref):
    n=delta_ref.shape[1]
    d=mm(delta_ref[...],x_ref[...],TN)
    out_ref[:n]=d.astype(BF)
    sums=jnp.sum(w_ref[...].astype(F32)*d,axis=0,keepdims=True)
    row=lax.broadcasted_iota(jnp.int32,(32,DN),0); col=lax.broadcasted_iota(jnp.int32,(32,DN),1)
    at=DR+1
    pick=((row<E)&(col==row+at+2))|((row==E)&(col==at))|((row==E+1)&(col==at+1))
    v=mm(jnp.where(pick,1.0,0.0).astype(BF),small_ref[...],NT)
    line=lax.broadcasted_iota(jnp.int32,v.shape,0)
    v=jnp.where(line==E+1,(v+sums)/g_ref[...],v)
    out_ref[n:n+32]=jnp.where(line==E+2,latent_ref[...],v).astype(BF)
    out_ref[n+32:]=more_ref[...]

def last_pack(delta, x, packed, first, small, gain, latent_row, more, bc=512):
    T,D=x.shape; n=delta.shape[1]
    def cols(a): return pl.BlockSpec((a.shape[0],bc),lambda j:(0,j))
    return pl.pallas_call(last_pack_kernel,grid=(D//bc,),
        in_specs=[pl.BlockSpec((T,n),lambda j:(0,0)),cols(x),
                  pl.BlockSpec((pl.Element(n),pl.Element(bc)),lambda j:(first,j*bc)),pl.BlockSpec((bc,DN),lambda j:(j,R//DN)),cols(gain),cols(latent_row),cols(more)],
        out_specs=pl.BlockSpec((n+32+more.shape[0],bc),lambda j:(0,j)),out_shape=jax.ShapeDtypeStruct((n+32+more.shape[0],D),BF),
        compiler_params=params(1),
        cost_estimate=pl.CostEstimate(flops=2*T*D*n,bytes_accessed=2*(T*D+2*n*D+T*n),transcendentals=0))(delta,x,packed,small,gain,latent_row,more)


def turn(x, cosine, sine):
    return x*cosine+pltpu.roll(x,64,1)*sine

def slot_mask(shape, head):
    lane=lax.broadcasted_iota(jnp.int32,shape,1)
    low=head*(DR//2)
    inside=((lane>=low)&(lane<low+DR//2))|((lane>=low+DR)&(lane<low+DR+DR//2))
    return inside

def causal_scores(q, k, first):
    s=mm(q,k,NT)*SCALE
    row=lax.broadcasted_iota(jnp.int32,s.shape,0)+first
    col=lax.broadcasted_iota(jnp.int32,s.shape,1)
    return jnp.where(col<=row,s,-1e30)

def attend_kernel(heads, proj_ref, up_ref, gain_ref, cos_ref, sin_ref, *refs):
    q_ref, kr_ref, kv_ref, latent_ref, mixed_ref, lse_ref = refs[-6:]
    content=heads*DN
    at=content+DN
    q_ref[:,:content]=proj_ref[:,:content].astype(BF)
    cosine,sine=cos_ref[...],sin_ref[...]
    q_ref[:,content:]=turn(proj_ref[:,content:at],cosine,sine).astype(BF)
    vl=proj_ref[:,at:at+R]
    latent_ref[...]=(vl*lax.rsqrt(jnp.mean(vl*vl,axis=-1,keepdims=True)+EPSILON)*gain_ref[...]).astype(BF)
    kr_ref[...]=turn(proj_ref[:,at+R:],cosine,sine).astype(BF)
    kv_ref[...]=mm(latent_ref[...],up_ref[...],NN).astype(BF)
    kr=kr_ref[...]
    for h in range(heads):
        kc=kv_ref[:,h*(DN+DV):h*(DN+DV)+DN]
        v=kv_ref[:,h*(DN+DV)+DN:(h+1)*(DN+DV)]
        k=jnp.concatenate([kc,jnp.where(slot_mask(kr.shape,h),kr,jnp.zeros_like(kr))],axis=1)
        for i in range(LEN//BLOCK):
            a,b=i*BLOCK,(i+1)*BLOCK
            q=jnp.concatenate([q_ref[a:b,h*DN:(h+1)*DN],q_ref[a:b,content:]],axis=1)
            s=causal_scores(q,k[:b],a)
            m=jnp.max(s,axis=-1,keepdims=True)
            e=jnp.exp(s-m)
            t=jnp.sum(e,axis=-1,keepdims=True)
            p=(e*(1.0/t)).astype(BF)
            mixed_ref[a:b,h*DV:(h+1)*DV]=mm(p,v[:b],NN).astype(BF)
            lse_ref[a:b,h:h+1]=m+jnp.log(t)

def attend(proj, up, gain, cosine, sine, heads, sequence, into=()):
    T=proj.shape[0]; wide=proj.shape[1]
    def rows(n): return pl.BlockSpec((LEN,n),lambda i:(sequence,0))
    def whole(a): return pl.BlockSpec(a.shape,lambda i:(0,0))
    qn=heads*DN+DN
    outs=[(qn,BF),(DN,BF),(heads*(DN+DV),BF),(R,BF),(heads*DV,BF),(heads,F32)]
    args=[proj,up,gain,cosine,sine]
    return pl.pallas_call(functools.partial(attend_kernel,heads),grid=(1,),
        in_specs=[rows(wide)]+[whole(a) for a in args[1:]]+[pl.BlockSpec(memory_space=pl.ANY)]*len(into),
        out_specs=[rows(n) for n,_ in outs],out_shape=[jax.ShapeDtypeStruct((T,n),d) for n,d in outs],
        input_output_aliases={len(args)+k:k for k in range(len(into))},compiler_params=params(1),
        cost_estimate=pl.CostEstimate(flops=LEN*LEN*heads*512,bytes_accessed=LEN*8000,transcendentals=LEN*LEN*heads//2))(*args,*into)

def attend_back_kernel(heads, q_ref, kr_ref, kv_ref, mixed_ref, lse_ref, do_ref, cos_ref, sin_ref, dq_ref, dkv_ref, dkr_ref, dot_ref, dk_acc, dv_acc):
    content=heads*DN
    kr=kr_ref[...]
    for h in range(heads):
        kc=kv_ref[:,h*(DN+DV):h*(DN+DV)+DN]
        v=kv_ref[:,h*(DN+DV)+DN:(h+1)*(DN+DV)]
        mask=slot_mask(kr.shape,h)
        k=jnp.concatenate([kc,jnp.where(mask,kr,jnp.zeros_like(kr))],axis=1)
        for i in reversed(range(LEN//BLOCK)):
            a,b=i*BLOCK,(i+1)*BLOCK
            q=jnp.concatenate([q_ref[a:b,h*DN:(h+1)*DN],q_ref[a:b,content:]],axis=1)
            do=do_ref[a:b,h*DV:(h+1)*DV]
            p=jnp.exp(causal_scores(q,k[:b],a)-lse_ref[a:b,h:h+1])
            dp=mm(do,v[:b],NT)
            along=jnp.sum(do.astype(F32)*mixed_ref[a:b,h*DV:(h+1)*DV].astype(F32),axis=-1,keepdims=True)
            ds=(p*(dp-along)).astype(BF)
            pv=mm(p.astype(BF),do,TN)
            pk=mm(ds,q,TN)
            if i==LEN//BLOCK-1:
                dv_acc[...]=pv; dk_acc[...]=pk
            else:
                dv_acc[:b]+=pv; dk_acc[:b]+=pk
            dq=mm(ds,k[:b],NN)*SCALE
            d=jnp.sum(dq*q.astype(F32),axis=-1,keepdims=True)
            if h==0: dot_ref[a:b]=d
            else: dot_ref[a:b]+=d
            dq_ref[a:b,h*DN:(h+1)*DN]=dq[:,:DN].astype(BF)
            turned=turn(dq[:,DN:],cos_ref[a:b],-sin_ref[a:b])
            turned=jnp.where(mask[:b-a],turned,0.0).astype(BF)
            if h==0: dq_ref[a:b,content:]=turned
            else: dq_ref[a:b,content:]+=turned
        dkv_ref[:,h*(DN+DV):h*(DN+DV)+DN]=(dk_acc[:,:DN]*SCALE).astype(BF)
        dkv_ref[:,h*(DN+DV)+DN:(h+1)*(DN+DV)]=dv_acc[...].astype(BF)
        part=jnp.where(mask,dk_acc[:,DN:]*SCALE,0.0)
        if h==0: dkr_ref[...]=part
        else: dkr_ref[...]+=part

def attend_back(q,kr,kv,mixed,lse,do,cosine,sine,heads):
    T=q.shape[0]
    def rows(n): return pl.BlockSpec((LEN,n),lambda i:(i,0))
    def whole(a): return pl.BlockSpec(a.shape,lambda i:(0,0))
    args=(q,kr,kv,mixed,lse,do)
    outs=[(q.shape[1],BF),(kv.shape[1],BF),(DN,F32),(1,F32)]
    return pl.pallas_call(functools.partial(attend_back_kernel,heads),grid=(T//LEN,),
        in_specs=[rows(a.shape[1]) for a in args]+[whole(cosine),whole(sine)],
        out_specs=[rows(n) for n,_ in outs],out_shape=[jax.ShapeDtypeStruct((T,n),d) for n,d in outs],
        scratch_shapes=[pltpu.VMEM((LEN,2*DN),F32),pltpu.VMEM((LEN,DV),F32)],
        compiler_params=params(1),
        cost_estimate=pl.CostEstimate(flops=T*LEN*heads*1400,bytes_accessed=T*6000,transcendentals=T*LEN*heads//2))(*args,cosine,sine)

def tables():
    position=np.arange(LEN,dtype=np.float32)
    spread=(10000.0**(-np.arange(DR//2,dtype=np.float32)/(DR//2))).astype(np.float32)
    phase=(position[:,None]*spread[None,:]).astype(np.float32)
    c,s=np.cos(phase),np.sin(phase)
    return np.concatenate([c]*4,1).astype(np.float32),np.concatenate([-s,-s,s,s],1).astype(np.float32)


class Line:
    def __init__(self):
        self.n = lax.axis_size("tensor")
        self.chips = self.n // 2
        index = lax.axis_index("tensor")
        self.index = index
        self.z = index // 2
        self.c = index % 2

    def swap(self, a):
        return lax.ppermute(a, "tensor", [(i, i ^ 1) for i in range(self.n)])

    def shift(self, a, step, sources):
        pairs = [
            (2 * s + c, 2 * (s + step) + c)
            for s in sources
            if 0 <= s + step < self.chips
            for c in (0, 1)
        ]
        return lax.ppermute(a, "tensor", pairs)

    def across(self, a, step):
        n = self.chips
        pairs = [(2 * k + c, 2 * ((k + step) % n) + c) for k in range(n) for c in (0, 1)]
        return lax.ppermute(a, "tensor", pairs)

    def pieces(self, own, order):
        n = self.chips
        out, at = [], []
        for k, piece in enumerate(own):
            chip = (self.z - k + n) % n
            out += [piece, self.swap(piece)]
            at += [order(chip, self.c), order(chip, 1 - self.c)]
        return out, jnp.stack(at).astype(jnp.int32)

    def row_pieces(self, own):
        return self.pieces(own, lambda chip, core: core * self.chips + chip)

    def column_pieces(self, own):
        return self.pieces(own, lambda chip, core: chip * 2 + core)

    def half(self, p, core):
        count = p.shape[0] // 2
        return lax.dynamic_slice_in_dim(p, core * count, count, 0)

    def row_scatter(self, p, first, arrived):
        ch = arrived.shape[0] // self.chips
        return Scatter(self, lambda j: total(
            lax.dynamic_slice_in_dim(p, first + j * ch, ch, 0), lax.dynamic_slice_in_dim(arrived, j * ch, ch, 0)
        ))

    def column_scatter(self, mine, arrived):
        return Scatter(self, lambda j: total(
            lax.dynamic_index_in_dim(mine, j, 0, False), lax.dynamic_index_in_dim(arrived, j, 0, False)
        ))

    def row_start(self, rows):
        ch = rows // self.n
        return (self.c * self.chips + self.z) * ch, ch


def total(mine, arrived):
    return (mine.astype(F32) + arrived.astype(F32)).astype(BF)


class Gather:
    def __init__(self, line, block):
        self.line, self.left, self.right = line, [block], [block]

    def start(self):
        n, k = self.line.chips, len(self.left)
        return (
            self.line.shift(self.left[-1], 1, range(k - 1, n)),
            self.line.shift(self.right[-1], -1, range(0, n - k + 1)),
        )

    def take(self, arrived):
        self.left.append(arrived[0])
        self.right.append(arrived[1])

    def result(self):
        n, z = self.line.chips, self.line.z
        return self.left[:1] + [jnp.where(z >= k, self.left[k], self.right[n - k]) for k in range(1, n)]


class Scatter:
    def __init__(self, line, block):
        self.line, self.block, self.step, self.left, self.right = line, block, 0, None, None

    def start(self):
        self.step += 1
        n, s, z = self.line.chips, self.step, self.line.z
        up = self.block(jnp.clip(n - s + z, 0, n - 1))
        down = self.block(jnp.clip(z - (n - s), 0, n - 1))
        if self.left is not None:
            up, down = total(up, self.left), total(down, self.right)
        return self.line.shift(up, 1, range(0, s)), self.line.shift(down, -1, range(n - s, n))

    def take(self, arrived):
        self.left, self.right = arrived

    def result(self):
        return self.block(self.line.z).astype(F32) + self.left.astype(F32) + self.right.astype(F32)


class GatherAtOnce:
    def __init__(self, line, block):
        self.line, self.block = line, block

    def start(self):
        return [self.line.across(self.block, k) for k in range(1, self.line.chips)]

    def take(self, arrived):
        self.arrived = list(arrived)

    def result(self):
        return [self.block] + self.arrived


class ScatterAtOnce:
    def __init__(self, line, block):
        self.line, self.block = line, block

    def start(self):
        n, z = self.line.chips, self.line.z
        return [self.line.across(self.block((z + k) % n), k) for k in range(1, n)]

    def take(self, arrived):
        self.arrived = list(arrived)

    def result(self):
        return sum((a.astype(F32) for a in self.arrived), self.block(self.line.z).astype(F32))


def beside(moves, job=None):
    arrived, done = lax.optimization_barrier(([m.start() for m in moves], job() if job else None))
    for move, a in zip(moves, arrived):
        move.take(a)
    return done


def steps(move, count, jobs=()):
    made = []
    for k in range(count):
        made.append(beside([move], jobs[k] if k < len(jobs) else None))
    return made


def gather_rows(packed):
    return lax.all_gather(packed, "dp", axis=1, tiled=True)


def scatter_rows(packed):
    return lax.psum_scatter(packed, "dp", scatter_dimension=1, tiled=True)


def split_rows(packed, counts):
    out, at = [], 0
    for count in counts:
        out.append(packed[at : at + count])
        at += count
    return out


def ranks(mask):
    number = mask.shape[0]
    block = 128
    pieces = mask.reshape(number // block, block, E).astype(BF)
    lower = jnp.tril(jnp.ones((block, block), BF), -1)
    inside = jnp.einsum("ij,bje->bie", lower, pieces, preferred_element_type=F32)
    totals = jnp.sum(pieces.astype(F32), axis=1).astype(BF)
    ahead = jnp.tril(jnp.ones((number // block, number // block), BF), -1)
    before = dot(ahead, totals, 1, 0)
    return (inside + before[:, None, :]).reshape(number, E)


def per_device(
    layer_input, cotangent, first_gain, query_weight, latent_down, latent_gain, latent_up,
    output_weight, second_gain, router_weight, expert_gate, expert_up, expert_down,
    shared_gate, shared_up, shared_down, routes,
):
    line = Line()
    n_dp = lax.axis_size("dp")
    wide = D // n_dp
    number = layer_input.shape[0]
    heads_here = output_weight.shape[0] // DV
    fe = expert_down.shape[1]
    my_columns = layer_input.shape[1]
    column_start = line.index * my_columns
    row_start, row_count = line.row_start(number)

    half = DR // 2
    spare_heads = 2 - heads_here
    up_rows = latent_up.size // wide
    by_head = query_weight.T.reshape(heads_here, DN + DR, wide)
    blank = jnp.zeros((spare_heads * half, wide), BF)
    gains = jnp.zeros((16, wide), BF)
    gains = gains.at[0].set(first_gain).at[1].set(second_gain)
    gains = gains.at[2, : latent_gain.shape[0]].set(latent_gain)
    down = latent_down.T
    queries_wide = heads_here * DN + DN
    latent_wide = R + DN
    attend_pack = [
        by_head[:, :DN].reshape(heads_here * DN, wide),
        by_head[:, DN : DN + half].reshape(heads_here * half, wide), blank,
        by_head[:, DN + half :].reshape(heads_here * half, wide), blank,
        down[: R + half], down[R : R + half], down[R + half :], down[R + half :],
        latent_up.reshape(up_rows, wide), gains, router_weight.T, output_weight,
    ]
    attend_packed = gather_rows(jnp.concatenate([m for m in attend_pack if m.shape[0]], axis=0))
    wproj, wup, gains, wr, wo = split_rows(
        attend_packed, [queries_wide + latent_wide, up_rows, 16, E, output_weight.shape[0]]
    )
    wup = wup.reshape(up_rows, n_dp, wide).transpose(1, 0, 2).reshape(R, -1)
    first_g = gains[0].astype(F32)
    second_g = gains[1].astype(F32)
    latent_g = gains[2].reshape(n_dp, wide)[:, : R // n_dp].reshape(R).astype(F32)
    cosine, sine = (jnp.asarray(table) for table in tables())

    n_units = E * fe + shared_down.shape[0]
    n0 = n_units // 2 // 256 * 256
    n1 = n_units - n0
    last_step = line.chips - 1
    gate = expert_gate.transpose(0, 2, 1).reshape(E * fe, wide)
    up = expert_up.transpose(0, 2, 1).reshape(E * fe, wide)
    move = Gather(line, layer_input[:LEN])
    downs, early, late = steps(move, 3, (
        lambda: jnp.concatenate([expert_down.reshape(E * fe, wide), shared_down], axis=0),
        lambda: jnp.concatenate([gate[:n0], up[:n0]], axis=0),
        lambda: jnp.concatenate([gate[n0:], shared_gate.T, up[n0:], shared_up.T], axis=0),
    ))
    steps(move, last_step - 3)
    downs, early, late = gather_rows(downs), gather_rows(early), gather_rows(late)

    tile = 256
    core = line.c.reshape(1).astype(jnp.int32)
    placed, attended = (), ()

    def place(move, sequence):
        pieces, at = line.column_pieces(move.result())
        return place_columns(
            pieces, at, first_g, attend_packed, queries_wide + latent_wide, number, sequence * LEN, placed
        )

    def attention(sequence):
        return attend(placed[3], wup, latent_g[None], cosine, sine, heads_here, sequence, attended)

    for sequence in range(1, number // LEN):
        ahead, after = move, layer_input[sequence * LEN : (sequence + 1) * LEN]
        ahead.left[-1], ahead.right[-1], after = lax.optimization_barrier((ahead.left[-1], ahead.right[-1], after))
        move = Gather(line, after)
        beside([move])
        placed = beside([move], lambda: place(ahead, sequence - 1))
        steps(move, last_step - 3)
        attended = beside([move], lambda: attention(sequence - 1))
    move.left[-1], move.right[-1], cotangent = lax.optimization_barrier((move.left[-1], move.right[-1], cotangent))
    grad_move = Gather(line, cotangent)
    placed = place(move, number // LEN - 1)
    attended = beside([grad_move], lambda: attention(number // LEN - 1))
    rows, first_round, r1, proj = placed
    q, kr, kv, latent, mixed, log_total = attended
    arrived = line.swap(dot(line.half(mixed, 1 - line.c), wo, 1, 0, BF))
    move = line.row_scatter(dot(line.half(mixed, line.c), wo, 1, 0, BF), 0, arrived)
    for _ in range(last_step - 1):
        beside([move, grad_move])
    (grad,) = beside([move], lambda: place_columns(*line.column_pieces(grad_move.result())))
    hidden_rows = (
        lax.dynamic_slice_in_dim(rows, row_start, row_count, 0).astype(F32) + move.result()
    ).astype(BF)
    move = Gather(line, hidden_rows)
    back0, back1 = steps(move, 2, (
        lambda: lift_back(grad, downs, 0, n0, tile),
        lambda: lift_back(grad, downs, n0, n1, tile),
    ))
    steps(move, last_step - 2)
    hidden_pieces, hidden_at = line.row_pieces(move.result())
    named = jnp.any(routes[:, :, None] == jnp.arange(E, dtype=jnp.int32)[None, None, :], axis=1)
    kept = jnp.where(named & (ranks(named) < CAP), 1.0, 0.0)
    second_round, hidden_columns, gating, weight = norm_rows(
        hidden_pieces, hidden_at, line.index.reshape(1).astype(jnp.int32), my_columns, second_g, wr, kept
    )

    stack0, pair0 = units(second_round, early, back0, weight, fe, 0, tile)
    deltas = outer(stack0, 0, 2, second_round, 3 * n0, 0)
    deltas = outer(stack0, 2, 1, grad, 3 * n0, 2, deltas)
    deltas, stack0 = lax.optimization_barrier((deltas, stack0))
    early_sums = scatter_rows(deltas)
    stack1, pair1 = units(second_round, late, back1, weight, fe, n0, tile)
    second_terms = back(
        [(stack0, 0, early, n0, 0), (stack0, 1, early, n0, n0), (stack1, 0, late, n1, 0), (stack1, 1, late, n1, n1)],
        None, BF, tile, (pair0, pair1),
    )

    branch_terms = [(stack0, 2, downs, n0, 0), (stack1, 2, downs, n1, n0)]
    move = line.row_scatter(
        second_terms, line.c * (number // 2), line.swap(line.half(second_terms, 1 - line.c))
    )
    deltas = beside([move], lambda: outer(stack1, 0, 1, second_round, 3 * n1, 0))
    deltas = beside([move], lambda: outer(stack1, 1, 1, second_round, 3 * n1, 1, deltas))
    branch_theirs = beside([move], lambda: back(branch_terms, None, BF, tile, (), 1 - core, line.chips))
    steps(move, last_step - 3)
    summed = move.result()

    def own_rows(a):
        return lax.dynamic_slice_in_dim(a, row_start, row_count, 0)

    gating_rows, kept_rows, x2 = own_rows(gating), own_rows(kept), own_rows(second_round)
    u = summed[:, D : D + E] * kept_rows
    logits_delta = gating_rows * (u - jnp.sum(gating_rows * u, axis=-1, keepdims=True))
    d2 = summed[:, :D] + dot(logits_delta.astype(BF), wr, 1, 0)
    v2 = hidden_rows.astype(F32)
    r2 = lax.rsqrt(jnp.mean(v2 * v2, axis=-1, keepdims=True) + EPSILON)
    vgd = jnp.mean(v2 * second_g * d2, axis=-1, keepdims=True)
    hidden_delta = own_rows(grad).astype(F32) + r2 * second_g * d2 - v2 * (r2**3) * vgd
    move = Gather(line, hidden_delta.astype(BF))
    branch_mine, branch_arrived = beside([move], lambda: (
        back(branch_terms, None, BF, tile, (), core, line.chips), line.swap(branch_theirs)
    ))
    branch_move = line.column_scatter(branch_mine, branch_arrived)
    deltas = beside([move, branch_move], lambda: outer(stack1, 2, 1, grad, 3 * n1, 2, deltas))
    router_delta = dot(x2, logits_delta.astype(BF), 0, 0)
    second_gain_delta = jnp.sum(d2 * v2 * r2, axis=0)
    early_sums, deltas, move.left[-1] = lax.optimization_barrier((early_sums, deltas, move.left[-1]))
    late_sums = scatter_rows(deltas)
    for _ in range(last_step - 2):
        beside([move, branch_move])
    delta_pieces, delta_at = line.row_pieces(move.result())

    def heads_back():
        placed, delta_mixed = place_rows(delta_pieces, delta_at, wo)
        return placed, attend_back(q, kr, kv, mixed, log_total, delta_mixed, cosine, sine, heads_here)

    hidden_delta, heads = beside([branch_move], heads_back)
    layer_output = (hidden_columns.astype(F32) + branch_move.result()).astype(BF)
    delta_queries, delta_pairs, delta_kr, query_dot = heads
    delta_wq = dot(delta_queries, first_round, 0, 0)
    query_gain = jnp.sum(wproj[:queries_wide].astype(F32) * delta_wq, axis=0)
    per_entry = jnp.concatenate([second_gain_delta[:, None], query_gain[:, None], router_delta], axis=1)
    if number > D:
        per_entry = jnp.concatenate([per_entry, jnp.zeros((number - D, E + 2), F32)], axis=0)
    small, late_queries = lax.optimization_barrier(
        (small_terms(delta_pairs, wup, delta_kr, query_dot, per_entry), delta_queries)
    )
    move = line.row_scatter(small, line.c * (number // 2), line.swap(line.half(small, 1 - line.c)))

    move = ScatterAtOnce(line, move.block)

    def attend_deltas():
        delta_wup = dot(latent, delta_pairs, 0, 0, BF)
        return jnp.concatenate(
            [delta_wq.astype(BF),
             delta_wup.reshape(n_dp, up_rows, wide).transpose(1, 0, 2).reshape(up_rows, D),
             dot(mixed, hidden_delta, 0, 0, BF)], axis=0)

    def first_products(which, queries):
        return back([(queries, 0, attend_packed, queries_wide, 0)], None, BF, tile, (), which, line.chips)

    deltas, theirs = beside([move], lambda: (attend_deltas(), first_products(1 - core, late_queries)))
    small, layer_output, late_queries = lax.optimization_barrier(
        (move.result().astype(BF), layer_output, late_queries)
    )
    move = GatherAtOnce(line, small)

    mine, arrived = beside([move], lambda: (first_products(core, late_queries), line.swap(theirs)))
    small_pieces, small_at = line.row_pieces(move.result())
    small_pieces, late_sums, mine = lax.optimization_barrier((small_pieces, late_sums, mine))
    first_move = line.column_scatter(mine, arrived)
    wld = wproj[queries_wide:]

    def last():
        (small,) = place_rows(small_pieces, small_at)
        delta_latent, dots, gain_delta = latent_back(small, proj, latent_g[None], cosine, sine)
        latent_row = jnp.pad(gain_delta.reshape(n_dp, R // n_dp), ((0, 0), (0, wide - R // n_dp))).reshape(1, D)
        return delta_latent, dots, last_pack(
            delta_latent, first_round, attend_packed, queries_wide, small, first_g[None], latent_row, deltas)

    delta_latent, dots, pack = beside([first_move], last)
    steps(first_move, last_step - 1)
    first_share = first_move.result()
    dwld, vectors, dwq, dwup, dwo = split_rows(
        scatter_rows(pack).astype(F32), [latent_wide, 32, queries_wide, up_rows, output_weight.shape[0]]
    )
    content = heads_here * DN
    dwq = jnp.concatenate(
        [dwq[:content].reshape(heads_here, DN, wide),
         dwq[content : content + heads_here * half].reshape(heads_here, half, wide),
         dwq[content + DR : content + DR + heads_here * half].reshape(heads_here, half, wide)], axis=1
    ).reshape(heads_here * (DN + DR), wide)
    dwld = jnp.concatenate([dwld[: R + half], dwld[R + DR : R + DR + half]], axis=0)

    first_share = first_share + dot(
        delta_latent, lax.dynamic_slice_in_dim(wld, column_start, my_columns, 1), 1, 0
    )
    vc = layer_input.astype(F32)
    gc = lax.dynamic_slice_in_dim(first_g, column_start, my_columns, 0)
    input_delta = (
        lax.dynamic_slice_in_dim(hidden_delta, column_start, my_columns, 1).astype(F32)
        + r1 * gc * first_share
        - vc * (r1 * r1) * (dots / D)
    )

    def units_delta(k):
        return early_sums[k * n0 : (k + 1) * n0], late_sums[k * n1 : (k + 1) * n1]

    def expert_delta(k):
        first, second = units_delta(k)
        return jnp.concatenate([first, second[: E * fe - n0]], axis=0).astype(F32).reshape(E, fe, wide)

    def shared_delta(k):
        return units_delta(k)[1][E * fe - n0 :].astype(F32)

    return (
        layer_output, input_delta, vectors[E + 1], dwq.T, dwld.T, vectors[E + 2, : R // n_dp],
        dwup.reshape(latent_up.shape), dwo, vectors[E], vectors[:E].T,
        expert_delta(0).transpose(0, 2, 1), expert_delta(1).transpose(0, 2, 1), expert_delta(2),
        shared_delta(0).T, shared_delta(1).T, shared_delta(2),
    )


def solution(mesh):
    in_specs = (
        P("dp", "tensor"), P("dp", "tensor"), P("dp"), P("dp", "tensor"), P("dp", None), P("dp"),
        P("dp", "tensor"), P("tensor", "dp"), P("dp"), P("dp", None), P(None, "dp", "tensor"),
        P(None, "dp", "tensor"), P(None, "tensor", "dp"), P("dp", "tensor"), P("dp", "tensor"),
        P("tensor", "dp"), P("dp", None),
    )
    out_specs = (
        P("dp", "tensor"), P("dp", "tensor"), P("dp"), P("dp", "tensor"), P("dp", None), P("dp"),
        P("dp", "tensor"), P("tensor", "dp"), P("dp"), P("dp", None), P(None, "dp", "tensor"),
        P(None, "dp", "tensor"), P(None, "tensor", "dp"), P("dp", "tensor"), P("dp", "tensor"),
        P("tensor", "dp"),
    )
    return jax.shard_map(
        per_device, mesh=mesh, in_specs=in_specs, out_specs=out_specs, check_vma=False
    )
```
